32 devices in a mesh: dp: 16 (over z, y, x), tensor: 2 (over core).
Axes of the slice: x: 2, y: 2, z: 4, core: 2. Of those that a mesh axis runs over, the one named last changes fastest.
Arguments:
- tokens: bfloat16 [50176, 768], P(('dp', 'tensor')), may hold values from -6 to 6
- cotangent: bfloat16 [50176, 768], P(('dp', 'tensor')), may hold values from -6 to 6
- attn_qkv: bfloat16 [1, 2, 768, 3, 768], P(None, None, 'dp', None, 'tensor'), may hold values from -0.21875 to 0.21875
- attn_out: bfloat16 [1, 2, 768, 768], P(None, None, 'tensor', 'dp'), may hold values from -0.875 to 0.875
- mlp_in: bfloat16 [1, 768, 3072], P(None, 'dp', 'tensor'), may hold values from -0.21875 to 0.21875
- mlp_out: bfloat16 [1, 3072, 768], P(None, 'tensor', 'dp'), may hold values from -0.109375 to 0.109375
- norm_gains: float32 [1, 3, 768], P(None, None, ('dp', 'tensor')), may hold values from 0.5 to 1.5
- biases: float32 [1, 10, 768], P(None, None, ('dp', 'tensor')), may hold values from -4 to 4
- hidden_bias: float32 [1, 3072], P(None, ('dp', 'tensor')), may hold values from -6 to 6
Outputs:
- output: bfloat16 [50176, 768], P(('dp', 'tensor'))
- grad_tokens: float32 [50176, 768], P(('dp', 'tensor'))
- grad_attn_qkv: float32 [1, 2, 768, 3, 768], P(None, None, 'dp', None, 'tensor')
- grad_attn_out: float32 [1, 2, 768, 768], P(None, None, 'tensor', 'dp')
- grad_mlp_in: float32 [1, 768, 3072], P(None, 'dp', 'tensor')
- grad_mlp_out: float32 [1, 3072, 768], P(None, 'tensor', 'dp')
- grad_norm_gains: float32 [1, 3, 768], P(None, None, ('dp', 'tensor'))
- grad_biases: float32 [1, 10, 768], P(None, None, ('dp', 'tensor'))
- grad_hidden_bias: float32 [1, 3072], P(None, ('dp', 'tensor'))
The draws below stay inside these ranges and needn't reach their ends.
All inputs are finite; a program needn't handle non-finite values.
Results may differ from the reference program's by a relative error of at most 0.023.
Values may be sent and summed in bfloat16 or wider, within the bound.
A program may use at most 320 MiB of HBM per device.

```python
import jax
import jax.numpy as jnp
from jax import lax

D = 768
HEAD = 64
FF = 3072
FRAMES = 16
PATCHES = 196
LAYERS = 1
TOKENS = 50176
N_TENSOR = 2


def steps_of(rng, shape, cuts, smallest, high):
    loudness = 1.0
    for position, parts in cuts:
        draws = jax.random.uniform(jax.random.fold_in(jax.random.fold_in(rng, 6), position), (parts,), jnp.float32, smallest / len(cuts), high / len(cuts))
        loudness = loudness * jnp.repeat(jnp.exp(draws), shape[position] // parts).reshape((-1,) + (1,) * (len(shape) - 1 - position))
    return loudness


def noise(rng, shape, scale, limit, split=(), dtype=jnp.bfloat16):
    level = steps_of(rng, shape, split, -0.22, 0.18) if split else 1.0
    array = jax.random.normal(rng, shape, jnp.float32) * scale * level
    return jnp.minimum(jnp.maximum(array, -limit), limit).astype(dtype)


def setup_inputs(seed: int = 0) -> dict:
    seeds = jax.random.split(jax.random.key(seed), 10)
    return {
        "tokens": noise(seeds[0], (TOKENS, D), 1.0, 6.0, ((0, 32),)),
        "cotangent": noise(seeds[1], (TOKENS, D), 1.0, 6.0, ((0, 32),)),
        "attn_qkv": noise(seeds[2], (LAYERS, 2, D, 3, D), D ** -0.5, 0.21875, ((2, 16), (4, 2))),
        "attn_out": noise(seeds[3], (LAYERS, 2, D, D), (D // 16) ** -0.5, 0.875, ((2, 2), (3, 16))),
        "mlp_in": noise(seeds[4], (LAYERS, D, FF), D ** -0.5, 0.21875, ((1, 16), (2, 2))),
        "mlp_out": noise(seeds[5], (LAYERS, FF, D), FF ** -0.5, 0.109375, ((1, 2), (2, 16))),
        "norm_gains": jnp.clip(1.0 + 0.1 * jax.random.normal(seeds[6], (LAYERS, 3, D), jnp.float32), 0.5, 1.5),
        "biases": noise(seeds[7], (LAYERS, 10, D), 0.3, 4.0, ((2, 32),), jnp.float32),
        "hidden_bias": noise(seeds[8], (LAYERS, FF), 0.5, 6.0, ((1, 32),), jnp.float32),
    }


@jax.custom_vjp
def low(v):
    return lax.optimization_barrier(v.astype(jnp.bfloat16)).astype(jnp.float32)

@jax.custom_vjp
def low_back(v):
    return v

def low_keep(v):
    return (low(v), None)

def low_pass(kept, grad):
    return (grad,)

def back_keep(v):
    return (v, None)

def back_low(kept, grad):
    return (low(grad),)
low.defvjp(low_keep, low_pass)
low_back.defvjp(back_keep, back_low)
EPSILON = 1e-06
HIGHEST = lax.Precision.HIGHEST
SCORE_FORMS = (('cfphe,cfqhe->cfhpq', 'cfhpq,cfqhe->cfphe', -1), ('cfphe,cgphe->chfgp', 'chfgp,cgphe->cfphe', -2))

def layer_norm(stream, gain_row, shift_row):
    row_mean = lax.optimization_barrier(jnp.mean(stream, axis=-1, keepdims=True))
    centred = stream - row_mean
    variance = lax.optimization_barrier(jnp.mean(centred * centred, axis=-1, keepdims=True))
    return centred * lax.rsqrt(variance + EPSILON) * gain_row + shift_row

def to_heads(row_block):
    clip_count = row_block.shape[0] // (FRAMES * PATCHES)
    return row_block.reshape(clip_count, FRAMES, PATCHES, row_block.shape[1] // HEAD, HEAD)

def gelu_exact(pre_act):
    return jax.nn.gelu(pre_act, approximate=False)

def attend(stream, sub_kind, qkv_all, out_all, gain_all, bias_all):
    row_base = 4 * sub_kind
    score_form, out_form, soft_axis = SCORE_FORMS[sub_kind]
    normed = low(layer_norm(stream, gain_all[sub_kind], bias_all[row_base]))
    col_width = D // N_TENSOR
    summed = jnp.zeros(stream.shape, jnp.float32)
    for group_index in range(N_TENSOR):
        col_start = group_index * col_width
        col_stop = col_start + col_width
        own_normed = low_back(normed)
        queries = jnp.dot(own_normed, qkv_all[sub_kind, :, 0, col_start:col_stop], precision=HIGHEST)
        queries = low_back(low(queries + bias_all[row_base + 1, col_start:col_stop]))
        key_rows = low_back(low(jnp.dot(own_normed, qkv_all[sub_kind, :, 1, col_start:col_stop], precision=HIGHEST)))
        values = jnp.dot(own_normed, qkv_all[sub_kind, :, 2, col_start:col_stop], precision=HIGHEST)
        values = low_back(low(values + bias_all[row_base + 2, col_start:col_stop]))
        scores = jnp.einsum(score_form, to_heads(queries), to_heads(key_rows), precision=HIGHEST)
        scores = low_back(scores * HEAD ** (-0.5))
        attn_probs = jax.nn.softmax(scores, axis=soft_axis)
        mixture = jnp.einsum(out_form, low(attn_probs), to_heads(values), precision=HIGHEST)
        mixture = low_back(low(mixture.reshape(queries.shape)))
        summed = summed + low(jnp.dot(mixture, out_all[sub_kind, col_start:col_stop, :], precision=HIGHEST))
    return stream + low_back(summed) + bias_all[row_base + 3]

def feed_forward(stream, in_weight, down_weight, gain_all, bias_all, hidden_all):
    normed = low(layer_norm(stream, gain_all[2], bias_all[8]))
    unit_width = FF // N_TENSOR
    summed = jnp.zeros(stream.shape, jnp.float32)
    for group_index in range(N_TENSOR):
        unit_start = group_index * unit_width
        unit_stop = unit_start + unit_width
        own_normed = low_back(normed)
        pre_act = jnp.dot(own_normed, in_weight[:, unit_start:unit_stop], precision=HIGHEST)
        pre_act = low_back(pre_act + hidden_all[unit_start:unit_stop])
        activated = low_back(low(gelu_exact(pre_act)))
        summed = summed + low(jnp.dot(activated, down_weight[unit_start:unit_stop, :], precision=HIGHEST))
    return stream + low_back(summed) + bias_all[9]

def clip_forward(stream, params):
    qkv_w, out_w, in_w, down_w, gains_w, bias_w, hidden_w = params
    for layer_index in range(LAYERS):
        for sub_kind in range(2):
            stream = attend(stream, sub_kind, qkv_w[layer_index], out_w[layer_index], gains_w[layer_index], bias_w[layer_index])
        stream = feed_forward(stream, in_w[layer_index], down_w[layer_index], gains_w[layer_index], bias_w[layer_index], hidden_w[layer_index])
    return stream

def run_all(inputs, params):
    checked = jax.checkpoint(clip_forward)
    return lax.map(lambda clip_rows: checked(clip_rows, params), inputs)

def reference(tokens, cotangent, attn_qkv, attn_out, mlp_in, mlp_out, norm_gains, biases, hidden_bias):
    clip_tokens = FRAMES * PATCHES
    inputs = tokens.astype(jnp.float32).reshape(-1, clip_tokens, D)
    params = (attn_qkv.astype(jnp.float32), attn_out.astype(jnp.float32), mlp_in.astype(jnp.float32), mlp_out.astype(jnp.float32), norm_gains.astype(jnp.float32), biases.astype(jnp.float32), hidden_bias.astype(jnp.float32))
    outputs, pullback = jax.vjp(run_all, inputs, params)
    grad_inputs, grad_params = pullback(cotangent.astype(jnp.float32).reshape(outputs.shape))
    return (outputs.reshape(tokens.shape).astype(jnp.bfloat16), grad_inputs.reshape(tokens.shape), grad_params[0], grad_params[1], grad_params[2], grad_params[3], grad_params[4], grad_params[5], grad_params[6])
```

```python
import functools
import jax
import jax.numpy as jnp
from jax import lax
from jax.experimental import pallas as pl
from jax.experimental.pallas import tpu as pltpu
from jax.sharding import PartitionSpec as P

HEAD = 64
FRAMES = 16
PATCHES = 196
PAD = 208
EPSILON = 1e-06
BF = jnp.bfloat16
F32 = jnp.float32
NN = (((1,), (0,)), ((), ()))
NT = (((1,), (1,)), ((), ()))
TN = (((0,), (0,)), ((), ()))
VMEM_BYTES = 60 * 1024 * 1024


def dot(a, b, dims):
    return lax.dot_general(a, b, dims, preferred_element_type=F32)


def norm_parts(x):
    mean = jnp.mean(x, axis=-1, keepdims=True)
    centred = x - mean
    var = jnp.mean(centred * centred, axis=-1, keepdims=True)
    rstd = lax.rsqrt(var + EPSILON)
    return centred * rstd, rstd


def norm_back(grad_normed, xhat, rstd, gain):
    scaled = grad_normed * gain
    first = jnp.mean(scaled, axis=-1, keepdims=True)
    second = jnp.mean(scaled * xhat, axis=-1, keepdims=True)
    return rstd * (scaled - first - xhat * second)


def split_halves(pair):
    lane = lax.broadcasted_iota(jnp.int32, pair.shape, 1)
    zero = jnp.zeros_like(pair)
    return jnp.where(lane < HEAD, pair, zero), jnp.where(lane < HEAD, zero, pair)


def project(normed, w_ref, vec_ref, row_base, cols):
    parts = []
    for g in range(2):
        w = w_ref[g, :, 0 : 3 * cols]
        qkv = dot(normed, w, NN)
        bq = vec_ref[row_base + 1 : row_base + 2, g * cols : (g + 1) * cols]
        bv = vec_ref[row_base + 2 : row_base + 3, g * cols : (g + 1) * cols]
        q = (qkv[:, :cols] + bq).astype(BF) * BF(0.125)
        k = qkv[:, cols : 2 * cols].astype(BF)
        v = (qkv[:, 2 * cols :] + bv).astype(BF)
        parts.append((q, k, v))
    return parts


def heads_forward(q, k, v, mask):
    exps, sums, outs = [], [], []
    for qh in split_halves(q):
        s = dot(qh, k, NT)
        s = jnp.where(mask, s, -1e30)
        top = jnp.max(s, axis=-1, keepdims=True)
        e = jnp.exp(s - top)
        recip = 1.0 / jnp.sum(e, axis=-1, keepdims=True)
        eb = e.astype(BF)
        outs.append(dot(eb, v, NN) * recip)
        exps.append(eb)
        sums.append(recip)
    lane = lax.broadcasted_iota(jnp.int32, q.shape, 1)
    return jnp.where(lane < HEAD, outs[0], outs[1]), exps, sums


def heads_backward(q, k, v, o, do, exps, recips):
    prod = do.astype(F32) * o.astype(F32)
    dq = dk = dv = None
    qs, ks, ps = split_halves(q), split_halves(k), split_halves(prod)
    dos = split_halves(do)
    for h in range(2):
        r = recips[h]
        delta = jnp.sum(ps[h], axis=-1, keepdims=True) * r
        dor = (dos[h].astype(F32) * r).astype(BF)
        dp = dot(dor, v, NT)
        e = exps[h]
        ds = (e.astype(F32) * (dp - delta)).astype(BF)
        dq_h = dot(ds, ks[h], NN)
        dk_h = dot(ds, qs[h], TN)
        dv_h = dot(e, dor, TN)
        dq = dq_h if dq is None else dq + dq_h
        dk = dk_h if dk is None else dk + dk_h
        dv = dv_h if dv is None else dv + dv_h
    return (dq * 0.125).astype(BF), dk.astype(BF), dv.astype(BF)


def spatial_mask():
    return lax.broadcasted_iota(jnp.int32, (PAD, PAD), 1) < PATCHES


def spatial_fwd_kernel(x_ref, w_ref, vec_ref, s_ref, qkv_ref, mix_ref, p_ref, r_ref):
    cols = w_ref.shape[2] // 4
    x = x_ref[0].astype(F32)
    xhat, _ = norm_parts(x)
    normed = (xhat * vec_ref[10:11, :] + vec_ref[0:1, :]).astype(BF)
    mask = spatial_mask()
    branch = vec_ref[3:4, :]
    lane = lax.broadcasted_iota(jnp.int32, (PAD, 128), 1)
    recips = jnp.zeros((PAD, 128), F32)
    for g, (q, k, v) in enumerate(project(normed, w_ref, vec_ref, 0, cols)):
        qkv_ref[0, g, :, 0:cols] = q
        qkv_ref[0, g, :, cols : 2 * cols] = k
        qkv_ref[0, g, :, 2 * cols : 3 * cols] = v
        mixes = []
        for j in range(cols // 128):
            sl = slice(128 * j, 128 * (j + 1))
            mix, exps, rec = heads_forward(q[:, sl], k[:, sl], v[:, sl], mask)
            mixes.append(mix.astype(BF))
            for h in range(2):
                head = (g * (cols // 128) + j) * 2 + h
                p_ref[0, head] = exps[h]
                recips = jnp.where(lane == head, rec[h], recips)
        mix = jnp.concatenate(mixes, axis=1)
        mix_ref[0, g] = mix
        branch = branch + dot(mix, w_ref[g, :, 3 * cols : 4 * cols], NT)
    r_ref[0] = recips
    s_ref[0] = x + branch


def spatial_fwd(x, weights, section, vec):
    frames = x.shape[0]
    D = x.shape[2]
    cols = D // 2
    heads = D // HEAD
    whole = lambda *shape: pl.BlockSpec(shape, lambda i: (0,) * len(shape))
    return pl.pallas_call(
        spatial_fwd_kernel,
        grid=(frames,),
        in_specs=[
            pl.BlockSpec((1, PAD, D), lambda i: (i, 0, 0)),
            pl.BlockSpec((2, D, 4 * cols), lambda i: (0, 0, section)),
            whole(*vec.shape),
        ],
        out_specs=[
            pl.BlockSpec((1, PAD, D), lambda i: (i, 0, 0)),
            pl.BlockSpec((1, 2, PAD, 3 * cols), lambda i: (i, 0, 0, 0)),
            pl.BlockSpec((1, 2, PAD, cols), lambda i: (i, 0, 0, 0)),
            pl.BlockSpec((1, heads, PAD, PAD), lambda i: (i, 0, 0, 0)),
            pl.BlockSpec((1, PAD, 128), lambda i: (i, 0, 0)),
        ],
        out_shape=[
            jax.ShapeDtypeStruct((frames, PAD, D), F32),
            jax.ShapeDtypeStruct((frames, 2, PAD, 3 * cols), BF),
            jax.ShapeDtypeStruct((frames, 2, PAD, cols), BF),
            jax.ShapeDtypeStruct((frames, heads, PAD, PAD), BF),
            jax.ShapeDtypeStruct((frames, PAD, 128), F32),
        ],
        name="spatial_fwd",
        compiler_params=pltpu.CompilerParams(vmem_limit_bytes=VMEM_BYTES),
    )(x, weights, vec)


def attn_back_common(x, ub, up, w_ref, vec_ref, row_base, gain_row, mix_of, qkv_of, exps_of, rec_of, gw_ref, gv_ref, cols, blocks):
    xhat, rstd = norm_parts(x)
    gain = vec_ref[gain_row : gain_row + 1, :]
    normed = (xhat * gain + vec_ref[row_base : row_base + 1, :]).astype(BF)
    dn = None
    gv_ref[3:4, :] += jnp.sum(up, axis=0, keepdims=True)
    rows = x.shape[0]
    step = rows // blocks
    for g in range(2):
        wo = w_ref[g, :, 3 * cols : 4 * cols]
        dmix = dot(ub, wo, NN).astype(BF)
        mix = mix_of(g)
        gw_ref[g, :, 3 * cols : 4 * cols] += dot(ub, mix, TN)
        parts = []
        for part in range(3):
            parts.append([[] for _ in range(blocks)])
        for b in range(blocks):
            rs = slice(step * b, step * (b + 1))
            for j in range(cols // 128):
                sl = slice(128 * j, 128 * (j + 1))
                q, k, v = qkv_of(g, j, rs)
                exps = [exps_of((g * (cols // 128) + j) * 2 + h, b) for h in range(2)]
                recs = [rec_of((g * (cols // 128) + j) * 2 + h, rs) for h in range(2)]
                trio = heads_backward(q, k, v, mix[rs, sl], dmix[rs, sl], exps, recs)
                for part in range(3):
                    parts[part][b].append(trio[part])
        cat = lambda rowsof: jnp.concatenate([jnp.concatenate(r, axis=1) for r in rowsof], axis=0)
        dq, dk, dv = cat(parts[0]), cat(parts[1]), cat(parts[2])
        span = slice(g * cols, (g + 1) * cols)
        gv_ref[1:2, span] += jnp.sum(dq.astype(F32), axis=0, keepdims=True)
        gv_ref[2:3, span] += jnp.sum(dv.astype(F32), axis=0, keepdims=True)
        dqkv = jnp.concatenate([dq, dk, dv], axis=1)
        gw_ref[g, :, 0 : 3 * cols] += dot(normed, dqkv, TN)
        term = dot(dqkv, w_ref[g, :, 0 : 3 * cols], NT)
        dn = term if dn is None else dn + term
    gv_ref[0:1, :] += jnp.sum(dn, axis=0, keepdims=True)
    gv_ref[4:5, :] += jnp.sum(dn * xhat, axis=0, keepdims=True)
    return up + norm_back(dn, xhat, rstd, gain)


def spatial_bwd_kernel(x_ref, up_ref, qkv_ref, mix_ref, p_ref, r_ref, w_ref, vec_ref, gx_ref, gb_ref, gv_ref, gw_ref):
    cols = w_ref.shape[2] // 4

    @pl.when(pl.program_id(0) == 0)
    def _():
        gw_ref[...] = jnp.zeros_like(gw_ref)
        gv_ref[...] = jnp.zeros_like(gv_ref)

    x = x_ref[0].astype(F32)
    up = up_ref[0]
    ub = up.astype(BF)
    gx_ref[0] = attn_back_common(
        x, ub, up, w_ref, vec_ref, 0, 10,
        lambda g: mix_ref[0, g],
        lambda g, j, rs: tuple(
            qkv_ref[0, g, :, cols * t + 128 * j : cols * t + 128 * (j + 1)] for t in range(3)
        ),
        lambda head, b: p_ref[0, head],
        lambda head, rs: r_ref[0, :, head : head + 1],
        gw_ref, gv_ref, cols, 1,
    )

    @pl.when(pl.program_id(0) == pl.num_programs(0) - 1)
    def _():
        gb_ref[...] = gw_ref[...].astype(BF)


def spatial_bwd(x, up, qkv, mix, p, r, weights, section, vec):
    frames = x.shape[0]
    D = x.shape[2]
    cols = D // 2
    heads = D // HEAD
    whole = lambda *shape: pl.BlockSpec(shape, lambda i: (0,) * len(shape))
    return pl.pallas_call(
        spatial_bwd_kernel,
        grid=(frames,),
        in_specs=[
            pl.BlockSpec((1, PAD, D), lambda i: (i, 0, 0)),
            pl.BlockSpec((1, PAD, D), lambda i: (i, 0, 0)),
            pl.BlockSpec((1, 2, PAD, 3 * cols), lambda i: (i, 0, 0, 0)),
            pl.BlockSpec((1, 2, PAD, cols), lambda i: (i, 0, 0, 0)),
            pl.BlockSpec((1, heads, PAD, PAD), lambda i: (i, 0, 0, 0)),
            pl.BlockSpec((1, PAD, 128), lambda i: (i, 0, 0)),
            pl.BlockSpec((2, D, 4 * cols), lambda i: (0, 0, section)),
            whole(*vec.shape),
        ],
        out_specs=[
            pl.BlockSpec((1, PAD, D), lambda i: (i, 0, 0)),
            whole(2, D, 4 * cols),
            whole(8, D),
        ],
        out_shape=[
            jax.ShapeDtypeStruct((frames, PAD, D), F32),
            jax.ShapeDtypeStruct((2, D, 4 * cols), BF),
            jax.ShapeDtypeStruct((8, D), F32),
        ],
        scratch_shapes=[pltpu.VMEM((2, D, 4 * cols), F32)],
        name="spatial_bwd",
        compiler_params=pltpu.CompilerParams(vmem_limit_bytes=VMEM_BYTES),
    )(x, up, qkv, mix, p, r, weights, vec)


GROUP = 8 * FRAMES
STEP_GROUPS = 2


def temporal_mask():
    a = lax.broadcasted_iota(jnp.int32, (GROUP, GROUP), 0)
    b = lax.broadcasted_iota(jnp.int32, (GROUP, GROUP), 1)
    return (a % 8) == (b % 8)


def live_rows(rows_per_step, rows):
    base = pl.program_id(0) * rows_per_step
    return base + lax.broadcasted_iota(jnp.int32, (rows_per_step, 1), 0) < rows


def temporal_fwd_kernel(rows, x_ref, w_ref, vec_ref, s_ref, qkv_ref, mix_ref, p_ref, r_ref):
    cols = w_ref.shape[2] // 4
    n = x_ref.shape[0]
    x = jnp.where(live_rows(n, rows), x_ref[...], 0.0)
    xhat, _ = norm_parts(x)
    normed = (xhat * vec_ref[11:12, :] + vec_ref[4:5, :]).astype(BF)
    mask = temporal_mask()
    branch = vec_ref[7:8, :]
    lane = lax.broadcasted_iota(jnp.int32, (GROUP, 128), 1)
    recips = [jnp.zeros((GROUP, 128), F32) for _ in range(n // GROUP)]
    for g, (q, k, v) in enumerate(project(normed, w_ref, vec_ref, 4, cols)):
        qkv_ref[g, :, 0:cols] = q
        qkv_ref[g, :, cols : 2 * cols] = k
        qkv_ref[g, :, 2 * cols : 3 * cols] = v
        blocks = []
        for b in range(n // GROUP):
            rs = slice(GROUP * b, GROUP * (b + 1))
            mixes = []
            for j in range(cols // 128):
                sl = slice(128 * j, 128 * (j + 1))
                mix, exps, rec = heads_forward(q[rs, sl], k[rs, sl], v[rs, sl], mask)
                mixes.append(mix.astype(BF))
                for h in range(2):
                    head = (g * (cols // 128) + j) * 2 + h
                    p_ref[head, rs] = exps[h]
                    recips[b] = jnp.where(lane == head, rec[h], recips[b])
            blocks.append(jnp.concatenate(mixes, axis=1))
        mix = jnp.concatenate(blocks, axis=0)
        mix_ref[g] = mix
        branch = branch + dot(mix, w_ref[g, :, 3 * cols : 4 * cols], NT)
    r_ref[...] = jnp.concatenate(recips, axis=0)
    s_ref[...] = x + branch


def temporal_fwd(x, weights, section, vec):
    rows, D = x.shape
    cols = D // 2
    heads = D // HEAD
    n = STEP_GROUPS * GROUP
    steps = -(-rows // n)
    padded = steps * n
    whole = lambda *shape: pl.BlockSpec(shape, lambda i: (0,) * len(shape))
    return pl.pallas_call(
        functools.partial(temporal_fwd_kernel, rows),
        grid=(steps,),
        in_specs=[
            pl.BlockSpec((n, D), lambda i: (i, 0)),
            pl.BlockSpec((2, D, 4 * cols), lambda i: (0, 0, section)),
            whole(*vec.shape),
        ],
        out_specs=[
            pl.BlockSpec((n, D), lambda i: (i, 0)),
            pl.BlockSpec((2, n, 3 * cols), lambda i: (0, i, 0)),
            pl.BlockSpec((2, n, cols), lambda i: (0, i, 0)),
            pl.BlockSpec((heads, n, GROUP), lambda i: (0, i, 0)),
            pl.BlockSpec((n, 128), lambda i: (i, 0)),
        ],
        out_shape=[
            jax.ShapeDtypeStruct((rows, D), F32),
            jax.ShapeDtypeStruct((2, padded, 3 * cols), BF),
            jax.ShapeDtypeStruct((2, padded, cols), BF),
            jax.ShapeDtypeStruct((heads, padded, GROUP), BF),
            jax.ShapeDtypeStruct((padded, 128), F32),
        ],
        name="temporal_fwd",
        compiler_params=pltpu.CompilerParams(vmem_limit_bytes=VMEM_BYTES),
    )(x, weights, vec)


def temporal_bwd_kernel(rows, x_ref, up_ref, qkv_ref, mix_ref, p_ref, r_ref, w_ref, vec_ref, gx_ref, gb_ref, gv_ref, gw_ref):
    cols = w_ref.shape[2] // 4
    n = x_ref.shape[0]

    @pl.when(pl.program_id(0) == 0)
    def _():
        gw_ref[...] = jnp.zeros_like(gw_ref)
        gv_ref[...] = jnp.zeros_like(gv_ref)

    live = live_rows(n, rows)
    x = jnp.where(live, x_ref[...], 0.0)
    up = jnp.where(live, up_ref[...], 0.0)
    ub = up.astype(BF)
    gx_ref[...] = attn_back_common(
        x, ub, up, w_ref, vec_ref, 4, 11,
        lambda g: mix_ref[g],
        lambda g, j, rs: tuple(
            qkv_ref[g, rs, cols * t + 128 * j : cols * t + 128 * (j + 1)] for t in range(3)
        ),
        lambda head, b: p_ref[head, GROUP * b : GROUP * (b + 1)],
        lambda head, rs: r_ref[rs, head : head + 1],
        gw_ref, gv_ref, cols, n // GROUP,
    )

    @pl.when(pl.program_id(0) == pl.num_programs(0) - 1)
    def _():
        gb_ref[...] = gw_ref[...].astype(BF)


def temporal_bwd(x, up, qkv, mix, p, r, weights, section, vec):
    rows, D = x.shape
    cols = D // 2
    heads = D // HEAD
    n = STEP_GROUPS * GROUP
    steps = -(-rows // n)
    whole = lambda *shape: pl.BlockSpec(shape, lambda i: (0,) * len(shape))
    return pl.pallas_call(
        functools.partial(temporal_bwd_kernel, rows),
        grid=(steps,),
        in_specs=[
            pl.BlockSpec((n, D), lambda i: (i, 0)),
            pl.BlockSpec((n, D), lambda i: (i, 0)),
            pl.BlockSpec((2, n, 3 * cols), lambda i: (0, i, 0)),
            pl.BlockSpec((2, n, cols), lambda i: (0, i, 0)),
            pl.BlockSpec((heads, n, GROUP), lambda i: (0, i, 0)),
            pl.BlockSpec((n, 128), lambda i: (i, 0)),
            pl.BlockSpec((2, D, 4 * cols), lambda i: (0, 0, section)),
            whole(*vec.shape),
        ],
        out_specs=[
            pl.BlockSpec((n, D), lambda i: (i, 0)),
            whole(2, D, 4 * cols),
            whole(8, D),
        ],
        out_shape=[
            jax.ShapeDtypeStruct((rows, D), F32),
            jax.ShapeDtypeStruct((2, D, 4 * cols), BF),
            jax.ShapeDtypeStruct((8, D), F32),
        ],
        scratch_shapes=[pltpu.VMEM((2, D, 4 * cols), F32)],
        name="temporal_bwd",
        compiler_params=pltpu.CompilerParams(vmem_limit_bytes=VMEM_BYTES),
    )(x, up, qkv, mix, p, r, weights, vec)


MLP_ROWS = 416
INV_SQRT2 = 0.7071067811865476
INV_SQRT2PI = 0.3989422804014327


def mlp_kernel(x_ref, cot_ref, wi_ref, wo_ref, vec_ref, hid_ref, out_ref, up_ref, gi_ref, go_ref, gv_ref, gh_ref, ai_ref, ao_ref):
    @pl.when(pl.program_id(0) == 0)
    def _():
        ai_ref[...] = jnp.zeros_like(ai_ref)
        ao_ref[...] = jnp.zeros_like(ao_ref)
        gv_ref[...] = jnp.zeros_like(gv_ref)
        gh_ref[...] = jnp.zeros_like(gh_ref)

    width = wi_ref.shape[2]
    x = x_ref[...]
    xhat, rstd = norm_parts(x)
    gain = vec_ref[12:13, :]
    normed = (xhat * gain + vec_ref[8:9, :]).astype(BF)
    ub = cot_ref[...]
    up = ub.astype(F32)
    gv_ref[3:4, :] += jnp.sum(up, axis=0, keepdims=True)
    branch = vec_ref[9:10, :]
    dn = None
    chunk = 768
    for g in range(2):
        for c in range(width // chunk):
            sl = slice(chunk * c, chunk * (c + 1))
            pre = dot(normed, wi_ref[g, :, sl], NN) + hid_ref[g : g + 1, sl]
            cdf = 0.5 + 0.5 * lax.erf(pre * INV_SQRT2)
            act = (pre * cdf).astype(BF)
            branch = branch + dot(act, wo_ref[g, :, sl], NT)
            ao_ref[g, :, sl] += dot(ub, act, TN)
            dact = dot(ub, wo_ref[g, :, sl], NN).astype(BF).astype(F32)
            slope = cdf + pre * (jnp.exp(pre * pre * -0.5) * INV_SQRT2PI)
            dpre32 = dact * slope
            dpre = dpre32.astype(BF)
            gh_ref[g : g + 1, sl] += jnp.sum(dpre.astype(F32), axis=0, keepdims=True)
            ai_ref[g, :, sl] += dot(normed, dpre, TN)
            term = dot(dpre, wi_ref[g, :, sl], NT)
            dn = term if dn is None else dn + term
    out_ref[...] = (x + branch).astype(BF)
    gv_ref[0:1, :] += jnp.sum(dn, axis=0, keepdims=True)
    gv_ref[4:5, :] += jnp.sum(dn * xhat, axis=0, keepdims=True)
    up_ref[...] = up + norm_back(dn, xhat, rstd, gain)

    @pl.when(pl.program_id(0) == pl.num_programs(0) - 1)
    def _():
        gi_ref[...] = ai_ref[...].astype(BF)
        go_ref[...] = ao_ref[...].astype(BF)


def mlp_both(x, cot, weights, section, vec, hidden):
    rows, D = x.shape
    width = hidden.shape[1]
    n = MLP_ROWS
    whole = lambda *shape: pl.BlockSpec(shape, lambda i: (0,) * len(shape))
    one = pl.Buffered(1)
    return pl.pallas_call(
        mlp_kernel,
        grid=(rows // n,),
        in_specs=[
            pl.BlockSpec((n, D), lambda i: (i, 0)),
            pl.BlockSpec((n, D), lambda i: (i, 0)),
            pl.BlockSpec((2, D, width), lambda i: (0, 0, section), pipeline_mode=one),
            pl.BlockSpec((2, D, width), lambda i: (0, 0, section + 1), pipeline_mode=one),
            whole(*vec.shape),
            whole(*hidden.shape),
        ],
        out_specs=[
            pl.BlockSpec((n, D), lambda i: (i, 0)),
            pl.BlockSpec((n, D), lambda i: (i, 0)),
            pl.BlockSpec((2, D, width), lambda i: (0, 0, 0)),
            pl.BlockSpec((2, D, width), lambda i: (0, 0, 0)),
            whole(8, D),
            whole(*hidden.shape),
        ],
        out_shape=[
            jax.ShapeDtypeStruct((rows, D), BF),
            jax.ShapeDtypeStruct((rows, D), F32),
            jax.ShapeDtypeStruct((2, D, width), BF),
            jax.ShapeDtypeStruct((2, D, width), BF),
            jax.ShapeDtypeStruct((8, D), F32),
            jax.ShapeDtypeStruct(hidden.shape, F32),
        ],
        scratch_shapes=[pltpu.VMEM((2, D, width), F32), pltpu.VMEM((2, D, width), F32)],
        name="mlp_both",
        compiler_params=pltpu.CompilerParams(vmem_limit_bytes=VMEM_BYTES),
    )(x, cot, weights, weights, vec, hidden)


def to_patch_groups(rows):
    frames, pad, D = rows.shape
    swapped = lax.all_to_all(
        rows.reshape(frames, 2, pad // 2, D), "tensor", split_axis=1, concat_axis=0, tiled=True
    )
    return (
        swapped.reshape(2 * frames, pad // 16, 8, D).transpose(1, 0, 2, 3).reshape(frames * pad, D)
    )


def to_frames(rows):
    total, D = rows.shape
    frames = total // PAD
    blocks = rows.reshape(PAD // 16, 2 * frames, 8, D).transpose(1, 0, 2, 3)
    swapped = lax.all_to_all(
        blocks.reshape(2 * frames, 1, PAD // 2, D), "tensor", split_axis=0, concat_axis=1, tiled=True
    )
    return swapped.reshape(frames, PAD, D)


def pad_frames(rows):
    D = rows.shape[1]
    return jnp.pad(rows.reshape(-1, PATCHES, D), ((0, 0), (0, PAD - PATCHES), (0, 0)))


def strip_frames(rows):
    D = rows.shape[2]
    return rows[:, :PATCHES].reshape(-1, D)


def shards(tokens, cotangent, attn_qkv, attn_out, mlp_in, mlp_out, norm_gains, biases, hidden_bias):
    D = tokens.shape[1]
    depth = mlp_in.shape[1]
    cols = attn_qkv.shape[4]
    units = mlp_in.shape[2]
    everyone = ("dp", "tensor")
    own = jnp.concatenate(
        [
            attn_qkv[0, 0].reshape(depth, 3 * cols),
            attn_out[0, 0].T,
            attn_qkv[0, 1].reshape(depth, 3 * cols),
            attn_out[0, 1].T,
            mlp_in[0],
            mlp_out[0].T,
        ],
        axis=1,
    )
    weights = lax.all_gather(own, ("tensor", "dp"), axis=0, tiled=True).reshape(2, D, own.shape[1])
    small = jnp.concatenate(
        [biases[0].reshape(-1), norm_gains[0].reshape(-1), hidden_bias[0].reshape(-1)]
    )
    small = lax.all_gather(small.reshape(1, -1), everyone, axis=0, tiled=True)
    devices = small.shape[0]
    share = D // devices
    vec = small[:, : 13 * share].reshape(devices, 13, share).transpose(1, 0, 2).reshape(13, D)
    hidden = small[:, 13 * share :].reshape(2, units)

    x = pad_frames(tokens)
    stream1, s_qkv, s_mix, s_p, s_r = spatial_fwd(x, weights, 0, vec)
    x1 = to_patch_groups(stream1)
    x2, t_qkv, t_mix, t_p, t_r = temporal_fwd(x1, weights, 1, vec)
    cot = to_patch_groups(pad_frames(cotangent))
    out_b, up2, g_in, g_down, gv_m, g_hidden = mlp_both(x2, cot, weights, 2, vec, hidden)
    output = strip_frames(to_frames(out_b))
    up1, g_t, gv_t = temporal_bwd(x1, up2, t_qkv, t_mix, t_p, t_r, weights, 1, vec)
    up1 = to_frames(up1)
    up0, g_s, gv_s = spatial_bwd(x, up1, s_qkv, s_mix, s_p, s_r, weights, 0, vec)
    grad_tokens = strip_frames(up0)

    def scatter(grad):
        return lax.psum_scatter(
            grad.reshape(2 * D, grad.shape[2]), ("tensor", "dp"), scatter_dimension=0, tiled=True
        ).astype(F32)

    g_in, g_down, g_t, g_s = scatter(g_in), scatter(g_down), scatter(g_t), scatter(g_s)
    grad_qkv = jnp.stack([g[:, : 3 * cols].reshape(depth, 3, cols) for g in (g_s, g_t)])[None]
    grad_out = jnp.stack([g[:, 3 * cols :].T for g in (g_s, g_t)])[None]
    vec_grad = jnp.concatenate([gv_s[0:4], gv_t[0:4], gv_m[0:1], gv_m[3:4], gv_s[4:5], gv_t[4:5], gv_m[4:5]])
    small_grad = jnp.concatenate(
        [
            vec_grad.reshape(13, devices, share).transpose(1, 0, 2).reshape(devices, 13 * share),
            g_hidden.reshape(devices, -1),
        ],
        axis=1,
    )
    small_grad = lax.psum_scatter(small_grad, everyone, scatter_dimension=0, tiled=True)[0]
    grad_biases = small_grad[: 10 * share].reshape(1, 10, share)
    grad_gains = small_grad[10 * share : 13 * share].reshape(1, 3, share)
    grad_hidden = small_grad[13 * share :].reshape(1, -1)
    return (
        output,
        grad_tokens,
        grad_qkv,
        grad_out,
        g_in[None],
        g_down.T[None],
        grad_gains,
        grad_biases,
        grad_hidden,
    )


def solution(mesh):
    placed = (
        P(("dp", "tensor"), None),
        P(("dp", "tensor"), None),
        P(None, None, "dp", None, "tensor"),
        P(None, None, "tensor", "dp"),
        P(None, "dp", "tensor"),
        P(None, "tensor", "dp"),
        P(None, None, ("dp", "tensor")),
        P(None, None, ("dp", "tensor")),
        P(None, ("dp", "tensor")),
    )
    return jax.shard_map(
        shards, mesh=mesh, in_specs=placed, out_specs=placed, check_vma=False
    )
```

```python
import functools
import jax
import jax.numpy as jnp
from jax import lax
from jax.experimental import pallas as pl
from jax.experimental.pallas import tpu as pltpu
from jax.sharding import PartitionSpec as P

HEAD = 64
FRAMES = 16
PATCHES = 196
PAD = 208
EPSILON = 1e-06
BF = jnp.bfloat16
F32 = jnp.float32
NN = (((1,), (0,)), ((), ()))
NT = (((1,), (1,)), ((), ()))
TN = (((0,), (0,)), ((), ()))
VMEM_BYTES = 60 * 1024 * 1024


def dot(a, b, dims):
    return lax.dot_general(a, b, dims, preferred_element_type=F32)


def norm_parts(x):
    mean = jnp.mean(x, axis=-1, keepdims=True)
    centred = x - mean
    var = jnp.mean(centred * centred, axis=-1, keepdims=True)
    rstd = lax.rsqrt(var + EPSILON)
    return centred * rstd, rstd


def norm_back(grad_normed, xhat, rstd, gain):
    scaled = grad_normed * gain
    first = jnp.mean(scaled, axis=-1, keepdims=True)
    second = jnp.mean(scaled * xhat, axis=-1, keepdims=True)
    return rstd * (scaled - first - xhat * second)


def split_halves(pair):
    lane = lax.broadcasted_iota(jnp.int32, pair.shape, 1)
    zero = jnp.zeros_like(pair)
    return jnp.where(lane < HEAD, pair, zero), jnp.where(lane < HEAD, zero, pair)


def project(normed, w_ref, vec_ref, row_base, cols):
    parts = []
    for g in range(2):
        w = w_ref[g, :, 0 : 3 * cols]
        qkv = dot(normed, w, NN)
        bq = vec_ref[row_base + 1 : row_base + 2, g * cols : (g + 1) * cols]
        bv = vec_ref[row_base + 2 : row_base + 3, g * cols : (g + 1) * cols]
        q = (qkv[:, :cols] + bq).astype(BF) * BF(0.125)
        k = qkv[:, cols : 2 * cols].astype(BF)
        v = (qkv[:, 2 * cols :] + bv).astype(BF)
        parts.append((q, k, v))
    return parts


def heads_forward(q, k, v, mask):
    exps, sums, outs = [], [], []
    for qh in split_halves(q):
        s = dot(qh, k, NT)
        s = jnp.where(mask, s, -1e30)
        top = jnp.max(s, axis=-1, keepdims=True)
        e = jnp.exp(s - top)
        recip = 1.0 / jnp.sum(e, axis=-1, keepdims=True)
        eb = e.astype(BF)
        outs.append(dot(eb, v, NN) * recip)
        exps.append(eb)
        sums.append(recip)
    lane = lax.broadcasted_iota(jnp.int32, q.shape, 1)
    return jnp.where(lane < HEAD, outs[0], outs[1]), exps, sums


def heads_backward(q, k, v, o, do, exps, recips):
    prod = do.astype(F32) * o.astype(F32)
    dq = dk = dv = None
    qs, ks, ps = split_halves(q), split_halves(k), split_halves(prod)
    dos = split_halves(do)
    for h in range(2):
        r = recips[h]
        delta = jnp.sum(ps[h], axis=-1, keepdims=True) * r
        dor = (dos[h].astype(F32) * r).astype(BF)
        dp = dot(dor, v, NT)
        e = exps[h]
        ds = (e.astype(F32) * (dp - delta)).astype(BF)
        dq_h = dot(ds, ks[h], NN)
        dk_h = dot(ds, qs[h], TN)
        dv_h = dot(e, dor, TN)
        dq = dq_h if dq is None else dq + dq_h
        dk = dk_h if dk is None else dk + dk_h
        dv = dv_h if dv is None else dv + dv_h
    return (dq * 0.125).astype(BF), dk.astype(BF), dv.astype(BF)


def spatial_mask():
    return lax.broadcasted_iota(jnp.int32, (PAD, PAD), 1) < PATCHES


def spatial_fwd_kernel(x_ref, w_ref, vec_ref, s_ref, qkv_ref, mix_ref, p_ref, r_ref):
    cols = w_ref.shape[2] // 4
    x = x_ref[0].astype(F32)
    xhat, _ = norm_parts(x)
    normed = (xhat * vec_ref[10:11, :] + vec_ref[0:1, :]).astype(BF)
    mask = spatial_mask()
    branch = vec_ref[3:4, :]
    lane = lax.broadcasted_iota(jnp.int32, (PAD, 128), 1)
    recips = jnp.zeros((PAD, 128), F32)
    for g, (q, k, v) in enumerate(project(normed, w_ref, vec_ref, 0, cols)):
        qkv_ref[0, g, :, 0:cols] = q
        qkv_ref[0, g, :, cols : 2 * cols] = k
        qkv_ref[0, g, :, 2 * cols : 3 * cols] = v
        mixes = []
        for j in range(cols // 128):
            sl = slice(128 * j, 128 * (j + 1))
            mix, exps, rec = heads_forward(q[:, sl], k[:, sl], v[:, sl], mask)
            mixes.append(mix.astype(BF))
            for h in range(2):
                head = (g * (cols // 128) + j) * 2 + h
                p_ref[0, head] = exps[h]
                recips = jnp.where(lane == head, rec[h], recips)
        mix = jnp.concatenate(mixes, axis=1)
        mix_ref[0, g] = mix
        branch = branch + dot(mix, w_ref[g, :, 3 * cols : 4 * cols], NT)
    r_ref[0] = recips
    s_ref[0] = x + branch


def spatial_fwd(x, weights, vec):
    frames = x.shape[0]
    D = x.shape[2]
    cols = D // 2
    heads = D // HEAD
    whole = lambda *shape: pl.BlockSpec(shape, lambda i: (0,) * len(shape))
    return pl.pallas_call(
        spatial_fwd_kernel,
        grid=(frames,),
        in_specs=[
            pl.BlockSpec((1, PAD, D), lambda i: (i, 0, 0)),
            pl.BlockSpec((2, D, 4 * cols), lambda i: (0, 0, 0)),
            whole(*vec.shape),
        ],
        out_specs=[
            pl.BlockSpec((1, PAD, D), lambda i: (i, 0, 0)),
            pl.BlockSpec((1, 2, PAD, 3 * cols), lambda i: (i, 0, 0, 0)),
            pl.BlockSpec((1, 2, PAD, cols), lambda i: (i, 0, 0, 0)),
            pl.BlockSpec((1, heads, PAD, PAD), lambda i: (i, 0, 0, 0)),
            pl.BlockSpec((1, PAD, 128), lambda i: (i, 0, 0)),
        ],
        out_shape=[
            jax.ShapeDtypeStruct((frames, PAD, D), F32),
            jax.ShapeDtypeStruct((frames, 2, PAD, 3 * cols), BF),
            jax.ShapeDtypeStruct((frames, 2, PAD, cols), BF),
            jax.ShapeDtypeStruct((frames, heads, PAD, PAD), BF),
            jax.ShapeDtypeStruct((frames, PAD, 128), F32),
        ],
        name="spatial_fwd",
        compiler_params=pltpu.CompilerParams(vmem_limit_bytes=VMEM_BYTES),
    )(x, weights, vec)


def attn_back_common(x, ub, up, w_ref, vec_ref, row_base, gain_row, mix_of, qkv_of, exps_of, rec_of, gw_ref, gv_ref, cols, blocks):
    xhat, rstd = norm_parts(x)
    gain = vec_ref[gain_row : gain_row + 1, :]
    normed = (xhat * gain + vec_ref[row_base : row_base + 1, :]).astype(BF)
    dn = None
    gv_ref[3:4, :] += jnp.sum(up, axis=0, keepdims=True)
    rows = x.shape[0]
    step = rows // blocks
    for g in range(2):
        wo = w_ref[g, :, 3 * cols : 4 * cols]
        dmix = dot(ub, wo, NN).astype(BF)
        mix = mix_of(g)
        gw_ref[g, :, 3 * cols : 4 * cols] += dot(ub, mix, TN)
        parts = []
        for part in range(3):
            parts.append([[] for _ in range(blocks)])
        for b in range(blocks):
            rs = slice(step * b, step * (b + 1))
            for j in range(cols // 128):
                sl = slice(128 * j, 128 * (j + 1))
                q, k, v = qkv_of(g, j, rs)
                exps = [exps_of((g * (cols // 128) + j) * 2 + h, b) for h in range(2)]
                recs = [rec_of((g * (cols // 128) + j) * 2 + h, rs) for h in range(2)]
                trio = heads_backward(q, k, v, mix[rs, sl], dmix[rs, sl], exps, recs)
                for part in range(3):
                    parts[part][b].append(trio[part])
        cat = lambda rowsof: jnp.concatenate([jnp.concatenate(r, axis=1) for r in rowsof], axis=0)
        dq, dk, dv = cat(parts[0]), cat(parts[1]), cat(parts[2])
        span = slice(g * cols, (g + 1) * cols)
        gv_ref[1:2, span] += jnp.sum(dq.astype(F32), axis=0, keepdims=True)
        gv_ref[2:3, span] += jnp.sum(dv.astype(F32), axis=0, keepdims=True)
        dqkv = jnp.concatenate([dq, dk, dv], axis=1)
        gw_ref[g, :, 0 : 3 * cols] += dot(normed, dqkv, TN)
        term = dot(dqkv, w_ref[g, :, 0 : 3 * cols], NT)
        dn = term if dn is None else dn + term
    gv_ref[0:1, :] += jnp.sum(dn, axis=0, keepdims=True)
    gv_ref[4:5, :] += jnp.sum(dn * xhat, axis=0, keepdims=True)
    return up + norm_back(dn, xhat, rstd, gain)


def spatial_bwd_kernel(x_ref, up_ref, qkv_ref, mix_ref, p_ref, r_ref, w_ref, vec_ref, gx_ref, gb_ref, gv_ref, gw_ref):
    cols = w_ref.shape[2] // 4

    @pl.when(pl.program_id(0) == 0)
    def _():
        gw_ref[...] = jnp.zeros_like(gw_ref)
        gv_ref[...] = jnp.zeros_like(gv_ref)

    x = x_ref[0].astype(F32)
    up = up_ref[0]
    ub = up.astype(BF)
    gx_ref[0] = attn_back_common(
        x, ub, up, w_ref, vec_ref, 0, 10,
        lambda g: mix_ref[0, g],
        lambda g, j, rs: tuple(
            qkv_ref[0, g, :, cols * t + 128 * j : cols * t + 128 * (j + 1)] for t in range(3)
        ),
        lambda head, b: p_ref[0, head],
        lambda head, rs: r_ref[0, :, head : head + 1],
        gw_ref, gv_ref, cols, 1,
    )

    @pl.when(pl.program_id(0) == pl.num_programs(0) - 1)
    def _():
        gb_ref[...] = gw_ref[...].astype(BF)


def spatial_bwd(x, up, qkv, mix, p, r, weights, vec):
    frames = x.shape[0]
    D = x.shape[2]
    cols = D // 2
    heads = D // HEAD
    whole = lambda *shape: pl.BlockSpec(shape, lambda i: (0,) * len(shape))
    return pl.pallas_call(
        spatial_bwd_kernel,
        grid=(frames,),
        in_specs=[
            pl.BlockSpec((1, PAD, D), lambda i: (i, 0, 0)),
            pl.BlockSpec((1, PAD, D), lambda i: (i, 0, 0)),
            pl.BlockSpec((1, 2, PAD, 3 * cols), lambda i: (i, 0, 0, 0)),
            pl.BlockSpec((1, 2, PAD, cols), lambda i: (i, 0, 0, 0)),
            pl.BlockSpec((1, heads, PAD, PAD), lambda i: (i, 0, 0, 0)),
            pl.BlockSpec((1, PAD, 128), lambda i: (i, 0, 0)),
            pl.BlockSpec((2, D, 4 * cols), lambda i: (0, 0, 0)),
            whole(*vec.shape),
        ],
        out_specs=[
            pl.BlockSpec((1, PAD, D), lambda i: (i, 0, 0)),
            whole(2, D, 4 * cols),
            whole(8, D),
        ],
        out_shape=[
            jax.ShapeDtypeStruct((frames, PAD, D), F32),
            jax.ShapeDtypeStruct((2, D, 4 * cols), BF),
            jax.ShapeDtypeStruct((8, D), F32),
        ],
        scratch_shapes=[pltpu.VMEM((2, D, 4 * cols), F32)],
        name="spatial_bwd",
        compiler_params=pltpu.CompilerParams(vmem_limit_bytes=VMEM_BYTES),
    )(x, up, qkv, mix, p, r, weights, vec)


GROUP = 8 * FRAMES
STEP_GROUPS = 2


def temporal_mask():
    a = lax.broadcasted_iota(jnp.int32, (GROUP, GROUP), 0)
    b = lax.broadcasted_iota(jnp.int32, (GROUP, GROUP), 1)
    return (a % 8) == (b % 8)


def live_rows(rows_per_step, rows):
    base = pl.program_id(0) * rows_per_step
    return base + lax.broadcasted_iota(jnp.int32, (rows_per_step, 1), 0) < rows


def temporal_fwd_kernel(rows, x_ref, w_ref, vec_ref, s_ref, qkv_ref, mix_ref, p_ref, r_ref):
    cols = w_ref.shape[2] // 4
    n = x_ref.shape[0]
    x = jnp.where(live_rows(n, rows), x_ref[...], 0.0)
    xhat, _ = norm_parts(x)
    normed = (xhat * vec_ref[11:12, :] + vec_ref[4:5, :]).astype(BF)
    mask = temporal_mask()
    branch = vec_ref[7:8, :]
    lane = lax.broadcasted_iota(jnp.int32, (GROUP, 128), 1)
    recips = [jnp.zeros((GROUP, 128), F32) for _ in range(n // GROUP)]
    for g, (q, k, v) in enumerate(project(normed, w_ref, vec_ref, 4, cols)):
        qkv_ref[g, :, 0:cols] = q
        qkv_ref[g, :, cols : 2 * cols] = k
        qkv_ref[g, :, 2 * cols : 3 * cols] = v
        blocks = []
        for b in range(n // GROUP):
            rs = slice(GROUP * b, GROUP * (b + 1))
            mixes = []
            for j in range(cols // 128):
                sl = slice(128 * j, 128 * (j + 1))
                mix, exps, rec = heads_forward(q[rs, sl], k[rs, sl], v[rs, sl], mask)
                mixes.append(mix.astype(BF))
                for h in range(2):
                    head = (g * (cols // 128) + j) * 2 + h
                    p_ref[head, rs] = exps[h]
                    recips[b] = jnp.where(lane == head, rec[h], recips[b])
            blocks.append(jnp.concatenate(mixes, axis=1))
        mix = jnp.concatenate(blocks, axis=0)
        mix_ref[g] = mix
        branch = branch + dot(mix, w_ref[g, :, 3 * cols : 4 * cols], NT)
    r_ref[...] = jnp.concatenate(recips, axis=0)
    s_ref[...] = x + branch


def temporal_fwd(x, weights, vec):
    rows, D = x.shape
    cols = D // 2
    heads = D // HEAD
    n = STEP_GROUPS * GROUP
    steps = -(-rows // n)
    padded = steps * n
    whole = lambda *shape: pl.BlockSpec(shape, lambda i: (0,) * len(shape))
    return pl.pallas_call(
        functools.partial(temporal_fwd_kernel, rows),
        grid=(steps,),
        in_specs=[
            pl.BlockSpec((n, D), lambda i: (i, 0)),
            pl.BlockSpec((2, D, 4 * cols), lambda i: (0, 0, 0)),
            whole(*vec.shape),
        ],
        out_specs=[
            pl.BlockSpec((n, D), lambda i: (i, 0)),
            pl.BlockSpec((2, n, 3 * cols), lambda i: (0, i, 0)),
            pl.BlockSpec((2, n, cols), lambda i: (0, i, 0)),
            pl.BlockSpec((heads, n, GROUP), lambda i: (0, i, 0)),
            pl.BlockSpec((n, 128), lambda i: (i, 0)),
        ],
        out_shape=[
            jax.ShapeDtypeStruct((rows, D), F32),
            jax.ShapeDtypeStruct((2, padded, 3 * cols), BF),
            jax.ShapeDtypeStruct((2, padded, cols), BF),
            jax.ShapeDtypeStruct((heads, padded, GROUP), BF),
            jax.ShapeDtypeStruct((padded, 128), F32),
        ],
        name="temporal_fwd",
        compiler_params=pltpu.CompilerParams(vmem_limit_bytes=VMEM_BYTES),
    )(x, weights, vec)


def temporal_bwd_kernel(rows, x_ref, up_ref, qkv_ref, mix_ref, p_ref, r_ref, w_ref, vec_ref, gx_ref, gb_ref, gv_ref, gw_ref):
    cols = w_ref.shape[2] // 4
    n = x_ref.shape[0]

    @pl.when(pl.program_id(0) == 0)
    def _():
        gw_ref[...] = jnp.zeros_like(gw_ref)
        gv_ref[...] = jnp.zeros_like(gv_ref)

    live = live_rows(n, rows)
    x = jnp.where(live, x_ref[...], 0.0)
    up = jnp.where(live, up_ref[...], 0.0)
    ub = up.astype(BF)
    gx_ref[...] = attn_back_common(
        x, ub, up, w_ref, vec_ref, 4, 11,
        lambda g: mix_ref[g],
        lambda g, j, rs: tuple(
            qkv_ref[g, rs, cols * t + 128 * j : cols * t + 128 * (j + 1)] for t in range(3)
        ),
        lambda head, b: p_ref[head, GROUP * b : GROUP * (b + 1)],
        lambda head, rs: r_ref[rs, head : head + 1],
        gw_ref, gv_ref, cols, n // GROUP,
    )

    @pl.when(pl.program_id(0) == pl.num_programs(0) - 1)
    def _():
        gb_ref[...] = gw_ref[...].astype(BF)


def temporal_bwd(x, up, qkv, mix, p, r, weights, vec):
    rows, D = x.shape
    cols = D // 2
    heads = D // HEAD
    n = STEP_GROUPS * GROUP
    steps = -(-rows // n)
    whole = lambda *shape: pl.BlockSpec(shape, lambda i: (0,) * len(shape))
    return pl.pallas_call(
        functools.partial(temporal_bwd_kernel, rows),
        grid=(steps,),
        in_specs=[
            pl.BlockSpec((n, D), lambda i: (i, 0)),
            pl.BlockSpec((n, D), lambda i: (i, 0)),
            pl.BlockSpec((2, n, 3 * cols), lambda i: (0, i, 0)),
            pl.BlockSpec((2, n, cols), lambda i: (0, i, 0)),
            pl.BlockSpec((heads, n, GROUP), lambda i: (0, i, 0)),
            pl.BlockSpec((n, 128), lambda i: (i, 0)),
            pl.BlockSpec((2, D, 4 * cols), lambda i: (0, 0, 0)),
            whole(*vec.shape),
        ],
        out_specs=[
            pl.BlockSpec((n, D), lambda i: (i, 0)),
            whole(2, D, 4 * cols),
            whole(8, D),
        ],
        out_shape=[
            jax.ShapeDtypeStruct((rows, D), F32),
            jax.ShapeDtypeStruct((2, D, 4 * cols), BF),
            jax.ShapeDtypeStruct((8, D), F32),
        ],
        scratch_shapes=[pltpu.VMEM((2, D, 4 * cols), F32)],
        name="temporal_bwd",
        compiler_params=pltpu.CompilerParams(vmem_limit_bytes=VMEM_BYTES),
    )(x, up, qkv, mix, p, r, weights, vec)


MLP_ROWS = 416
INV_SQRT2 = 0.7071067811865476
INV_SQRT2PI = 0.3989422804014327


def mlp_kernel(x_ref, cot_ref, wi_ref, wo_ref, vec_ref, hid_ref, out_ref, up_ref, gi_ref, go_ref, gv_ref, gh_ref, ai_ref, ao_ref):
    @pl.when(pl.program_id(0) == 0)
    def _():
        ai_ref[...] = jnp.zeros_like(ai_ref)
        ao_ref[...] = jnp.zeros_like(ao_ref)
        gv_ref[...] = jnp.zeros_like(gv_ref)
        gh_ref[...] = jnp.zeros_like(gh_ref)

    width = wi_ref.shape[2]
    x = x_ref[...]
    xhat, rstd = norm_parts(x)
    gain = vec_ref[12:13, :]
    normed = (xhat * gain + vec_ref[8:9, :]).astype(BF)
    ub = cot_ref[...]
    up = ub.astype(F32)
    gv_ref[3:4, :] += jnp.sum(up, axis=0, keepdims=True)
    branch = vec_ref[9:10, :]
    dn = None
    chunk = 768
    for g in range(2):
        for c in range(width // chunk):
            sl = slice(chunk * c, chunk * (c + 1))
            pre = dot(normed, wi_ref[g, :, sl], NN) + hid_ref[g : g + 1, sl]
            cdf = 0.5 + 0.5 * lax.erf(pre * INV_SQRT2)
            act = (pre * cdf).astype(BF)
            branch = branch + dot(act, wo_ref[g, :, sl], NT)
            ao_ref[g, :, sl] += dot(ub, act, TN)
            dact = dot(ub, wo_ref[g, :, sl], NN).astype(BF).astype(F32)
            slope = cdf + pre * (jnp.exp(pre * pre * -0.5) * INV_SQRT2PI)
            dpre32 = dact * slope
            dpre = dpre32.astype(BF)
            gh_ref[g : g + 1, sl] += jnp.sum(dpre.astype(F32), axis=0, keepdims=True)
            ai_ref[g, :, sl] += dot(normed, dpre, TN)
            term = dot(dpre, wi_ref[g, :, sl], NT)
            dn = term if dn is None else dn + term
    out_ref[...] = (x + branch).astype(BF)
    gv_ref[0:1, :] += jnp.sum(dn, axis=0, keepdims=True)
    gv_ref[4:5, :] += jnp.sum(dn * xhat, axis=0, keepdims=True)
    up_ref[...] = up + norm_back(dn, xhat, rstd, gain)

    @pl.when(pl.program_id(0) == pl.num_programs(0) - 1)
    def _():
        gi_ref[...] = ai_ref[...].astype(BF)
        go_ref[...] = ao_ref[...].astype(BF)


def mlp_both(x, cot, w_in, w_down, vec, hidden):
    rows, D = x.shape
    width = hidden.shape[1]
    n = MLP_ROWS
    whole = lambda *shape: pl.BlockSpec(shape, lambda i: (0,) * len(shape))
    one = pl.Buffered(1)
    return pl.pallas_call(
        mlp_kernel,
        grid=(rows // n,),
        in_specs=[
            pl.BlockSpec((n, D), lambda i: (i, 0)),
            pl.BlockSpec((n, D), lambda i: (i, 0)),
            pl.BlockSpec((2, D, width), lambda i: (0, 0, 0), pipeline_mode=one),
            pl.BlockSpec((2, D, width), lambda i: (0, 0, 0), pipeline_mode=one),
            whole(*vec.shape),
            whole(*hidden.shape),
        ],
        out_specs=[
            pl.BlockSpec((n, D), lambda i: (i, 0)),
            pl.BlockSpec((n, D), lambda i: (i, 0)),
            pl.BlockSpec((2, D, width), lambda i: (0, 0, 0)),
            pl.BlockSpec((2, D, width), lambda i: (0, 0, 0)),
            whole(8, D),
            whole(*hidden.shape),
        ],
        out_shape=[
            jax.ShapeDtypeStruct((rows, D), BF),
            jax.ShapeDtypeStruct((rows, D), F32),
            jax.ShapeDtypeStruct((2, D, width), BF),
            jax.ShapeDtypeStruct((2, D, width), BF),
            jax.ShapeDtypeStruct((8, D), F32),
            jax.ShapeDtypeStruct(hidden.shape, F32),
        ],
        scratch_shapes=[pltpu.VMEM((2, D, width), F32), pltpu.VMEM((2, D, width), F32)],
        name="mlp_both",
        compiler_params=pltpu.CompilerParams(vmem_limit_bytes=VMEM_BYTES),
    )(x, cot, w_in, w_down, vec, hidden)


MESH = pl.DeviceIdType.MESH


class Place:
    def __init__(self, lines):
        self.lines = lines
        self.dp = lax.axis_index("dp")
        self.t = lax.axis_index("tensor")
        self.z = self.dp // 4
        self.y = (self.dp // 2) % 2
        self.x = self.dp % 2
        self.a = self.y * (1 - self.t) + self.x * self.t
        self.b = self.x * (1 - self.t) + self.y * self.t
        toward_y = self.dp + 2 - 4 * self.y
        toward_x = self.dp + 1 - 2 * self.x
        self.first = (toward_y * (1 - self.t) + toward_x * self.t, self.t)
        self.second = (toward_x * (1 - self.t) + toward_y * self.t, self.t)
        self.core = (self.dp, 1 - self.t)
        self.up = (self.dp + 4, self.t)
        self.down = (self.dp - 4, self.t)

    def yx(self, a, b, t):
        return a * (1 - t) + b * t, b * (1 - t) + a * t

    def greet(self):
        bar = pltpu.get_barrier_semaphore()
        for who in (self.core, self.first, self.second):
            pl.semaphore_signal(bar, inc=1, device_id=who, device_id_type=MESH)

        @pl.when(self.z > 0)
        def _():
            pl.semaphore_signal(bar, inc=1, device_id=self.down, device_id_type=MESH)

        @pl.when(self.z < self.lines - 1)
        def _():
            pl.semaphore_signal(bar, inc=1, device_id=self.up, device_id_type=MESH)

        inner = (self.z > 0).astype(jnp.int32) + (self.z < self.lines - 1).astype(jnp.int32)
        pl.semaphore_wait(bar, 3 + inner)


def remote(src, dst, sems, i, who):
    return pltpu.make_async_remote_copy(
        src_ref=src, dst_ref=dst, send_sem=sems[0].at[i], recv_sem=sems[1].at[i],
        device_id=who, device_id_type=MESH,
    )


class Reduce:
    @staticmethod
    def scratch(lines, rows, width, dtype):
        block = (rows, width)
        n = 4 + 2 * lines
        return [
            pltpu.VMEM((lines, 2, 2) + block, dtype),
            pltpu.VMEM((lines, 2, 2) + block, dtype),
            pltpu.VMEM((lines, 2) + block, dtype),
            pltpu.VMEM((lines,) + block, dtype),
            pltpu.VMEM((lines,) + block, dtype),
            pltpu.VMEM((lines,) + block, dtype),
            pltpu.SemaphoreType.DMA((n,)),
            pltpu.SemaphoreType.DMA((n,)),
            pltpu.SemaphoreType.DMA((4,)),
        ]

    n_scratch = 9

    def __init__(self, place, g_ref, out_ref, scratch):
        self.p = place
        self.g, self.out = g_ref, out_ref
        self.own, self.land0, self.land1, self.land2, self.from_down, self.from_up = scratch[:6]
        self.sems = scratch[6:8]
        self.local = scratch[8]
        self.stages = 3 + place.lines

    def _core(self):
        p = self.p
        copies = []
        for a in range(2):
            for b in range(2):
                y, x = p.yx(a, b, 1 - p.t)
                copies.append(
                    remote(self.g.at[1 - p.t, :, y, x], self.land0.at[:, a, b], self.sems, 2 * a + b, p.core)
                )
        return copies

    def _load(self):
        p = self.p
        copies = []
        for a in range(2):
            for b in range(2):
                y, x = p.yx(a, b, p.t)
                copies.append(
                    pltpu.make_async_copy(self.g.at[p.t, :, y, x], self.own.at[:, a, b], self.local.at[2 * a + b])
                )
        return copies

    def _first(self):
        p = self.p
        return remote(self.own.at[:, 1 - p.a], self.land1, self.sems, 4, p.first)

    def _second(self):
        p = self.p
        return remote(self.own.at[:, p.a, 1 - p.b], self.land2, self.sems, 5, p.second)

    def _up(self, slab, i):
        return remote(self.from_down.at[slab], self.from_down.at[slab], self.sems, 6 + i, self.p.up)

    def _down(self, slab, i):
        return remote(self.from_up.at[slab], self.from_up.at[slab], self.sems, 6 + self.p.lines - 1 + i, self.p.down)

    def stage(self, k):
        p, n = self.p, self.p.lines
        add = lambda u, v: (u.astype(F32) + v.astype(F32)).astype(self.own.dtype)
        if k == 0:
            for c in self._core():
                c.start()
            for c in self._load():
                c.start()
        elif k == 1:
            for c in self._load():
                c.wait()
            for c in self._core():
                c.wait()

            def body(i, _):
                self.own[i] = add(self.own[i], self.land0[i])
                return _

            lax.fori_loop(0, n, body, 0)
            self._first().start()
        elif k == 2:
            self._first().wait()

            def body(i, _):
                self.own[i, p.a] = add(self.own[i, p.a], self.land1[i])
                return _

            lax.fori_loop(0, n, body, 0)
            self._second().start()
        elif k == 3:
            self._second().wait()

            def body(i, _):
                total = add(self.own[i, p.a, p.b], self.land2[i])
                self.own[i, p.a, p.b] = total
                return _

            lax.fori_loop(0, n, body, 0)
            self._line(0)
        elif k < 3 + n - 1:
            self._line(k - 3)
        else:
            self._finish()

    def _line(self, step):
        p, n = self.p, self.p.lines
        for z in range(n):
            mine = lambda slab: self.own[slab, p.a, p.b]
            @pl.when(p.z == z)
            def _():
                if z < n - 1:
                    for d in range(z + 1, n):
                        i = n - 1 - d
                        if z + i == step:
                            if z > 0:
                                self._up_wait(d, i)
                                self.from_down[d] = (
                                    self.from_down[d].astype(F32) + mine(d).astype(F32)
                                ).astype(self.own.dtype)
                            else:
                                self.from_down[d] = mine(d)
                            self._up(d, i).start()
                if z > 0:
                    for d in range(0, z):
                        i = d
                        if (n - 1 - z) + i == step:
                            if z < n - 1:
                                self._down_wait(d, i)
                                self.from_up[d] = (
                                    self.from_up[d].astype(F32) + mine(d).astype(F32)
                                ).astype(self.own.dtype)
                            else:
                                self.from_up[d] = mine(d)
                            self._down(d, i).start()

    def _up_wait(self, d, i):
        self._up(d, i).wait_recv()

    def _down_wait(self, d, i):
        self._down(d, i).wait_recv()

    def _finish(self):
        p, n = self.p, self.p.lines
        for z in range(n):
            @pl.when(p.z == z)
            def _():
                total = self.own[z, p.a, p.b].astype(F32)
                if z > 0:
                    self._up_wait(z, n - 1 - z)
                    total = total + self.from_down[z].astype(F32)
                if z < n - 1:
                    self._down_wait(z, z)
                    total = total + self.from_up[z].astype(F32)
                self.out[...] = total
                for d in range(z + 1, n):
                    self._up(d, n - 1 - d).wait_send()
                for d in range(0, z):
                    self._down(d, d).wait_send()


def reduce_kernel(n, lines, *refs):
    place = Place(lines)
    place.greet()
    g_refs, out_refs, scratch = refs[:n], refs[n : 2 * n], refs[2 * n :]
    m = Reduce.n_scratch
    jobs = [Reduce(place, g_refs[i], out_refs[i], scratch[i * m : (i + 1) * m]) for i in range(n)]
    for step in range(jobs[0].stages + n - 1):
        for i, job in enumerate(jobs):
            if 0 <= step - i < job.stages:
                job.stage(step - i)


def reduce_all(grads, lines, collective_id):
    n = len(grads)
    shapes = []
    for g in grads:
        shapes += Reduce.scratch(lines, g.shape[4], g.shape[5], g.dtype)
    return pl.pallas_call(
        functools.partial(reduce_kernel, n, lines),
        in_specs=[pl.BlockSpec(memory_space=pl.ANY)] * n,
        out_specs=[pl.BlockSpec(memory_space=pltpu.VMEM)] * n,
        out_shape=[jax.ShapeDtypeStruct(g.shape[4:], F32) for g in grads],
        scratch_shapes=shapes,
        name="reduce_all",
        compiler_params=pltpu.CompilerParams(
            collective_id=collective_id, has_side_effects=True, vmem_limit_bytes=60 * 1024 * 1024
        ),
    )(*grads)


class Gather:
    @staticmethod
    def scratch(lines):
        n = 2 * (lines - 1) + 5
        return [pltpu.SemaphoreType.DMA((n,)), pltpu.SemaphoreType.DMA((n,)), pltpu.SemaphoreType.DMA((1,))]

    n_scratch = 3

    def __init__(self, place, own_ref, full_ref, scratch):
        self.p, self.own, self.full = place, own_ref, full_ref
        self.sems, self.local = scratch[:2], scratch[2]
        self.hops = place.lines - 1
        self.stages = self.hops + 4

    def _slab(self, z):
        p = self.p
        return self.full.at[p.t, z, p.y, p.x]

    def _up(self, k):
        src = self.own if k == 0 else self._slab(self.p.z - k)
        return remote(src, self._slab(self.p.z - k), self.sems, k, self.p.up)

    def _down(self, k):
        src = self.own if k == 0 else self._slab(self.p.z + k)
        return remote(src, self._slab(self.p.z + k), self.sems, self.hops + k, self.p.down)

    def _send_line(self, k):
        p = self.p

        @pl.when((p.z < self.hops) & (p.z >= k))
        def _():
            self._up(k).start()

        @pl.when((p.z > 0) & (p.z + k <= self.hops))
        def _():
            self._down(k).start()

    def _take_line(self, k):
        p = self.p

        @pl.when(p.z >= k + 1)
        def _():
            self._up(k).wait_recv()

        @pl.when(p.z + k + 1 <= self.hops)
        def _():
            self._down(k).wait_recv()

    def _column(self, i, who, y, x):
        block = self.full.at[self.p.t, :, y, x]
        return remote(block, block, self.sems, 2 * self.hops + i, who)

    def _first(self):
        return self._column(0, self.p.first, self.p.y, self.p.x)

    def _plane(self, i, who, b):
        p = self.p
        block0 = self.full.at[p.t, :, :, b]
        block1 = self.full.at[p.t, :, b, :]
        return (
            remote(block0, block0, self.sems, 2 * self.hops + i, who),
            remote(block1, block1, self.sems, 2 * self.hops + i, who),
        )

    def _each(self, pair, act):
        @pl.when(self.p.t == 0)
        def _():
            act(pair[0])

        @pl.when(self.p.t == 1)
        def _():
            act(pair[1])

    def _core(self, i):
        p = self.p
        if i == 0:
            return self._column(2, p.core, p.y, p.x)
        y, x = p.yx(1 - p.a, p.b, p.t)
        return self._column(3, p.core, y, x)

    def stage(self, k):
        p = self.p
        if k == 0:
            pltpu.make_async_copy(self.own, self._slab(p.z), self.local.at[0]).start()
            self._send_line(0)
        elif k < self.hops:
            self._take_line(k - 1)
            self._send_line(k)
        elif k == self.hops:
            self._take_line(k - 1)
            pltpu.make_async_copy(self.own, self._slab(p.z), self.local.at[0]).wait()
            self._first().start()
            self._core(0).start()
        elif k == self.hops + 1:
            self._first().wait_recv()
            self._each(self._plane(1, p.second, p.b), lambda c: c.start())
            self._core(1).start()
        elif k == self.hops + 2:
            self._each(self._plane(1, p.second, p.b), lambda c: c.wait_recv())
            self._each(self._plane(4, p.core, 1 - p.b), lambda c: c.start())
        else:
            self._core(0).wait()
            self._core(1).wait()
            self._each(self._plane(4, p.core, 1 - p.b), lambda c: c.wait())
            self._first().wait_send()
            self._each(self._plane(1, p.second, p.b), lambda c: c.wait_send())
            for k in range(self.hops):
                @pl.when((p.z < self.hops) & (p.z >= k))
                def _():
                    self._up(k).wait_send()

                @pl.when((p.z > 0) & (p.z + k <= self.hops))
                def _():
                    self._down(k).wait_send()


def gather_kernel(n, lines, *refs):
    place = Place(lines)
    place.greet()
    own_refs, full_refs, scratch = refs[:n], refs[n : 2 * n], refs[2 * n :]
    m = Gather.n_scratch
    jobs = [Gather(place, own_refs[i], full_refs[i], scratch[i * m : (i + 1) * m]) for i in range(n)]
    for step in range(jobs[0].stages + n - 1):
        for i, job in enumerate(jobs):
            if 0 <= step - i < job.stages:
                job.stage(step - i)


def gather_all(owns, lines, collective_id):
    n = len(owns)
    scratch = []
    for _ in owns:
        scratch += Gather.scratch(lines)
    return pl.pallas_call(
        functools.partial(gather_kernel, n, lines),
        in_specs=[pl.BlockSpec(memory_space=pl.ANY)] * n,
        out_specs=[pl.BlockSpec(memory_space=pl.ANY)] * n,
        out_shape=[jax.ShapeDtypeStruct((2, lines, 2, 2) + o.shape, o.dtype) for o in owns],
        scratch_shapes=scratch,
        name="gather_all",
        compiler_params=pltpu.CompilerParams(collective_id=collective_id, has_side_effects=True),
    )(*owns)


def to_patch_groups(rows):
    frames, pad, D = rows.shape
    swapped = lax.all_to_all(
        rows.reshape(frames, 2, pad // 2, D), "tensor", split_axis=1, concat_axis=0, tiled=True
    )
    return (
        swapped.reshape(2 * frames, pad // 16, 8, D).transpose(1, 0, 2, 3).reshape(frames * pad, D)
    )


def to_frames(rows):
    total, D = rows.shape
    frames = total // PAD
    blocks = rows.reshape(PAD // 16, 2 * frames, 8, D).transpose(1, 0, 2, 3)
    swapped = lax.all_to_all(
        blocks.reshape(2 * frames, 1, PAD // 2, D), "tensor", split_axis=0, concat_axis=1, tiled=True
    )
    return swapped.reshape(frames, PAD, D)


def pad_frames(rows):
    D = rows.shape[1]
    return jnp.pad(rows.reshape(-1, PATCHES, D), ((0, 0), (0, PAD - PATCHES), (0, 0)))


def strip_frames(rows):
    D = rows.shape[2]
    return rows[:, :PATCHES].reshape(-1, D)


def shards(tokens, cotangent, attn_qkv, attn_out, mlp_in, mlp_out, norm_gains, biases, hidden_bias):
    D = tokens.shape[1]
    depth = mlp_in.shape[1]
    cols = attn_qkv.shape[4]
    units = mlp_in.shape[2]
    everyone = ("dp", "tensor")
    owns = [
        jnp.concatenate([attn_qkv[0, s].reshape(depth, 3 * cols), attn_out[0, s].T], axis=1)
        for s in range(2)
    ]
    owns += [mlp_in[0], mlp_out[0].T]
    small = jnp.concatenate(
        [biases[0].reshape(-1), norm_gains[0].reshape(-1), hidden_bias[0].reshape(-1)]
    )
    count = small.shape[0]
    direct = depth % 16 == 0
    if direct:
        lines = D // depth // 4
        tile = jnp.pad(small, (0, 1024 - count)).reshape(8, 128)
        tile, *weights = gather_all([tile] + owns, lines, 1)
        small = tile.reshape(2, D // depth, 1024).transpose(1, 0, 2).reshape(-1, 1024)[:, :count]
        weights = [w.reshape(2, D, w.shape[5]) for w in weights]
    else:
        small = lax.all_gather(small.reshape(1, -1), everyone, axis=0, tiled=True)
        weights = [
            lax.all_gather(w, ("tensor", "dp"), axis=0, tiled=True).reshape(2, D, -1) for w in owns
        ]
    devices = small.shape[0]
    share = D // devices
    vec = small[:, : 13 * share].reshape(devices, 13, share).transpose(1, 0, 2).reshape(13, D)
    hidden = small[:, 13 * share :].reshape(2, units)

    x = pad_frames(tokens)
    stream1, s_qkv, s_mix, s_p, s_r = spatial_fwd(x, weights[0], vec)
    x1 = to_patch_groups(stream1)
    x2, t_qkv, t_mix, t_p, t_r = temporal_fwd(x1, weights[1], vec)
    cot = to_patch_groups(pad_frames(cotangent))
    out_b, up2, g_in, g_down, gv_m, g_hidden = mlp_both(x2, cot, weights[2], weights[3], vec, hidden)
    output = strip_frames(to_frames(out_b))
    up1, g_t, gv_t = temporal_bwd(x1, up2, t_qkv, t_mix, t_p, t_r, weights[1], vec)
    up1 = to_frames(up1)
    up0, g_s, gv_s = spatial_bwd(x, up1, s_qkv, s_mix, s_p, s_r, weights[0], vec)
    grad_tokens = strip_frames(up0)

    vec_grad = jnp.concatenate([gv_s[0:4], gv_t[0:4], gv_m[0:1], gv_m[3:4], gv_s[4:5], gv_t[4:5], gv_m[4:5]])
    small_grad = jnp.concatenate(
        [
            vec_grad.reshape(13, devices, share).transpose(1, 0, 2).reshape(devices, 13 * share),
            g_hidden.reshape(devices, -1),
        ],
        axis=1,
    )
    grads = [g_s, g_t, g_in, g_down]
    if direct:
        tiles = jnp.pad(small_grad, ((0, 0), (0, 1024 - count))).reshape(-1, 2, 8, 128)
        tiles = tiles.transpose(1, 0, 2, 3).reshape(2, lines, 2, 2, 8, 128)
        grads = [g.reshape(2, lines, 2, 2, depth, g.shape[2]) for g in grads]
        *grads, small_grad = reduce_all(grads + [tiles], lines, 2)
        small_grad = small_grad.reshape(-1)[:count]
    else:
        grads = [
            lax.psum_scatter(
                g.reshape(2 * D, g.shape[2]), ("tensor", "dp"), scatter_dimension=0, tiled=True
            ).astype(F32)
            for g in grads
        ]
        small_grad = lax.psum_scatter(small_grad, everyone, scatter_dimension=0, tiled=True)[0]
    g_s, g_t, g_in, g_down = grads
    grad_qkv = jnp.stack([g[:, : 3 * cols].reshape(depth, 3, cols) for g in (g_s, g_t)])[None]
    grad_out = jnp.stack([g[:, 3 * cols :].T for g in (g_s, g_t)])[None]
    grad_biases = small_grad[: 10 * share].reshape(1, 10, share)
    grad_gains = small_grad[10 * share : 13 * share].reshape(1, 3, share)
    grad_hidden = small_grad[13 * share :].reshape(1, -1)
    return (
        output,
        grad_tokens,
        grad_qkv,
        grad_out,
        g_in[None],
        g_down.T[None],
        grad_gains,
        grad_biases,
        grad_hidden,
    )


def solution(mesh):
    placed = (
        P(("dp", "tensor"), None),
        P(("dp", "tensor"), None),
        P(None, None, "dp", None, "tensor"),
        P(None, None, "tensor", "dp"),
        P(None, "dp", "tensor"),
        P(None, "tensor", "dp"),
        P(None, None, ("dp", "tensor")),
        P(None, None, ("dp", "tensor")),
        P(None, ("dp", "tensor")),
    )
    return jax.shard_map(
        shards, mesh=mesh, in_specs=placed, out_specs=placed, check_vma=False
    )
```

```python
import functools
import jax
import jax.numpy as jnp
from jax import lax
from jax.experimental import pallas as pl
from jax.experimental.pallas import tpu as pltpu
from jax.sharding import PartitionSpec as P

HEAD = 64
FRAMES = 16
PATCHES = 196
PAD = 208
EPSILON = 1e-06
BF = jnp.bfloat16
F32 = jnp.float32
NN = (((1,), (0,)), ((), ()))
NT = (((1,), (1,)), ((), ()))
TN = (((0,), (0,)), ((), ()))
VMEM_BYTES = 60 * 1024 * 1024


def dot(a, b, dims):
    return lax.dot_general(a, b, dims, preferred_element_type=F32)


def norm_parts(x):
    mean = jnp.mean(x, axis=-1, keepdims=True)
    centred = x - mean
    var = jnp.mean(centred * centred, axis=-1, keepdims=True)
    rstd = lax.rsqrt(var + EPSILON)
    return centred * rstd, rstd


def norm_back(grad_normed, xhat, rstd, gain):
    scaled = grad_normed * gain
    first = jnp.mean(scaled, axis=-1, keepdims=True)
    second = jnp.mean(scaled * xhat, axis=-1, keepdims=True)
    return rstd * (scaled - first - xhat * second)


def split_halves(pair):
    lane = lax.broadcasted_iota(jnp.int32, pair.shape, 1)
    zero = jnp.zeros_like(pair)
    return jnp.where(lane < HEAD, pair, zero), jnp.where(lane < HEAD, zero, pair)


def project(normed, w_ref, vec_ref, row_base, cols):
    parts = []
    for g in range(2):
        w = w_ref[g, :, 0 : 3 * cols]
        qkv = dot(normed, w, NN)
        bq = vec_ref[row_base + 1 : row_base + 2, g * cols : (g + 1) * cols]
        bv = vec_ref[row_base + 2 : row_base + 3, g * cols : (g + 1) * cols]
        q = (qkv[:, :cols] + bq).astype(BF) * BF(0.125)
        k = qkv[:, cols : 2 * cols].astype(BF)
        v = (qkv[:, 2 * cols :] + bv).astype(BF)
        parts.append((q, k, v))
    return parts


def stack_halves(pair):
    return jnp.concatenate(split_halves(pair), axis=0)


def merge_halves(both):
    rows = both.shape[0] // 2
    lane = lax.broadcasted_iota(jnp.int32, (rows, both.shape[1]), 1)
    return jnp.where(lane < HEAD, both[:rows], both[rows:])


def heads_forward(pairs, mask):
    scores = [dot(stack_halves(q), k, NT) for q, k, _ in pairs]
    exps, recips = [], []
    for s in scores:
        s = jnp.where(mask, s, -1e30)
        e = jnp.exp(s - jnp.max(s, axis=-1, keepdims=True))
        recips.append(1.0 / jnp.sum(e, axis=-1, keepdims=True))
        exps.append(e.astype(BF))
    outs = [merge_halves(dot(e, v, NN) * r) for e, r, (_, _, v) in zip(exps, recips, pairs)]
    return outs, exps, recips


def heads_backward(pairs):
    dors, deltas = [], []
    for q, k, v, o, do, e, r in pairs:
        both = stack_halves(do.astype(F32)) * r
        deltas.append(jnp.sum(both * jnp.concatenate([o, o], axis=0).astype(F32), axis=-1, keepdims=True))
        dors.append(both.astype(BF))
    dps = [dot(dor, p[2], NT) for dor, p in zip(dors, pairs)]
    dss = [(p[5].astype(F32) * (dp - delta)).astype(BF) for dp, delta, p in zip(dps, deltas, pairs)]
    dq = [(merge_halves(dot(ds, p[1], NN)) * 0.125).astype(BF) for ds, p in zip(dss, pairs)]
    dk = [dot(ds, stack_halves(p[0]), TN).astype(BF) for ds, p in zip(dss, pairs)]
    dv = [dot(p[5], dor, TN).astype(BF) for dor, p in zip(dors, pairs)]
    return dq, dk, dv


def spatial_mask():
    return lax.broadcasted_iota(jnp.int32, (2 * PAD, PAD), 1) < PATCHES


def attn_back_common(x, ub, up, w_ref, vec_ref, row_base, gain_row, mix_of, qkv_of, exps_of, gw_ref, gv_ref, cols, blocks):
    xhat, rstd = norm_parts(x)
    gain = vec_ref[gain_row : gain_row + 1, :]
    normed = (xhat * gain + vec_ref[row_base : row_base + 1, :]).astype(BF)
    dn = None
    gv_ref[3:4, :] += jnp.sum(up, axis=0, keepdims=True)
    rows = x.shape[0]
    step = rows // blocks
    for g in range(2):
        wo = w_ref[g, :, 3 * cols : 4 * cols]
        dmix = dot(ub, wo, NN).astype(BF)
        mix = mix_of(g)
        gw_ref[g, :, 3 * cols : 4 * cols] += dot(ub, mix, TN)
        parts = [[], [], []]
        for b in range(blocks):
            rs = slice(step * b, step * (b + 1))
            pairs = []
            for j in range(cols // 128):
                sl = slice(128 * j, 128 * (j + 1))
                q, k, v = qkv_of(g, j, rs)
                e, r = exps_of(g * (cols // 128) + j, b)
                pairs.append((q, k, v, mix[rs, sl], dmix[rs, sl], e, r))
            for part, got in zip(parts, heads_backward(pairs)):
                part.append(jnp.concatenate(got, axis=1))
        dq, dk, dv = [jnp.concatenate(part, axis=0) for part in parts]
        span = slice(g * cols, (g + 1) * cols)
        gv_ref[1:2, span] += jnp.sum(dq.astype(F32), axis=0, keepdims=True)
        gv_ref[2:3, span] += jnp.sum(dv.astype(F32), axis=0, keepdims=True)
        dqkv = jnp.concatenate([dq, dk, dv], axis=1)
        gw_ref[g, :, 0 : 3 * cols] += dot(normed, dqkv, TN)
        term = dot(dqkv, w_ref[g, :, 0 : 3 * cols], NT)
        dn = term if dn is None else dn + term
    gv_ref[0:1, :] += jnp.sum(dn, axis=0, keepdims=True)
    gv_ref[4:5, :] += jnp.sum(dn * xhat, axis=0, keepdims=True)
    return up + norm_back(dn, xhat, rstd, gain)


MESH = pl.DeviceIdType.MESH


class Place:
    def __init__(self, lines):
        self.lines = lines
        self.dp = lax.axis_index("dp")
        self.t = lax.axis_index("tensor")
        self.z = self.dp // 4
        self.y = (self.dp // 2) % 2
        self.x = self.dp % 2
        self.a = self.y * (1 - self.t) + self.x * self.t
        self.b = self.x * (1 - self.t) + self.y * self.t
        toward_y = self.dp + 2 - 4 * self.y
        toward_x = self.dp + 1 - 2 * self.x
        self.first = (toward_y * (1 - self.t) + toward_x * self.t, self.t)
        self.second = (toward_x * (1 - self.t) + toward_y * self.t, self.t)
        self.core = (self.dp, 1 - self.t)
        self.up = (self.dp + 4, self.t)
        self.down = (self.dp - 4, self.t)

    def yx(self, a, b, t):
        return a * (1 - t) + b * t, b * (1 - t) + a * t

    def greet(self, line):
        bar = pltpu.get_barrier_semaphore()
        for who in (self.core, self.first, self.second):
            pl.semaphore_signal(bar, inc=1, device_id=who, device_id_type=MESH)
        if not line:
            pl.semaphore_wait(bar, 3)
            return

        @pl.when(self.z > 0)
        def _():
            pl.semaphore_signal(bar, inc=1, device_id=self.down, device_id_type=MESH)

        @pl.when(self.z < self.lines - 1)
        def _():
            pl.semaphore_signal(bar, inc=1, device_id=self.up, device_id_type=MESH)

        inner = (self.z > 0).astype(jnp.int32) + (self.z < self.lines - 1).astype(jnp.int32)
        pl.semaphore_wait(bar, 3 + inner)


def remote(src, dst, sems, i, who):
    return pltpu.make_async_remote_copy(
        src_ref=src, dst_ref=dst, send_sem=sems[0].at[i], recv_sem=sems[1].at[i],
        device_id=who, device_id_type=MESH,
    )


def dma_sems(n):
    return pltpu.SemaphoreType.DMA((n,))


class LineGather:
    @staticmethod
    def scratch(lines):
        return [dma_sems(2 * (lines - 1)), dma_sems(2 * (lines - 1)), dma_sems(1)]

    def __init__(self, place, own_ref, col_ref, scratch):
        self.p, self.own, self.col = place, own_ref, col_ref
        self.sems, self.local = scratch[:2], scratch[2]
        self.hops = place.lines - 1
        self.stages = self.hops + 1

    def _keep(self):
        return pltpu.make_async_copy(self.own, self.col.at[self.p.z], self.local.at[0])

    def _up(self, k):
        block = self.col.at[self.p.z - k]
        return remote(self.own if k == 0 else block, block, self.sems, k, self.p.up)

    def _down(self, k):
        block = self.col.at[self.p.z + k]
        return remote(self.own if k == 0 else block, block, self.sems, self.hops + k, self.p.down)

    def _each(self, k, up, down):
        p = self.p

        @pl.when((p.z < self.hops) & (p.z >= k))
        def _():
            up(self._up(k))

        @pl.when((p.z > 0) & (p.z + k <= self.hops))
        def _():
            down(self._down(k))

    def _take(self, k):
        p = self.p

        @pl.when(p.z >= k + 1)
        def _():
            self._up(k).wait_recv()

        @pl.when(p.z + k + 1 <= self.hops)
        def _():
            self._down(k).wait_recv()

    def stage(self, k):
        start = lambda c: c.start()
        if k == 0:
            self._keep().start()
            self._each(0, start, start)
            return
        self._take(k - 1)
        if k < self.hops:
            self._each(k, start, start)
        else:
            self._keep().wait()
            done = lambda c: c.wait_send()
            for i in range(self.hops):
                self._each(i, done, done)


class PlaneGather:
    @staticmethod
    def scratch():
        return [dma_sems(5), dma_sems(5), dma_sems(1)]

    stages = 4

    def __init__(self, place, col_ref, full_ref, scratch):
        self.p, self.col, self.full = place, col_ref, full_ref
        self.sems, self.local = scratch[:2], scratch[2]

    def _keep(self):
        p = self.p
        return pltpu.make_async_copy(self.col, self.full.at[p.t, :, p.y, p.x], self.local.at[0])

    def _own(self, i, who):
        p = self.p
        return remote(self.col, self.full.at[p.t, :, p.y, p.x], self.sems, i, who)

    def _plane(self, i, who, b, act):
        p = self.p
        block0 = self.full.at[p.t, :, :, b]
        block1 = self.full.at[p.t, :, b, :]

        @pl.when(p.t == 0)
        def _():
            act(remote(block0, block0, self.sems, i, who))

        @pl.when(p.t == 1)
        def _():
            act(remote(block1, block1, self.sems, i, who))

    def _pass_on(self):
        p = self.p
        y, x = p.yx(1 - p.a, p.b, p.t)
        block = self.full.at[p.t, :, y, x]
        return remote(block, block, self.sems, 3, p.core)

    def stage(self, k):
        p = self.p
        if k == 0:
            self._keep().start()
            self._own(0, p.first).start()
            self._own(2, p.core).start()
        elif k == 1:
            self._keep().wait()
            self._own(0, p.first).wait_recv()
            self._plane(1, p.second, p.b, lambda c: c.start())
            self._pass_on().start()
        elif k == 2:
            self._plane(1, p.second, p.b, lambda c: c.wait_recv())
            self._plane(4, p.core, 1 - p.b, lambda c: c.start())
        else:
            self._own(2, p.core).wait()
            self._pass_on().wait()
            self._plane(4, p.core, 1 - p.b, lambda c: c.wait())
            self._own(0, p.first).wait_send()
            self._plane(1, p.second, p.b, lambda c: c.wait_send())


def add_blocks(u, v, dtype):
    return (u.astype(F32) + v.astype(F32)).astype(dtype)


class PlaneReduce:
    @staticmethod
    def scratch(lines, rows, width, dtype):
        block = (rows, width)
        return [
            pltpu.VMEM((lines, 2, 2) + block, dtype),
            pltpu.VMEM((lines, 2, 2) + block, dtype),
            pltpu.VMEM((lines, 2) + block, dtype),
            pltpu.VMEM((lines,) + block, dtype),
            dma_sems(6),
            dma_sems(6),
            dma_sems(4),
        ]

    n_scratch = 7
    stages = 4

    def __init__(self, place, g_ref, col_ref, scratch, span=None):
        self.p, self.g, self.col = place, g_ref, col_ref
        self.own, self.land0, self.land1, self.land2 = scratch[:4]
        self.sems, self.local = scratch[4:6], scratch[6]
        self.span = span

    def _part(self, t, y, x):
        if self.span is None:
            return self.g.at[t, :, y, x]
        return self.g.at[t, :, y, x, :, self.span]

    def _core(self):
        p, copies = self.p, []
        for a in range(2):
            for b in range(2):
                y, x = p.yx(a, b, 1 - p.t)
                copies.append(remote(self._part(1 - p.t, y, x), self.land0.at[:, a, b], self.sems, 2 * a + b, p.core))
        return copies

    def _load(self):
        p, copies = self.p, []
        for a in range(2):
            for b in range(2):
                y, x = p.yx(a, b, p.t)
                copies.append(
                    pltpu.make_async_copy(self._part(p.t, y, x), self.own.at[:, a, b], self.local.at[2 * a + b])
                )
        return copies

    def _first(self):
        return remote(self.own.at[:, 1 - self.p.a], self.land1, self.sems, 4, self.p.first)

    def _second(self):
        return remote(self.own.at[:, self.p.a, 1 - self.p.b], self.land2, self.sems, 5, self.p.second)

    def stage(self, k):
        p, dtype = self.p, self.own.dtype
        if k == 0:
            for c in self._core() + self._load():
                c.start()
            return
        if k == 1:
            for c in self._load() + self._core():
                c.wait()

            def away(i, _):
                self.own[i, 1 - p.a] = add_blocks(self.own[i, 1 - p.a], self.land0[i, 1 - p.a], dtype)
                return _

            lax.fori_loop(0, p.lines, away, 0)
            self._first().start()

            def stay(i, _):
                self.own[i, p.a] = add_blocks(self.own[i, p.a], self.land0[i, p.a], dtype)
                return _

            lax.fori_loop(0, p.lines, stay, 0)
        elif k == 2:
            self._first().wait()

            def body(i, _):
                self.own[i, p.a] = add_blocks(self.own[i, p.a], self.land1[i], dtype)
                return _

            lax.fori_loop(0, p.lines, body, 0)
            self._second().start()
        else:
            self._second().wait()

            def body(i, _):
                self.col[i] = add_blocks(self.own[i, p.a, p.b], self.land2[i], dtype)
                return _

            lax.fori_loop(0, p.lines, body, 0)


class LineReduce:
    @staticmethod
    def scratch(lines, rows, width, dtype):
        return [
            pltpu.VMEM((lines, rows, width), dtype),
            pltpu.VMEM((lines, rows, width), dtype),
            dma_sems(2 * (lines - 1)),
            dma_sems(2 * (lines - 1)),
        ]

    n_scratch = 4

    def __init__(self, place, col_ref, out_ref, scratch):
        self.p, self.col, self.out = place, col_ref, out_ref
        self.from_down, self.from_up = scratch[:2]
        self.sems = scratch[2:4]
        self.stages = place.lines

    def _up(self, d):
        block = self.from_down.at[d]
        return remote(block, block, self.sems, d - 1, self.p.up)

    def _down(self, d):
        block = self.from_up.at[d]
        return remote(block, block, self.sems, self.p.lines - 1 + d, self.p.down)

    def stage(self, step):
        p, n = self.p, self.p.lines
        dtype = self.from_down.dtype
        for z in range(n):
            sends_up = [d for d in range(z + 1, n) if z + (n - 1 - d) == step]
            sends_down = [d for d in range(z) if (n - 1 - z) + d == step]
            if step == n - 1:
                pass
            elif not sends_up and not sends_down:
                continue

            @pl.when(p.z == z)
            def _():
                for d in sends_up:
                    if z > 0:
                        self._up(d).wait_recv()
                        self.from_down[d] = add_blocks(self.from_down[d], self.col[d], dtype)
                    else:
                        self.from_down[d] = self.col[d]
                    self._up(d).start()
                for d in sends_down:
                    if z < n - 1:
                        self._down(d).wait_recv()
                        self.from_up[d] = add_blocks(self.from_up[d], self.col[d], dtype)
                    else:
                        self.from_up[d] = self.col[d]
                    self._down(d).start()
                if step == n - 1:
                    total = self.col[z].astype(F32)
                    if z > 0:
                        self._up(z).wait_recv()
                        total = total + self.from_down[z].astype(F32)
                    if z < n - 1:
                        self._down(z).wait_recv()
                        total = total + self.from_up[z].astype(F32)
                    self.out[...] = total
                    for d in range(z + 1, n):
                        self._up(d).wait_send()
                    for d in range(z):
                        self._down(d).wait_send()


def at_step(step, *stages):
    @pl.when(pl.program_id(0) == step)
    def _():
        for job, k in stages:
            job.stage(k)


def take(refs, *counts):
    out, i = [], 0
    for c in counts:
        out.append(refs[i : i + c])
        i += c
    return out


GROUP = 8 * FRAMES
STEP_GROUPS = 2


def temporal_mask():
    a = lax.broadcasted_iota(jnp.int32, (2 * GROUP, GROUP), 0)
    b = lax.broadcasted_iota(jnp.int32, (2 * GROUP, GROUP), 1)
    return (a % 8) == (b % 8)


def any_spec():
    return pl.BlockSpec(memory_space=pl.ANY)


def whole_spec(shape):
    return pl.BlockSpec(tuple(shape), lambda i: (0,) * len(shape))


def struct(shape, dtype):
    return jax.ShapeDtypeStruct(tuple(shape), dtype)


def full_shape(lines, rows, width):
    return (2, lines, 2, 2, rows, width)


def kernel_params(collective_id):
    if collective_id is None:
        return pltpu.CompilerParams(vmem_limit_bytes=VMEM_BYTES)
    return pltpu.CompilerParams(
        vmem_limit_bytes=VMEM_BYTES, collective_id=collective_id, has_side_effects=True
    )


def first_body(lines, tok, cot, tile, own0, own1, own2, x_out, cot_b, full_tile, full0, col_tile, col0, col1, col2,
               tok_v, cot_v, frames_v, ex_send, ex_recv, ex_local, loads, *scratch):
    place = Place(lines)
    t = place.t
    load_cot = pltpu.make_async_copy(cot, cot_v, loads.at[0])
    load_tok = pltpu.make_async_copy(tok, tok_v, loads.at[1])
    load_cot.start()
    load_tok.start()
    place.greet(True)
    parts = take(scratch, 3, 3, 3, 3, 3, 3)
    tile_line = LineGather(place, tile, col_tile, parts[0])
    line0 = LineGather(place, own0, col0, parts[1])
    line1 = LineGather(place, own1, col1, parts[2])
    line2 = LineGather(place, own2, col2, parts[3])
    tile_plane = PlaneGather(place, col_tile, full_tile, parts[4])
    plane0 = PlaneGather(place, col0, full0, parts[5])
    hops = lines - 1

    def line_stage(k):
        tile_line.stage(k)
        line0.stage(k)

    line_stage(0)
    frames = x_out.shape[0]
    half = frames // 2
    D = x_out.shape[2]
    zeros = jnp.zeros((PAD - PATCHES, D), F32)
    load_cot.wait()
    for part in range(2):
        rows = cot_v[half * PATCHES * part : half * PATCHES * (part + 1)].astype(F32)
        for f in range(half):
            frame = jnp.concatenate([rows[PATCHES * f : PATCHES * (f + 1)], zeros], axis=0)
            frames_v[half * part + f] = frame.reshape(PAD // 8, 8, D)
    groups = PAD // 16
    mine = pltpu.make_async_copy(
        frames_v.at[:, pl.ds(groups * t, groups)], cot_b.at[pl.ds(frames * t, frames)], ex_local.at[0]
    )
    theirs = remote(
        frames_v.at[:, pl.ds(groups * (1 - t), groups)], cot_b.at[pl.ds(frames * t, frames)],
        (ex_send, ex_recv), 0, place.core,
    )
    mine.start()
    theirs.start()
    line_stage(1)
    load_tok.wait()
    for part in range(2):
        rows = tok_v[half * PATCHES * part : half * PATCHES * (part + 1)].astype(F32)
        for f in range(half):
            frame = jnp.concatenate([rows[PATCHES * f : PATCHES * (f + 1)], zeros], axis=0)
            x_out[half * part + f] = frame.astype(BF)
    for k in range(2, hops + 1):
        line_stage(k)
    tile_plane.stage(0)
    plane0.stage(0)
    line1.stage(0)
    line1.stage(1)
    tile_plane.stage(1)
    plane0.stage(1)
    for k in range(2, hops + 1):
        line1.stage(k)
    for k in range(hops):
        line2.stage(k)
    tile_plane.stage(2)
    plane0.stage(2)
    line2.stage(hops)
    tile_plane.stage(3)
    plane0.stage(3)
    mine.wait()
    theirs.wait()


def first_call(tokens, cot, tile, own0, own1, own2, lines, collective_id):
    rows, D = tokens.shape
    frames = rows // PATCHES
    groups = PAD // 16
    depth, width = own0.shape
    line = LineGather.scratch(lines)
    plane = PlaneGather.scratch()
    return pl.pallas_call(
        functools.partial(first_body, lines),
        in_specs=[any_spec()] * 6,
        out_specs=[pl.BlockSpec(memory_space=pltpu.VMEM)] + [any_spec()] * 7,
        out_shape=[
            struct((frames, PAD, D), BF),
            struct((2 * frames, groups, 8, D), F32),
            struct(full_shape(lines, 8, 128), F32),
            struct(full_shape(lines, depth, width), BF),
            struct((lines, 8, 128), F32),
            struct((lines, depth, width), BF),
            struct((lines, depth, width), BF),
            struct((lines, depth, width), BF),
        ],
        scratch_shapes=[
            pltpu.VMEM((rows, D), BF),
            pltpu.VMEM((rows, D), BF),
            pltpu.VMEM((frames, PAD // 8, 8, D), F32),
            dma_sems(1),
            dma_sems(1),
            dma_sems(1),
            dma_sems(2),
        ]
        + line * 4
        + plane * 2,
        name="first_gather",
        compiler_params=kernel_params(collective_id),
    )(tokens, cot, tile, own0, own1, own2)


def spatial_forward(x, w_ref, vec_ref, qkv_ref, mix_ref, p_ref, r_ref):
    cols = w_ref.shape[2] // 4
    xhat, _ = norm_parts(x)
    normed = (xhat * vec_ref[10:11, :] + vec_ref[0:1, :]).astype(BF)
    mask = spatial_mask()
    branch = vec_ref[3:4, :]
    for g, (q, k, v) in enumerate(project(normed, w_ref, vec_ref, 0, cols)):
        qkv_ref[0, g, :, 0:cols] = q
        qkv_ref[0, g, :, cols : 2 * cols] = k
        qkv_ref[0, g, :, 2 * cols : 3 * cols] = v
        pairs = []
        for j in range(cols // 128):
            sl = slice(128 * j, 128 * (j + 1))
            pairs.append((q[:, sl], k[:, sl], v[:, sl]))
        mixes, exps, recips = heads_forward(pairs, mask)
        for j in range(cols // 128):
            pair = g * (cols // 128) + j
            p_ref[0, pair] = exps[j]
            r_ref[0, :, pair : pair + 1] = recips[j]
        mix = jnp.concatenate(mixes, axis=1).astype(BF)
        mix_ref[0, g] = mix
        branch = branch + dot(mix, w_ref[g, :, 3 * cols : 4 * cols], NT)
    return x + branch


def spatial_fwd_kernel(lines, *refs):
    if lines is None:
        x_ref, w_ref, vec_ref, s_ref, qkv_ref, mix_ref, p_ref, r_ref = refs
        s = spatial_forward(x_ref[0].astype(F32), w_ref, vec_ref, qkv_ref, mix_ref, p_ref, r_ref)
        s_ref[0] = s.reshape(s_ref.shape[1:])
        return
    (x_ref, w_ref, vec_ref, col1, own3), (s_b, qkv_ref, mix_ref, p_ref, r_ref, full1, col3), (
        slots, ex_send, ex_recv, ex_local), parts = take(refs, 5, 7, 4, 6)
    place = Place(lines)
    t = place.t
    i = pl.program_id(0)
    frames = pl.num_programs(0)
    groups = PAD // 16
    plane1 = PlaneGather(place, col1, full1, parts[:3])
    line3 = LineGather(place, own3, col3, parts[3:])
    last = line3.stages - 1

    @pl.when(i == 0)
    def _():
        place.greet(True)

    at_step(0, (plane1, 0), (line3, 0))
    for k in range(1, last):
        at_step(k, (line3, k))
    at_step(2, (plane1, 1))
    at_step(4, (line3, last))
    at_step(7, (plane1, 2))

    def sends(f):
        slot = slots.at[f % 2]
        return (
            pltpu.make_async_copy(
                slot.at[pl.ds(groups * t, groups)], s_b.at[frames * t + f], ex_local.at[f]
            ),
            remote(
                slot.at[pl.ds(groups * (1 - t), groups)], s_b.at[frames * t + f], (ex_send, ex_recv), f, place.core
            ),
        )

    def sent(f):
        here, there = sends(f)
        here.wait()
        there.wait_send()

    s = spatial_forward(x_ref[0].astype(F32), w_ref, vec_ref, qkv_ref, mix_ref, p_ref, r_ref)

    @pl.when(i >= 2)
    def _():
        sent(i - 2)

    slots[i % 2] = s.reshape(slots.shape[1:])
    for c in sends(i):
        c.start()

    @pl.when(i == frames - 1)
    def _():
        plane1.stage(3)
        sent(i - 1)
        sent(i)

        def body(f, _):
            sends(f)[1].wait_recv()
            return _

        lax.fori_loop(0, frames, body, 0)


def spatial_fwd(x, w, vec, links=None):
    frames, _, D = x.shape
    cols = D // 2
    pairs = D // 128
    groups = PAD // 16
    in_specs = [
        pl.BlockSpec((1, PAD, D), lambda i: (i, 0, 0)),
        whole_spec(w.shape),
        whole_spec(vec.shape),
    ]
    out_specs = [
        pl.BlockSpec((1, PAD // 8, 8, D), lambda i: (i, 0, 0, 0)),
        pl.BlockSpec((1, 2, PAD, 3 * cols), lambda i: (i, 0, 0, 0)),
        pl.BlockSpec((1, 2, PAD, cols), lambda i: (i, 0, 0, 0)),
        pl.BlockSpec((1, pairs, 2 * PAD, PAD), lambda i: (i, 0, 0, 0)),
        pl.BlockSpec((1, 2 * PAD, 128), lambda i: (i, 0, 0)),
    ]
    out_shape = [
        struct((frames, PAD // 8, 8, D), F32),
        struct((frames, 2, PAD, 3 * cols), BF),
        struct((frames, 2, PAD, cols), BF),
        struct((frames, pairs, 2 * PAD, PAD), BF),
        struct((frames, 2 * PAD, 128), F32),
    ]
    args, scratch, lines, collective_id = [x, w, vec], [], None, None
    if links is not None:
        col1, own3, lines, collective_id = links
        args += [col1, own3]
        in_specs += [any_spec()] * 2
        out_specs[0] = any_spec()
        out_shape[0] = struct((2 * frames, groups, 8, D), F32)
        out_specs += [any_spec()] * 2
        out_shape += [struct(full_shape(*col1.shape), BF), struct(col1.shape, BF)]
        scratch = [pltpu.VMEM((2, PAD // 8, 8, D), F32)] + [dma_sems(frames)] * 3
        scratch += PlaneGather.scratch() + LineGather.scratch(lines)
    return pl.pallas_call(
        functools.partial(spatial_fwd_kernel, lines),
        grid=(frames,),
        in_specs=in_specs,
        out_specs=out_specs,
        out_shape=out_shape,
        scratch_shapes=scratch,
        name="spatial_fwd",
        compiler_params=kernel_params(collective_id),
    )(*args)


def spatial_bwd_kernel(lines, *refs):
    ins, outs, (gw_ref,), rest = take(refs, 8 if lines is None else 12, 3 if lines is None else 7, 1, len(refs))
    x_ref, up_ref, qkv_ref, mix_ref, p_ref, r_ref, w_ref, vec_ref = ins[:8]
    gx_ref, gb_ref, gv_ref = outs[:3]
    cols = w_ref.shape[2] // 4
    i = pl.program_id(0)

    @pl.when(i == 0)
    def _():
        gw_ref[...] = jnp.zeros_like(gw_ref)
        gv_ref[...] = jnp.zeros_like(gv_ref)

    if lines is not None:
        out_a, g1, col2, col3 = ins[8:]
        out_ref, colsum1, sum2, sum3 = outs[3:]
        place = Place(lines)
        parts = take(rest, PlaneReduce.n_scratch, LineReduce.n_scratch, LineReduce.n_scratch)
        plane1 = PlaneReduce(place, g1, colsum1, parts[0])
        line2 = LineReduce(place, col2, sum2, parts[1])
        line3 = LineReduce(place, col3, sum3, parts[2])

        @pl.when(i == 0)
        def _():
            place.greet(True)

        for k in range(line2.stages):
            at_step(k, (line2, k), (line3, k))
        at_step(0, (plane1, 0))
        at_step(1, (plane1, 1))
        at_step(4, (plane1, 2))
        at_step(6, (plane1, 3))
        out = out_a[0].reshape(PAD, out_a.shape[3])
        out_ref[0] = out[: out_ref.shape[1]].astype(BF)

    up = up_ref[0].reshape(PAD, up_ref.shape[3])
    gx = attn_back_common(
        x_ref[0].astype(F32), up.astype(BF), up, w_ref, vec_ref, 0, 10,
        lambda g: mix_ref[0, g],
        lambda g, j, rs: tuple(
            qkv_ref[0, g, :, cols * t + 128 * j : cols * t + 128 * (j + 1)] for t in range(3)
        ),
        lambda pair, b: (p_ref[0, pair], r_ref[0, :, pair : pair + 1]),
        gw_ref, gv_ref, cols, 1,
    )
    gx_ref[0] = gx[: gx_ref.shape[1]]

    @pl.when(i == pl.num_programs(0) - 1)
    def _():
        gb_ref[...] = gw_ref[...].astype(BF)


def spatial_bwd(x, up, qkv, mix, p, r, w, vec, links=None):
    frames, _, D = x.shape
    cols = D // 2
    pairs = D // 128
    in_specs = [
        pl.BlockSpec((1, PAD, D), lambda i: (i, 0, 0)),
        pl.BlockSpec((1, PAD // 8, 8, D), lambda i: (i, 0, 0, 0)),
        pl.BlockSpec((1, 2, PAD, 3 * cols), lambda i: (i, 0, 0, 0)),
        pl.BlockSpec((1, 2, PAD, cols), lambda i: (i, 0, 0, 0)),
        pl.BlockSpec((1, pairs, 2 * PAD, PAD), lambda i: (i, 0, 0, 0)),
        pl.BlockSpec((1, 2 * PAD, 128), lambda i: (i, 0, 0)),
        whole_spec(w.shape),
        whole_spec(vec.shape),
    ]
    out_specs = [
        pl.BlockSpec((1, PATCHES, D), lambda i: (i, 0, 0)),
        whole_spec((2, D, 4 * cols)),
        whole_spec((8, D)),
    ]
    out_shape = [
        struct((frames, PATCHES, D), F32),
        struct((2, D, 4 * cols), BF),
        struct((8, D), F32),
    ]
    args = [x, up, qkv, mix, p, r, w, vec]
    scratch, lines, collective_id = [pltpu.VMEM((2, D, 4 * cols), F32)], None, None
    if links is not None:
        out_a, g1, col2, col3, lines, collective_id = links
        args += [out_a, g1, col2, col3]
        block = col2.shape[1:]
        in_specs += [
            pl.BlockSpec((1, PAD // 8, 8, D), lambda i: (i, 0, 0, 0)),
            any_spec(),
            whole_spec(col2.shape),
            whole_spec(col3.shape),
        ]
        out_specs += [
            pl.BlockSpec((1, PATCHES, D), lambda i: (i, 0, 0)),
            whole_spec(col2.shape),
            whole_spec(block),
            whole_spec(block),
        ]
        out_shape += [struct((frames, PATCHES, D), BF), struct(col2.shape, BF), struct(block, F32), struct(block, F32)]
        scratch += PlaneReduce.scratch(lines, *block, BF) + LineReduce.scratch(lines, *block, BF) * 2
    return pl.pallas_call(
        functools.partial(spatial_bwd_kernel, lines),
        grid=(frames,),
        in_specs=in_specs,
        out_specs=out_specs,
        out_shape=out_shape,
        scratch_shapes=scratch,
        name="spatial_bwd",
        compiler_params=kernel_params(collective_id),
    )(*args)


def group_rows(block, live):
    parts = []
    for b in range(block.shape[1]):
        rows = block[:, b].reshape(GROUP, block.shape[3])
        parts.append(rows if b == 0 else jnp.where(live(b), rows, 0.0))
    return jnp.concatenate(parts, axis=0)


def temporal_forward(x, w_ref, vec_ref, qkv_ref, mix_ref, p_ref, r_ref):
    cols = w_ref.shape[2] // 4
    n = x.shape[0]
    xhat, _ = norm_parts(x)
    normed = (xhat * vec_ref[11:12, :] + vec_ref[4:5, :]).astype(BF)
    mask = temporal_mask()
    branch = vec_ref[7:8, :]
    for g, (q, k, v) in enumerate(project(normed, w_ref, vec_ref, 4, cols)):
        qkv_ref[g, :, 0:cols] = q
        qkv_ref[g, :, cols : 2 * cols] = k
        qkv_ref[g, :, 2 * cols : 3 * cols] = v
        pairs = []
        for b in range(n // GROUP):
            rs = slice(GROUP * b, GROUP * (b + 1))
            for j in range(cols // 128):
                sl = slice(128 * j, 128 * (j + 1))
                pairs.append((q[rs, sl], k[rs, sl], v[rs, sl]))
        mixes, exps, recips = heads_forward(pairs, mask)
        blocks = []
        for b in range(n // GROUP):
            for j in range(cols // 128):
                pair, i = g * (cols // 128) + j, b * (cols // 128) + j
                p_ref[pair, 2 * GROUP * b : 2 * GROUP * (b + 1)] = exps[i]
                r_ref[2 * GROUP * b : 2 * GROUP * (b + 1), pair : pair + 1] = recips[i]
            blocks.append(jnp.concatenate(mixes[b * (cols // 128) : (b + 1) * (cols // 128)], axis=1))
        mix = jnp.concatenate(blocks, axis=0).astype(BF)
        mix_ref[g] = mix
        branch = branch + dot(mix, w_ref[g, :, 3 * cols : 4 * cols], NT)
    return x + branch


def temporal_fwd_kernel(lines, groups, *refs):
    ins, (s_ref, qkv_ref, mix_ref, p_ref, r_ref), rest = take(refs, 3 if lines is None else 5, 5, len(refs))
    x_ref, w_ref, vec_ref = ins[:3]
    i = pl.program_id(0)
    steps = pl.num_programs(0)
    if lines is not None:
        col2, col3 = ins[3:]
        full2, full3 = rest[:2]
        place = Place(lines)
        plane2 = PlaneGather(place, col2, full2, rest[2:5])
        plane3 = PlaneGather(place, col3, full3, rest[5:8])

        @pl.when(i == 0)
        def _():
            place.greet(False)

        at_step(0, (plane2, 0))
        at_step(2, (plane2, 1), (plane3, 0))
    x = group_rows(x_ref[...], lambda b: STEP_GROUPS * i + b < groups)
    s = temporal_forward(x, w_ref, vec_ref, qkv_ref, mix_ref, p_ref, r_ref)
    for b in range(STEP_GROUPS):
        s_ref[:, b] = s[GROUP * b : GROUP * (b + 1)].reshape(FRAMES, 8, s.shape[1])
    if lines is not None:
        at_step(6, (plane3, 1), (plane2, 2), (plane3, 2), (plane2, 3), (plane3, 3))


def temporal_specs(groups, D):
    cols = D // 2
    n = STEP_GROUPS * GROUP
    steps = -(-groups // STEP_GROUPS)
    pairs = D // 128
    stream = pl.BlockSpec((FRAMES, STEP_GROUPS, 8, D), lambda i: (0, i, 0, 0))
    specs = [
        pl.BlockSpec((2, n, 3 * cols), lambda i: (0, i, 0)),
        pl.BlockSpec((2, n, cols), lambda i: (0, i, 0)),
        pl.BlockSpec((pairs, 2 * n, GROUP), lambda i: (0, i, 0)),
        pl.BlockSpec((2 * n, 128), lambda i: (i, 0)),
    ]
    shapes = [
        struct((2, steps * n, 3 * cols), BF),
        struct((2, steps * n, cols), BF),
        struct((pairs, 2 * steps * n, GROUP), BF),
        struct((2 * steps * n, 128), F32),
    ]
    return steps, stream, specs, shapes


def temporal_fwd(x, w, vec, links=None):
    groups, D = x.shape[1], x.shape[3]
    steps, stream, kept_specs, kept_shapes = temporal_specs(groups, D)
    in_specs = [stream, whole_spec(w.shape), whole_spec(vec.shape)]
    out_specs = [stream] + kept_specs
    out_shape = [struct(x.shape, F32)] + kept_shapes
    args, scratch, lines, collective_id = [x, w, vec], [], None, None
    if links is not None:
        col2, col3, lines, collective_id = links
        args += [col2, col3]
        in_specs += [any_spec()] * 2
        out_specs += [any_spec()] * 2
        out_shape += [struct(full_shape(*col2.shape), BF)] * 2
        scratch = PlaneGather.scratch() * 2
    return pl.pallas_call(
        functools.partial(temporal_fwd_kernel, lines, groups),
        grid=(steps,),
        in_specs=in_specs,
        out_specs=out_specs,
        out_shape=out_shape,
        scratch_shapes=scratch,
        name="temporal_fwd",
        compiler_params=kernel_params(collective_id),
    )(*args)


def temporal_bwd_kernel(lines, groups, *refs):
    ins, outs, (gw_ref,), rest = take(refs, 8 if lines is None else 11, 3 if lines is None else 6, 1, len(refs))
    x_ref, up_ref, qkv_ref, mix_ref, p_ref, r_ref, w_ref, vec_ref = ins[:8]
    gx_ref, gb_ref, gv_ref = outs[:3]
    cols = w_ref.shape[2] // 4
    i = pl.program_id(0)
    steps = pl.num_programs(0)

    @pl.when(i == 0)
    def _():
        gw_ref[...] = jnp.zeros_like(gw_ref)
        gv_ref[...] = jnp.zeros_like(gv_ref)

    if lines is not None:
        out_b, g2, g3 = ins[8:]
        out_a, col2, col3 = outs[3:]
        place = Place(lines)
        t = place.t
        frames = FRAMES // 2
        (slots, ex_send, ex_recv, ex_local), parts2, parts3 = take(
            rest, 4, PlaneReduce.n_scratch, PlaneReduce.n_scratch)
        plane2 = PlaneReduce(place, g2, col2, parts2)
        plane3 = PlaneReduce(place, g3, col3, parts3)
        out_here = pltpu.make_async_copy(
            out_b.at[pl.ds(frames * t, frames)], out_a.at[:, pl.ds(groups * t, groups)], ex_local.at[steps]
        )
        out_there = remote(
            out_b.at[pl.ds(frames * (1 - t), frames)], out_a.at[:, pl.ds(groups * t, groups)],
            (ex_send, ex_recv), steps, place.core,
        )

        @pl.when(i == 0)
        def _():
            place.greet(False)

        at_step(0, (plane2, 0), (plane3, 0))

        @pl.when(i == 0)
        def _():
            out_here.start()
            out_there.start()

        at_step(1, (plane2, 1))
        at_step(3, (plane2, 2), (plane3, 1))
        at_step(5, (plane2, 3))
        at_step(6, (plane3, 2))

    live = lambda b: STEP_GROUPS * i + b < groups
    x = group_rows(x_ref[...], live)
    up = group_rows(up_ref[...], live)
    gx = attn_back_common(
        x, up.astype(BF), up, w_ref, vec_ref, 4, 11,
        lambda g: mix_ref[g],
        lambda g, j, rs: tuple(
            qkv_ref[g, rs, cols * t + 128 * j : cols * t + 128 * (j + 1)] for t in range(3)
        ),
        lambda pair, b: (
            p_ref[pair, 2 * GROUP * b : 2 * GROUP * (b + 1)],
            r_ref[2 * GROUP * b : 2 * GROUP * (b + 1), pair : pair + 1],
        ),
        gw_ref, gv_ref, cols, x.shape[0] // GROUP,
    )

    @pl.when(i == steps - 1)
    def _():
        gb_ref[...] = gw_ref[...].astype(BF)

    if lines is None:
        for b in range(STEP_GROUPS):
            gx_ref[:, b] = gx[GROUP * b : GROUP * (b + 1)].reshape(FRAMES, 8, gx.shape[1])
        return

    odd = groups % STEP_GROUPS

    def sends(s, count):
        slot = slots.at[s % 2]
        dst = gx_ref.at[:, pl.ds(groups * t + STEP_GROUPS * s, count)]
        return (
            pltpu.make_async_copy(slot.at[pl.ds(frames * t, frames), pl.ds(0, count)], dst, ex_local.at[s]),
            remote(
                slot.at[pl.ds(frames * (1 - t), frames), pl.ds(0, count)], dst, (ex_send, ex_recv), s, place.core
            ),
        )

    def sent(s, count):
        here, there = sends(s, count)
        here.wait()
        there.wait_send()

    @pl.when(i >= 2)
    def _():
        sent(i - 2, STEP_GROUPS)

    for b in range(STEP_GROUPS):
        slots[i % 2, :, b] = gx[GROUP * b : GROUP * (b + 1)].reshape(FRAMES, 8, gx.shape[1])

    @pl.when(i < steps - 1)
    def _():
        for c in sends(i, STEP_GROUPS):
            c.start()

    @pl.when(i == steps - 1)
    def _():
        tail = odd if odd else STEP_GROUPS
        for c in sends(i, tail):
            c.start()
        plane3.stage(3)
        out_here.wait()
        out_there.wait()
        sent(i - 1, STEP_GROUPS)
        sent(i, tail)

        def body(s, _):
            sends(s, STEP_GROUPS)[1].wait_recv()
            return _

        lax.fori_loop(0, steps - 1, body, 0)
        sends(i, tail)[1].wait_recv()


def temporal_bwd(x, up, qkv, mix, p, r, w, vec, links=None):
    groups, D = x.shape[1], x.shape[3]
    cols = D // 2
    steps, stream, kept_specs, _ = temporal_specs(groups, D)
    in_specs = [stream, stream] + kept_specs + [whole_spec(w.shape), whole_spec(vec.shape)]
    out_specs = [stream, whole_spec((2, D, 4 * cols)), whole_spec((8, D))]
    out_shape = [struct(x.shape, F32), struct((2, D, 4 * cols), BF), struct((8, D), F32)]
    args = [x, up, qkv, mix, p, r, w, vec]
    scratch, lines, collective_id = [pltpu.VMEM((2, D, 4 * cols), F32)], None, None
    if links is not None:
        out_b, g2, g3, lines, collective_id = links
        args += [out_b, g2, g3]
        rows, width = g2.shape[4:]
        in_specs += [any_spec()] * 3
        out_specs[0] = any_spec()
        a_shape = (FRAMES // 2, 2 * groups, 8, D)
        out_shape[0] = struct(a_shape, F32)
        col = (lines, rows, width)
        out_specs += [any_spec(), whole_spec(col), whole_spec(col)]
        out_shape += [struct(a_shape, F32), struct(col, BF), struct(col, BF)]
        scratch += [pltpu.VMEM((2, FRAMES, STEP_GROUPS, 8, D), F32)] + [dma_sems(steps + 1)] * 3
        scratch += PlaneReduce.scratch(*col, BF) * 2
    return pl.pallas_call(
        functools.partial(temporal_bwd_kernel, lines, groups),
        grid=(steps,),
        in_specs=in_specs,
        out_specs=out_specs,
        out_shape=out_shape,
        scratch_shapes=scratch,
        name="temporal_bwd",
        compiler_params=kernel_params(collective_id),
    )(*args)


def last_kernel(lines, g0, tiles, col1, sum0, sum_tile, sum1, colsum0, colsum_tile, *scratch):
    place = Place(lines)
    place.greet(True)
    width = g0.shape[5] // 2
    n, m = PlaneReduce.n_scratch, LineReduce.n_scratch
    parts = take(scratch, n, n, n, m, m, m, m)
    spans = [slice(0, width), slice(width, 2 * width)]
    planes = [PlaneReduce(place, g0, colsum0.at[h], parts[h], pl.ds(width * h, width)) for h in range(2)]
    small = PlaneReduce(place, tiles, colsum_tile, parts[2])
    line1 = LineReduce(place, col1, sum1, parts[3])
    lines0 = [LineReduce(place, colsum0.at[h], sum0.at[:, spans[h]], parts[4 + h]) for h in range(2)]
    line_small = LineReduce(place, colsum_tile, sum_tile, parts[6])
    planes[0].stage(0)
    small.stage(0)
    planes[1].stage(0)
    line1.stage(0)
    planes[0].stage(1)
    small.stage(1)
    planes[1].stage(1)
    line1.stage(1)
    planes[0].stage(2)
    small.stage(2)
    line1.stage(2)
    planes[1].stage(2)
    for k in range(3, line1.stages):
        line1.stage(k)
    planes[0].stage(3)
    small.stage(3)
    lines0[0].stage(0)
    line_small.stage(0)
    lines0[0].stage(1)
    line_small.stage(1)
    planes[1].stage(3)
    lines0[1].stage(0)
    for k in range(2, lines + 1):
        if k < lines:
            lines0[0].stage(k)
            line_small.stage(k)
        lines0[1].stage(k - 1)


def last_call(g0, tiles, col1, lines, collective_id):
    rows, width = g0.shape[4:]
    half = width // 2
    vmem = pl.BlockSpec(memory_space=pltpu.VMEM)
    return pl.pallas_call(
        functools.partial(last_kernel, lines),
        in_specs=[any_spec(), any_spec(), vmem],
        out_specs=[vmem] * 3,
        out_shape=[struct((rows, width), F32), struct(tiles.shape[4:], F32), struct((rows, width), F32)],
        scratch_shapes=[
            pltpu.VMEM((2, lines, rows, half), BF),
            pltpu.VMEM((lines,) + tiles.shape[4:], F32),
        ]
        + PlaneReduce.scratch(lines, rows, half, BF) * 2
        + PlaneReduce.scratch(lines, *tiles.shape[4:], F32)
        + LineReduce.scratch(lines, rows, width, BF)
        + LineReduce.scratch(lines, rows, half, BF) * 2
        + LineReduce.scratch(lines, *tiles.shape[4:], F32),
        name="last_reduce",
        compiler_params=kernel_params(collective_id),
    )(g0, tiles, col1)


MLP_ROWS = 416
INV_SQRT2 = 0.7071067811865476
INV_SQRT2PI = 0.3989422804014327


def mlp_kernel(x_ref, cot_ref, wi_ref, wo_ref, vec_ref, hid_ref, out_ref, up_ref, gi_ref, go_ref, gv_ref, gh_ref, ai_ref, ao_ref):
    @pl.when(pl.program_id(0) == 0)
    def _():
        ai_ref[...] = jnp.zeros_like(ai_ref)
        ao_ref[...] = jnp.zeros_like(ao_ref)
        gv_ref[...] = jnp.zeros_like(gv_ref)
        gh_ref[...] = jnp.zeros_like(gh_ref)

    width = wi_ref.shape[2]
    x = x_ref[...]
    xhat, rstd = norm_parts(x)
    gain = vec_ref[12:13, :]
    normed = (xhat * gain + vec_ref[8:9, :]).astype(BF)
    up = cot_ref[...]
    ub = up.astype(BF)
    gv_ref[3:4, :] += jnp.sum(up, axis=0, keepdims=True)
    branch = vec_ref[9:10, :]
    dn = None
    chunk = 768
    for g in range(2):
        for c in range(width // chunk):
            sl = slice(chunk * c, chunk * (c + 1))
            pre = dot(normed, wi_ref[g, :, sl], NN) + hid_ref[g : g + 1, sl]
            cdf = 0.5 + 0.5 * lax.erf(pre * INV_SQRT2)
            act = (pre * cdf).astype(BF)
            branch = branch + dot(act, wo_ref[g, :, sl], NT)
            ao_ref[g, :, sl] += dot(ub, act, TN)
            dact = dot(ub, wo_ref[g, :, sl], NN).astype(BF).astype(F32)
            slope = cdf + pre * (jnp.exp(pre * pre * -0.5) * INV_SQRT2PI)
            dpre32 = dact * slope
            dpre = dpre32.astype(BF)
            gh_ref[g : g + 1, sl] += jnp.sum(dpre.astype(F32), axis=0, keepdims=True)
            ai_ref[g, :, sl] += dot(normed, dpre, TN)
            term = dot(dpre, wi_ref[g, :, sl], NT)
            dn = term if dn is None else dn + term
    out_ref[...] = x + branch
    gv_ref[0:1, :] += jnp.sum(dn, axis=0, keepdims=True)
    gv_ref[4:5, :] += jnp.sum(dn * xhat, axis=0, keepdims=True)
    up_ref[...] = up + norm_back(dn, xhat, rstd, gain)

    @pl.when(pl.program_id(0) == pl.num_programs(0) - 1)
    def _():
        gi_ref[...] = ai_ref[...].astype(BF)
        go_ref[...] = ao_ref[...].astype(BF)


def mlp_both(x, cot, w_in, w_down, vec, hidden):
    rows, D = x.shape
    width = hidden.shape[1]
    n = MLP_ROWS
    whole = lambda *shape: pl.BlockSpec(shape, lambda i: (0,) * len(shape))
    one = pl.Buffered(1)
    return pl.pallas_call(
        mlp_kernel,
        grid=(rows // n,),
        in_specs=[
            pl.BlockSpec((n, D), lambda i: (i, 0)),
            pl.BlockSpec((n, D), lambda i: (i, 0)),
            pl.BlockSpec((2, D, width), lambda i: (0, 0, 0), pipeline_mode=one),
            pl.BlockSpec((2, D, width), lambda i: (0, 0, 0), pipeline_mode=one),
            whole(*vec.shape),
            whole(*hidden.shape),
        ],
        out_specs=[
            pl.BlockSpec((n, D), lambda i: (i, 0)),
            pl.BlockSpec((n, D), lambda i: (i, 0)),
            pl.BlockSpec((2, D, width), lambda i: (0, 0, 0)),
            pl.BlockSpec((2, D, width), lambda i: (0, 0, 0)),
            whole(8, D),
            whole(*hidden.shape),
        ],
        out_shape=[
            jax.ShapeDtypeStruct((rows, D), F32),
            jax.ShapeDtypeStruct((rows, D), F32),
            jax.ShapeDtypeStruct((2, D, width), BF),
            jax.ShapeDtypeStruct((2, D, width), BF),
            jax.ShapeDtypeStruct((8, D), F32),
            jax.ShapeDtypeStruct(hidden.shape, F32),
        ],
        scratch_shapes=[pltpu.VMEM((2, D, width), F32), pltpu.VMEM((2, D, width), F32)],
        name="mlp_both",
        compiler_params=pltpu.CompilerParams(vmem_limit_bytes=VMEM_BYTES),
    )(x, cot, w_in, w_down, vec, hidden)


def swap_to_patches(rows):
    return lax.all_to_all(rows, "tensor", split_axis=1, concat_axis=0, tiled=True)


def swap_to_frames(rows):
    return lax.all_to_all(rows, "tensor", split_axis=0, concat_axis=1, tiled=True)


def pad_frames(rows):
    D = rows.shape[1]
    return jnp.pad(rows.reshape(-1, PATCHES, D), ((0, 0), (0, PAD - PATCHES), (0, 0)))


def shards(tokens, cotangent, attn_qkv, attn_out, mlp_in, mlp_out, norm_gains, biases, hidden_bias):
    D = tokens.shape[1]
    depth = mlp_in.shape[1]
    cols = attn_qkv.shape[4]
    units = mlp_in.shape[2]
    frames = tokens.shape[0] // PATCHES
    everyone = ("dp", "tensor")
    chips = D // depth
    devices = 2 * chips
    share = D // devices
    owns = [
        jnp.concatenate([attn_qkv[0, s].reshape(depth, 3 * cols), attn_out[0, s].T], axis=1)
        for s in range(2)
    ]
    owns += [mlp_in[0], mlp_out[0].T]
    small = jnp.concatenate(
        [biases[0].reshape(-1), norm_gains[0].reshape(-1), hidden_bias[0].reshape(-1)]
    )
    count = small.shape[0]

    def vectors(small):
        vec = small[:, : 13 * share].reshape(devices, 13, share).transpose(1, 0, 2).reshape(13, D)
        return vec, small[:, 13 * share :].reshape(2, units)

    def spread(gv_s, gv_t, gv_m, g_hidden):
        vec_grad = jnp.concatenate(
            [gv_s[0:4], gv_t[0:4], gv_m[0:1], gv_m[3:4], gv_s[4:5], gv_t[4:5], gv_m[4:5]]
        )
        vec_grad = vec_grad.reshape(13, devices, share).transpose(1, 0, 2).reshape(devices, 13 * share)
        return jnp.concatenate([vec_grad, g_hidden.reshape(devices, -1)], axis=1)

    flat = lambda w: w.reshape(2, D, w.shape[-1])
    rows_of = lambda v: v.reshape(-1, D)
    if depth % 16 == 0 and chips % 4 == 0:
        lines = chips // 4
        cut = lambda g: g.reshape(full_shape(lines, depth, g.shape[2]))
        tile = jnp.pad(small, (0, 1024 - count)).reshape(8, 128)
        x, cot, full_tile, full0, _, _, col1, col2 = first_call(
            tokens, cotangent, tile, owns[0], owns[1], owns[2], lines, 1
        )
        vec, hidden = vectors(
            full_tile.reshape(2, chips, 1024).transpose(1, 0, 2).reshape(devices, 1024)[:, :count]
        )
        w0 = flat(full0)
        x1, *kept_s, full1, col3 = spatial_fwd(x, w0, vec, (col1, owns[3], lines, 2))
        w1 = flat(full1)
        x2, *kept_t, full2, full3 = temporal_fwd(x1, w1, vec, (col2, col3, lines, 3))
        out_b, up2, g_in, g_down, gv_m, g_hidden = mlp_both(
            rows_of(x2), rows_of(cot), flat(full2), flat(full3), vec, hidden
        )
        up1, g_t, gv_t, out_a, col2, col3 = temporal_bwd(
            x1, up2.reshape(x1.shape), *kept_t, w1, vec,
            (out_b.reshape(x1.shape), cut(g_in), cut(g_down), lines, 4),
        )
        up0, g_s, gv_s, output, col1, g_in, g_down = spatial_bwd(
            x, up1, *kept_s, w0, vec, (out_a, cut(g_t), col2, col3, lines, 5)
        )
        tiles = jnp.pad(spread(gv_s, gv_t, gv_m, g_hidden), ((0, 0), (0, 1024 - count)))
        tiles = tiles.reshape(chips, 2, 1024).transpose(1, 0, 2).reshape(full_shape(lines, 8, 128))
        g_s, small_grad, g_t = last_call(cut(g_s), tiles, col1, lines, 6)
        small_grad = small_grad.reshape(-1)[:count]
    else:
        small = lax.all_gather(small.reshape(1, -1), everyone, axis=0, tiled=True)
        vec, hidden = vectors(small)
        weights = [flat(lax.all_gather(w, ("tensor", "dp"), axis=0, tiled=True).reshape(2, D, -1)) for w in owns]
        x = pad_frames(tokens)
        fold = lambda v: v.reshape(frames, PAD // 8, 8, D)
        x1, *kept_s = spatial_fwd(x, weights[0], vec)
        x1 = swap_to_patches(x1)
        x2, *kept_t = temporal_fwd(x1, weights[1], vec)
        cot = swap_to_patches(fold(pad_frames(cotangent).astype(F32)))
        out_b, up2, g_in, g_down, gv_m, g_hidden = mlp_both(
            rows_of(x2), rows_of(cot), weights[2], weights[3], vec, hidden
        )
        output = swap_to_frames(out_b.reshape(x1.shape)).reshape(frames, PAD, D)[:, :PATCHES].astype(BF)
        up1, g_t, gv_t = temporal_bwd(x1, up2.reshape(x1.shape), *kept_t, weights[1], vec)
        up0, g_s, gv_s = spatial_bwd(x, swap_to_frames(up1), *kept_s, weights[0], vec)
        g_s, g_t, g_in, g_down = [
            lax.psum_scatter(
                g.reshape(2 * D, g.shape[2]), ("tensor", "dp"), scatter_dimension=0, tiled=True
            ).astype(F32)
            for g in (g_s, g_t, g_in, g_down)
        ]
        small_grad = lax.psum_scatter(
            spread(gv_s, gv_t, gv_m, g_hidden), everyone, scatter_dimension=0, tiled=True
        )[0]
    grad_qkv = jnp.stack([g[:, : 3 * cols].reshape(depth, 3, cols) for g in (g_s, g_t)])[None]
    grad_out = jnp.stack([g[:, 3 * cols :].T for g in (g_s, g_t)])[None]
    grad_biases = small_grad[: 10 * share].reshape(1, 10, share)
    grad_gains = small_grad[10 * share : 13 * share].reshape(1, 3, share)
    grad_hidden = small_grad[13 * share :].reshape(1, -1)
    return (
        rows_of(output),
        rows_of(up0),
        grad_qkv,
        grad_out,
        g_in[None],
        g_down.T[None],
        grad_gains,
        grad_biases,
        grad_hidden,
    )


def solution(mesh):
    placed = (
        P(("dp", "tensor"), None),
        P(("dp", "tensor"), None),
        P(None, None, "dp", None, "tensor"),
        P(None, None, "tensor", "dp"),
        P(None, "dp", "tensor"),
        P(None, "tensor", "dp"),
        P(None, None, ("dp", "tensor")),
        P(None, None, ("dp", "tensor")),
        P(None, ("dp", "tensor")),
    )
    return jax.shard_map(
        shards, mesh=mesh, in_specs=placed, out_specs=placed, check_vma=False
    )
```

```python
import functools
import jax
import jax.numpy as jnp
from jax import lax
from jax.experimental import pallas as pl
from jax.experimental.pallas import tpu as pltpu
from jax.sharding import PartitionSpec as P

HEAD = 64
FRAMES = 16
PATCHES = 196
PAD = 208
EPSILON = 1e-06
BF = jnp.bfloat16
F32 = jnp.float32
NN = (((1,), (0,)), ((), ()))
NT = (((1,), (1,)), ((), ()))
TN = (((0,), (0,)), ((), ()))
VMEM_BYTES = 60 * 1024 * 1024


def dot(a, b, dims):
    return lax.dot_general(a, b, dims, preferred_element_type=F32)


def norm_parts(x):
    mean = jnp.mean(x, axis=-1, keepdims=True)
    centred = x - mean
    var = jnp.mean(centred * centred, axis=-1, keepdims=True)
    rstd = lax.rsqrt(var + EPSILON)
    return centred * rstd, rstd


def norm_back(grad_normed, xhat, rstd, gain):
    scaled = grad_normed * gain
    first = jnp.mean(scaled, axis=-1, keepdims=True)
    second = jnp.mean(scaled * xhat, axis=-1, keepdims=True)
    return rstd * (scaled - first - xhat * second)


def split_halves(pair):
    lane = lax.broadcasted_iota(jnp.int32, pair.shape, 1)
    zero = jnp.zeros_like(pair)
    return jnp.where(lane < HEAD, pair, zero), jnp.where(lane < HEAD, zero, pair)


def project(normed, w_ref, vec_ref, row_base, cols):
    parts = []
    for g in range(2):
        qkv = dot(normed, w_ref[g], NN)
        bq = vec_ref[row_base + 1 : row_base + 2, g * cols : (g + 1) * cols]
        bv = vec_ref[row_base + 2 : row_base + 3, g * cols : (g + 1) * cols]
        q = (qkv[:, :cols] + bq).astype(BF) * BF(0.125)
        k = qkv[:, cols : 2 * cols].astype(BF)
        v = (qkv[:, 2 * cols :] + bv).astype(BF)
        parts.append((q, k, v))
    return parts


def stack_halves(pair):
    return jnp.concatenate(split_halves(pair), axis=0)


def merge_halves(both):
    rows = both.shape[0] // 2
    lane = lax.broadcasted_iota(jnp.int32, (rows, both.shape[1]), 1)
    return jnp.where(lane < HEAD, both[:rows], both[rows:])


def heads_forward(pairs, mask):
    scores = [dot(stack_halves(q), k, NT) for q, k, _ in pairs]
    exps, recips = [], []
    for s in scores:
        s = jnp.where(mask, s, -1e30)
        e = jnp.exp(s - jnp.max(s, axis=-1, keepdims=True))
        recips.append(1.0 / jnp.sum(e, axis=-1, keepdims=True))
        exps.append(e.astype(BF))
    outs = [merge_halves(dot(e, v, NN) * r) for e, r, (_, _, v) in zip(exps, recips, pairs)]
    return outs, exps, recips


def heads_backward(pairs):
    dors, deltas = [], []
    for q, k, v, o, do, e, r in pairs:
        both = stack_halves(do.astype(F32)) * r
        deltas.append(jnp.sum(both * jnp.concatenate([o, o], axis=0).astype(F32), axis=-1, keepdims=True))
        dors.append(both.astype(BF))
    dps = [dot(dor, p[2], NT) for dor, p in zip(dors, pairs)]
    dss = [(p[5].astype(F32) * (dp - delta)).astype(BF) for dp, delta, p in zip(dps, deltas, pairs)]
    dq = [(merge_halves(dot(ds, p[1], NN)) * 0.125).astype(BF) for ds, p in zip(dss, pairs)]
    dk = [dot(ds, stack_halves(p[0]), TN).astype(BF) for ds, p in zip(dss, pairs)]
    dv = [dot(p[5], dor, TN).astype(BF) for dor, p in zip(dors, pairs)]
    return dq, dk, dv


def spatial_mask():
    return lax.broadcasted_iota(jnp.int32, (2 * PAD, PAD), 1) < PATCHES


def attn_back_common(x, ub, up, w_ref, wo_ref, vec_ref, row_base, gain_row, mix_of, qkv_of, exps_of, gw_ref, go_ref, gv_ref, cols, blocks):
    xhat, rstd = norm_parts(x)
    gain = vec_ref[gain_row : gain_row + 1, :]
    normed = (xhat * gain + vec_ref[row_base : row_base + 1, :]).astype(BF)
    dn = None
    gv_ref[3:4, :] += jnp.sum(up, axis=0, keepdims=True)
    rows = x.shape[0]
    step = rows // blocks
    for g in range(2):
        dmix = dot(ub, wo_ref[g], NN).astype(BF)
        mix = mix_of(g)
        go_ref[g] += dot(ub, mix, TN)
        parts = [[], [], []]
        for b in range(blocks):
            rs = slice(step * b, step * (b + 1))
            pairs = []
            for j in range(cols // 128):
                sl = slice(128 * j, 128 * (j + 1))
                q, k, v = qkv_of(g, j, rs)
                e, r = exps_of(g * (cols // 128) + j, b)
                pairs.append((q, k, v, mix[rs, sl], dmix[rs, sl], e, r))
            for part, got in zip(parts, heads_backward(pairs)):
                part.append(jnp.concatenate(got, axis=1))
        dq, dk, dv = [jnp.concatenate(part, axis=0) for part in parts]
        span = slice(g * cols, (g + 1) * cols)
        gv_ref[1:2, span] += jnp.sum(dq.astype(F32), axis=0, keepdims=True)
        gv_ref[2:3, span] += jnp.sum(dv.astype(F32), axis=0, keepdims=True)
        dqkv = jnp.concatenate([dq, dk, dv], axis=1)
        gw_ref[g] += dot(normed, dqkv, TN)
        term = dot(dqkv, w_ref[g], NT)
        dn = term if dn is None else dn + term
    gv_ref[0:1, :] += jnp.sum(dn, axis=0, keepdims=True)
    gv_ref[4:5, :] += jnp.sum(dn * xhat, axis=0, keepdims=True)
    return up + norm_back(dn, xhat, rstd, gain)


MESH = pl.DeviceIdType.MESH


class Place:
    def __init__(self, lines):
        self.lines = lines
        self.dp = lax.axis_index("dp")
        self.t = lax.axis_index("tensor")
        self.z = self.dp // 4
        self.y = (self.dp // 2) % 2
        self.x = self.dp % 2
        self.a = self.y * (1 - self.t) + self.x * self.t
        self.b = self.x * (1 - self.t) + self.y * self.t
        toward_y = self.dp + 2 - 4 * self.y
        toward_x = self.dp + 1 - 2 * self.x
        self.first = (toward_y * (1 - self.t) + toward_x * self.t, self.t)
        self.second = (toward_x * (1 - self.t) + toward_y * self.t, self.t)
        self.core = (self.dp, 1 - self.t)
        self.up = (self.dp + 4, self.t)
        self.down = (self.dp - 4, self.t)

    def yx(self, a, b, t):
        return a * (1 - t) + b * t, b * (1 - t) + a * t

    def greet(self):
        bar = pltpu.get_barrier_semaphore()
        for who in (self.core, self.first, self.second):
            pl.semaphore_signal(bar, inc=1, device_id=who, device_id_type=MESH)

        @pl.when(self.z > 0)
        def _():
            pl.semaphore_signal(bar, inc=1, device_id=self.down, device_id_type=MESH)

        @pl.when(self.z < self.lines - 1)
        def _():
            pl.semaphore_signal(bar, inc=1, device_id=self.up, device_id_type=MESH)

        inner = (self.z > 0).astype(jnp.int32) + (self.z < self.lines - 1).astype(jnp.int32)
        pl.semaphore_wait(bar, 3 + inner)


def remote(src, dst, sems, i, who):
    return pltpu.make_async_remote_copy(
        src_ref=src, dst_ref=dst, send_sem=sems[0].at[i], recv_sem=sems[1].at[i],
        device_id=who, device_id_type=MESH,
    )


def dma_sems(n):
    return pltpu.SemaphoreType.DMA((n,))


def begin(c):
    c.start()


def arrived(c):
    c.wait_recv()


def left(c):
    c.wait_send()


def whole(c):
    c.wait()


class LineGather:
    @staticmethod
    def scratch(lines):
        n = 2 * (lines - 1) + 1
        return [dma_sems(n), dma_sems(n), dma_sems(1)]

    n_scratch = 3

    def __init__(self, place, own, col, scratch, to_core=None, kept=False):
        self.p, self.own, self.col, self.to_core, self.kept = place, own, col, to_core, kept
        self.sems, self.local = scratch[:2], scratch[2]
        self.hops = place.lines - 1
        self.stages = self.hops + (1 if to_core is None else 2)

    def keep(self):
        return pltpu.make_async_copy(self.own, self.col.at[self.p.z], self.local.at[0])

    def _up(self, k):
        block = self.col.at[self.p.z - k]
        return remote(self.own if k == 0 else block, block, self.sems, k, self.p.up)

    def _down(self, k):
        block = self.col.at[self.p.z + k]
        return remote(self.own if k == 0 else block, block, self.sems, self.hops + k, self.p.down)

    def _sent(self, k, act):
        p = self.p

        @pl.when((p.z < self.hops) & (p.z >= k))
        def _():
            act(self._up(k))

        @pl.when((p.z > 0) & (p.z + k <= self.hops))
        def _():
            act(self._down(k))

    def _take(self, k):
        p = self.p

        @pl.when(p.z >= k + 1)
        def _():
            arrived(self._up(k))

        @pl.when(p.z + k + 1 <= self.hops)
        def _():
            arrived(self._down(k))

    def _core(self):
        return remote(self.to_core, self.to_core, self.sems, 2 * self.hops, self.p.core)

    def stage(self, k):
        if k == 0:
            if not self.kept:
                self.keep().start()
            self._sent(0, begin)
        elif k <= self.hops:
            self._take(k - 1)
            if k < self.hops:
                self._sent(k, begin)
                return
            if not self.kept:
                self.keep().wait()
            if self.to_core is not None:
                self._core().start()
            for i in range(self.hops):
                self._sent(i, left)
        else:
            self._core().wait()


class PlaneGather:
    @staticmethod
    def scratch():
        return [dma_sems(5), dma_sems(5), dma_sems(1)]

    n_scratch = 3
    stages = 4

    def __init__(self, place, block, spot, scratch, cores=True, kept=False):
        self.p, self.block, self.spot, self.cores, self.kept = place, block, spot, cores, kept
        self.sems, self.local = scratch[:2], scratch[2]

    def _keep(self):
        return pltpu.make_async_copy(self.block, self.spot(self.p.y, self.p.x), self.local.at[0])

    def _own(self, i, who):
        return remote(self.block, self.spot(self.p.y, self.p.x), self.sems, i, who)

    def _plane(self, i, who, b, act):
        p = self.p
        every = slice(None)

        @pl.when(p.t == 0)
        def _():
            part = self.spot(every, b)
            act(remote(part, part, self.sems, i, who))

        @pl.when(p.t == 1)
        def _():
            part = self.spot(b, every)
            act(remote(part, part, self.sems, i, who))

    def _pass_on(self):
        p = self.p
        part = self.spot(*p.yx(1 - p.a, p.b, p.t))
        return remote(part, part, self.sems, 3, p.core)

    def stage(self, k):
        p = self.p
        if k == 0:
            if not self.kept:
                self._keep().start()
            self._own(0, p.first).start()
            if self.cores:
                self._own(2, p.core).start()
        elif k == 1:
            if not self.kept:
                self._keep().wait()
            arrived(self._own(0, p.first))
            self._plane(1, p.second, p.b, begin)
            if self.cores:
                self._pass_on().start()
        elif k == 2:
            self._plane(1, p.second, p.b, arrived)
            if self.cores:
                self._plane(4, p.core, 1 - p.b, begin)
        else:
            if self.cores:
                self._own(2, p.core).wait()
                self._pass_on().wait()
                self._plane(4, p.core, 1 - p.b, whole)
            left(self._own(0, p.first))
            self._plane(1, p.second, p.b, left)


class When:
    def __init__(self, valid, make):
        self.valid, self.make = valid, make

    def stage(self, k):
        @pl.when(self.valid)
        def _():
            self.make().stage(k)


def add_blocks(u, v, dtype):
    return (u.astype(F32) + v.astype(F32)).astype(dtype)


class CoreSum:
    @staticmethod
    def scratch(n, block, dtype):
        return [
            pltpu.VMEM((n, 2, 2) + block, dtype),
            pltpu.VMEM((n, 2, 2) + block, dtype),
            dma_sems(4),
            dma_sems(4),
            dma_sems(4),
        ]

    n_scratch = 5

    def __init__(self, place, g_ref, scratch, span=None):
        self.p, self.g, self.span = place, g_ref, span
        self.own, self.land, self.sems, self.local = scratch[0], scratch[1], scratch[2:4], scratch[4]

    def _part(self, t, y, x):
        if self.span is None:
            return self.g.at[t, :, y, x]
        return self.g.at[t, :, y, x, :, self.span]

    def _copies(self):
        p, copies = self.p, []
        for a in range(2):
            for b in range(2):
                y, x = p.yx(a, b, 1 - p.t)
                copies.append(
                    remote(self._part(1 - p.t, y, x), self.land.at[:, a, b], self.sems, 2 * a + b, p.core)
                )
                y, x = p.yx(a, b, p.t)
                copies.append(
                    pltpu.make_async_copy(self._part(p.t, y, x), self.own.at[:, a, b], self.local.at[2 * a + b])
                )
        return copies

    def start(self):
        for c in self._copies():
            c.start()

    def wait(self):
        for c in self._copies():
            c.wait()

    def add(self, a):
        def body(i, _):
            self.own[i, a] = add_blocks(self.own[i, a], self.land[i, a], self.own.dtype)
            return _

        lax.fori_loop(0, self.own.shape[0], body, 0)


class PlaneSum:
    @staticmethod
    def scratch(n, block, dtype):
        return [pltpu.VMEM((n, 2) + block, dtype), pltpu.VMEM((n,) + block, dtype), dma_sems(2), dma_sems(2)]

    n_scratch = 4
    stages = 3

    def __init__(self, place, own, col, scratch):
        self.p, self.own, self.col = place, own, col
        self.land1, self.land2, self.sems = scratch[0], scratch[1], scratch[2:4]
        self.n = self.land2.shape[0]

    def _first(self):
        return remote(self.own.at[:, 1 - self.p.a], self.land1, self.sems, 0, self.p.first)

    def _second(self):
        return remote(self.land1.at[:, 1 - self.p.b], self.land2, self.sems, 1, self.p.second)

    def stage(self, k):
        p = self.p
        if k == 0:
            self._first().start()
        elif k == 1:
            self._first().wait()

            def away(i, _):
                self.land1[i, 1 - p.b] = add_blocks(
                    self.own[i, p.a, 1 - p.b], self.land1[i, 1 - p.b], self.land1.dtype
                )
                return _

            lax.fori_loop(0, self.n, away, 0)
            self._second().start()
        else:
            self._second().wait()

            def body(i, _):
                total = self.own[i, p.a, p.b].astype(F32) + self.land1[i, p.b].astype(F32)
                self.col[i] = (total + self.land2[i].astype(F32)).astype(self.col.dtype)
                return _

            lax.fori_loop(0, self.n, body, 0)


class LineSum:
    @staticmethod
    def scratch(lines, block, dtype):
        return [
            pltpu.VMEM((lines,) + block, dtype),
            pltpu.VMEM((lines,) + block, dtype),
            dma_sems(2 * (lines - 1)),
            dma_sems(2 * (lines - 1)),
        ]

    n_scratch = 4

    def __init__(self, place, col, out, scratch):
        self.p, self.col, self.out = place, col, out
        self.from_down, self.from_up = scratch[:2]
        self.sems = scratch[2:4]
        self.stages = place.lines

    def _up(self, d):
        block = self.from_down.at[d]
        return remote(block, block, self.sems, d - 1, self.p.up)

    def _down(self, d):
        block = self.from_up.at[d]
        return remote(block, block, self.sems, self.p.lines - 1 + d, self.p.down)

    def stage(self, step):
        n = self.p.lines
        for z in range(n):
            up = [d for d in range(z + 1, n) if z + (n - 1 - d) == step]
            down = [d for d in range(z) if (n - 1 - z) + d == step]
            if step < n - 1 and not up and not down:
                continue
            pl.when(self.p.z == z)(functools.partial(self._at, z, up, down, step == n - 1))

    def _at(self, z, up, down, last):
        n, dtype = self.p.lines, self.from_down.dtype
        for d in up:
            if z > 0:
                arrived(self._up(d))
                self.from_down[d] = add_blocks(self.from_down[d], self.col[d], dtype)
            else:
                self.from_down[d] = self.col[d]
            self._up(d).start()
        for d in down:
            if z < n - 1:
                arrived(self._down(d))
                self.from_up[d] = add_blocks(self.from_up[d], self.col[d], dtype)
            else:
                self.from_up[d] = self.col[d]
            self._down(d).start()
        if not last:
            return
        total = self.col[z].astype(F32)
        if z > 0:
            arrived(self._up(z))
            total = total + self.from_down[z].astype(F32)
        if z < n - 1:
            arrived(self._down(z))
            total = total + self.from_up[z].astype(F32)
        self.out[...] = total.astype(self.out.dtype)
        for d in range(z + 1, n):
            left(self._up(d))
        for d in range(z):
            left(self._down(d))


class PlaneReduce:
    @staticmethod
    def scratch(n, block, dtype):
        return CoreSum.scratch(n, block, dtype) + PlaneSum.scratch(n, block, dtype)

    n_scratch = 9

    def __init__(self, place, g_ref, col, scratch, span=None):
        self.p = place
        self.cores = CoreSum(place, g_ref, scratch[:5], span)
        self.plane = PlaneSum(place, self.cores.own, col, scratch[5:])

    def stage(self, k):
        if k == 0:
            self.cores.start()
        elif k == 1:
            self.cores.wait()
            self.cores.add(1 - self.p.a)
            self.plane.stage(0)
            self.cores.add(self.p.a)
        else:
            self.plane.stage(k - 1)


class LineReduce:
    @staticmethod
    def scratch(n, block, dtype):
        return CoreSum.scratch(n, block, dtype) + LineSum.scratch(n, (2, 2) + block, dtype)

    n_scratch = 9

    def __init__(self, place, g_ref, out, scratch):
        self.cores = CoreSum(place, g_ref, scratch[:5])
        self.line = LineSum(place, self.cores.own, out, scratch[5:])

    def stage(self, k):
        if k == 0:
            self.cores.start()
            return
        if k == 1:
            self.cores.wait()
            self.cores.add(0)
            self.cores.add(1)
        self.line.stage(k - 1)


def at_step(step, *stages):
    @pl.when(pl.program_id(0) == step)
    def _():
        for job, k in stages:
            job.stage(k)


def take(refs, *counts):
    out, i = [], 0
    for c in counts:
        out.append(refs[i : i + c])
        i += c
    return out


GROUP = 8 * FRAMES
STEP_GROUPS = 2


def temporal_mask():
    a = lax.broadcasted_iota(jnp.int32, (2 * GROUP, GROUP), 0)
    b = lax.broadcasted_iota(jnp.int32, (2 * GROUP, GROUP), 1)
    return (a % 8) == (b % 8)


def any_spec():
    return pl.BlockSpec(memory_space=pl.ANY)


def whole_spec(shape):
    return pl.BlockSpec(tuple(shape), lambda i: (0,) * len(shape))


def struct(shape, dtype):
    return jax.ShapeDtypeStruct(tuple(shape), dtype)


def full_shape(lines, rows, width):
    return (2, lines, 2, 2, rows, width)


def kernel_params(collective_id):
    if collective_id is None:
        return pltpu.CompilerParams(vmem_limit_bytes=VMEM_BYTES)
    return pltpu.CompilerParams(
        vmem_limit_bytes=VMEM_BYTES, collective_id=collective_id, has_side_effects=True
    )


def padded_frames(rows, put):
    frames = rows.shape[0] // PATCHES
    half = frames // 2
    zeros = jnp.zeros((PAD - PATCHES, rows.shape[1]), F32)
    for part in range(2):
        block = rows[half * PATCHES * part : half * PATCHES * (part + 1)].astype(F32)
        for f in range(half):
            put(half * part + f, jnp.concatenate([block[PATCHES * f : PATCHES * (f + 1)], zeros], axis=0))


def first_kernel(lines, *refs):
    (tok, cot, tile, q0, o0, q1, o1), (x_out, cot_b, full_tile, full_q, full_o, *results), (
        col_q1, block_o1, col_tile, block_o0, tok_v, cot_v, frames_v, ex_send, ex_recv, ex_local, loads), scratch = take(
        refs, 7, 7, 11, len(refs))
    place = Place(lines)
    t, z, y, x = place.t, place.z, place.y, place.x
    hops = lines - 1
    load_cot = pltpu.make_async_copy(cot, cot_v, loads.at[0])
    load_tok = pltpu.make_async_copy(tok, tok_v, loads.at[1])
    load_cot.start()
    load_tok.start()
    place.greet()
    pool = list(scratch)

    def sems():
        three = pool[:3]
        del pool[:3]
        return three

    tile_line = LineGather(place, tile, col_tile, sems())
    q0_line = LineGather(place, q0, full_q.at[t, :, y, x], sems(), kept=True)
    o0_line = LineGather(place, block_o0, full_o.at[t], sems(), to_core=full_o.at[t])
    q1_line = LineGather(place, q1, col_q1, sems())
    tile_plane = PlaneGather(place, col_tile, lambda v, u: full_tile.at[t, :, v, u], sems())
    o0_plane = PlaneGather(place, o0, lambda v, u: block_o0.at[v, u], sems(), cores=False)
    o1_plane = PlaneGather(place, o1, lambda v, u: block_o1.at[v, u], sems(), cores=False)
    own_slab = PlaneGather(place, q0, lambda v, u: full_q.at[t, z, v, u], sems())
    slabs = {}
    for k in range(1, lines):
        for sign in (-1, 1):
            far, own_sems = z + sign * k, sems()
            slabs[k, sign] = When(
                (far >= 0) & (far <= hops),
                functools.partial(
                    PlaneGather, place, full_q.at[t, far, y, x],
                    lambda v, u, far=far: full_q.at[t, far, v, u], own_sems, kept=True,
                ),
            )

    def pair(k, stage):
        slabs[k, -1].stage(stage)
        slabs[k, 1].stage(stage)

    q0_line.stage(0)
    own_slab.stage(0)
    o0_plane.stage(0)
    tile_line.stage(0)
    load_cot.wait()
    D = tok.shape[1]
    frames = x_out.shape[0]

    def put_cot(f, rows):
        frames_v[f] = rows.reshape(PAD // 8, 8, D)

    padded_frames(cot_v, put_cot)
    own_slab.stage(1)
    q0_line.stage(1)
    pair(1, 0)
    o0_plane.stage(1)
    tile_line.stage(1)
    q1_line.stage(0)
    o1_plane.stage(0)
    groups = PAD // 16
    mine = pltpu.make_async_copy(
        frames_v.at[:, pl.ds(groups * t, groups)], cot_b.at[pl.ds(frames * t, frames)], ex_local.at[0]
    )
    theirs = remote(
        frames_v.at[:, pl.ds(groups * (1 - t), groups)], cot_b.at[pl.ds(frames * t, frames)],
        (ex_send, ex_recv), 0, place.core,
    )
    mine.start()
    theirs.start()
    load_tok.wait()

    def put_tok(f, rows):
        x_out[f] = rows.astype(BF)

    padded_frames(tok_v, put_tok)
    o0_plane.stage(2)
    o0_plane.stage(3)
    o0_line.stage(0)
    pair(1, 1)
    own_slab.stage(2)
    for k in range(2, lines):
        q0_line.stage(k)
        pair(k, 0)
        tile_line.stage(k)
        q1_line.stage(k - 1)
        pair(k, 1)
        pair(k - 1, 2)
        o0_line.stage(k - 1)
    tile_plane.stage(0)
    o1_plane.stage(1)
    tile_plane.stage(1)
    o1_plane.stage(2)
    pair(hops, 2)
    o0_line.stage(hops)
    tile_plane.stage(2)
    q1_line.stage(hops)
    o1_plane.stage(3)
    tile_plane.stage(3)
    o0_line.stage(hops + 1)
    own_slab.stage(3)
    for k in range(1, lines):
        pair(k, 3)
    for result, part in zip(results, (col_q1, block_o1)):
        result[...] = part[...]
    mine.wait()
    theirs.wait()


def first_call(tokens, cot, tile, q0, o0, q1, o1, lines, collective_id):
    rows, D = tokens.shape
    frames = rows // PATCHES
    groups = PAD // 16
    vmem = pl.BlockSpec(memory_space=pltpu.VMEM)
    col = lambda own: struct((lines,) + own.shape, own.dtype)
    block = lambda own: struct((2, 2) + own.shape, own.dtype)
    full = lambda own: struct(full_shape(lines, *own.shape), own.dtype)
    vmem_like = lambda s: pltpu.VMEM(s.shape, s.dtype)
    return pl.pallas_call(
        functools.partial(first_kernel, lines),
        in_specs=[any_spec()] * 2 + [vmem] * 5,
        out_specs=[vmem] + [any_spec()] * 4 + [vmem] * 2,
        out_shape=[
            struct((frames, PAD, D), BF),
            struct((2 * frames, groups, 8, D), F32),
            full(tile),
            full(q0),
            full(o0),
            col(q1),
            block(o1),
        ],
        scratch_shapes=[
            vmem_like(col(q1)),
            vmem_like(block(o1)),
            vmem_like(col(tile)),
            vmem_like(block(o0)),
            pltpu.VMEM((rows, D), BF),
            pltpu.VMEM((rows, D), BF),
            pltpu.VMEM((frames, PAD // 8, 8, D), F32),
            dma_sems(1),
            dma_sems(1),
            dma_sems(1),
            dma_sems(2),
        ]
        + LineGather.scratch(lines) * 4
        + PlaneGather.scratch() * (4 + 2 * (lines - 1)),
        name="first_gather",
        compiler_params=kernel_params(collective_id),
    )(tokens, cot, tile, q0, o0, q1, o1)


def spatial_forward(x, w_ref, wo_ref, vec_ref, qkv_ref, mix_ref, p_ref, r_ref):
    cols = wo_ref.shape[2]
    xhat, _ = norm_parts(x)
    normed = (xhat * vec_ref[10:11, :] + vec_ref[0:1, :]).astype(BF)
    mask = spatial_mask()
    branch = vec_ref[3:4, :]
    for g, (q, k, v) in enumerate(project(normed, w_ref, vec_ref, 0, cols)):
        qkv_ref[0, g, :, 0:cols] = q
        qkv_ref[0, g, :, cols : 2 * cols] = k
        qkv_ref[0, g, :, 2 * cols : 3 * cols] = v
        pairs = []
        for j in range(cols // 128):
            sl = slice(128 * j, 128 * (j + 1))
            pairs.append((q[:, sl], k[:, sl], v[:, sl]))
        mixes, exps, recips = heads_forward(pairs, mask)
        for j in range(cols // 128):
            pair = g * (cols // 128) + j
            p_ref[0, pair] = exps[j]
            r_ref[0, :, pair : pair + 1] = recips[j]
        mix = jnp.concatenate(mixes, axis=1).astype(BF)
        mix_ref[0, g] = mix
        branch = branch + dot(mix, wo_ref[g], NT)
    return x + branch


def spatial_fwd_kernel(lines, *refs):
    if lines is None:
        x_ref, w_ref, wo_ref, vec_ref, s_ref, qkv_ref, mix_ref, p_ref, r_ref = refs
        s = spatial_forward(x_ref[0].astype(F32), w_ref, wo_ref, vec_ref, qkv_ref, mix_ref, p_ref, r_ref)
        s_ref[0] = s.reshape(s_ref.shape[1:])
        return
    (x_ref, w_ref, wo_ref, vec_ref), (col_q1, block_o1, q2, o2, q3, o3), (s_b, qkv_ref, mix_ref, p_ref, r_ref), (
        full_q1, full_o1), results, landed, (slots, ex_send, ex_recv, ex_local), *parts = take(
        refs, 4, 6, 5, 2, 4, 4, 4, 3, 3, 3, 3, 3, 3)
    col_q2, col_q3, block_o2, block_o3 = landed
    place = Place(lines)
    t = place.t
    i = pl.program_id(0)
    frames = pl.num_programs(0)
    groups = PAD // 16
    hops = lines - 1
    q1 = PlaneGather(place, col_q1, lambda v, u: full_q1.at[t, :, v, u], parts[0])
    o1 = LineGather(place, block_o1, full_o1.at[t], parts[1], to_core=full_o1.at[t])
    l2 = LineGather(place, q2, col_q2, parts[2])
    l3 = LineGather(place, q3, col_q3, parts[3])
    p2 = PlaneGather(place, o2, lambda v, u: block_o2.at[v, u], parts[4], cores=False)
    p3 = PlaneGather(place, o3, lambda v, u: block_o3.at[v, u], parts[5], cores=False)

    @pl.when(i == 0)
    def _():
        place.greet()

    at_step(0, (q1, 0), (o1, 0), (l2, 0), (l3, 0), (p2, 0), (p3, 0))
    at_step(2, (p2, 1), (p3, 1))
    at_step(3, (q1, 1), (o1, 1), (l2, 1), (l3, 1))
    at_step(5, (p2, 2), (p2, 3), (p3, 2), (p3, 3))
    at_step(6, *[(job, k) for k in range(2, hops) for job in (o1, l2, l3)])
    at_step(7, (q1, 2))

    def here(f):
        return pltpu.make_async_copy(
            slots.at[f % 2, pl.ds(groups * t, groups)], s_b.at[frames * t + f], ex_local.at[f]
        )

    def there(f):
        return remote(
            slots.at[f % 2, pl.ds(groups * (1 - t), groups)], s_b.at[frames * t + f], (ex_send, ex_recv), f, place.core
        )

    def sent(f):
        here(f).wait()
        left(there(f))

    s = spatial_forward(x_ref[0].astype(F32), w_ref, wo_ref, vec_ref, qkv_ref, mix_ref, p_ref, r_ref)

    @pl.when(i >= 2)
    def _():
        sent(i - 2)

    slots[i % 2] = s.reshape(slots.shape[1:])
    here(i).start()
    there(i).start()

    @pl.when(i == frames - 1)
    def _():
        o1.stage(hops)
        l2.stage(hops)
        l3.stage(hops)
        q1.stage(3)
        o1.stage(hops + 1)
        for result, part in zip(results, landed):
            result[...] = part[...]
        sent(i - 1)
        sent(i)

        def body(f, _):
            arrived(there(f))
            return _

        lax.fori_loop(0, frames, body, 0)


def spatial_fwd(x, w, wo, vec, links=None):
    frames, _, D = x.shape
    cols = D // 2
    pairs = D // 128
    groups = PAD // 16
    in_specs = [
        pl.BlockSpec((1, PAD, D), lambda i: (i, 0, 0)),
        whole_spec(w.shape),
        whole_spec(wo.shape),
        whole_spec(vec.shape),
    ]
    out_specs = [
        pl.BlockSpec((1, PAD // 8, 8, D), lambda i: (i, 0, 0, 0)),
        pl.BlockSpec((1, 2, PAD, 3 * cols), lambda i: (i, 0, 0, 0)),
        pl.BlockSpec((1, 2, PAD, cols), lambda i: (i, 0, 0, 0)),
        pl.BlockSpec((1, pairs, 2 * PAD, PAD), lambda i: (i, 0, 0, 0)),
        pl.BlockSpec((1, 2 * PAD, 128), lambda i: (i, 0, 0)),
    ]
    out_shape = [
        struct((frames, PAD // 8, 8, D), F32),
        struct((frames, 2, PAD, 3 * cols), BF),
        struct((frames, 2, PAD, cols), BF),
        struct((frames, pairs, 2 * PAD, PAD), BF),
        struct((frames, 2 * PAD, 128), F32),
    ]
    args, scratch, lines, collective_id = [x, w, wo, vec], [], None, None
    if links is not None:
        col_q1, block_o1, q2, o2, q3, o3, lines, collective_id = links
        args += [col_q1, block_o1, q2, o2, q3, o3]
        in_specs += [whole_spec(v.shape) for v in args[4:]]
        out_specs[0] = any_spec()
        out_shape[0] = struct((2 * frames, groups, 8, D), F32)
        col, block = col_q1.shape, block_o1.shape
        out_specs += [any_spec()] * 2 + [whole_spec(col)] * 2 + [whole_spec(block)] * 2
        out_shape += [struct(full_shape(*col), BF), struct((2, lines) + block, BF)]
        out_shape += [struct(col, BF)] * 2 + [struct(block, BF)] * 2
        scratch = [pltpu.VMEM(col, BF)] * 2 + [pltpu.VMEM(block, BF)] * 2
        scratch += [pltpu.VMEM((2, PAD // 8, 8, D), F32)] + [dma_sems(frames)] * 3
        scratch += PlaneGather.scratch() + LineGather.scratch(lines) * 3 + PlaneGather.scratch() * 2
    return pl.pallas_call(
        functools.partial(spatial_fwd_kernel, lines),
        grid=(frames,),
        in_specs=in_specs,
        out_specs=out_specs,
        out_shape=out_shape,
        scratch_shapes=scratch,
        name="spatial_fwd",
        compiler_params=kernel_params(collective_id),
    )(*args)


def spatial_bwd_kernel(lines, *refs):
    linked = lines is not None
    ins, joins, outs, results, (gw_ref, go_ref), rest = take(
        refs, 9, 7 if linked else 0, 4, 7 if linked else 0, 2, len(refs))
    x_ref, up_ref, qkv_ref, mix_ref, p_ref, r_ref, w_ref, wo_ref, vec_ref = ins
    gx_ref, gbw_ref, gbo_ref, gv_ref = outs
    cols = wo_ref.shape[2]
    i = pl.program_id(0)
    last = pl.num_programs(0) - 1

    @pl.when(i == 0)
    def _():
        gw_ref[...] = jnp.zeros_like(gw_ref)
        go_ref[...] = jnp.zeros_like(go_ref)
        gv_ref[...] = jnp.zeros_like(gv_ref)

    if linked:
        out_a, gw1, go1, col2, col3, block2, block3 = joins
        out_ref, col1, block1, sum_q2, sum_q3, sum_o2, sum_o3 = results
        place = Place(lines)
        parts = take(rest, PlaneReduce.n_scratch, LineReduce.n_scratch, 4, 4, 4, 4)
        q1 = PlaneReduce(place, gw1, col1, parts[0])
        o1 = LineReduce(place, go1, block1.at[0], parts[1])
        l2 = LineSum(place, col2, sum_q2, parts[2])
        l3 = LineSum(place, col3, sum_q3, parts[3])
        p2 = PlaneSum(place, block2, sum_o2, parts[4])
        p3 = PlaneSum(place, block3, sum_o3, parts[5])

        @pl.when(i == 0)
        def _():
            place.greet()

        at_step(0, (q1, 0), (o1, 0), (l2, 0), (l3, 0), (p2, 0), (p3, 0))
        at_step(1, (q1, 1))
        at_step(2, (o1, 1), (l2, 1), (l3, 1), (p2, 1), (p3, 1))
        at_step(3, (p2, 2), (p3, 2))
        at_step(4, (q1, 2), (o1, 2), *[(job, k) for k in range(2, lines - 1) for job in (l2, l3)])
        at_step(5, (l2, lines - 1), (l3, lines - 1))
        at_step(6, (q1, 3), *[(o1, k) for k in range(3, lines)])
        at_step(7, (o1, lines))
        out = out_a[0].reshape(PAD, out_a.shape[3])
        out_ref[0] = out[: out_ref.shape[1]].astype(BF)

    up = up_ref[0].reshape(PAD, up_ref.shape[3])
    gx = attn_back_common(
        x_ref[0].astype(F32), up.astype(BF), up, w_ref, wo_ref, vec_ref, 0, 10,
        lambda g: mix_ref[0, g],
        lambda g, j, rs: tuple(
            qkv_ref[0, g, :, cols * t + 128 * j : cols * t + 128 * (j + 1)] for t in range(3)
        ),
        lambda pair, b: (p_ref[0, pair], r_ref[0, :, pair : pair + 1]),
        gw_ref, go_ref, gv_ref, cols, 1,
    )
    gx_ref[0] = gx[: gx_ref.shape[1]]

    @pl.when(i == last)
    def _():
        gbw_ref[...] = gw_ref[...].astype(BF)
        gbo_ref[...] = go_ref[...].astype(BF)


def spatial_bwd(x, up, qkv, mix, p, r, w, wo, vec, links=None):
    frames, _, D = x.shape
    cols = D // 2
    pairs = D // 128
    frame_spec = pl.BlockSpec((1, PAD // 8, 8, D), lambda i: (i, 0, 0, 0))
    in_specs = [
        pl.BlockSpec((1, PAD, D), lambda i: (i, 0, 0)),
        frame_spec,
        pl.BlockSpec((1, 2, PAD, 3 * cols), lambda i: (i, 0, 0, 0)),
        pl.BlockSpec((1, 2, PAD, cols), lambda i: (i, 0, 0, 0)),
        pl.BlockSpec((1, pairs, 2 * PAD, PAD), lambda i: (i, 0, 0, 0)),
        pl.BlockSpec((1, 2 * PAD, 128), lambda i: (i, 0, 0)),
        whole_spec(w.shape),
        whole_spec(wo.shape),
        whole_spec(vec.shape),
    ]
    live_spec = pl.BlockSpec((1, PATCHES, D), lambda i: (i, 0, 0))
    out_specs = [live_spec, whole_spec(w.shape), whole_spec(wo.shape), whole_spec((8, D))]
    out_shape = [
        struct((frames, PATCHES, D), F32), struct(w.shape, BF), struct(wo.shape, BF), struct((8, D), F32)
    ]
    args = [x, up, qkv, mix, p, r, w, wo, vec]
    scratch, lines, collective_id = [pltpu.VMEM(w.shape, F32), pltpu.VMEM(wo.shape, F32)], None, None
    if links is not None:
        out_a, gw1, go1, col2, col3, block2, block3, lines, collective_id = links
        args += [out_a, gw1, go1, col2, col3, block2, block3]
        q_block, o_block = gw1.shape[4:], go1.shape[4:]
        in_specs += [frame_spec] + [any_spec()] * 2 + [whole_spec(v.shape) for v in args[-4:]]
        more = [
            struct(col2.shape, BF), struct(block2.shape, BF), struct(q_block, F32), struct(q_block, F32),
            struct((1,) + o_block, F32), struct((1,) + o_block, F32),
        ]
        out_specs += [live_spec] + [whole_spec(s.shape) for s in more]
        out_shape += [struct((frames, PATCHES, D), BF)] + more
        scratch += PlaneReduce.scratch(lines, q_block, BF) + LineReduce.scratch(lines, o_block, BF)
        scratch += LineSum.scratch(lines, q_block, BF) * 2 + PlaneSum.scratch(1, o_block, BF) * 2
    return pl.pallas_call(
        functools.partial(spatial_bwd_kernel, lines),
        grid=(frames,),
        in_specs=in_specs,
        out_specs=out_specs,
        out_shape=out_shape,
        scratch_shapes=scratch,
        name="spatial_bwd",
        compiler_params=kernel_params(collective_id),
    )(*args)


def group_rows(block, live):
    parts = []
    for b in range(block.shape[1]):
        rows = block[:, b].reshape(GROUP, block.shape[3])
        parts.append(rows if b == 0 else jnp.where(live(b), rows, 0.0))
    return jnp.concatenate(parts, axis=0)


def temporal_forward(x, w_ref, wo_ref, vec_ref, qkv_ref, mix_ref, p_ref, r_ref):
    cols = wo_ref.shape[2]
    n = x.shape[0]
    xhat, _ = norm_parts(x)
    normed = (xhat * vec_ref[11:12, :] + vec_ref[4:5, :]).astype(BF)
    mask = temporal_mask()
    branch = vec_ref[7:8, :]
    for g, (q, k, v) in enumerate(project(normed, w_ref, vec_ref, 4, cols)):
        qkv_ref[g, :, 0:cols] = q
        qkv_ref[g, :, cols : 2 * cols] = k
        qkv_ref[g, :, 2 * cols : 3 * cols] = v
        pairs = []
        for b in range(n // GROUP):
            rs = slice(GROUP * b, GROUP * (b + 1))
            for j in range(cols // 128):
                sl = slice(128 * j, 128 * (j + 1))
                pairs.append((q[rs, sl], k[rs, sl], v[rs, sl]))
        mixes, exps, recips = heads_forward(pairs, mask)
        blocks = []
        for b in range(n // GROUP):
            for j in range(cols // 128):
                pair, i = g * (cols // 128) + j, b * (cols // 128) + j
                p_ref[pair, 2 * GROUP * b : 2 * GROUP * (b + 1)] = exps[i]
                r_ref[2 * GROUP * b : 2 * GROUP * (b + 1), pair : pair + 1] = recips[i]
            blocks.append(jnp.concatenate(mixes[b * (cols // 128) : (b + 1) * (cols // 128)], axis=1))
        mix = jnp.concatenate(blocks, axis=0).astype(BF)
        mix_ref[g] = mix
        branch = branch + dot(mix, wo_ref[g], NT)
    return x + branch


def temporal_fwd_kernel(lines, groups, *refs):
    linked = lines is not None
    (x_ref, w_ref, wo_ref, vec_ref), joins, (s_ref, qkv_ref, mix_ref, p_ref, r_ref), results, *parts = take(
        refs, 4, 4 if linked else 0, 5, 4 if linked else 0, 3, 3, 3, 3)
    i = pl.program_id(0)
    if linked:
        col_q2, col_q3, block_o2, block_o3 = joins
        full_q2, full_q3, full_o2, full_o3 = results
        place = Place(lines)
        t, hops = place.t, lines - 1
        q2 = PlaneGather(place, col_q2, lambda v, u: full_q2.at[t, :, v, u], parts[0])
        q3 = PlaneGather(place, col_q3, lambda v, u: full_q3.at[t, :, v, u], parts[1])
        o2 = LineGather(place, block_o2, full_o2.at[t], parts[2], to_core=full_o2.at[t])
        o3 = LineGather(place, block_o3, full_o3.at[t], parts[3], to_core=full_o3.at[t])

        @pl.when(i == 0)
        def _():
            place.greet()

        at_step(0, (q2, 0), (o2, 0), (o3, 0))
        at_step(2, (q2, 1), (q3, 0))
        at_step(3, (o2, 1), (o3, 1))
        at_step(5, *[(job, k) for k in range(2, hops) for job in (o2, o3)])
        at_step(6, (q3, 1))
    x = group_rows(x_ref[...], lambda b: STEP_GROUPS * i + b < groups)
    s = temporal_forward(x, w_ref, wo_ref, vec_ref, qkv_ref, mix_ref, p_ref, r_ref)
    for b in range(STEP_GROUPS):
        s_ref[:, b] = s[GROUP * b : GROUP * (b + 1)].reshape(FRAMES, 8, s.shape[1])
    if linked:
        at_step(
            6, (q2, 2), (o2, hops), (o3, hops), (q2, 3), (o2, hops + 1), (o3, hops + 1), (q3, 2), (q3, 3)
        )


def temporal_specs(groups, D):
    cols = D // 2
    n = STEP_GROUPS * GROUP
    steps = -(-groups // STEP_GROUPS)
    pairs = D // 128
    stream = pl.BlockSpec((FRAMES, STEP_GROUPS, 8, D), lambda i: (0, i, 0, 0))
    specs = [
        pl.BlockSpec((2, n, 3 * cols), lambda i: (0, i, 0)),
        pl.BlockSpec((2, n, cols), lambda i: (0, i, 0)),
        pl.BlockSpec((pairs, 2 * n, GROUP), lambda i: (0, i, 0)),
        pl.BlockSpec((2 * n, 128), lambda i: (i, 0)),
    ]
    shapes = [
        struct((2, steps * n, 3 * cols), BF),
        struct((2, steps * n, cols), BF),
        struct((pairs, 2 * steps * n, GROUP), BF),
        struct((2 * steps * n, 128), F32),
    ]
    return steps, stream, specs, shapes


def temporal_fwd(x, w, wo, vec, links=None):
    groups, D = x.shape[1], x.shape[3]
    steps, stream, kept_specs, kept_shapes = temporal_specs(groups, D)
    in_specs = [stream, whole_spec(w.shape), whole_spec(wo.shape), whole_spec(vec.shape)]
    out_specs = [stream] + kept_specs
    out_shape = [struct(x.shape, F32)] + kept_shapes
    args, scratch, lines, collective_id = [x, w, wo, vec], [], None, None
    if links is not None:
        col_q2, col_q3, block_o2, block_o3, lines, collective_id = links
        args += [col_q2, col_q3, block_o2, block_o3]
        in_specs += [whole_spec(v.shape) for v in args[4:]]
        out_specs += [any_spec()] * 4
        out_shape += [struct(full_shape(*col_q2.shape), BF)] * 2 + [struct((2, lines) + block_o2.shape, BF)] * 2
        scratch = PlaneGather.scratch() * 2 + LineGather.scratch(lines) * 2
    return pl.pallas_call(
        functools.partial(temporal_fwd_kernel, lines, groups),
        grid=(steps,),
        in_specs=in_specs,
        out_specs=out_specs,
        out_shape=out_shape,
        scratch_shapes=scratch,
        name="temporal_fwd",
        compiler_params=kernel_params(collective_id),
    )(*args)


def temporal_bwd_kernel(lines, groups, *refs):
    linked = lines is not None
    ins, joins, outs, results, (gw_ref, go_ref), rest = take(
        refs, 9, 5 if linked else 0, 4, 5 if linked else 0, 2, len(refs))
    x_ref, up_ref, qkv_ref, mix_ref, p_ref, r_ref, w_ref, wo_ref, vec_ref = ins
    gx_ref, gbw_ref, gbo_ref, gv_ref = outs
    cols = wo_ref.shape[2]
    i = pl.program_id(0)
    steps = pl.num_programs(0)

    @pl.when(i == 0)
    def _():
        gw_ref[...] = jnp.zeros_like(gw_ref)
        go_ref[...] = jnp.zeros_like(go_ref)
        gv_ref[...] = jnp.zeros_like(gv_ref)

    if linked:
        out_b, gq2, gq3, go2, go3 = joins
        out_a, col2, col3, block2, block3 = results
        place = Place(lines)
        t = place.t
        frames = FRAMES // 2
        (slots, held, ex_send, ex_recv, ex_local), *parts = take(
            rest, 5, PlaneReduce.n_scratch, PlaneReduce.n_scratch, LineReduce.n_scratch, LineReduce.n_scratch)
        q2 = PlaneReduce(place, gq2, col2, parts[0])
        q3 = PlaneReduce(place, gq3, col3, parts[1])
        o2 = LineReduce(place, go2, block2.at[0], parts[2])
        o3 = LineReduce(place, go3, block3.at[0], parts[3])
        out_load = pltpu.make_async_copy(out_b.at[pl.ds(frames * t, frames)], held, ex_local.at[steps])
        out_here = pltpu.make_async_copy(held, out_a.at[:, pl.ds(groups * t, groups)], ex_local.at[steps])
        out_there = remote(
            out_b.at[pl.ds(frames * (1 - t), frames)], out_a.at[:, pl.ds(groups * t, groups)],
            (ex_send, ex_recv), steps, place.core,
        )

        @pl.when(i == 0)
        def _():
            place.greet()

        at_step(0, (q2, 0), (o2, 0), (q3, 0), (o3, 0))

        @pl.when(i == 2)
        def _():
            out_load.start()
            out_there.start()

        @pl.when(i == 3)
        def _():
            out_load.wait()
            out_here.start()

        at_step(1, (q2, 1))
        at_step(2, (o2, 1), (q3, 1), (o3, 1))
        at_step(4, (q2, 2), (o2, 2), (o3, 2))
        at_step(5, (q3, 2))
        at_step(6, (q2, 3), *[(job, k) for k in range(3, lines) for job in (o2, o3)])

    live = lambda b: STEP_GROUPS * i + b < groups
    x = group_rows(x_ref[...], live)
    up = group_rows(up_ref[...], live)
    gx = attn_back_common(
        x, up.astype(BF), up, w_ref, wo_ref, vec_ref, 4, 11,
        lambda g: mix_ref[g],
        lambda g, j, rs: tuple(
            qkv_ref[g, rs, cols * t + 128 * j : cols * t + 128 * (j + 1)] for t in range(3)
        ),
        lambda pair, b: (
            p_ref[pair, 2 * GROUP * b : 2 * GROUP * (b + 1)],
            r_ref[2 * GROUP * b : 2 * GROUP * (b + 1), pair : pair + 1],
        ),
        gw_ref, go_ref, gv_ref, cols, x.shape[0] // GROUP,
    )

    @pl.when(i == steps - 1)
    def _():
        gbw_ref[...] = gw_ref[...].astype(BF)
        gbo_ref[...] = go_ref[...].astype(BF)

    if not linked:
        for b in range(STEP_GROUPS):
            gx_ref[:, b] = gx[GROUP * b : GROUP * (b + 1)].reshape(FRAMES, 8, gx.shape[1])
        return

    tail = groups % STEP_GROUPS or STEP_GROUPS

    def target(s, count):
        return gx_ref.at[:, pl.ds(groups * t + STEP_GROUPS * s, count)]

    def here(s, count):
        part = slots.at[s % 2, pl.ds(frames * t, frames), pl.ds(0, count)]
        return pltpu.make_async_copy(part, target(s, count), ex_local.at[s])

    def there(s, count):
        part = slots.at[s % 2, pl.ds(frames * (1 - t), frames), pl.ds(0, count)]
        return remote(part, target(s, count), (ex_send, ex_recv), s, place.core)

    def sent(s, count):
        here(s, count).wait()
        left(there(s, count))

    @pl.when(i >= 2)
    def _():
        sent(i - 2, STEP_GROUPS)

    for b in range(STEP_GROUPS):
        slots[i % 2, :, b] = gx[GROUP * b : GROUP * (b + 1)].reshape(FRAMES, 8, gx.shape[1])

    @pl.when(i < steps - 1)
    def _():
        here(i, STEP_GROUPS).start()
        there(i, STEP_GROUPS).start()

    @pl.when(i == steps - 1)
    def _():
        here(i, tail).start()
        there(i, tail).start()
        o2.stage(lines)
        o3.stage(lines)
        q3.stage(3)
        out_here.wait()
        out_there.wait()
        sent(i - 1, STEP_GROUPS)
        sent(i, tail)

        def body(s, _):
            arrived(there(s, STEP_GROUPS))
            return _

        lax.fori_loop(0, steps - 1, body, 0)
        arrived(there(i, tail))


def temporal_bwd(x, up, qkv, mix, p, r, w, wo, vec, links=None):
    groups, D = x.shape[1], x.shape[3]
    steps, stream, kept_specs, _ = temporal_specs(groups, D)
    in_specs = [stream, stream] + kept_specs + [whole_spec(v.shape) for v in (w, wo, vec)]
    out_specs = [stream, whole_spec(w.shape), whole_spec(wo.shape), whole_spec((8, D))]
    out_shape = [struct(x.shape, F32), struct(w.shape, BF), struct(wo.shape, BF), struct((8, D), F32)]
    args = [x, up, qkv, mix, p, r, w, wo, vec]
    scratch, lines, collective_id = [pltpu.VMEM(w.shape, F32), pltpu.VMEM(wo.shape, F32)], None, None
    if links is not None:
        out_b, gq2, gq3, go2, go3, lines, collective_id = links
        args += [out_b, gq2, gq3, go2, go3]
        q_block, o_block = gq2.shape[4:], go2.shape[4:]
        in_specs += [any_spec()] * 5
        out_specs[0] = any_spec()
        a_shape = (FRAMES // 2, 2 * groups, 8, D)
        out_shape[0] = struct(a_shape, F32)
        more = [struct((lines,) + q_block, BF)] * 2 + [struct((1, 2, 2) + o_block, BF)] * 2
        out_specs += [any_spec()] + [whole_spec(s.shape) for s in more]
        out_shape += [struct(a_shape, F32)] + more
        scratch += [pltpu.VMEM((2, FRAMES, STEP_GROUPS, 8, D), F32), pltpu.VMEM((FRAMES // 2, groups, 8, D), F32)]
        scratch += [dma_sems(steps + 1)] * 3
        scratch += PlaneReduce.scratch(lines, q_block, BF) * 2 + LineReduce.scratch(lines, o_block, BF) * 2
    return pl.pallas_call(
        functools.partial(temporal_bwd_kernel, lines, groups),
        grid=(steps,),
        in_specs=in_specs,
        out_specs=out_specs,
        out_shape=out_shape,
        scratch_shapes=scratch,
        name="temporal_bwd",
        compiler_params=kernel_params(collective_id),
    )(*args)


LAST_CUT = 640


def last_kernel(lines, *refs):
    (gq0, go0, tiles, col1, block1), (sum_q0, sum_o0, sum_tile, sum_q1, sum_o1), (
        col_a, col_b, col_tile, block0), *parts = take(
        refs, 5, 5, 4, 9, 9, 9, 9, 4, 4, 4, 4, 4, 4)
    place = Place(lines)
    place.greet()
    width = sum_q0.shape[1]
    qa = PlaneReduce(place, gq0, col_a, parts[0], pl.ds(0, LAST_CUT))
    qb = PlaneReduce(place, gq0, col_b, parts[1], pl.ds(LAST_CUT, width - LAST_CUT))
    small = PlaneReduce(place, tiles, col_tile, parts[2])
    o0 = LineReduce(place, go0, block0.at[0], parts[3])
    qa_line = LineSum(place, col_a, sum_q0.at[:, 0:LAST_CUT], parts[4])
    qb_line = LineSum(place, col_b, sum_q0.at[:, LAST_CUT:width], parts[5])
    small_line = LineSum(place, col_tile, sum_tile, parts[6])
    q1_line = LineSum(place, col1, sum_q1, parts[7])
    o1_plane = PlaneSum(place, block1, sum_o1, parts[8])
    o0_plane = PlaneSum(place, block0, sum_o0, parts[9])
    n = lines
    qa.stage(0)
    qb.stage(0)
    o0.stage(0)
    small.stage(0)
    q1_line.stage(0)
    qa.stage(1)
    qb.stage(1)
    o1_plane.stage(0)
    small.stage(1)
    o0.stage(1)
    q1_line.stage(1)
    qa.stage(2)
    small.stage(2)
    o0.stage(2)
    for k in range(2, n - 1):
        q1_line.stage(k)
    qb.stage(2)
    qa.stage(3)
    qa_line.stage(0)
    small.stage(3)
    small_line.stage(0)
    q1_line.stage(n - 1)
    for k in range(3, n + 1):
        o0.stage(k)
    o0_plane.stage(0)
    o1_plane.stage(1)
    qb.stage(3)
    qb_line.stage(0)
    for k in range(1, n):
        qa_line.stage(k)
        small_line.stage(k)
        qb_line.stage(k)
        if k == 1:
            o0_plane.stage(1)
            o1_plane.stage(2)
    o0_plane.stage(2)


def last_call(gq0, go0, tiles, col1, block1, lines, collective_id):
    q_block, o_block, tile = gq0.shape[4:], go0.shape[4:], tiles.shape[4:]
    rows, width = q_block
    cut_a, cut_b = (rows, LAST_CUT), (rows, width - LAST_CUT)
    vmem = pl.BlockSpec(memory_space=pltpu.VMEM)
    return pl.pallas_call(
        functools.partial(last_kernel, lines),
        in_specs=[any_spec()] * 3 + [vmem] * 2,
        out_specs=[vmem] * 5,
        out_shape=[
            struct(q_block, F32), struct((1,) + o_block, F32), struct(tile, F32), struct(q_block, F32),
            struct((1,) + o_block, F32),
        ],
        scratch_shapes=[
            pltpu.VMEM((lines,) + cut_a, BF),
            pltpu.VMEM((lines,) + cut_b, BF),
            pltpu.VMEM((lines,) + tile, F32),
            pltpu.VMEM((1, 2, 2) + o_block, BF),
        ]
        + PlaneReduce.scratch(lines, cut_a, BF)
        + PlaneReduce.scratch(lines, cut_b, BF)
        + PlaneReduce.scratch(lines, tile, F32)
        + LineReduce.scratch(lines, o_block, BF)
        + LineSum.scratch(lines, cut_a, BF)
        + LineSum.scratch(lines, cut_b, BF)
        + LineSum.scratch(lines, tile, F32)
        + LineSum.scratch(lines, q_block, BF)
        + PlaneSum.scratch(1, o_block, BF) * 2,
        name="last_reduce",
        compiler_params=kernel_params(collective_id),
    )(gq0, go0, tiles, col1, block1)


MLP_ROWS = 416
MLP_CHUNK = 1536
INV_SQRT2 = 0.7071067811865476
INV_SQRT2PI = 0.3989422804014327


def mlp_kernel(x_ref, cot_ref, wia, wib, woa, wob, vec_ref, hid_ref, out_ref, up_ref,
               gia, gib, goa, gob, gv_ref, gh_ref, wi_ref, wo_ref, ai_ref, ao_ref, dn_ref, sems):
    i = pl.program_id(0)
    last = pl.num_programs(0) - 1
    chunks = wi_ref.shape[0]
    per = chunks // 2
    wide, width = wia.shape[2], per * MLP_CHUNK

    def copies(table, out):
        found = []
        for vmem, first, second in table:
            for g in range(2):
                for c in range(per):
                    start, stop = MLP_CHUNK * c, MLP_CHUNK * (c + 1)
                    for array, low, high in ((first, 0, wide), (second, wide, width)):
                        lo, hi = max(start, low), min(stop, high)
                        if lo < hi:
                            here = vmem.at[g * per + c, :, pl.ds(lo - start, hi - lo)]
                            there = array.at[g, :, pl.ds(lo - low, hi - lo)]
                            sem = sems.at[int(out), len(found)]
                            found.append(pltpu.make_async_copy(*((here, there) if out else (there, here)), sem))
        return found

    @pl.when(i == 0)
    def _():
        loads = copies(((wi_ref, wia, wib), (wo_ref, woa, wob)), False)
        for copy in loads:
            copy.start()
        for ref in (ai_ref, ao_ref, gv_ref, gh_ref):
            ref[...] = jnp.zeros_like(ref)
        for copy in loads:
            copy.wait()

    x = x_ref[...]
    xhat, rstd = norm_parts(x)
    gain = vec_ref[12:13, :]
    normed = (xhat * gain + vec_ref[8:9, :]).astype(BF)
    up = cot_ref[...]
    ub = up.astype(BF)
    gv_ref[3:4, :] += jnp.sum(up, axis=0, keepdims=True)
    out_ref[...] = x + vec_ref[9:10, :]
    dn_ref[...] = jnp.zeros_like(dn_ref)

    def chunk(k, _):
        pre = dot(normed, wi_ref[k], NN) + hid_ref[k]
        cdf = 0.5 + 0.5 * lax.erf(pre * INV_SQRT2)
        act = (pre * cdf).astype(BF)
        out_ref[...] += dot(act, wo_ref[k], NT)
        ao_ref[k] += dot(ub, act, TN)
        dact = dot(ub, wo_ref[k], NN).astype(BF).astype(F32)
        slope = cdf + pre * (jnp.exp(pre * pre * -0.5) * INV_SQRT2PI)
        dpre = (dact * slope).astype(BF)
        gh_ref[k] += jnp.sum(dpre.astype(F32), axis=0, keepdims=True)
        ai_ref[k] += dot(normed, dpre, TN)
        dn_ref[...] += dot(dpre, wi_ref[k], NT)
        return _

    lax.fori_loop(0, chunks, chunk, 0)
    dn = dn_ref[...]
    gv_ref[0:1, :] += jnp.sum(dn, axis=0, keepdims=True)
    gv_ref[4:5, :] += jnp.sum(dn * xhat, axis=0, keepdims=True)
    up_ref[...] = up + norm_back(dn, xhat, rstd, gain)

    @pl.when(i == last)
    def _():
        def place(k, _):
            wi_ref[k] = ai_ref[k].astype(BF)
            wo_ref[k] = ao_ref[k].astype(BF)
            return _

        lax.fori_loop(0, chunks, place, 0)
        stores = copies(((wi_ref, gia, gib), (wo_ref, goa, gob)), True)
        for copy in stores:
            copy.start()
        for copy in stores:
            copy.wait()


def mlp_both(x, cot, wia, wib, woa, wob, vec, hidden):
    rows, D = x.shape
    width = hidden.shape[1]
    chunks = 2 * width // MLP_CHUNK
    row_spec = pl.BlockSpec((MLP_ROWS, D), lambda i: (i, 0))
    mats = [wia, wib, woa, wob]
    both = (chunks, D, MLP_CHUNK)
    units = (chunks, 1, MLP_CHUNK)
    outs = pl.pallas_call(
        mlp_kernel,
        grid=(rows // MLP_ROWS,),
        in_specs=[row_spec, row_spec] + [any_spec()] * 4 + [whole_spec(vec.shape), whole_spec(units)],
        out_specs=[row_spec, row_spec] + [any_spec()] * 4 + [whole_spec((8, D)), whole_spec(units)],
        out_shape=[struct((rows, D), F32)] * 2
        + [struct(m.shape, BF) for m in mats]
        + [struct((8, D), F32), struct(units, F32)],
        scratch_shapes=[pltpu.VMEM(both, BF)] * 2
        + [pltpu.VMEM(both, F32)] * 2
        + [pltpu.VMEM((MLP_ROWS, D), F32), pltpu.SemaphoreType.DMA((2, 6 * chunks))],
        name="mlp_both",
        compiler_params=kernel_params(None),
    )(x, cot, *mats, vec, hidden.reshape(units))
    return (*outs[:-1], outs[-1].reshape(hidden.shape))


def swap_to_patches(rows):
    return lax.all_to_all(rows, "tensor", split_axis=1, concat_axis=0, tiled=True)


def swap_to_frames(rows):
    return lax.all_to_all(rows, "tensor", split_axis=0, concat_axis=1, tiled=True)


def pad_frames(rows):
    D = rows.shape[1]
    return jnp.pad(rows.reshape(-1, PATCHES, D), ((0, 0), (0, PAD - PATCHES), (0, 0)))


def shards(tokens, cotangent, attn_qkv, attn_out, mlp_in, mlp_out, norm_gains, biases, hidden_bias):
    D = tokens.shape[1]
    depth = mlp_in.shape[1]
    cols = attn_qkv.shape[4]
    units = mlp_in.shape[2]
    frames = tokens.shape[0] // PATCHES
    everyone = ("dp", "tensor")
    chips = D // depth
    devices = 2 * chips
    share = D // devices
    wide = 3 * cols
    down = mlp_out[0].T
    owns = []
    for s in range(2):
        owns += [attn_qkv[0, s].reshape(depth, wide), attn_out[0, s].T]
    owns += [mlp_in[0, :, :wide], mlp_in[0, :, wide:], down[:, :wide], down[:, wide:]]
    small = jnp.concatenate(
        [biases[0].reshape(-1), norm_gains[0].reshape(-1), hidden_bias[0].reshape(-1)]
    )
    count = small.shape[0]

    def vectors(small):
        vec = small[:, : 13 * share].reshape(devices, 13, share).transpose(1, 0, 2).reshape(13, D)
        return vec, small[:, 13 * share :].reshape(2, units)

    def spread(gv_s, gv_t, gv_m, g_hidden):
        vec_grad = jnp.concatenate(
            [gv_s[0:4], gv_t[0:4], gv_m[0:1], gv_m[3:4], gv_s[4:5], gv_t[4:5], gv_m[4:5]]
        )
        vec_grad = vec_grad.reshape(13, devices, share).transpose(1, 0, 2).reshape(devices, 13 * share)
        return jnp.concatenate([vec_grad, g_hidden.reshape(devices, -1)], axis=1)

    flat = lambda w: w.reshape(2, D, w.shape[-1])
    rows_of = lambda v: v.reshape(-1, D)
    if depth % 16 == 0 and chips % 4 == 0:
        lines = chips // 4
        cut = lambda g: g.reshape(full_shape(lines, depth, g.shape[2]))
        tile = jnp.pad(small, (0, 1024 - count)).reshape(8, 128)
        x, cot, full_tile, *w0, col_q1, block_o1 = first_call(tokens, cotangent, tile, *owns[:4], lines, 1)
        vec, hidden = vectors(
            full_tile.reshape(2, chips, 1024).transpose(1, 0, 2).reshape(devices, 1024)[:, :count]
        )
        w0 = [flat(w) for w in w0]
        x1, *kept_s, q1, o1, col_q2, col_q3, block_o2, block_o3 = spatial_fwd(
            x, *w0, vec, (col_q1, block_o1, *owns[4:], lines, 2)
        )
        w1 = [flat(q1), flat(o1)]
        x2, *kept_t, q2, q3, o2, o3 = temporal_fwd(
            x1, *w1, vec, (col_q2, col_q3, block_o2, block_o3, lines, 3)
        )
        out_b, up2, gq2, go2, gq3, go3, gv_m, g_hidden = mlp_both(
            rows_of(x2), rows_of(cot), flat(q2), flat(o2), flat(q3), flat(o3), vec, hidden
        )
        up1, gq1, go1, gv_t, out_a, col2, col3, block2, block3 = temporal_bwd(
            x1, up2.reshape(x1.shape), *kept_t, *w1, vec,
            (out_b.reshape(x1.shape), cut(gq2), cut(gq3), cut(go2), cut(go3), lines, 4),
        )
        up0, gq0, go0, gv_s, output, col1, block1, gq2, gq3, go2, go3 = spatial_bwd(
            x, up1, *kept_s, *w0, vec, (out_a, cut(gq1), cut(go1), col2, col3, block2, block3, lines, 5)
        )
        tiles = jnp.pad(spread(gv_s, gv_t, gv_m, g_hidden), ((0, 0), (0, 1024 - count)))
        tiles = tiles.reshape(chips, 2, 1024).transpose(1, 0, 2).reshape(full_shape(lines, 8, 128))
        gq0, go0, small_grad, gq1, go1 = last_call(cut(gq0), cut(go0), tiles, col1, block1, lines, 6)
        small_grad = small_grad.reshape(-1)[:count]
        go0, go1, go2, go3 = [g[0] for g in (go0, go1, go2, go3)]
    else:
        small = lax.all_gather(small.reshape(1, -1), everyone, axis=0, tiled=True)
        vec, hidden = vectors(small)
        weights = [flat(lax.all_gather(w, ("tensor", "dp"), axis=0, tiled=True).reshape(2, D, -1)) for w in owns]
        x = pad_frames(tokens)
        fold = lambda v: v.reshape(frames, PAD // 8, 8, D)
        x1, *kept_s = spatial_fwd(x, *weights[0:2], vec)
        x1 = swap_to_patches(x1)
        x2, *kept_t = temporal_fwd(x1, *weights[2:4], vec)
        cot = swap_to_patches(fold(pad_frames(cotangent).astype(F32)))
        out_b, up2, *mlp_grads, gv_m, g_hidden = mlp_both(
            rows_of(x2), rows_of(cot), *weights[4:], vec, hidden
        )
        output = swap_to_frames(out_b.reshape(x1.shape)).reshape(frames, PAD, D)[:, :PATCHES].astype(BF)
        up1, *grads1, gv_t = temporal_bwd(x1, up2.reshape(x1.shape), *kept_t, *weights[2:4], vec)
        up0, *grads0, gv_s = spatial_bwd(x, swap_to_frames(up1), *kept_s, *weights[0:2], vec)
        gq0, go0, gq1, go1, gq2, go2, gq3, go3 = [
            lax.psum_scatter(
                g.reshape(2 * D, g.shape[2]), ("tensor", "dp"), scatter_dimension=0, tiled=True
            ).astype(F32)
            for g in grads0 + grads1 + mlp_grads
        ]
        small_grad = lax.psum_scatter(
            spread(gv_s, gv_t, gv_m, g_hidden), everyone, scatter_dimension=0, tiled=True
        )[0]
    grad_qkv = jnp.stack([gq0.reshape(depth, 3, cols), gq1.reshape(depth, 3, cols)])[None]
    grad_out = jnp.stack([go0.T, go1.T])[None]
    grad_biases = small_grad[: 10 * share].reshape(1, 10, share)
    grad_gains = small_grad[10 * share : 13 * share].reshape(1, 3, share)
    grad_hidden = small_grad[13 * share :].reshape(1, -1)
    return (
        rows_of(output),
        rows_of(up0),
        grad_qkv,
        grad_out,
        jnp.concatenate([gq2, go2], axis=1)[None],
        jnp.concatenate([gq3, go3], axis=1).T[None],
        grad_gains,
        grad_biases,
        grad_hidden,
    )


def solution(mesh):
    placed = (
        P(("dp", "tensor"), None),
        P(("dp", "tensor"), None),
        P(None, None, "dp", None, "tensor"),
        P(None, None, "tensor", "dp"),
        P(None, "dp", "tensor"),
        P(None, "tensor", "dp"),
        P(None, None, ("dp", "tensor")),
        P(None, None, ("dp", "tensor")),
        P(None, ("dp", "tensor")),
    )
    return jax.shard_map(
        shards, mesh=mesh, in_specs=placed, out_specs=placed, check_vma=False
    )
```

```python
import functools
import jax
import jax.numpy as jnp
from jax import lax
from jax.experimental import pallas as pl
from jax.experimental.pallas import tpu as pltpu
from jax.sharding import PartitionSpec as P

HEAD = 64
FRAMES = 16
PATCHES = 196
PAD = 208
EPSILON = 1e-06
BF = jnp.bfloat16
F32 = jnp.float32
NN = (((1,), (0,)), ((), ()))
NT = (((1,), (1,)), ((), ()))
TN = (((0,), (0,)), ((), ()))
VMEM_BYTES = 60 * 1024 * 1024


def dot(a, b, dims):
    return lax.dot_general(a, b, dims, preferred_element_type=F32)


def norm_parts(x):
    mean = jnp.mean(x, axis=-1, keepdims=True)
    centred = x - mean
    var = jnp.mean(centred * centred, axis=-1, keepdims=True)
    rstd = lax.rsqrt(var + EPSILON)
    return centred * rstd, rstd


def norm_back(grad_normed, xhat, rstd, gain):
    scaled = grad_normed * gain
    first = jnp.mean(scaled, axis=-1, keepdims=True)
    second = jnp.mean(scaled * xhat, axis=-1, keepdims=True)
    return rstd * (scaled - first - xhat * second)


def split_halves(pair):
    lane = lax.broadcasted_iota(jnp.int32, pair.shape, 1)
    zero = jnp.zeros_like(pair)
    return jnp.where(lane < HEAD, pair, zero), jnp.where(lane < HEAD, zero, pair)


def project(normed, w_ref, vec_ref, row_base, cols):
    parts = []
    for g in range(2):
        qkv = dot(normed, w_ref[g], NN)
        bq = vec_ref[row_base + 1 : row_base + 2, g * cols : (g + 1) * cols]
        bv = vec_ref[row_base + 2 : row_base + 3, g * cols : (g + 1) * cols]
        q = (qkv[:, :cols] + bq).astype(BF) * BF(0.125)
        k = qkv[:, cols : 2 * cols].astype(BF)
        v = (qkv[:, 2 * cols :] + bv).astype(BF)
        parts.append((q, k, v))
    return parts


def stack_halves(pair):
    return jnp.concatenate(split_halves(pair), axis=0)


def merge_halves(both):
    rows = both.shape[0] // 2
    lane = lax.broadcasted_iota(jnp.int32, (rows, both.shape[1]), 1)
    return jnp.where(lane < HEAD, both[:rows], both[rows:])


def heads_forward(pairs, mask):
    scores = [dot(stack_halves(q), k, NT) for q, k, _ in pairs]
    exps, recips = [], []
    for s in scores:
        s = jnp.where(mask, s, -1e30)
        e = jnp.exp(s - jnp.max(s, axis=-1, keepdims=True))
        recips.append(1.0 / jnp.sum(e, axis=-1, keepdims=True))
        exps.append(e.astype(BF))
    outs = [merge_halves(dot(e, v, NN) * r) for e, r, (_, _, v) in zip(exps, recips, pairs)]
    return outs, exps, recips


def heads_backward(pairs):
    dors, deltas = [], []
    for q, k, v, o, do, e, r in pairs:
        both = stack_halves(do.astype(F32)) * r
        deltas.append(jnp.sum(both * jnp.concatenate([o, o], axis=0).astype(F32), axis=-1, keepdims=True))
        dors.append(both.astype(BF))
    dps = [dot(dor, p[2], NT) for dor, p in zip(dors, pairs)]
    dss = [(p[5].astype(F32) * (dp - delta)).astype(BF) for dp, delta, p in zip(dps, deltas, pairs)]
    dq = [(merge_halves(dot(ds, p[1], NN)) * 0.125).astype(BF) for ds, p in zip(dss, pairs)]
    dk = [dot(ds, stack_halves(p[0]), TN).astype(BF) for ds, p in zip(dss, pairs)]
    dv = [dot(p[5], dor, TN).astype(BF) for dor, p in zip(dors, pairs)]
    return dq, dk, dv


def spatial_mask():
    return lax.broadcasted_iota(jnp.int32, (2 * PAD, PAD), 1) < PATCHES


def attn_back_common(x, ub, up, w_ref, wo_ref, vec_ref, row_base, gain_row, mix_of, qkv_of, exps_of, gw_ref, go_ref, gv_ref, cols, blocks):
    xhat, rstd = norm_parts(x)
    gain = vec_ref[gain_row : gain_row + 1, :]
    normed = (xhat * gain + vec_ref[row_base : row_base + 1, :]).astype(BF)
    dn = None
    gv_ref[3:4, :] += jnp.sum(up, axis=0, keepdims=True)
    rows = x.shape[0]
    step = rows // blocks
    for g in range(2):
        dmix = dot(ub, wo_ref[g], NN).astype(BF)
        mix = mix_of(g)
        go_ref[g] += dot(ub, mix, TN)
        parts = [[], [], []]
        for b in range(blocks):
            rs = slice(step * b, step * (b + 1))
            pairs = []
            for j in range(cols // 128):
                sl = slice(128 * j, 128 * (j + 1))
                q, k, v = qkv_of(g, j, rs)
                e, r = exps_of(g * (cols // 128) + j, b)
                pairs.append((q, k, v, mix[rs, sl], dmix[rs, sl], e, r))
            for part, got in zip(parts, heads_backward(pairs)):
                part.append(jnp.concatenate(got, axis=1))
        dq, dk, dv = [jnp.concatenate(part, axis=0) for part in parts]
        span = slice(g * cols, (g + 1) * cols)
        gv_ref[1:2, span] += jnp.sum(dq.astype(F32), axis=0, keepdims=True)
        gv_ref[2:3, span] += jnp.sum(dv.astype(F32), axis=0, keepdims=True)
        dqkv = jnp.concatenate([dq, dk, dv], axis=1)
        gw_ref[g] += dot(normed, dqkv, TN)
        term = dot(dqkv, w_ref[g], NT)
        dn = term if dn is None else dn + term
    gv_ref[0:1, :] += jnp.sum(dn, axis=0, keepdims=True)
    gv_ref[4:5, :] += jnp.sum(dn * xhat, axis=0, keepdims=True)
    return up + norm_back(dn, xhat, rstd, gain)


MESH = pl.DeviceIdType.MESH


class Place:
    def __init__(self, lines):
        self.lines = lines
        self.dp = lax.axis_index("dp")
        self.t = lax.axis_index("tensor")
        self.z = self.dp // 4
        self.y = (self.dp // 2) % 2
        self.x = self.dp % 2
        self.a = self.y * (1 - self.t) + self.x * self.t
        self.b = self.x * (1 - self.t) + self.y * self.t
        toward_y = self.dp + 2 - 4 * self.y
        toward_x = self.dp + 1 - 2 * self.x
        self.first = (toward_y * (1 - self.t) + toward_x * self.t, self.t)
        self.second = (toward_x * (1 - self.t) + toward_y * self.t, self.t)
        self.core = (self.dp, 1 - self.t)
        self.up = (self.dp + 4, self.t)
        self.down = (self.dp - 4, self.t)

    def yx(self, a, b, t):
        return a * (1 - t) + b * t, b * (1 - t) + a * t

    def greet(self):
        bar = pltpu.get_barrier_semaphore()
        for who in (self.core, self.first, self.second):
            pl.semaphore_signal(bar, inc=1, device_id=who, device_id_type=MESH)

        @pl.when(self.z > 0)
        def _():
            pl.semaphore_signal(bar, inc=1, device_id=self.down, device_id_type=MESH)

        @pl.when(self.z < self.lines - 1)
        def _():
            pl.semaphore_signal(bar, inc=1, device_id=self.up, device_id_type=MESH)

        inner = (self.z > 0).astype(jnp.int32) + (self.z < self.lines - 1).astype(jnp.int32)
        pl.semaphore_wait(bar, 3 + inner)


def remote(src, dst, sems, i, who):
    return pltpu.make_async_remote_copy(
        src_ref=src, dst_ref=dst, send_sem=sems[0].at[i], recv_sem=sems[1].at[i],
        device_id=who, device_id_type=MESH,
    )


def dma_sems(n):
    return pltpu.SemaphoreType.DMA((n,))


def begin(c):
    c.start()


def arrived(c):
    c.wait_recv()


def left(c):
    c.wait_send()


def whole(c):
    c.wait()


class LineGather:
    @staticmethod
    def scratch(lines):
        n = 2 * (lines - 1) + 1
        return [dma_sems(n), dma_sems(n), dma_sems(1)]

    n_scratch = 3

    def __init__(self, place, own, col, scratch, to_core=None, kept=False):
        self.p, self.own, self.col, self.to_core, self.kept = place, own, col, to_core, kept
        self.sems, self.local = scratch[:2], scratch[2]
        self.hops = place.lines - 1
        self.stages = self.hops + (1 if to_core is None else 2)

    def keep(self):
        return pltpu.make_async_copy(self.own, self.col.at[self.p.z], self.local.at[0])

    def _up(self, k):
        block = self.col.at[self.p.z - k]
        return remote(self.own if k == 0 else block, block, self.sems, k, self.p.up)

    def _down(self, k):
        block = self.col.at[self.p.z + k]
        return remote(self.own if k == 0 else block, block, self.sems, self.hops + k, self.p.down)

    def _sent(self, k, act):
        p = self.p

        @pl.when((p.z < self.hops) & (p.z >= k))
        def _():
            act(self._up(k))

        @pl.when((p.z > 0) & (p.z + k <= self.hops))
        def _():
            act(self._down(k))

    def _take(self, k):
        p = self.p

        @pl.when(p.z >= k + 1)
        def _():
            arrived(self._up(k))

        @pl.when(p.z + k + 1 <= self.hops)
        def _():
            arrived(self._down(k))

    def _core(self):
        return remote(self.to_core, self.to_core, self.sems, 2 * self.hops, self.p.core)

    def stage(self, k):
        if k == 0:
            if not self.kept:
                self.keep().start()
            self._sent(0, begin)
        elif k <= self.hops:
            self._take(k - 1)
            if k < self.hops:
                self._sent(k, begin)
                return
            if not self.kept:
                self.keep().wait()
            if self.to_core is not None:
                self._core().start()
            for i in range(self.hops):
                self._sent(i, left)
        else:
            self._core().wait()


class PlaneGather:
    @staticmethod
    def scratch():
        return [dma_sems(5), dma_sems(5), dma_sems(1)]

    n_scratch = 3
    stages = 4

    def __init__(self, place, block, spot, scratch, cores=True, kept=False):
        self.p, self.block, self.spot, self.cores, self.kept = place, block, spot, cores, kept
        self.sems, self.local = scratch[:2], scratch[2]

    def _keep(self):
        return pltpu.make_async_copy(self.block, self.spot(self.p.y, self.p.x), self.local.at[0])

    def _own(self, i, who):
        return remote(self.block, self.spot(self.p.y, self.p.x), self.sems, i, who)

    def _plane(self, i, who, b, act):
        p = self.p
        every = slice(None)

        @pl.when(p.t == 0)
        def _():
            part = self.spot(every, b)
            act(remote(part, part, self.sems, i, who))

        @pl.when(p.t == 1)
        def _():
            part = self.spot(b, every)
            act(remote(part, part, self.sems, i, who))

    def _pass_on(self):
        p = self.p
        part = self.spot(*p.yx(1 - p.a, p.b, p.t))
        return remote(part, part, self.sems, 3, p.core)

    def stage(self, k):
        p = self.p
        if k == 0:
            if not self.kept:
                self._keep().start()
            self._own(0, p.first).start()
            if self.cores:
                self._own(2, p.core).start()
        elif k == 1:
            if not self.kept:
                self._keep().wait()
            arrived(self._own(0, p.first))
            self._plane(1, p.second, p.b, begin)
            if self.cores:
                self._pass_on().start()
        elif k == 2:
            self._plane(1, p.second, p.b, arrived)
            if self.cores:
                self._plane(4, p.core, 1 - p.b, begin)
        else:
            if self.cores:
                self._own(2, p.core).wait()
                self._pass_on().wait()
                self._plane(4, p.core, 1 - p.b, whole)
            left(self._own(0, p.first))
            self._plane(1, p.second, p.b, left)


class When:
    def __init__(self, valid, make):
        self.valid, self.make = valid, make

    def stage(self, k):
        @pl.when(self.valid)
        def _():
            self.make().stage(k)


def add_blocks(u, v, dtype):
    if u.dtype == v.dtype == dtype:
        return u + v
    return (u.astype(F32) + v.astype(F32)).astype(dtype)


class CoreSum:
    @staticmethod
    def scratch(n, block, dtype):
        return [
            pltpu.VMEM((n, 2, 2) + block, dtype),
            pltpu.VMEM((n, 2, 2) + block, dtype),
            dma_sems(4),
            dma_sems(4),
            dma_sems(4),
        ]

    n_scratch = 5

    def __init__(self, place, g_ref, scratch, span=None):
        self.p, self.g, self.span = place, g_ref, span
        self.own, self.land, self.sems, self.local = scratch[0], scratch[1], scratch[2:4], scratch[4]

    def _part(self, t, y, x):
        if self.span is None:
            return self.g.at[t, :, y, x]
        return self.g.at[t, :, y, x, :, self.span]

    def _copies(self):
        p, copies = self.p, []
        for a in range(2):
            for b in range(2):
                y, x = p.yx(a, b, 1 - p.t)
                copies.append(
                    remote(self._part(1 - p.t, y, x), self.land.at[:, a, b], self.sems, 2 * a + b, p.core)
                )
                y, x = p.yx(a, b, p.t)
                copies.append(
                    pltpu.make_async_copy(self._part(p.t, y, x), self.own.at[:, a, b], self.local.at[2 * a + b])
                )
        return copies

    def start(self):
        for c in self._copies():
            c.start()

    def wait(self):
        for c in self._copies():
            c.wait()

    def add(self, a):
        def body(i, _):
            self.own[i, a] = add_blocks(self.own[i, a], self.land[i, a], self.own.dtype)
            return _

        lax.fori_loop(0, self.own.shape[0], body, 0)


class PlaneSum:
    @staticmethod
    def scratch(n, block, dtype):
        return [pltpu.VMEM((n, 2) + block, dtype), pltpu.VMEM((n,) + block, dtype), dma_sems(2), dma_sems(2)]

    n_scratch = 4
    stages = 3

    def __init__(self, place, own, col, scratch):
        self.p, self.own, self.col = place, own, col
        self.land1, self.land2, self.sems = scratch[0], scratch[1], scratch[2:4]
        self.n = self.land2.shape[0]

    def _first(self):
        return remote(self.own.at[:, 1 - self.p.a], self.land1, self.sems, 0, self.p.first)

    def _second(self):
        return remote(self.land1.at[:, 1 - self.p.b], self.land2, self.sems, 1, self.p.second)

    def stage(self, k):
        p = self.p
        if k == 0:
            self._first().start()
        elif k == 1:
            self._first().wait()

            def away(i, _):
                self.land1[i, 1 - p.b] = add_blocks(
                    self.own[i, p.a, 1 - p.b], self.land1[i, 1 - p.b], self.land1.dtype
                )
                return _

            lax.fori_loop(0, self.n, away, 0)
            self._second().start()
        else:
            self._second().wait()

            def body(i, _):
                total = self.own[i, p.a, p.b].astype(F32) + self.land1[i, p.b].astype(F32)
                self.col[i] = (total + self.land2[i].astype(F32)).astype(self.col.dtype)
                return _

            lax.fori_loop(0, self.n, body, 0)


class LineSum:
    @staticmethod
    def scratch(lines, block, dtype):
        return [
            pltpu.VMEM((lines,) + block, dtype),
            pltpu.VMEM((lines,) + block, dtype),
            dma_sems(2 * (lines - 1)),
            dma_sems(2 * (lines - 1)),
        ]

    n_scratch = 4

    def __init__(self, place, col, out, scratch):
        self.p, self.col, self.out = place, col, out
        self.from_down, self.from_up = scratch[:2]
        self.sems = scratch[2:4]
        self.stages = place.lines

    def _up(self, d):
        block = self.from_down.at[d]
        return remote(block, block, self.sems, d - 1, self.p.up)

    def _down(self, d):
        block = self.from_up.at[d]
        return remote(block, block, self.sems, self.p.lines - 1 + d, self.p.down)

    def stage(self, step):
        n = self.p.lines
        for z in range(n):
            up = [d for d in range(z + 1, n) if z + (n - 1 - d) == step]
            down = [d for d in range(z) if (n - 1 - z) + d == step]
            if step < n - 1 and not up and not down:
                continue
            pl.when(self.p.z == z)(functools.partial(self._at, z, up, down, step == n - 1))

    def _at(self, z, up, down, last):
        n, dtype = self.p.lines, self.from_down.dtype
        for d in up:
            if z > 0:
                arrived(self._up(d))
                self.from_down[d] = add_blocks(self.from_down[d], self.col[d], dtype)
            else:
                self.from_down[d] = self.col[d]
            self._up(d).start()
        for d in down:
            if z < n - 1:
                arrived(self._down(d))
                self.from_up[d] = add_blocks(self.from_up[d], self.col[d], dtype)
            else:
                self.from_up[d] = self.col[d]
            self._down(d).start()
        if not last:
            return
        total = self.col[z].astype(F32)
        if z > 0:
            arrived(self._up(z))
            total = total + self.from_down[z].astype(F32)
        if z < n - 1:
            arrived(self._down(z))
            total = total + self.from_up[z].astype(F32)
        self.out[...] = total.astype(self.out.dtype)
        for d in range(z + 1, n):
            left(self._up(d))
        for d in range(z):
            left(self._down(d))


class PlaneReduce:
    @staticmethod
    def scratch(n, block, dtype):
        return CoreSum.scratch(n, block, dtype) + PlaneSum.scratch(n, block, dtype)

    n_scratch = 9

    def __init__(self, place, g_ref, col, scratch, span=None):
        self.p = place
        self.cores = CoreSum(place, g_ref, scratch[:5], span)
        self.plane = PlaneSum(place, self.cores.own, col, scratch[5:])

    def stage(self, k):
        if k == 0:
            self.cores.start()
        elif k == 1:
            self.cores.wait()
            self.cores.add(1 - self.p.a)
            self.plane.stage(0)
            self.cores.add(self.p.a)
        else:
            self.plane.stage(k - 1)


class LineReduce:
    @staticmethod
    def scratch(n, block, dtype):
        return CoreSum.scratch(n, block, dtype) + LineSum.scratch(n, (2, 2) + block, dtype)

    n_scratch = 9

    def __init__(self, place, g_ref, out, scratch):
        self.cores = CoreSum(place, g_ref, scratch[:5])
        self.line = LineSum(place, self.cores.own, out, scratch[5:])

    def stage(self, k):
        if k == 0:
            self.cores.start()
            return
        if k == 1:
            self.cores.wait()
            self.cores.add(0)
            self.cores.add(1)
        self.line.stage(k - 1)


def at_step(step, *stages):
    @pl.when(pl.program_id(0) == step)
    def _():
        for job, k in stages:
            job.stage(k)


def take(refs, *counts):
    out, i = [], 0
    for c in counts:
        out.append(refs[i : i + c])
        i += c
    return out


GROUP = 8 * FRAMES
STEP_GROUPS = 2


def temporal_mask():
    a = lax.broadcasted_iota(jnp.int32, (2 * GROUP, GROUP), 0)
    b = lax.broadcasted_iota(jnp.int32, (2 * GROUP, GROUP), 1)
    return (a % 8) == (b % 8)


def any_spec():
    return pl.BlockSpec(memory_space=pl.ANY)


def whole_spec(shape):
    return pl.BlockSpec(tuple(shape), lambda i: (0,) * len(shape))


def struct(shape, dtype):
    return jax.ShapeDtypeStruct(tuple(shape), dtype)


def full_shape(lines, rows, width):
    return (2, lines, 2, 2, rows, width)


def kernel_params(collective_id):
    if collective_id is None:
        return pltpu.CompilerParams(vmem_limit_bytes=VMEM_BYTES)
    return pltpu.CompilerParams(
        vmem_limit_bytes=VMEM_BYTES, collective_id=collective_id, has_side_effects=True
    )


TILE = (24, 128)


def padded_frames(rows, put):
    frames = rows.shape[0] // PATCHES
    half = frames // 2
    zeros = jnp.zeros((PAD - PATCHES, rows.shape[1]), F32)
    for part in range(2):
        block = rows[half * PATCHES * part : half * PATCHES * (part + 1)].astype(F32)
        for f in range(half):
            put(half * part + f, jnp.concatenate([block[PATCHES * f : PATCHES * (f + 1)], zeros], axis=0))


def first_kernel(lines, *refs):
    (tok, cot, gains, biases, hidden, qkv, outs), (x_out, cot_b, full_tile, full_q, full_o, *results), (
        tile, q0, q1, col_q1, block_o1, col_tile, block_o0, tok_v, cot_v, frames_v, ex_send, ex_recv, ex_local, loads), scratch = take(
        refs, 7, 7, 14, len(refs))
    place = Place(lines)
    t, z, y, x = place.t, place.z, place.y, place.x
    hops = lines - 1
    load_cot = pltpu.make_async_copy(cot, cot_v, loads.at[0])
    load_tok = pltpu.make_async_copy(tok, tok_v, loads.at[1])
    part = qkv.shape[3]
    load_qkv = [
        pltpu.make_async_copy(qkv.at[s, k], own.at[:, pl.ds(part * k, part)], loads.at[2 + 3 * s + k])
        for s, own in enumerate((q0, q1))
        for k in range(3)
    ]
    for copy in load_qkv:
        copy.start()
    load_cot.start()
    load_tok.start()
    tile[...] = jnp.zeros_like(tile)
    tile[0:10, 0 : biases.shape[1]] = biases[...]
    tile[10:13, 0 : gains.shape[1]] = gains[...]
    tile[16:17, 0 : hidden.shape[1]] = hidden[...]
    o0, o1 = outs.at[0], outs.at[1]
    place.greet()
    for copy in load_qkv:
        copy.wait()
    pool = list(scratch)

    def sems():
        three = pool[:3]
        del pool[:3]
        return three

    tile_line = LineGather(place, tile, col_tile, sems())
    q0_line = LineGather(place, q0, full_q.at[t, :, y, x], sems(), kept=True)
    o0_line = LineGather(place, block_o0, full_o.at[t], sems(), to_core=full_o.at[t])
    q1_line = LineGather(place, q1, col_q1, sems())
    tile_plane = PlaneGather(place, col_tile, lambda v, u: full_tile.at[t, :, v, u], sems())
    o0_plane = PlaneGather(place, o0, lambda v, u: block_o0.at[v, u], sems(), cores=False)
    o1_plane = PlaneGather(place, o1, lambda v, u: block_o1.at[v, u], sems(), cores=False)
    own_slab = PlaneGather(place, q0, lambda v, u: full_q.at[t, z, v, u], sems())
    slabs = {}
    for k in range(1, lines):
        for sign in (-1, 1):
            far, own_sems = z + sign * k, sems()
            slabs[k, sign] = When(
                (far >= 0) & (far <= hops),
                functools.partial(
                    PlaneGather, place, full_q.at[t, far, y, x],
                    lambda v, u, far=far: full_q.at[t, far, v, u], own_sems, kept=True,
                ),
            )

    def pair(k, stage):
        slabs[k, -1].stage(stage)
        slabs[k, 1].stage(stage)

    q0_line.stage(0)
    own_slab.stage(0)
    o0_plane.stage(0)
    tile_line.stage(0)
    load_cot.wait()
    D = tok.shape[1]
    frames = x_out.shape[0]

    def put_cot(f, rows):
        frames_v[f] = rows.reshape(PAD // 8, 8, D)

    padded_frames(cot_v, put_cot)
    own_slab.stage(1)
    q0_line.stage(1)
    pair(1, 0)
    o0_plane.stage(1)
    tile_line.stage(1)
    q1_line.stage(0)
    o1_plane.stage(0)
    groups = PAD // 16
    mine = pltpu.make_async_copy(
        frames_v.at[:, pl.ds(groups * t, groups)], cot_b.at[pl.ds(frames * t, frames)], ex_local.at[0]
    )
    theirs = remote(
        frames_v.at[:, pl.ds(groups * (1 - t), groups)], cot_b.at[pl.ds(frames * t, frames)],
        (ex_send, ex_recv), 0, place.core,
    )
    mine.start()
    theirs.start()
    load_tok.wait()

    def put_tok(f, rows):
        x_out[f] = rows.astype(BF)

    padded_frames(tok_v, put_tok)
    o0_plane.stage(2)
    o0_plane.stage(3)
    o0_line.stage(0)
    pair(1, 1)
    own_slab.stage(2)
    for k in range(2, lines):
        q0_line.stage(k)
        pair(k, 0)
        tile_line.stage(k)
        q1_line.stage(k - 1)
        pair(k, 1)
        pair(k - 1, 2)
        o0_line.stage(k - 1)
    tile_plane.stage(0)
    o1_plane.stage(1)
    tile_plane.stage(1)
    o1_plane.stage(2)
    pair(hops, 2)
    o0_line.stage(hops)
    tile_plane.stage(2)
    q1_line.stage(hops)
    o1_plane.stage(3)
    tile_plane.stage(3)
    o0_line.stage(hops + 1)
    own_slab.stage(3)
    for k in range(1, lines):
        pair(k, 3)
    for result, part in zip(results, (col_q1, block_o1)):
        result[...] = part[...]
    mine.wait()
    theirs.wait()


def first_call(tokens, cot, gains, biases, hidden, qkv, outs, lines, collective_id):
    rows, D = tokens.shape
    frames = rows // PATCHES
    groups = PAD // 16
    vmem = pl.BlockSpec(memory_space=pltpu.VMEM)
    depth, part = qkv.shape[2:]
    tile = struct(TILE, F32)
    q0 = q1 = struct((depth, 3 * part), BF)
    o0 = o1 = struct(outs.shape[1:], BF)
    col = lambda own: struct((lines,) + own.shape, own.dtype)
    block = lambda own: struct((2, 2) + own.shape, own.dtype)
    full = lambda own: struct(full_shape(lines, *own.shape), own.dtype)
    vmem_like = lambda s: pltpu.VMEM(s.shape, s.dtype)
    return pl.pallas_call(
        functools.partial(first_kernel, lines),
        in_specs=[any_spec()] * 2 + [vmem] * 3 + [any_spec(), vmem],
        out_specs=[vmem] + [any_spec()] * 4 + [vmem] * 2,
        out_shape=[
            struct((frames, PAD, D), BF),
            struct((2 * frames, groups, 8, D), F32),
            full(tile),
            full(q0),
            full(o0),
            col(q1),
            block(o1),
        ],
        scratch_shapes=[
            vmem_like(tile),
            vmem_like(q0),
            vmem_like(q1),
            vmem_like(col(q1)),
            vmem_like(block(o1)),
            vmem_like(col(tile)),
            vmem_like(block(o0)),
            pltpu.VMEM((rows, D), BF),
            pltpu.VMEM((rows, D), BF),
            pltpu.VMEM((frames, PAD // 8, 8, D), F32),
            dma_sems(1),
            dma_sems(1),
            dma_sems(1),
            dma_sems(8),
        ]
        + LineGather.scratch(lines) * 4
        + PlaneGather.scratch() * (4 + 2 * (lines - 1)),
        name="first_gather",
        compiler_params=kernel_params(collective_id),
    )(tokens, cot, gains, biases, hidden, qkv, outs)


def spatial_forward(x, w_ref, wo_ref, vec_ref, qkv_ref, mix_ref, p_ref, r_ref):
    cols = wo_ref.shape[2]
    xhat, _ = norm_parts(x)
    normed = (xhat * vec_ref[10:11, :] + vec_ref[0:1, :]).astype(BF)
    mask = spatial_mask()
    branch = vec_ref[3:4, :]
    for g, (q, k, v) in enumerate(project(normed, w_ref, vec_ref, 0, cols)):
        qkv_ref[0, g, :, 0:cols] = q
        qkv_ref[0, g, :, cols : 2 * cols] = k
        qkv_ref[0, g, :, 2 * cols : 3 * cols] = v
        pairs = []
        for j in range(cols // 128):
            sl = slice(128 * j, 128 * (j + 1))
            pairs.append((q[:, sl], k[:, sl], v[:, sl]))
        mixes, exps, recips = heads_forward(pairs, mask)
        for j in range(cols // 128):
            pair = g * (cols // 128) + j
            p_ref[0, pair] = exps[j]
            r_ref[0, :, pair : pair + 1] = recips[j]
        mix = jnp.concatenate(mixes, axis=1).astype(BF)
        mix_ref[0, g] = mix
        branch = branch + dot(mix, wo_ref[g], NT)
    return x + branch


def spatial_fwd_kernel(lines, *refs):
    if lines is None:
        x_ref, w_ref, wo_ref, vec_ref, s_ref, qkv_ref, mix_ref, p_ref, r_ref = refs
        s = spatial_forward(x_ref[0].astype(F32), w_ref, wo_ref, vec_ref, qkv_ref, mix_ref, p_ref, r_ref)
        s_ref[0] = s.reshape(s_ref.shape[1:])
        return
    (x_ref, w_ref, wo_ref, vec_ref), (col_q1, block_o1, own2, own3), (s_b, qkv_ref, mix_ref, p_ref, r_ref), (
        full_q1, full_o1), results, landed, (slots, ex_send, ex_recv, ex_local), *parts = take(
        refs, 4, 4, 5, 2, 4, 4, 4, 3, 3, 3, 3, 3, 3)
    col_q2, col_q3, block_o2, block_o3 = landed
    place = Place(lines)
    t = place.t
    i = pl.program_id(0)
    frames = pl.num_programs(0)
    groups = PAD // 16
    hops = lines - 1
    wide = col_q2.shape[2]
    q2, q3 = [own.at[:, pl.ds(0, wide)] for own in (own2, own3)]
    o2, o3 = [own.at[:, pl.ds(wide, own.shape[1] - wide)] for own in (own2, own3)]
    q1 = PlaneGather(place, col_q1, lambda v, u: full_q1.at[t, :, v, u], parts[0])
    o1 = LineGather(place, block_o1, full_o1.at[t], parts[1], to_core=full_o1.at[t])
    l2 = LineGather(place, q2, col_q2, parts[2])
    l3 = LineGather(place, q3, col_q3, parts[3])
    p2 = PlaneGather(place, o2, lambda v, u: block_o2.at[v, u], parts[4], cores=False)
    p3 = PlaneGather(place, o3, lambda v, u: block_o3.at[v, u], parts[5], cores=False)

    @pl.when(i == 0)
    def _():
        place.greet()

    at_step(0, (q1, 0), (o1, 0), (l2, 0), (l3, 0), (p2, 0), (p3, 0))
    at_step(2, (p2, 1), (p3, 1))
    at_step(3, (q1, 1), (o1, 1), (l2, 1), (l3, 1))
    at_step(5, (p2, 2), (p2, 3), (p3, 2), (p3, 3))
    at_step(6, *[(job, k) for k in range(2, hops) for job in (o1, l2, l3)])
    at_step(7, (q1, 2))

    def here(f):
        return pltpu.make_async_copy(
            slots.at[f % 2, pl.ds(groups * t, groups)], s_b.at[frames * t + f], ex_local.at[f]
        )

    def there(f):
        return remote(
            slots.at[f % 2, pl.ds(groups * (1 - t), groups)], s_b.at[frames * t + f], (ex_send, ex_recv), f, place.core
        )

    def sent(f):
        here(f).wait()
        left(there(f))

    s = spatial_forward(x_ref[0].astype(F32), w_ref, wo_ref, vec_ref, qkv_ref, mix_ref, p_ref, r_ref)

    @pl.when(i >= 2)
    def _():
        sent(i - 2)

    slots[i % 2] = s.reshape(slots.shape[1:])
    here(i).start()
    there(i).start()

    @pl.when(i == frames - 1)
    def _():
        o1.stage(hops)
        l2.stage(hops)
        l3.stage(hops)
        q1.stage(3)
        o1.stage(hops + 1)
        for result, part in zip(results, landed):
            result[...] = part[...]
        sent(i - 1)
        sent(i)

        def body(f, _):
            arrived(there(f))
            return _

        lax.fori_loop(0, frames, body, 0)


def spatial_fwd(x, w, wo, vec, links=None):
    frames, _, D = x.shape
    cols = D // 2
    pairs = D // 128
    groups = PAD // 16
    in_specs = [
        pl.BlockSpec((1, PAD, D), lambda i: (i, 0, 0)),
        whole_spec(w.shape),
        whole_spec(wo.shape),
        whole_spec(vec.shape),
    ]
    out_specs = [
        pl.BlockSpec((1, PAD // 8, 8, D), lambda i: (i, 0, 0, 0)),
        pl.BlockSpec((1, 2, PAD, 3 * cols), lambda i: (i, 0, 0, 0)),
        pl.BlockSpec((1, 2, PAD, cols), lambda i: (i, 0, 0, 0)),
        pl.BlockSpec((1, pairs, 2 * PAD, PAD), lambda i: (i, 0, 0, 0)),
        pl.BlockSpec((1, 2 * PAD, 128), lambda i: (i, 0, 0)),
    ]
    out_shape = [
        struct((frames, PAD // 8, 8, D), F32),
        struct((frames, 2, PAD, 3 * cols), BF),
        struct((frames, 2, PAD, cols), BF),
        struct((frames, pairs, 2 * PAD, PAD), BF),
        struct((frames, 2 * PAD, 128), F32),
    ]
    args, scratch, lines, collective_id = [x, w, wo, vec], [], None, None
    if links is not None:
        col_q1, block_o1, own2, own3, lines, collective_id = links
        args += [col_q1, block_o1, own2, own3]
        in_specs += [whole_spec(v.shape) for v in args[4:]]
        out_specs[0] = any_spec()
        out_shape[0] = struct((2 * frames, groups, 8, D), F32)
        col, block = col_q1.shape, block_o1.shape
        out_specs += [any_spec()] * 2 + [whole_spec(col)] * 2 + [whole_spec(block)] * 2
        out_shape += [struct(full_shape(*col), BF), struct((2, lines) + block, BF)]
        out_shape += [struct(col, BF)] * 2 + [struct(block, BF)] * 2
        scratch = [pltpu.VMEM(col, BF)] * 2 + [pltpu.VMEM(block, BF)] * 2
        scratch += [pltpu.VMEM((2, PAD // 8, 8, D), F32)] + [dma_sems(frames)] * 3
        scratch += PlaneGather.scratch() + LineGather.scratch(lines) * 3 + PlaneGather.scratch() * 2
    return pl.pallas_call(
        functools.partial(spatial_fwd_kernel, lines),
        grid=(frames,),
        in_specs=in_specs,
        out_specs=out_specs,
        out_shape=out_shape,
        scratch_shapes=scratch,
        name="spatial_fwd",
        compiler_params=kernel_params(collective_id),
    )(*args)


SHARED = 4


def place_frame(i, ref, rows):
    for f in range(SHARED):
        @pl.when(i % SHARED == f)
        def _():
            ref[PATCHES * f : PATCHES * (f + 1)] = rows


def spatial_bwd_kernel(lines, *refs):
    linked = lines is not None
    ins, joins, outs, results, (gw_ref, go_ref), rest = take(
        refs, 9, 7 if linked else 0, 4, 7 if linked else 0, 2, len(refs))
    x_ref, up_ref, qkv_ref, mix_ref, p_ref, r_ref, w_ref, wo_ref, vec_ref = ins
    gx_ref, gbw_ref, gbo_ref, gv_ref = outs
    cols = wo_ref.shape[2]
    i = pl.program_id(0)
    last = pl.num_programs(0) - 1

    @pl.when(i == 0)
    def _():
        gw_ref[...] = jnp.zeros_like(gw_ref)
        go_ref[...] = jnp.zeros_like(go_ref)
        gv_ref[...] = jnp.zeros_like(gv_ref)

    if linked:
        out_a, gw1, go1, col2, col3, block2, block3 = joins
        out_ref, col1, block1, sum_q2, sum_q3, sum_o2, sum_o3 = results
        place = Place(lines)
        parts = take(rest, PlaneReduce.n_scratch, LineReduce.n_scratch, 4, 4, 4, 4)
        q1 = PlaneReduce(place, gw1, col1, parts[0])
        o1 = LineReduce(place, go1, block1.at[0], parts[1])
        l2 = LineSum(place, col2, sum_q2, parts[2])
        l3 = LineSum(place, col3, sum_q3, parts[3])
        p2 = PlaneSum(place, block2, sum_o2, parts[4])
        p3 = PlaneSum(place, block3, sum_o3, parts[5])

        @pl.when(i == 0)
        def _():
            place.greet()

        at_step(0, (q1, 0), (o1, 0), (l2, 0), (l3, 0), (p2, 0), (p3, 0))
        at_step(1, (q1, 1))
        at_step(2, (o1, 1), (l2, 1), (l3, 1), (p2, 1), (p3, 1))
        at_step(3, (p2, 2), (p3, 2))
        at_step(4, (q1, 2), (o1, 2), *[(job, k) for k in range(2, lines - 1) for job in (l2, l3)])
        at_step(5, (l2, lines - 1), (l3, lines - 1))
        at_step(6, (q1, 3), *[(o1, k) for k in range(3, lines)])
        at_step(7, (o1, lines))
        place_frame(i, rest[-1], out_a[0].reshape(PAD, out_a.shape[3])[:PATCHES])

        @pl.when(i % SHARED == SHARED - 1)
        def _():
            out_ref[...] = rest[-1][...].astype(BF)

    up = up_ref[0].reshape(PAD, up_ref.shape[3])
    gx = attn_back_common(
        x_ref[0].astype(F32), up.astype(BF), up, w_ref, wo_ref, vec_ref, 0, 10,
        lambda g: mix_ref[0, g],
        lambda g, j, rs: tuple(
            qkv_ref[0, g, :, cols * t + 128 * j : cols * t + 128 * (j + 1)] for t in range(3)
        ),
        lambda pair, b: (p_ref[0, pair], r_ref[0, :, pair : pair + 1]),
        gw_ref, go_ref, gv_ref, cols, 1,
    )
    place_frame(i, gx_ref, gx[:PATCHES])

    @pl.when(i == last)
    def _():
        gbw_ref[...] = gw_ref[...].astype(BF)
        gbo_ref[...] = go_ref[...].astype(BF)


def spatial_bwd(x, up, qkv, mix, p, r, w, wo, vec, links=None):
    frames, _, D = x.shape
    cols = D // 2
    pairs = D // 128
    frame_spec = pl.BlockSpec((1, PAD // 8, 8, D), lambda i: (i, 0, 0, 0))
    in_specs = [
        pl.BlockSpec((1, PAD, D), lambda i: (i, 0, 0)),
        frame_spec,
        pl.BlockSpec((1, 2, PAD, 3 * cols), lambda i: (i, 0, 0, 0)),
        pl.BlockSpec((1, 2, PAD, cols), lambda i: (i, 0, 0, 0)),
        pl.BlockSpec((1, pairs, 2 * PAD, PAD), lambda i: (i, 0, 0, 0)),
        pl.BlockSpec((1, 2 * PAD, 128), lambda i: (i, 0, 0)),
        whole_spec(w.shape),
        whole_spec(wo.shape),
        whole_spec(vec.shape),
    ]
    live_spec = pl.BlockSpec((SHARED * PATCHES, D), lambda i: (i // SHARED, 0))
    out_specs = [live_spec, whole_spec(w.shape), whole_spec(wo.shape), whole_spec((8, D))]
    out_shape = [
        struct((frames * PATCHES, D), F32), struct(w.shape, BF), struct(wo.shape, BF), struct((8, D), F32)
    ]
    args = [x, up, qkv, mix, p, r, w, wo, vec]
    scratch, lines, collective_id = [pltpu.VMEM(w.shape, F32), pltpu.VMEM(wo.shape, F32)], None, None
    if links is not None:
        out_a, gw1, go1, col2, col3, block2, block3, lines, collective_id = links
        args += [out_a, gw1, go1, col2, col3, block2, block3]
        q_block, o_block = gw1.shape[4:], go1.shape[4:]
        in_specs += [frame_spec] + [any_spec()] * 2 + [whole_spec(v.shape) for v in args[-4:]]
        more = [
            struct(col2.shape, BF), struct(block2.shape, BF), struct(q_block, F32), struct(q_block, F32),
            struct((1,) + o_block, F32), struct((1,) + o_block, F32),
        ]
        out_specs += [live_spec] + [whole_spec(s.shape) for s in more]
        out_shape += [struct((frames * PATCHES, D), BF)] + more
        scratch += PlaneReduce.scratch(lines, q_block, BF) + LineReduce.scratch(lines, o_block, BF)
        scratch += LineSum.scratch(lines, q_block, BF) * 2 + PlaneSum.scratch(1, o_block, BF) * 2
        scratch += [pltpu.VMEM((SHARED * PATCHES, D), F32)]
    return pl.pallas_call(
        functools.partial(spatial_bwd_kernel, lines),
        grid=(frames,),
        in_specs=in_specs,
        out_specs=out_specs,
        out_shape=out_shape,
        scratch_shapes=scratch,
        name="spatial_bwd",
        compiler_params=kernel_params(collective_id),
    )(*args)


def group_rows(block, live):
    parts = []
    for b in range(block.shape[1]):
        rows = block[:, b].reshape(GROUP, block.shape[3])
        parts.append(rows if b == 0 else jnp.where(live(b), rows, 0.0))
    return jnp.concatenate(parts, axis=0)


def temporal_forward(x, w_ref, wo_ref, vec_ref, qkv_ref, mix_ref, p_ref, r_ref):
    cols = wo_ref.shape[2]
    n = x.shape[0]
    xhat, _ = norm_parts(x)
    normed = (xhat * vec_ref[11:12, :] + vec_ref[4:5, :]).astype(BF)
    mask = temporal_mask()
    branch = vec_ref[7:8, :]
    for g, (q, k, v) in enumerate(project(normed, w_ref, vec_ref, 4, cols)):
        qkv_ref[g, :, 0:cols] = q
        qkv_ref[g, :, cols : 2 * cols] = k
        qkv_ref[g, :, 2 * cols : 3 * cols] = v
        pairs = []
        for b in range(n // GROUP):
            rs = slice(GROUP * b, GROUP * (b + 1))
            for j in range(cols // 128):
                sl = slice(128 * j, 128 * (j + 1))
                pairs.append((q[rs, sl], k[rs, sl], v[rs, sl]))
        mixes, exps, recips = heads_forward(pairs, mask)
        blocks = []
        for b in range(n // GROUP):
            for j in range(cols // 128):
                pair, i = g * (cols // 128) + j, b * (cols // 128) + j
                p_ref[pair, 2 * GROUP * b : 2 * GROUP * (b + 1)] = exps[i]
                r_ref[2 * GROUP * b : 2 * GROUP * (b + 1), pair : pair + 1] = recips[i]
            blocks.append(jnp.concatenate(mixes[b * (cols // 128) : (b + 1) * (cols // 128)], axis=1))
        mix = jnp.concatenate(blocks, axis=0).astype(BF)
        mix_ref[g] = mix
        branch = branch + dot(mix, wo_ref[g], NT)
    return x + branch


def temporal_fwd_kernel(lines, groups, *refs):
    linked = lines is not None
    (x_ref, w_ref, wo_ref, vec_ref), joins, (s_ref, qkv_ref, mix_ref, p_ref, r_ref), results, *parts = take(
        refs, 4, 4 if linked else 0, 5, 4 if linked else 0, 3, 3, 3, 3)
    i = pl.program_id(0)
    if linked:
        col_q2, col_q3, block_o2, block_o3 = joins
        full_q2, full_q3, full_o2, full_o3 = results
        place = Place(lines)
        t, hops = place.t, lines - 1
        q2 = PlaneGather(place, col_q2, lambda v, u: full_q2.at[t, :, v, u], parts[0])
        q3 = PlaneGather(place, col_q3, lambda v, u: full_q3.at[t, :, v, u], parts[1])
        o2 = LineGather(place, block_o2, full_o2.at[t], parts[2], to_core=full_o2.at[t])
        o3 = LineGather(place, block_o3, full_o3.at[t], parts[3], to_core=full_o3.at[t])

        @pl.when(i == 0)
        def _():
            place.greet()

        at_step(0, (q2, 0), (o2, 0), (o3, 0))
        at_step(2, (q2, 1), (q3, 0))
        at_step(3, (o2, 1), (o3, 1))
        at_step(5, *[(job, k) for k in range(2, hops) for job in (o2, o3)])
        at_step(6, (q3, 1))
    x = group_rows(x_ref[...], lambda b: STEP_GROUPS * i + b < groups)
    s = temporal_forward(x, w_ref, wo_ref, vec_ref, qkv_ref, mix_ref, p_ref, r_ref)
    for b in range(STEP_GROUPS):
        s_ref[:, b] = s[GROUP * b : GROUP * (b + 1)].reshape(FRAMES, 8, s.shape[1])
    if linked:
        at_step(
            6, (q2, 2), (o2, hops), (o3, hops), (q2, 3), (o2, hops + 1), (o3, hops + 1), (q3, 2), (q3, 3)
        )


def temporal_specs(groups, D):
    cols = D // 2
    n = STEP_GROUPS * GROUP
    steps = -(-groups // STEP_GROUPS)
    pairs = D // 128
    stream = pl.BlockSpec((FRAMES, STEP_GROUPS, 8, D), lambda i: (0, i, 0, 0))
    specs = [
        pl.BlockSpec((2, n, 3 * cols), lambda i: (0, i, 0)),
        pl.BlockSpec((2, n, cols), lambda i: (0, i, 0)),
        pl.BlockSpec((pairs, 2 * n, GROUP), lambda i: (0, i, 0)),
        pl.BlockSpec((2 * n, 128), lambda i: (i, 0)),
    ]
    shapes = [
        struct((2, steps * n, 3 * cols), BF),
        struct((2, steps * n, cols), BF),
        struct((pairs, 2 * steps * n, GROUP), BF),
        struct((2 * steps * n, 128), F32),
    ]
    return steps, stream, specs, shapes


def temporal_fwd(x, w, wo, vec, links=None):
    groups, D = x.shape[1], x.shape[3]
    steps, stream, kept_specs, kept_shapes = temporal_specs(groups, D)
    in_specs = [stream, whole_spec(w.shape), whole_spec(wo.shape), whole_spec(vec.shape)]
    out_specs = [stream] + kept_specs
    out_shape = [struct(x.shape, F32)] + kept_shapes
    args, scratch, lines, collective_id = [x, w, wo, vec], [], None, None
    if links is not None:
        col_q2, col_q3, block_o2, block_o3, lines, collective_id = links
        args += [col_q2, col_q3, block_o2, block_o3]
        in_specs += [whole_spec(v.shape) for v in args[4:]]
        out_specs += [any_spec()] * 4
        out_shape += [struct(full_shape(*col_q2.shape), BF)] * 2 + [struct((2, lines) + block_o2.shape, BF)] * 2
        scratch = PlaneGather.scratch() * 2 + LineGather.scratch(lines) * 2
    return pl.pallas_call(
        functools.partial(temporal_fwd_kernel, lines, groups),
        grid=(steps,),
        in_specs=in_specs,
        out_specs=out_specs,
        out_shape=out_shape,
        scratch_shapes=scratch,
        name="temporal_fwd",
        compiler_params=kernel_params(collective_id),
    )(*args)


def temporal_bwd_kernel(lines, groups, *refs):
    linked = lines is not None
    ins, joins, outs, results, (gw_ref, go_ref), rest = take(
        refs, 9, 5 if linked else 0, 4, 5 if linked else 0, 2, len(refs))
    x_ref, up_ref, qkv_ref, mix_ref, p_ref, r_ref, w_ref, wo_ref, vec_ref = ins
    gx_ref, gbw_ref, gbo_ref, gv_ref = outs
    cols = wo_ref.shape[2]
    i = pl.program_id(0)
    steps = pl.num_programs(0)

    @pl.when(i == 0)
    def _():
        gw_ref[...] = jnp.zeros_like(gw_ref)
        go_ref[...] = jnp.zeros_like(go_ref)
        gv_ref[...] = jnp.zeros_like(gv_ref)

    if linked:
        out_b, gq2, gq3, go2, go3 = joins
        out_a, col2, col3, block2, block3 = results
        place = Place(lines)
        t = place.t
        frames = FRAMES // 2
        (slots, held, ex_send, ex_recv, ex_local), *parts = take(
            rest, 5, PlaneReduce.n_scratch, PlaneReduce.n_scratch, LineReduce.n_scratch, LineReduce.n_scratch)
        q2 = PlaneReduce(place, gq2, col2, parts[0])
        q3 = PlaneReduce(place, gq3, col3, parts[1])
        o2 = LineReduce(place, go2, block2.at[0], parts[2])
        o3 = LineReduce(place, go3, block3.at[0], parts[3])
        out_load = pltpu.make_async_copy(out_b.at[pl.ds(frames * t, frames)], held, ex_local.at[steps])
        out_here = pltpu.make_async_copy(held, out_a.at[:, pl.ds(groups * t, groups)], ex_local.at[steps])
        out_there = remote(
            out_b.at[pl.ds(frames * (1 - t), frames)], out_a.at[:, pl.ds(groups * t, groups)],
            (ex_send, ex_recv), steps, place.core,
        )

        @pl.when(i == 0)
        def _():
            place.greet()

        at_step(0, (q2, 0), (o2, 0), (q3, 0), (o3, 0))

        @pl.when(i == 2)
        def _():
            out_load.start()
            out_there.start()

        @pl.when(i == 3)
        def _():
            out_load.wait()
            out_here.start()

        at_step(1, (q2, 1))
        at_step(2, (o2, 1), (q3, 1), (o3, 1))
        at_step(4, (q2, 2), (o2, 2), (o3, 2))
        at_step(5, (q3, 2))
        at_step(6, (q2, 3), *[(job, k) for k in range(3, lines) for job in (o2, o3)])

    live = lambda b: STEP_GROUPS * i + b < groups
    x = group_rows(x_ref[...], live)
    up = group_rows(up_ref[...], live)
    gx = attn_back_common(
        x, up.astype(BF), up, w_ref, wo_ref, vec_ref, 4, 11,
        lambda g: mix_ref[g],
        lambda g, j, rs: tuple(
            qkv_ref[g, rs, cols * t + 128 * j : cols * t + 128 * (j + 1)] for t in range(3)
        ),
        lambda pair, b: (
            p_ref[pair, 2 * GROUP * b : 2 * GROUP * (b + 1)],
            r_ref[2 * GROUP * b : 2 * GROUP * (b + 1), pair : pair + 1],
        ),
        gw_ref, go_ref, gv_ref, cols, x.shape[0] // GROUP,
    )

    @pl.when(i == steps - 1)
    def _():
        gbw_ref[...] = gw_ref[...].astype(BF)
        gbo_ref[...] = go_ref[...].astype(BF)

    if not linked:
        for b in range(STEP_GROUPS):
            gx_ref[:, b] = gx[GROUP * b : GROUP * (b + 1)].reshape(FRAMES, 8, gx.shape[1])
        return

    tail = groups % STEP_GROUPS or STEP_GROUPS

    def target(s, count):
        return gx_ref.at[:, pl.ds(groups * t + STEP_GROUPS * s, count)]

    def here(s, count):
        part = slots.at[s % 2, pl.ds(frames * t, frames), pl.ds(0, count)]
        return pltpu.make_async_copy(part, target(s, count), ex_local.at[s])

    def there(s, count):
        part = slots.at[s % 2, pl.ds(frames * (1 - t), frames), pl.ds(0, count)]
        return remote(part, target(s, count), (ex_send, ex_recv), s, place.core)

    def sent(s, count):
        here(s, count).wait()
        left(there(s, count))

    @pl.when(i >= 2)
    def _():
        sent(i - 2, STEP_GROUPS)

    for b in range(STEP_GROUPS):
        slots[i % 2, :, b] = gx[GROUP * b : GROUP * (b + 1)].reshape(FRAMES, 8, gx.shape[1])

    @pl.when(i < steps - 1)
    def _():
        here(i, STEP_GROUPS).start()
        there(i, STEP_GROUPS).start()

    @pl.when(i == steps - 1)
    def _():
        here(i, tail).start()
        there(i, tail).start()
        o2.stage(lines)
        o3.stage(lines)
        q3.stage(3)
        out_here.wait()
        out_there.wait()
        sent(i - 1, STEP_GROUPS)
        sent(i, tail)

        def body(s, _):
            arrived(there(s, STEP_GROUPS))
            return _

        lax.fori_loop(0, steps - 1, body, 0)
        arrived(there(i, tail))


def temporal_bwd(x, up, qkv, mix, p, r, w, wo, vec, links=None):
    groups, D = x.shape[1], x.shape[3]
    steps, stream, kept_specs, _ = temporal_specs(groups, D)
    in_specs = [stream, stream] + kept_specs + [whole_spec(v.shape) for v in (w, wo, vec)]
    out_specs = [stream, whole_spec(w.shape), whole_spec(wo.shape), whole_spec((8, D))]
    out_shape = [struct(x.shape, F32), struct(w.shape, BF), struct(wo.shape, BF), struct((8, D), F32)]
    args = [x, up, qkv, mix, p, r, w, wo, vec]
    scratch, lines, collective_id = [pltpu.VMEM(w.shape, F32), pltpu.VMEM(wo.shape, F32)], None, None
    if links is not None:
        out_b, gq2, gq3, go2, go3, lines, collective_id = links
        args += [out_b, gq2, gq3, go2, go3]
        q_block, o_block = gq2.shape[4:], go2.shape[4:]
        in_specs += [any_spec()] * 5
        out_specs[0] = any_spec()
        a_shape = (FRAMES // 2, 2 * groups, 8, D)
        out_shape[0] = struct(a_shape, F32)
        more = [struct((lines,) + q_block, BF)] * 2 + [struct((1, 2, 2) + o_block, BF)] * 2
        out_specs += [any_spec()] + [whole_spec(s.shape) for s in more]
        out_shape += [struct(a_shape, F32)] + more
        scratch += [pltpu.VMEM((2, FRAMES, STEP_GROUPS, 8, D), F32), pltpu.VMEM((FRAMES // 2, groups, 8, D), F32)]
        scratch += [dma_sems(steps + 1)] * 3
        scratch += PlaneReduce.scratch(lines, q_block, BF) * 2 + LineReduce.scratch(lines, o_block, BF) * 2
    return pl.pallas_call(
        functools.partial(temporal_bwd_kernel, lines, groups),
        grid=(steps,),
        in_specs=in_specs,
        out_specs=out_specs,
        out_shape=out_shape,
        scratch_shapes=scratch,
        name="temporal_bwd",
        compiler_params=kernel_params(collective_id),
    )(*args)


LAST_CUT = 640


def last_kernel(lines, *refs):
    (gq0, go0, tiles, col1, block1), (sum_q0, sum_o0, sum_tile, sum_q1, sum_o1), (
        col_a, col_b, col_tile, block0), *parts = take(
        refs, 5, 5, 4, 9, 9, 9, 9, 4, 4, 4, 4, 4, 4)
    place = Place(lines)
    place.greet()
    width = sum_q0.shape[1]
    qa = PlaneReduce(place, gq0, col_a, parts[0], pl.ds(0, LAST_CUT))
    qb = PlaneReduce(place, gq0, col_b, parts[1], pl.ds(LAST_CUT, width - LAST_CUT))
    small = PlaneReduce(place, tiles, col_tile, parts[2])
    o0 = LineReduce(place, go0, block0.at[0], parts[3])
    qa_line = LineSum(place, col_a, sum_q0.at[:, 0:LAST_CUT], parts[4])
    qb_line = LineSum(place, col_b, sum_q0.at[:, LAST_CUT:width], parts[5])
    small_line = LineSum(place, col_tile, sum_tile, parts[6])
    q1_line = LineSum(place, col1, sum_q1, parts[7])
    o1_plane = PlaneSum(place, block1, sum_o1, parts[8])
    o0_plane = PlaneSum(place, block0, sum_o0, parts[9])
    n = lines
    o0.stage(0)
    qa.stage(0)
    qb.stage(0)
    small.stage(0)
    o1_plane.stage(0)
    o0.stage(1)
    qa.stage(1)
    q1_line.stage(0)
    qb.stage(1)
    small.stage(1)
    o0.stage(2)
    qa.stage(2)
    small.stage(2)
    o1_plane.stage(1)
    q1_line.stage(1)
    qb.stage(2)
    qa.stage(3)
    qa_line.stage(0)
    small.stage(3)
    small_line.stage(0)
    o0.stage(3)
    for k in range(2, n - 1):
        q1_line.stage(k)
    qb.stage(3)
    qb_line.stage(0)
    qa_line.stage(1)
    small_line.stage(1)
    for k in range(4, n + 1):
        o0.stage(k)
    o0_plane.stage(0)
    qb_line.stage(1)
    q1_line.stage(n - 1)
    o1_plane.stage(2)
    for k in range(2, n):
        qa_line.stage(k)
        small_line.stage(k)
        if k == 2:
            o0_plane.stage(1)
        qb_line.stage(k)
    o0_plane.stage(2)


def last_call(gq0, go0, tiles, col1, block1, lines, collective_id):
    q_block, o_block, tile = gq0.shape[4:], go0.shape[4:], tiles.shape[4:]
    rows, width = q_block
    cut_a, cut_b = (rows, LAST_CUT), (rows, width - LAST_CUT)
    vmem = pl.BlockSpec(memory_space=pltpu.VMEM)
    return pl.pallas_call(
        functools.partial(last_kernel, lines),
        in_specs=[any_spec()] * 3 + [vmem] * 2,
        out_specs=[vmem] * 5,
        out_shape=[
            struct(q_block, F32), struct((1,) + o_block, F32), struct(tile, F32), struct(q_block, F32),
            struct((1,) + o_block, F32),
        ],
        scratch_shapes=[
            pltpu.VMEM((lines,) + cut_a, BF),
            pltpu.VMEM((lines,) + cut_b, BF),
            pltpu.VMEM((lines,) + tile, F32),
            pltpu.VMEM((1, 2, 2) + o_block, BF),
        ]
        + PlaneReduce.scratch(lines, cut_a, BF)
        + PlaneReduce.scratch(lines, cut_b, BF)
        + PlaneReduce.scratch(lines, tile, F32)
        + LineReduce.scratch(lines, o_block, BF)
        + LineSum.scratch(lines, cut_a, BF)
        + LineSum.scratch(lines, cut_b, BF)
        + LineSum.scratch(lines, tile, F32)
        + LineSum.scratch(lines, q_block, BF)
        + PlaneSum.scratch(1, o_block, BF) * 2,
        name="last_reduce",
        compiler_params=kernel_params(collective_id),
    )(gq0, go0, tiles, col1, block1)


MLP_ROWS = 416
MLP_CHUNK = 1536
INV_SQRT2 = 0.7071067811865476
INV_SQRT2PI = 0.3989422804014327


def mlp_kernel(x_ref, cot_ref, wia, wib, woa, wob, vec_ref, hid_ref, out_ref, up_ref,
               gia, gib, goa, gob, gv_ref, gh_ref, wi_ref, wo_ref, ai_ref, ao_ref, dn_ref, sems):
    i = pl.program_id(0)
    last = pl.num_programs(0) - 1
    chunks = wi_ref.shape[0]
    per = chunks // 2
    wide, width = wia.shape[2], per * MLP_CHUNK

    def copies(table, out):
        found = []
        for vmem, first, second in table:
            for g in range(2):
                for c in range(per):
                    start, stop = MLP_CHUNK * c, MLP_CHUNK * (c + 1)
                    for array, low, high in ((first, 0, wide), (second, wide, width)):
                        lo, hi = max(start, low), min(stop, high)
                        if lo < hi:
                            here = vmem.at[g * per + c, :, pl.ds(lo - start, hi - lo)]
                            there = array.at[g, :, pl.ds(lo - low, hi - lo)]
                            sem = sems.at[int(out), len(found)]
                            found.append(pltpu.make_async_copy(*((here, there) if out else (there, here)), sem))
        return found

    @pl.when(i == 0)
    def _():
        loads = copies(((wi_ref, wia, wib), (wo_ref, woa, wob)), False)
        for copy in loads:
            copy.start()
        for ref in (ai_ref, ao_ref, gv_ref, gh_ref):
            ref[...] = jnp.zeros_like(ref)
        for copy in loads:
            copy.wait()

    x = x_ref[...]
    xhat, rstd = norm_parts(x)
    gain = vec_ref[12:13, :]
    normed = (xhat * gain + vec_ref[8:9, :]).astype(BF)
    up = cot_ref[...]
    ub = up.astype(BF)
    gv_ref[3:4, :] += jnp.sum(up, axis=0, keepdims=True)
    out_ref[...] = x + vec_ref[9:10, :]
    dn_ref[...] = jnp.zeros_like(dn_ref)

    def chunk(k, _):
        pre = dot(normed, wi_ref[k], NN) + hid_ref[k]
        cdf = 0.5 + 0.5 * lax.erf(pre * INV_SQRT2)
        act = (pre * cdf).astype(BF)
        out_ref[...] += dot(act, wo_ref[k], NT)
        ao_ref[k] += dot(ub, act, TN)
        dact = dot(ub, wo_ref[k], NN).astype(BF).astype(F32)
        slope = cdf + pre * (jnp.exp(pre * pre * -0.5) * INV_SQRT2PI)
        dpre = (dact * slope).astype(BF)
        gh_ref[k] += jnp.sum(dpre.astype(F32), axis=0, keepdims=True)
        ai_ref[k] += dot(normed, dpre, TN)
        dn_ref[...] += dot(dpre, wi_ref[k], NT)
        return _

    lax.fori_loop(0, chunks, chunk, 0)
    dn = dn_ref[...]
    gv_ref[0:1, :] += jnp.sum(dn, axis=0, keepdims=True)
    gv_ref[4:5, :] += jnp.sum(dn * xhat, axis=0, keepdims=True)
    up_ref[...] = up + norm_back(dn, xhat, rstd, gain)

    @pl.when(i == last)
    def _():
        def place(k, _):
            wi_ref[k] = ai_ref[k].astype(BF)
            wo_ref[k] = ao_ref[k].astype(BF)
            return _

        lax.fori_loop(0, chunks, place, 0)
        stores = copies(((wi_ref, gia, gib), (wo_ref, goa, gob)), True)
        for copy in stores:
            copy.start()
        for copy in stores:
            copy.wait()


def mlp_both(x, cot, wia, wib, woa, wob, vec, hidden):
    rows, D = x.shape
    width = hidden.shape[1]
    chunks = 2 * width // MLP_CHUNK
    row_spec = pl.BlockSpec((MLP_ROWS, D), lambda i: (i, 0))
    mats = [wia, wib, woa, wob]
    both = (chunks, D, MLP_CHUNK)
    units = (chunks, 1, MLP_CHUNK)
    outs = pl.pallas_call(
        mlp_kernel,
        grid=(rows // MLP_ROWS,),
        in_specs=[row_spec, row_spec] + [any_spec()] * 4 + [whole_spec(vec.shape), whole_spec(units)],
        out_specs=[row_spec, row_spec] + [any_spec()] * 4 + [whole_spec((8, D)), whole_spec(units)],
        out_shape=[struct((rows, D), F32)] * 2
        + [struct(m.shape, BF) for m in mats]
        + [struct((8, D), F32), struct(units, F32)],
        scratch_shapes=[pltpu.VMEM(both, BF)] * 2
        + [pltpu.VMEM(both, F32)] * 2
        + [pltpu.VMEM((MLP_ROWS, D), F32), pltpu.SemaphoreType.DMA((2, 6 * chunks))],
        name="mlp_both",
        compiler_params=kernel_params(None),
    )(x, cot, *mats, vec, hidden.reshape(units))
    return (*outs[:-1], outs[-1].reshape(hidden.shape))


def swap_to_patches(rows):
    return lax.all_to_all(rows, "tensor", split_axis=1, concat_axis=0, tiled=True)


def swap_to_frames(rows):
    return lax.all_to_all(rows, "tensor", split_axis=0, concat_axis=1, tiled=True)


def pad_frames(rows):
    D = rows.shape[1]
    return jnp.pad(rows.reshape(-1, PATCHES, D), ((0, 0), (0, PAD - PATCHES), (0, 0)))


def shards(tokens, cotangent, attn_qkv, attn_out, mlp_in, mlp_out, norm_gains, biases, hidden_bias):
    D = tokens.shape[1]
    depth = mlp_in.shape[1]
    cols = attn_qkv.shape[4]
    units = mlp_in.shape[2]
    frames = tokens.shape[0] // PATCHES
    everyone = ("dp", "tensor")
    chips = D // depth
    devices = 2 * chips
    share = D // devices
    count = 13 * share + 2 * units // devices
    wide = 3 * cols
    down = mlp_out[0].T

    def spread(gv_s, gv_t, gv_m, g_hidden):
        vec_grad = jnp.concatenate(
            [gv_s[0:4], gv_t[0:4], gv_m[0:1], gv_m[3:4], gv_s[4:5], gv_t[4:5], gv_m[4:5]]
        )
        vec_grad = vec_grad.reshape(13, devices, share).transpose(1, 0, 2).reshape(devices, 13 * share)
        return jnp.concatenate([vec_grad, g_hidden.reshape(devices, -1)], axis=1)

    flat = lambda w: w.reshape(2, D, w.shape[-1])
    rows_of = lambda v: v.reshape(-1, D)
    if depth % 16 == 0 and chips % 4 == 0:
        lines = chips // 4
        cut = lambda g: g.reshape(full_shape(lines, depth, g.shape[2]))
        x, cot, tiles, *w0, col_q1, block_o1 = first_call(
            tokens, cotangent, norm_gains[0], biases[0], hidden_bias,
            attn_qkv[0].transpose(0, 2, 1, 3), attn_out[0].transpose(0, 2, 1), lines, 1,
        )
        tiles = tiles.reshape((2, chips) + TILE)
        vec = tiles[:, :, :13, :share].transpose(2, 1, 0, 3).reshape(13, D)
        hidden = tiles[:, :, 16, : 2 * units // devices].transpose(1, 0, 2).reshape(2, units)
        w0 = [flat(w) for w in w0]
        x1, *kept_s, q1, o1, col_q2, col_q3, block_o2, block_o3 = spatial_fwd(
            x, *w0, vec, (col_q1, block_o1, mlp_in[0], down, lines, 2)
        )
        w1 = [flat(q1), flat(o1)]
        x2, *kept_t, q2, q3, o2, o3 = temporal_fwd(
            x1, *w1, vec, (col_q2, col_q3, block_o2, block_o3, lines, 3)
        )
        out_b, up2, gq2, go2, gq3, go3, gv_m, g_hidden = mlp_both(
            rows_of(x2), rows_of(cot), flat(q2), flat(o2), flat(q3), flat(o3), vec, hidden
        )
        up1, gq1, go1, gv_t, out_a, col2, col3, block2, block3 = temporal_bwd(
            x1, up2.reshape(x1.shape), *kept_t, *w1, vec,
            (out_b.reshape(x1.shape), cut(gq2), cut(gq3), cut(go2), cut(go3), lines, 4),
        )
        up0, gq0, go0, gv_s, output, col1, block1, gq2, gq3, go2, go3 = spatial_bwd(
            x, up1, *kept_s, *w0, vec, (out_a, cut(gq1), cut(go1), col2, col3, block2, block3, lines, 5)
        )
        tiles = jnp.pad(spread(gv_s, gv_t, gv_m, g_hidden), ((0, 0), (0, 1024 - count)))
        tiles = tiles.reshape(chips, 2, 1024).transpose(1, 0, 2).reshape(full_shape(lines, 8, 128))
        gq0, go0, small_grad, gq1, go1 = last_call(cut(gq0), cut(go0), tiles, col1, block1, lines, 6)
        small_grad = small_grad.reshape(-1)[:count]
        go0, go1, go2, go3 = [g[0] for g in (go0, go1, go2, go3)]
    else:
        owns = []
        for s in range(2):
            owns += [attn_qkv[0, s].reshape(depth, wide), attn_out[0, s].T]
        owns += [mlp_in[0, :, :wide], mlp_in[0, :, wide:], down[:, :wide], down[:, wide:]]
        small = jnp.concatenate(
            [biases[0].reshape(-1), norm_gains[0].reshape(-1), hidden_bias[0].reshape(-1)]
        )
        small = lax.all_gather(small.reshape(1, -1), everyone, axis=0, tiled=True)
        vec = small[:, : 13 * share].reshape(devices, 13, share).transpose(1, 0, 2).reshape(13, D)
        hidden = small[:, 13 * share :].reshape(2, units)
        weights = [flat(lax.all_gather(w, ("tensor", "dp"), axis=0, tiled=True).reshape(2, D, -1)) for w in owns]
        x = pad_frames(tokens)
        fold = lambda v: v.reshape(frames, PAD // 8, 8, D)
        x1, *kept_s = spatial_fwd(x, *weights[0:2], vec)
        x1 = swap_to_patches(x1)
        x2, *kept_t = temporal_fwd(x1, *weights[2:4], vec)
        cot = swap_to_patches(fold(pad_frames(cotangent).astype(F32)))
        out_b, up2, *mlp_grads, gv_m, g_hidden = mlp_both(
            rows_of(x2), rows_of(cot), *weights[4:], vec, hidden
        )
        output = swap_to_frames(out_b.reshape(x1.shape)).reshape(frames, PAD, D)[:, :PATCHES].astype(BF)
        output = rows_of(output)
        up1, *grads1, gv_t = temporal_bwd(x1, up2.reshape(x1.shape), *kept_t, *weights[2:4], vec)
        up0, *grads0, gv_s = spatial_bwd(x, swap_to_frames(up1), *kept_s, *weights[0:2], vec)
        gq0, go0, gq1, go1, gq2, go2, gq3, go3 = [
            lax.psum_scatter(
                g.reshape(2 * D, g.shape[2]), ("tensor", "dp"), scatter_dimension=0, tiled=True
            ).astype(F32)
            for g in grads0 + grads1 + mlp_grads
        ]
        small_grad = lax.psum_scatter(
            spread(gv_s, gv_t, gv_m, g_hidden), everyone, scatter_dimension=0, tiled=True
        )[0]
    grad_qkv = jnp.stack([gq0.reshape(depth, 3, cols), gq1.reshape(depth, 3, cols)])[None]
    grad_out = jnp.stack([go0.T, go1.T])[None]
    grad_biases = small_grad[: 10 * share].reshape(1, 10, share)
    grad_gains = small_grad[10 * share : 13 * share].reshape(1, 3, share)
    grad_hidden = small_grad[13 * share :].reshape(1, -1)
    return (
        output,
        up0,
        grad_qkv,
        grad_out,
        jnp.concatenate([gq2, go2], axis=1)[None],
        jnp.concatenate([gq3, go3], axis=1).T[None],
        grad_gains,
        grad_biases,
        grad_hidden,
    )


def solution(mesh):
    placed = (
        P(("dp", "tensor"), None),
        P(("dp", "tensor"), None),
        P(None, None, "dp", None, "tensor"),
        P(None, None, "tensor", "dp"),
        P(None, "dp", "tensor"),
        P(None, "tensor", "dp"),
        P(None, None, ("dp", "tensor")),
        P(None, None, ("dp", "tensor")),
        P(None, ("dp", "tensor")),
    )
    return jax.shard_map(
        shards, mesh=mesh, in_specs=placed, out_specs=placed, check_vma=False
    )
```

```python
import functools
import jax
import jax.numpy as jnp
from jax import lax
from jax.experimental import pallas as pl
from jax.experimental.pallas import tpu as pltpu
from jax.sharding import PartitionSpec as P

HEAD = 64
FRAMES = 16
PATCHES = 196
PAD = 208
EPSILON = 1e-06
BF = jnp.bfloat16
F32 = jnp.float32
NN = (((1,), (0,)), ((), ()))
NT = (((1,), (1,)), ((), ()))
TN = (((0,), (0,)), ((), ()))
VMEM_BYTES = 60 * 1024 * 1024


def dot(a, b, dims):
    return lax.dot_general(a, b, dims, preferred_element_type=F32)


def norm_parts(x):
    mean = jnp.mean(x, axis=-1, keepdims=True)
    centred = x - mean
    var = jnp.mean(centred * centred, axis=-1, keepdims=True)
    rstd = lax.rsqrt(var + EPSILON)
    return centred * rstd, rstd


def norm_back(grad_normed, xhat, rstd, gain):
    scaled = grad_normed * gain
    first = jnp.mean(scaled, axis=-1, keepdims=True)
    second = jnp.mean(scaled * xhat, axis=-1, keepdims=True)
    return rstd * (scaled - first - xhat * second)


def split_halves(pair):
    lane = lax.broadcasted_iota(jnp.int32, pair.shape, 1)
    zero = jnp.zeros_like(pair)
    return jnp.where(lane < HEAD, pair, zero), jnp.where(lane < HEAD, zero, pair)


def project(normed, w_ref, vec_ref, row_base, cols):
    parts = []
    for g in range(2):
        qkv = dot(normed, w_ref[g], NN)
        bq = vec_ref[row_base + 1 : row_base + 2, g * cols : (g + 1) * cols]
        bv = vec_ref[row_base + 2 : row_base + 3, g * cols : (g + 1) * cols]
        q = (qkv[:, :cols] + bq).astype(BF) * BF(0.125)
        k = qkv[:, cols : 2 * cols].astype(BF)
        v = (qkv[:, 2 * cols :] + bv).astype(BF)
        parts.append((q, k, v))
    return parts


def stack_halves(pair):
    return jnp.concatenate(split_halves(pair), axis=0)


def merge_halves(both):
    rows = both.shape[0] // 2
    lane = lax.broadcasted_iota(jnp.int32, (rows, both.shape[1]), 1)
    return jnp.where(lane < HEAD, both[:rows], both[rows:])


def heads_forward(pairs, mask):
    scores = [dot(stack_halves(q), k, NT) for q, k, _ in pairs]
    exps, recips = [], []
    for s in scores:
        s = jnp.where(mask, s, -1e30)
        e = jnp.exp(s - jnp.max(s, axis=-1, keepdims=True))
        recips.append(1.0 / jnp.sum(e, axis=-1, keepdims=True))
        exps.append(e.astype(BF))
    outs = [merge_halves(dot(e, v, NN) * r) for e, r, (_, _, v) in zip(exps, recips, pairs)]
    return outs, exps, recips


def heads_backward(pairs):
    dors, deltas = [], []
    for q, k, v, o, do, e, r in pairs:
        both = stack_halves(do.astype(F32)) * r
        deltas.append(jnp.sum(both * jnp.concatenate([o, o], axis=0).astype(F32), axis=-1, keepdims=True))
        dors.append(both.astype(BF))
    dps = [dot(dor, p[2], NT) for dor, p in zip(dors, pairs)]
    dss = [(p[5].astype(F32) * (dp - delta)).astype(BF) for dp, delta, p in zip(dps, deltas, pairs)]
    dq = [(merge_halves(dot(ds, p[1], NN)) * 0.125).astype(BF) for ds, p in zip(dss, pairs)]
    dk = [dot(ds, stack_halves(p[0]), TN).astype(BF) for ds, p in zip(dss, pairs)]
    dv = [dot(p[5], dor, TN).astype(BF) for dor, p in zip(dors, pairs)]
    return dq, dk, dv


def spatial_mask():
    return lax.broadcasted_iota(jnp.int32, (2 * PAD, PAD), 1) < PATCHES


def attn_back_common(x, ub, up, w_ref, wo_ref, vec_ref, row_base, gain_row, mix_of, qkv_of, exps_of, gw_ref, go_ref, gv_ref, cols, blocks):
    xhat, rstd = norm_parts(x)
    gain = vec_ref[gain_row : gain_row + 1, :]
    normed = (xhat * gain + vec_ref[row_base : row_base + 1, :]).astype(BF)
    dn = None
    gv_ref[3:4, :] += jnp.sum(up, axis=0, keepdims=True)
    rows = x.shape[0]
    step = rows // blocks
    for g in range(2):
        dmix = dot(ub, wo_ref[g], NN).astype(BF)
        mix = mix_of(g)
        go_ref[g] += dot(ub, mix, TN)
        parts = [[], [], []]
        for b in range(blocks):
            rs = slice(step * b, step * (b + 1))
            pairs = []
            for j in range(cols // 128):
                sl = slice(128 * j, 128 * (j + 1))
                q, k, v = qkv_of(g, j, rs)
                e, r = exps_of(g * (cols // 128) + j, b)
                pairs.append((q, k, v, mix[rs, sl], dmix[rs, sl], e, r))
            for part, got in zip(parts, heads_backward(pairs)):
                part.append(jnp.concatenate(got, axis=1))
        dq, dk, dv = [jnp.concatenate(part, axis=0) for part in parts]
        span = slice(g * cols, (g + 1) * cols)
        gv_ref[1:2, span] += jnp.sum(dq.astype(F32), axis=0, keepdims=True)
        gv_ref[2:3, span] += jnp.sum(dv.astype(F32), axis=0, keepdims=True)
        dqkv = jnp.concatenate([dq, dk, dv], axis=1)
        gw_ref[g] += dot(normed, dqkv, TN)
        term = dot(dqkv, w_ref[g], NT)
        dn = term if dn is None else dn + term
    gv_ref[0:1, :] += jnp.sum(dn, axis=0, keepdims=True)
    gv_ref[4:5, :] += jnp.sum(dn * xhat, axis=0, keepdims=True)
    return up + norm_back(dn, xhat, rstd, gain)


MESH = pl.DeviceIdType.MESH


class Place:
    def __init__(self, lines):
        self.lines = lines
        self.dp = lax.axis_index("dp")
        self.t = lax.axis_index("tensor")
        self.z = self.dp // 4
        self.y = (self.dp // 2) % 2
        self.x = self.dp % 2
        self.a = self.y * (1 - self.t) + self.x * self.t
        self.b = self.x * (1 - self.t) + self.y * self.t
        toward_y = self.dp + 2 - 4 * self.y
        toward_x = self.dp + 1 - 2 * self.x
        self.first = (toward_y * (1 - self.t) + toward_x * self.t, self.t)
        self.second = (toward_x * (1 - self.t) + toward_y * self.t, self.t)
        self.core = (self.dp, 1 - self.t)
        self.up = (self.dp + 4, self.t)
        self.down = (self.dp - 4, self.t)

    def yx(self, a, b, t):
        return a * (1 - t) + b * t, b * (1 - t) + a * t

    def greet(self):
        bar = pltpu.get_barrier_semaphore()
        for who in (self.core, self.first, self.second):
            pl.semaphore_signal(bar, inc=1, device_id=who, device_id_type=MESH)

        @pl.when(self.z > 0)
        def _():
            pl.semaphore_signal(bar, inc=1, device_id=self.down, device_id_type=MESH)

        @pl.when(self.z < self.lines - 1)
        def _():
            pl.semaphore_signal(bar, inc=1, device_id=self.up, device_id_type=MESH)

        inner = (self.z > 0).astype(jnp.int32) + (self.z < self.lines - 1).astype(jnp.int32)
        pl.semaphore_wait(bar, 3 + inner)


def remote(src, dst, sems, i, who):
    return pltpu.make_async_remote_copy(
        src_ref=src, dst_ref=dst, send_sem=sems[0].at[i], recv_sem=sems[1].at[i],
        device_id=who, device_id_type=MESH,
    )


def dma_sems(n):
    return pltpu.SemaphoreType.DMA((n,))


def begin(c):
    c.start()


def arrived(c):
    c.wait_recv()


def left(c):
    c.wait_send()


def whole(c):
    c.wait()


class LineGather:
    @staticmethod
    def scratch(lines):
        n = 2 * (lines - 1) + 1
        return [dma_sems(n), dma_sems(n), dma_sems(1)]

    n_scratch = 3

    def __init__(self, place, own, col, scratch, to_core=None, kept=False):
        self.p, self.own, self.col, self.to_core, self.kept = place, own, col, to_core, kept
        self.sems, self.local = scratch[:2], scratch[2]
        self.hops = place.lines - 1
        self.stages = self.hops + (1 if to_core is None else 2)

    def keep(self):
        return pltpu.make_async_copy(self.own, self.col.at[self.p.z], self.local.at[0])

    def _up(self, k):
        block = self.col.at[self.p.z - k]
        return remote(self.own if k == 0 else block, block, self.sems, k, self.p.up)

    def _down(self, k):
        block = self.col.at[self.p.z + k]
        return remote(self.own if k == 0 else block, block, self.sems, self.hops + k, self.p.down)

    def _sent(self, k, act):
        p = self.p

        @pl.when((p.z < self.hops) & (p.z >= k))
        def _():
            act(self._up(k))

        @pl.when((p.z > 0) & (p.z + k <= self.hops))
        def _():
            act(self._down(k))

    def _take(self, k):
        p = self.p

        @pl.when(p.z >= k + 1)
        def _():
            arrived(self._up(k))

        @pl.when(p.z + k + 1 <= self.hops)
        def _():
            arrived(self._down(k))

    def _core(self):
        return remote(self.to_core, self.to_core, self.sems, 2 * self.hops, self.p.core)

    def stage(self, k):
        if k == 0:
            if not self.kept:
                self.keep().start()
            self._sent(0, begin)
        elif k <= self.hops:
            self._take(k - 1)
            if k < self.hops:
                self._sent(k, begin)
                return
            if not self.kept:
                self.keep().wait()
            if self.to_core is not None:
                self._core().start()
            for i in range(self.hops):
                self._sent(i, left)
        else:
            self._core().wait()


class PlaneGather:
    @staticmethod
    def scratch():
        return [dma_sems(5), dma_sems(5), dma_sems(1)]

    n_scratch = 3
    stages = 4

    def __init__(self, place, block, spot, scratch, cores=True, kept=False):
        self.p, self.block, self.spot, self.cores, self.kept = place, block, spot, cores, kept
        self.sems, self.local = scratch[:2], scratch[2]

    def _keep(self):
        return pltpu.make_async_copy(self.block, self.spot(self.p.y, self.p.x), self.local.at[0])

    def _own(self, i, who):
        return remote(self.block, self.spot(self.p.y, self.p.x), self.sems, i, who)

    def _plane(self, i, who, b, act):
        p = self.p
        every = slice(None)

        @pl.when(p.t == 0)
        def _():
            part = self.spot(every, b)
            act(remote(part, part, self.sems, i, who))

        @pl.when(p.t == 1)
        def _():
            part = self.spot(b, every)
            act(remote(part, part, self.sems, i, who))

    def _pass_on(self):
        p = self.p
        part = self.spot(*p.yx(1 - p.a, p.b, p.t))
        return remote(part, part, self.sems, 3, p.core)

    def stage(self, k):
        p = self.p
        if k == 0:
            if not self.kept:
                self._keep().start()
            self._own(0, p.first).start()
            if self.cores:
                self._own(2, p.core).start()
        elif k == 1:
            if not self.kept:
                self._keep().wait()
            arrived(self._own(0, p.first))
            self._plane(1, p.second, p.b, begin)
            if self.cores:
                self._pass_on().start()
        elif k == 2:
            self._plane(1, p.second, p.b, arrived)
            if self.cores:
                self._plane(4, p.core, 1 - p.b, begin)
        else:
            if self.cores:
                self._own(2, p.core).wait()
                self._pass_on().wait()
                self._plane(4, p.core, 1 - p.b, whole)
            left(self._own(0, p.first))
            self._plane(1, p.second, p.b, left)


class When:
    def __init__(self, valid, make):
        self.valid, self.make = valid, make

    def stage(self, k):
        @pl.when(self.valid)
        def _():
            self.make().stage(k)


def add_blocks(u, v, dtype):
    if u.dtype == v.dtype == dtype:
        return u + v
    return (u.astype(F32) + v.astype(F32)).astype(dtype)


class CoreSum:
    @staticmethod
    def scratch(n, block, dtype):
        return [
            pltpu.VMEM((n, 2, 2) + block, dtype),
            pltpu.VMEM((n, 2, 2) + block, dtype),
            dma_sems(4),
            dma_sems(4),
            dma_sems(4),
        ]

    n_scratch = 5

    def __init__(self, place, g_ref, scratch, span=None):
        self.p, self.g, self.span = place, g_ref, span
        self.own, self.land, self.sems, self.local = scratch[0], scratch[1], scratch[2:4], scratch[4]

    def _part(self, t, y, x):
        if self.span is None:
            return self.g.at[t, :, y, x]
        return self.g.at[t, :, y, x, :, self.span]

    def _copies(self):
        p, copies = self.p, []
        for a in range(2):
            for b in range(2):
                y, x = p.yx(a, b, 1 - p.t)
                copies.append(
                    remote(self._part(1 - p.t, y, x), self.land.at[:, a, b], self.sems, 2 * a + b, p.core)
                )
                y, x = p.yx(a, b, p.t)
                copies.append(
                    pltpu.make_async_copy(self._part(p.t, y, x), self.own.at[:, a, b], self.local.at[2 * a + b])
                )
        return copies

    def start(self):
        for c in self._copies():
            c.start()

    def wait(self):
        for c in self._copies():
            c.wait()

    def add(self, a):
        def body(i, _):
            self.own[i, a] = add_blocks(self.own[i, a], self.land[i, a], self.own.dtype)
            return _

        lax.fori_loop(0, self.own.shape[0], body, 0)


class PlaneSum:
    @staticmethod
    def scratch(n, block, dtype):
        return [pltpu.VMEM((n, 2) + block, dtype), pltpu.VMEM((n,) + block, dtype), dma_sems(2), dma_sems(2)]

    n_scratch = 4
    stages = 3

    def __init__(self, place, own, col, scratch):
        self.p, self.own, self.col = place, own, col
        self.land1, self.land2, self.sems = scratch[0], scratch[1], scratch[2:4]
        self.n = self.land2.shape[0]

    def _first(self):
        return remote(self.own.at[:, 1 - self.p.a], self.land1, self.sems, 0, self.p.first)

    def _second(self):
        return remote(self.land1.at[:, 1 - self.p.b], self.land2, self.sems, 1, self.p.second)

    def stage(self, k):
        p = self.p
        if k == 0:
            self._first().start()
        elif k == 1:
            self._first().wait()

            def away(i, _):
                self.land1[i, 1 - p.b] = add_blocks(
                    self.own[i, p.a, 1 - p.b], self.land1[i, 1 - p.b], self.land1.dtype
                )
                return _

            lax.fori_loop(0, self.n, away, 0)
            self._second().start()
        else:
            self._second().wait()

            def body(i, _):
                total = self.own[i, p.a, p.b].astype(F32) + self.land1[i, p.b].astype(F32)
                self.col[i] = (total + self.land2[i].astype(F32)).astype(self.col.dtype)
                return _

            lax.fori_loop(0, self.n, body, 0)


class LineSum:
    @staticmethod
    def scratch(lines, block, dtype):
        return [
            pltpu.VMEM((lines,) + block, dtype),
            pltpu.VMEM((lines,) + block, dtype),
            dma_sems(2 * (lines - 1)),
            dma_sems(2 * (lines - 1)),
        ]

    n_scratch = 4

    def __init__(self, place, col, out, scratch):
        self.p, self.col, self.out = place, col, out
        self.from_down, self.from_up = scratch[:2]
        self.sems = scratch[2:4]
        self.stages = place.lines

    def _up(self, d):
        block = self.from_down.at[d]
        return remote(block, block, self.sems, d - 1, self.p.up)

    def _down(self, d):
        block = self.from_up.at[d]
        return remote(block, block, self.sems, self.p.lines - 1 + d, self.p.down)

    def stage(self, step):
        n = self.p.lines
        for z in range(n):
            up = [d for d in range(z + 1, n) if z + (n - 1 - d) == step]
            down = [d for d in range(z) if (n - 1 - z) + d == step]
            if step < n - 1 and not up and not down:
                continue
            pl.when(self.p.z == z)(functools.partial(self._at, z, up, down, step == n - 1))

    def _at(self, z, up, down, last):
        n, dtype = self.p.lines, self.from_down.dtype
        for d in up:
            if z > 0:
                arrived(self._up(d))
                self.from_down[d] = add_blocks(self.from_down[d], self.col[d], dtype)
            else:
                self.from_down[d] = self.col[d]
            self._up(d).start()
        for d in down:
            if z < n - 1:
                arrived(self._down(d))
                self.from_up[d] = add_blocks(self.from_up[d], self.col[d], dtype)
            else:
                self.from_up[d] = self.col[d]
            self._down(d).start()
        if not last:
            return
        total = self.col[z].astype(F32)
        if z > 0:
            arrived(self._up(z))
            total = total + self.from_down[z].astype(F32)
        if z < n - 1:
            arrived(self._down(z))
            total = total + self.from_up[z].astype(F32)
        self.out[...] = total.astype(self.out.dtype)
        for d in range(z + 1, n):
            left(self._up(d))
        for d in range(z):
            left(self._down(d))


class PlaneReduce:
    @staticmethod
    def scratch(n, block, dtype):
        return CoreSum.scratch(n, block, dtype) + PlaneSum.scratch(n, block, dtype)

    n_scratch = 9

    def __init__(self, place, g_ref, col, scratch, span=None):
        self.p = place
        self.cores = CoreSum(place, g_ref, scratch[:5], span)
        self.plane = PlaneSum(place, self.cores.own, col, scratch[5:])

    def stage(self, k):
        if k == 0:
            self.cores.start()
        elif k == 1:
            self.cores.wait()
            self.cores.add(1 - self.p.a)
            self.plane.stage(0)
            self.cores.add(self.p.a)
        else:
            self.plane.stage(k - 1)


class LineReduce:
    @staticmethod
    def scratch(n, block, dtype):
        return CoreSum.scratch(n, block, dtype) + LineSum.scratch(n, (2, 2) + block, dtype)

    n_scratch = 9

    def __init__(self, place, g_ref, out, scratch):
        self.cores = CoreSum(place, g_ref, scratch[:5])
        self.line = LineSum(place, self.cores.own, out, scratch[5:])

    def stage(self, k):
        if k == 0:
            self.cores.start()
            return
        if k == 1:
            self.cores.wait()
            self.cores.add(0)
            self.cores.add(1)
        self.line.stage(k - 1)


def at_step(step, *stages):
    @pl.when(pl.program_id(0) == step)
    def _():
        for job, k in stages:
            job.stage(k)


def take(refs, *counts):
    out, i = [], 0
    for c in counts:
        out.append(refs[i : i + c])
        i += c
    return out


GROUP = 8 * FRAMES
STEP_GROUPS = 2


def temporal_mask():
    a = lax.broadcasted_iota(jnp.int32, (2 * GROUP, GROUP), 0)
    b = lax.broadcasted_iota(jnp.int32, (2 * GROUP, GROUP), 1)
    return (a % 8) == (b % 8)


def any_spec():
    return pl.BlockSpec(memory_space=pl.ANY)


def whole_spec(shape):
    return pl.BlockSpec(tuple(shape), lambda i: (0,) * len(shape))


def struct(shape, dtype):
    return jax.ShapeDtypeStruct(tuple(shape), dtype)


def full_shape(lines, rows, width):
    return (2, lines, 2, 2, rows, width)


def kernel_params(collective_id):
    if collective_id is None:
        return pltpu.CompilerParams(vmem_limit_bytes=VMEM_BYTES)
    return pltpu.CompilerParams(
        vmem_limit_bytes=VMEM_BYTES, collective_id=collective_id, has_side_effects=True
    )


TILE = (24, 128)


def padded_frame(rows, f, frames):
    half = frames // 2
    start = half * PATCHES * (f // half)
    inside = PATCHES * (f % half)
    low = inside // 16 * 16
    high = -(-(inside + PATCHES) // 16) * 16
    block = rows[start + low : start + high].astype(F32)[inside - low : inside - low + PATCHES]
    return jnp.concatenate([block, jnp.zeros((PAD - PATCHES, rows.shape[1]), F32)], axis=0)


def first_kernel(lines, *refs):
    (tok, cot, gains, biases, hidden, qkv, outs), (x_out, cot_b, full_tile, full_q, full_o, *results), (
        tile, q0, q1, col_q1, block_o1, col_tile, block_o0, tok_v, cot_v, frames_v, ex_send, ex_recv, ex_local, loads), scratch = take(
        refs, 7, 7, 14, len(refs))
    place = Place(lines)
    t, z, y, x = place.t, place.z, place.y, place.x
    hops = lines - 1
    load_cot = pltpu.make_async_copy(cot, cot_v, loads.at[0])
    load_tok = pltpu.make_async_copy(tok, tok_v, loads.at[1])
    part = qkv.shape[3]
    load_qkv = [
        pltpu.make_async_copy(qkv.at[s, k], own.at[:, pl.ds(part * k, part)], loads.at[2 + 3 * s + k])
        for s, own in enumerate((q0, q1))
        for k in range(3)
    ]
    for copy in load_qkv:
        copy.start()
    load_cot.start()
    load_tok.start()
    tile[...] = jnp.zeros_like(tile)
    tile[0:10, 0 : biases.shape[1]] = biases[...]
    tile[10:13, 0 : gains.shape[1]] = gains[...]
    tile[16:17, 0 : hidden.shape[1]] = hidden[...]
    o0, o1 = outs.at[0], outs.at[1]
    place.greet()
    for copy in load_qkv:
        copy.wait()
    pool = list(scratch)

    def sems():
        three = pool[:3]
        del pool[:3]
        return three

    tile_line = LineGather(place, tile, col_tile, sems())
    q0_line = LineGather(place, q0, full_q.at[t, :, y, x], sems(), kept=True)
    o0_line = LineGather(place, block_o0, full_o.at[t], sems(), to_core=full_o.at[t])
    q1_line = LineGather(place, q1, col_q1, sems())
    tile_plane = PlaneGather(place, col_tile, lambda v, u: full_tile.at[t, :, v, u], sems())
    o0_plane = PlaneGather(place, o0, lambda v, u: block_o0.at[v, u], sems(), cores=False)
    o1_plane = PlaneGather(place, o1, lambda v, u: block_o1.at[v, u], sems(), cores=False)
    own_slab = PlaneGather(place, q0, lambda v, u: full_q.at[t, z, v, u], sems())
    slabs = {}
    for k in range(1, lines):
        for sign in (-1, 1):
            far, own_sems = z + sign * k, sems()
            slabs[k, sign] = When(
                (far >= 0) & (far <= hops),
                functools.partial(
                    PlaneGather, place, full_q.at[t, far, y, x],
                    lambda v, u, far=far: full_q.at[t, far, v, u], own_sems, kept=True,
                ),
            )

    def pair(k, stage):
        slabs[k, -1].stage(stage)
        slabs[k, 1].stage(stage)

    q0_line.stage(0)
    own_slab.stage(0)
    o0_plane.stage(0)
    tile_line.stage(0)
    D = tok.shape[1]
    frames = x_out.shape[0]
    pieces = [("cot", f) for f in range(frames)] + [("tok", f) for f in range(frames)]

    def work(count=1):
        for kind, f in [pieces.pop(0) for _ in range(min(count, len(pieces)))]:
            if f == 0:
                (load_cot if kind == "cot" else load_tok).wait()
            if kind == "cot":
                frames_v[f] = padded_frame(cot_v, f, frames).reshape(PAD // 8, 8, D)
            else:
                x_out[f] = padded_frame(tok_v, f, frames).astype(BF)

    work(5)
    own_slab.stage(1)
    q0_line.stage(1)
    pair(1, 0)
    o0_plane.stage(1)
    tile_line.stage(1)
    q1_line.stage(0)
    o1_plane.stage(0)
    groups = PAD // 16
    mine = pltpu.make_async_copy(
        frames_v.at[:, pl.ds(groups * t, groups)], cot_b.at[pl.ds(frames * t, frames)], ex_local.at[0]
    )
    theirs = remote(
        frames_v.at[:, pl.ds(groups * (1 - t), groups)], cot_b.at[pl.ds(frames * t, frames)],
        (ex_send, ex_recv), 0, place.core,
    )
    work(frames - 5)
    mine.start()
    theirs.start()
    o0_plane.stage(2)
    o0_plane.stage(3)
    o0_line.stage(0)
    pair(1, 1)
    own_slab.stage(2)
    work(2)
    for k in range(2, lines):
        q0_line.stage(k)
        pair(k, 0)
        tile_line.stage(k)
        q1_line.stage(k - 1)
        work()
        pair(k, 1)
        pair(k - 1, 2)
        work()
        o0_line.stage(k - 1)
    tile_plane.stage(0)
    o1_plane.stage(1)
    work()
    tile_plane.stage(1)
    o1_plane.stage(2)
    pair(hops, 2)
    work(frames)
    o0_line.stage(hops)
    tile_plane.stage(2)
    q1_line.stage(hops)
    o1_plane.stage(3)
    tile_plane.stage(3)
    o0_line.stage(hops + 1)
    own_slab.stage(3)
    for k in range(1, lines):
        pair(k, 3)
    for result, part in zip(results, (col_q1, block_o1)):
        result[...] = part[...]
    mine.wait()
    theirs.wait()


def first_call(tokens, cot, gains, biases, hidden, qkv, outs, lines, collective_id):
    rows, D = tokens.shape
    frames = rows // PATCHES
    groups = PAD // 16
    vmem = pl.BlockSpec(memory_space=pltpu.VMEM)
    depth, part = qkv.shape[2:]
    tile = struct(TILE, F32)
    q0 = q1 = struct((depth, 3 * part), BF)
    o0 = o1 = struct(outs.shape[1:], BF)
    col = lambda own: struct((lines,) + own.shape, own.dtype)
    block = lambda own: struct((2, 2) + own.shape, own.dtype)
    full = lambda own: struct(full_shape(lines, *own.shape), own.dtype)
    vmem_like = lambda s: pltpu.VMEM(s.shape, s.dtype)
    return pl.pallas_call(
        functools.partial(first_kernel, lines),
        in_specs=[any_spec()] * 2 + [vmem] * 3 + [any_spec(), vmem],
        out_specs=[vmem] + [any_spec()] * 4 + [vmem] * 2,
        out_shape=[
            struct((frames, PAD, D), BF),
            struct((2 * frames, groups, 8, D), F32),
            full(tile),
            full(q0),
            full(o0),
            col(q1),
            block(o1),
        ],
        scratch_shapes=[
            vmem_like(tile),
            vmem_like(q0),
            vmem_like(q1),
            vmem_like(col(q1)),
            vmem_like(block(o1)),
            vmem_like(col(tile)),
            vmem_like(block(o0)),
            pltpu.VMEM((rows, D), BF),
            pltpu.VMEM((rows, D), BF),
            pltpu.VMEM((frames, PAD // 8, 8, D), F32),
            dma_sems(1),
            dma_sems(1),
            dma_sems(1),
            dma_sems(8),
        ]
        + LineGather.scratch(lines) * 4
        + PlaneGather.scratch() * (4 + 2 * (lines - 1)),
        name="first_gather",
        compiler_params=kernel_params(collective_id),
    )(tokens, cot, gains, biases, hidden, qkv, outs)


def spatial_forward(x, w_ref, wo_ref, vec_ref, qkv_ref, mix_ref, p_ref, r_ref):
    cols = wo_ref.shape[2]
    xhat, _ = norm_parts(x)
    normed = (xhat * vec_ref[10:11, :] + vec_ref[0:1, :]).astype(BF)
    mask = spatial_mask()
    branch = vec_ref[3:4, :]
    for g, (q, k, v) in enumerate(project(normed, w_ref, vec_ref, 0, cols)):
        qkv_ref[0, g, :, 0:cols] = q
        qkv_ref[0, g, :, cols : 2 * cols] = k
        qkv_ref[0, g, :, 2 * cols : 3 * cols] = v
        pairs = []
        for j in range(cols // 128):
            sl = slice(128 * j, 128 * (j + 1))
            pairs.append((q[:, sl], k[:, sl], v[:, sl]))
        mixes, exps, recips = heads_forward(pairs, mask)
        for j in range(cols // 128):
            pair = g * (cols // 128) + j
            p_ref[0, pair] = exps[j]
            r_ref[0, :, pair : pair + 1] = recips[j]
        mix = jnp.concatenate(mixes, axis=1).astype(BF)
        mix_ref[0, g] = mix
        branch = branch + dot(mix, wo_ref[g], NT)
    return x + branch


def spatial_fwd_kernel(lines, *refs):
    if lines is None:
        x_ref, w_ref, wo_ref, vec_ref, s_ref, qkv_ref, mix_ref, p_ref, r_ref = refs
        s = spatial_forward(x_ref[0].astype(F32), w_ref, wo_ref, vec_ref, qkv_ref, mix_ref, p_ref, r_ref)
        s_ref[0] = s.reshape(s_ref.shape[1:])
        return
    (x_ref, w_ref, wo_ref, vec_ref), (col_q1, block_o1, own2, own3), (s_b, qkv_ref, mix_ref, p_ref, r_ref), (
        full_q1, full_o1), results, landed, (slots, ex_send, ex_recv, ex_local), *parts = take(
        refs, 4, 4, 5, 2, 4, 4, 4, 3, 3, 3, 3, 3, 3)
    col_q2, col_q3, block_o2, block_o3 = landed
    place = Place(lines)
    t = place.t
    i = pl.program_id(0)
    frames = pl.num_programs(0)
    groups = PAD // 16
    hops = lines - 1
    wide = col_q2.shape[2]
    q2, q3 = [own.at[:, pl.ds(0, wide)] for own in (own2, own3)]
    o2, o3 = [own.at[:, pl.ds(wide, own.shape[1] - wide)] for own in (own2, own3)]
    q1 = PlaneGather(place, col_q1, lambda v, u: full_q1.at[t, :, v, u], parts[0])
    o1 = LineGather(place, block_o1, full_o1.at[t], parts[1], to_core=full_o1.at[t])
    l2 = LineGather(place, q2, col_q2, parts[2])
    l3 = LineGather(place, q3, col_q3, parts[3])
    p2 = PlaneGather(place, o2, lambda v, u: block_o2.at[v, u], parts[4], cores=False)
    p3 = PlaneGather(place, o3, lambda v, u: block_o3.at[v, u], parts[5], cores=False)

    @pl.when(i == 0)
    def _():
        place.greet()

    at_step(0, (q1, 0), (o1, 0), (l2, 0), (l3, 0), (p2, 0), (p3, 0))
    at_step(2, (p2, 1), (p3, 1))
    at_step(3, (q1, 1), (o1, 1), (l2, 1), (l3, 1))
    at_step(5, (p2, 2), (p2, 3), (p3, 2), (p3, 3))
    at_step(6, *[(job, k) for k in range(2, hops) for job in (o1, l2, l3)])
    at_step(7, (q1, 2))

    def here(f):
        return pltpu.make_async_copy(
            slots.at[f % 2, pl.ds(groups * t, groups)], s_b.at[frames * t + f], ex_local.at[f]
        )

    def there(f):
        return remote(
            slots.at[f % 2, pl.ds(groups * (1 - t), groups)], s_b.at[frames * t + f], (ex_send, ex_recv), f, place.core
        )

    def sent(f):
        here(f).wait()
        left(there(f))

    s = spatial_forward(x_ref[0].astype(F32), w_ref, wo_ref, vec_ref, qkv_ref, mix_ref, p_ref, r_ref)

    @pl.when(i >= 2)
    def _():
        sent(i - 2)

    slots[i % 2] = s.reshape(slots.shape[1:])
    here(i).start()
    there(i).start()

    @pl.when(i == frames - 1)
    def _():
        o1.stage(hops)
        l2.stage(hops)
        l3.stage(hops)
        q1.stage(3)
        o1.stage(hops + 1)
        for result, part in zip(results, landed):
            result[...] = part[...]
        sent(i - 1)
        sent(i)

        def body(f, _):
            arrived(there(f))
            return _

        lax.fori_loop(0, frames, body, 0)


def spatial_fwd(x, w, wo, vec, links=None):
    frames, _, D = x.shape
    cols = D // 2
    pairs = D // 128
    groups = PAD // 16
    in_specs = [
        pl.BlockSpec((1, PAD, D), lambda i: (i, 0, 0)),
        whole_spec(w.shape),
        whole_spec(wo.shape),
        whole_spec(vec.shape),
    ]
    out_specs = [
        pl.BlockSpec((1, PAD // 8, 8, D), lambda i: (i, 0, 0, 0)),
        pl.BlockSpec((1, 2, PAD, 3 * cols), lambda i: (i, 0, 0, 0)),
        pl.BlockSpec((1, 2, PAD, cols), lambda i: (i, 0, 0, 0)),
        pl.BlockSpec((1, pairs, 2 * PAD, PAD), lambda i: (i, 0, 0, 0)),
        pl.BlockSpec((1, 2 * PAD, 128), lambda i: (i, 0, 0)),
    ]
    out_shape = [
        struct((frames, PAD // 8, 8, D), F32),
        struct((frames, 2, PAD, 3 * cols), BF),
        struct((frames, 2, PAD, cols), BF),
        struct((frames, pairs, 2 * PAD, PAD), BF),
        struct((frames, 2 * PAD, 128), F32),
    ]
    args, scratch, lines, collective_id = [x, w, wo, vec], [], None, None
    if links is not None:
        col_q1, block_o1, own2, own3, lines, collective_id = links
        args += [col_q1, block_o1, own2, own3]
        in_specs += [whole_spec(v.shape) for v in args[4:]]
        out_specs[0] = any_spec()
        out_shape[0] = struct((2 * frames, groups, 8, D), F32)
        col, block = col_q1.shape, block_o1.shape
        out_specs += [any_spec()] * 2 + [whole_spec(col)] * 2 + [whole_spec(block)] * 2
        out_shape += [struct(full_shape(*col), BF), struct((2, lines) + block, BF)]
        out_shape += [struct(col, BF)] * 2 + [struct(block, BF)] * 2
        scratch = [pltpu.VMEM(col, BF)] * 2 + [pltpu.VMEM(block, BF)] * 2
        scratch += [pltpu.VMEM((2, PAD // 8, 8, D), F32)] + [dma_sems(frames)] * 3
        scratch += PlaneGather.scratch() + LineGather.scratch(lines) * 3 + PlaneGather.scratch() * 2
    return pl.pallas_call(
        functools.partial(spatial_fwd_kernel, lines),
        grid=(frames,),
        in_specs=in_specs,
        out_specs=out_specs,
        out_shape=out_shape,
        scratch_shapes=scratch,
        name="spatial_fwd",
        compiler_params=kernel_params(collective_id),
    )(*args)


SHARED = 4


def place_frame(i, ref, rows):
    for f in range(SHARED):
        @pl.when(i % SHARED == f)
        def _():
            ref[PATCHES * f : PATCHES * (f + 1)] = rows


def spatial_bwd_kernel(lines, *refs):
    linked = lines is not None
    ins, joins, outs, results, (gw_ref, go_ref), rest = take(
        refs, 9, 7 if linked else 0, 4, 7 if linked else 0, 2, len(refs))
    x_ref, up_ref, qkv_ref, mix_ref, p_ref, r_ref, w_ref, wo_ref, vec_ref = ins
    gx_ref, gbw_ref, gbo_ref, gv_ref = outs
    cols = wo_ref.shape[2]
    i = pl.program_id(0)
    last = pl.num_programs(0) - 1

    @pl.when(i == 0)
    def _():
        gw_ref[...] = jnp.zeros_like(gw_ref)
        go_ref[...] = jnp.zeros_like(go_ref)
        gv_ref[...] = jnp.zeros_like(gv_ref)

    if linked:
        out_a, gw1, go1, col2, col3, block2, block3 = joins
        out_ref, sum_q1, sum_o1, sum_q2, sum_q3, sum_o2, sum_o3 = results
        (col1, block1), rest = rest[:2], rest[2:]
        place = Place(lines)
        parts = take(rest, PlaneReduce.n_scratch, LineReduce.n_scratch, 4, 4, 4, 4, 4, 4)
        q1 = PlaneReduce(place, gw1, col1, parts[0])
        o1 = LineReduce(place, go1, block1.at[0], parts[1])
        l2 = LineSum(place, col2, sum_q2, parts[2])
        l3 = LineSum(place, col3, sum_q3, parts[3])
        p2 = PlaneSum(place, block2, sum_o2, parts[4])
        p3 = PlaneSum(place, block3, sum_o3, parts[5])

        @pl.when(i == 0)
        def _():
            place.greet()

        l1 = LineSum(place, col1, sum_q1, parts[6])
        p1 = PlaneSum(place, block1, sum_o1, parts[7])
        at_step(0, (q1, 0), (o1, 0), (l2, 0), (l3, 0), (p2, 0), (p3, 0))
        at_step(1, (q1, 1), (o1, 1), (l2, 1), (l3, 1))
        at_step(2, (p2, 1), (p3, 1), (o1, 2), *[(job, k) for k in range(2, lines - 1) for job in (l2, l3)])
        at_step(3, (q1, 2), (p2, 2), (p3, 2), (l2, lines - 1), (l3, lines - 1), *[(o1, k) for k in range(3, lines)])
        at_step(4, (q1, 3), (l1, 0), (o1, lines), (p1, 0))
        at_step(5, (l1, 1), (p1, 1))
        at_step(6, (p1, 2), *[(l1, k) for k in range(2, lines - 1)])
        at_step(7, (l1, lines - 1))
        place_frame(i, rest[-1], out_a[0].reshape(PAD, out_a.shape[3])[:PATCHES])

        @pl.when(i % SHARED == SHARED - 1)
        def _():
            out_ref[...] = rest[-1][...].astype(BF)

    up = up_ref[0].reshape(PAD, up_ref.shape[3])
    gx = attn_back_common(
        x_ref[0].astype(F32), up.astype(BF), up, w_ref, wo_ref, vec_ref, 0, 10,
        lambda g: mix_ref[0, g],
        lambda g, j, rs: tuple(
            qkv_ref[0, g, :, cols * t + 128 * j : cols * t + 128 * (j + 1)] for t in range(3)
        ),
        lambda pair, b: (p_ref[0, pair], r_ref[0, :, pair : pair + 1]),
        gw_ref, go_ref, gv_ref, cols, 1,
    )
    place_frame(i, gx_ref, gx[:PATCHES])

    @pl.when(i == last)
    def _():
        gbw_ref[...] = gw_ref[...].astype(BF)
        gbo_ref[...] = go_ref[...].astype(BF)


def spatial_bwd(x, up, qkv, mix, p, r, w, wo, vec, links=None):
    frames, _, D = x.shape
    cols = D // 2
    pairs = D // 128
    frame_spec = pl.BlockSpec((1, PAD // 8, 8, D), lambda i: (i, 0, 0, 0))
    in_specs = [
        pl.BlockSpec((1, PAD, D), lambda i: (i, 0, 0)),
        frame_spec,
        pl.BlockSpec((1, 2, PAD, 3 * cols), lambda i: (i, 0, 0, 0)),
        pl.BlockSpec((1, 2, PAD, cols), lambda i: (i, 0, 0, 0)),
        pl.BlockSpec((1, pairs, 2 * PAD, PAD), lambda i: (i, 0, 0, 0)),
        pl.BlockSpec((1, 2 * PAD, 128), lambda i: (i, 0, 0)),
        whole_spec(w.shape),
        whole_spec(wo.shape),
        whole_spec(vec.shape),
    ]
    live_spec = pl.BlockSpec((SHARED * PATCHES, D), lambda i: (i // SHARED, 0))
    out_specs = [live_spec, whole_spec(w.shape), whole_spec(wo.shape), whole_spec((8, D))]
    out_shape = [
        struct((frames * PATCHES, D), F32), struct(w.shape, BF), struct(wo.shape, BF), struct((8, D), F32)
    ]
    args = [x, up, qkv, mix, p, r, w, wo, vec]
    scratch, lines, collective_id = [pltpu.VMEM(w.shape, F32), pltpu.VMEM(wo.shape, F32)], None, None
    if links is not None:
        out_a, gw1, go1, col2, col3, block2, block3, lines, collective_id = links
        args += [out_a, gw1, go1, col2, col3, block2, block3]
        q_block, o_block = gw1.shape[4:], go1.shape[4:]
        in_specs += [frame_spec] + [any_spec()] * 2 + [whole_spec(v.shape) for v in args[-4:]]
        more = [
            struct(q_block, F32), struct((1,) + o_block, F32), struct(q_block, F32), struct(q_block, F32),
            struct((1,) + o_block, F32), struct((1,) + o_block, F32),
        ]
        out_specs += [live_spec] + [whole_spec(s.shape) for s in more]
        out_shape += [struct((frames * PATCHES, D), BF)] + more
        scratch += [pltpu.VMEM(col2.shape, BF), pltpu.VMEM(block2.shape, BF)]
        scratch += PlaneReduce.scratch(lines, q_block, BF) + LineReduce.scratch(lines, o_block, BF)
        scratch += LineSum.scratch(lines, q_block, BF) * 2 + PlaneSum.scratch(1, o_block, BF) * 2
        scratch += LineSum.scratch(lines, q_block, BF) + PlaneSum.scratch(1, o_block, BF)
        scratch += [pltpu.VMEM((SHARED * PATCHES, D), F32)]
    return pl.pallas_call(
        functools.partial(spatial_bwd_kernel, lines),
        grid=(frames,),
        in_specs=in_specs,
        out_specs=out_specs,
        out_shape=out_shape,
        scratch_shapes=scratch,
        name="spatial_bwd",
        compiler_params=kernel_params(collective_id),
    )(*args)


def group_rows(block, live):
    parts = []
    for b in range(block.shape[1]):
        rows = block[:, b].reshape(GROUP, block.shape[3])
        parts.append(rows if b == 0 else jnp.where(live(b), rows, 0.0))
    return jnp.concatenate(parts, axis=0)


def temporal_forward(x, w_ref, wo_ref, vec_ref, qkv_ref, mix_ref, p_ref, r_ref):
    cols = wo_ref.shape[2]
    n = x.shape[0]
    xhat, _ = norm_parts(x)
    normed = (xhat * vec_ref[11:12, :] + vec_ref[4:5, :]).astype(BF)
    mask = temporal_mask()
    branch = vec_ref[7:8, :]
    for g, (q, k, v) in enumerate(project(normed, w_ref, vec_ref, 4, cols)):
        qkv_ref[g, :, 0:cols] = q
        qkv_ref[g, :, cols : 2 * cols] = k
        qkv_ref[g, :, 2 * cols : 3 * cols] = v
        pairs = []
        for b in range(n // GROUP):
            rs = slice(GROUP * b, GROUP * (b + 1))
            for j in range(cols // 128):
                sl = slice(128 * j, 128 * (j + 1))
                pairs.append((q[rs, sl], k[rs, sl], v[rs, sl]))
        mixes, exps, recips = heads_forward(pairs, mask)
        blocks = []
        for b in range(n // GROUP):
            for j in range(cols // 128):
                pair, i = g * (cols // 128) + j, b * (cols // 128) + j
                p_ref[pair, 2 * GROUP * b : 2 * GROUP * (b + 1)] = exps[i]
                r_ref[2 * GROUP * b : 2 * GROUP * (b + 1), pair : pair + 1] = recips[i]
            blocks.append(jnp.concatenate(mixes[b * (cols // 128) : (b + 1) * (cols // 128)], axis=1))
        mix = jnp.concatenate(blocks, axis=0).astype(BF)
        mix_ref[g] = mix
        branch = branch + dot(mix, wo_ref[g], NT)
    return x + branch


def temporal_fwd_kernel(lines, groups, *refs):
    linked = lines is not None
    (x_ref, w_ref, wo_ref, vec_ref), joins, (s_ref, qkv_ref, mix_ref, p_ref, r_ref), results, *parts = take(
        refs, 4, 4 if linked else 0, 5, 4 if linked else 0, 3, 3, 3, 3)
    i = pl.program_id(0)
    if linked:
        col_q2, col_q3, block_o2, block_o3 = joins
        full_q2, full_q3, full_o2, full_o3 = results
        place = Place(lines)
        t, hops = place.t, lines - 1
        q2 = PlaneGather(place, col_q2, lambda v, u: full_q2.at[t, :, v, u], parts[0])
        q3 = PlaneGather(place, col_q3, lambda v, u: full_q3.at[t, :, v, u], parts[1])
        o2 = LineGather(place, block_o2, full_o2.at[t], parts[2], to_core=full_o2.at[t])
        o3 = LineGather(place, block_o3, full_o3.at[t], parts[3], to_core=full_o3.at[t])

        @pl.when(i == 0)
        def _():
            place.greet()

        at_step(0, (q2, 0), (o2, 0), (o3, 0))
        at_step(2, (q2, 1), (q3, 0))
        at_step(3, (o2, 1), (o3, 1))
        at_step(5, *[(job, k) for k in range(2, hops) for job in (o2, o3)])
        at_step(6, (q3, 1))
    x = group_rows(x_ref[...], lambda b: STEP_GROUPS * i + b < groups)
    s = temporal_forward(x, w_ref, wo_ref, vec_ref, qkv_ref, mix_ref, p_ref, r_ref)
    for b in range(STEP_GROUPS):
        s_ref[:, b] = s[GROUP * b : GROUP * (b + 1)].reshape(FRAMES, 8, s.shape[1])
    if linked:
        at_step(
            6, (q2, 2), (o2, hops), (o3, hops), (q2, 3), (o2, hops + 1), (o3, hops + 1), (q3, 2), (q3, 3)
        )


def temporal_specs(groups, D):
    cols = D // 2
    n = STEP_GROUPS * GROUP
    steps = -(-groups // STEP_GROUPS)
    pairs = D // 128
    stream = pl.BlockSpec((FRAMES, STEP_GROUPS, 8, D), lambda i: (0, i, 0, 0))
    specs = [
        pl.BlockSpec((2, n, 3 * cols), lambda i: (0, i, 0)),
        pl.BlockSpec((2, n, cols), lambda i: (0, i, 0)),
        pl.BlockSpec((pairs, 2 * n, GROUP), lambda i: (0, i, 0)),
        pl.BlockSpec((2 * n, 128), lambda i: (i, 0)),
    ]
    shapes = [
        struct((2, steps * n, 3 * cols), BF),
        struct((2, steps * n, cols), BF),
        struct((pairs, 2 * steps * n, GROUP), BF),
        struct((2 * steps * n, 128), F32),
    ]
    return steps, stream, specs, shapes


def temporal_fwd(x, w, wo, vec, links=None):
    groups, D = x.shape[1], x.shape[3]
    steps, stream, kept_specs, kept_shapes = temporal_specs(groups, D)
    in_specs = [stream, whole_spec(w.shape), whole_spec(wo.shape), whole_spec(vec.shape)]
    out_specs = [stream] + kept_specs
    out_shape = [struct(x.shape, F32)] + kept_shapes
    args, scratch, lines, collective_id = [x, w, wo, vec], [], None, None
    if links is not None:
        col_q2, col_q3, block_o2, block_o3, lines, collective_id = links
        args += [col_q2, col_q3, block_o2, block_o3]
        in_specs += [whole_spec(v.shape) for v in args[4:]]
        out_specs += [any_spec()] * 4
        out_shape += [struct(full_shape(*col_q2.shape), BF)] * 2 + [struct((2, lines) + block_o2.shape, BF)] * 2
        scratch = PlaneGather.scratch() * 2 + LineGather.scratch(lines) * 2
    return pl.pallas_call(
        functools.partial(temporal_fwd_kernel, lines, groups),
        grid=(steps,),
        in_specs=in_specs,
        out_specs=out_specs,
        out_shape=out_shape,
        scratch_shapes=scratch,
        name="temporal_fwd",
        compiler_params=kernel_params(collective_id),
    )(*args)


def temporal_bwd_kernel(lines, groups, *refs):
    linked = lines is not None
    ins, joins, outs, results, (gw_ref, go_ref), rest = take(
        refs, 9, 5 if linked else 0, 4, 5 if linked else 0, 2, len(refs))
    x_ref, up_ref, qkv_ref, mix_ref, p_ref, r_ref, w_ref, wo_ref, vec_ref = ins
    gx_ref, gbw_ref, gbo_ref, gv_ref = outs
    cols = wo_ref.shape[2]
    i = pl.program_id(0)
    steps = pl.num_programs(0)

    @pl.when(i == 0)
    def _():
        gw_ref[...] = jnp.zeros_like(gw_ref)
        go_ref[...] = jnp.zeros_like(go_ref)
        gv_ref[...] = jnp.zeros_like(gv_ref)

    if linked:
        out_b, gq2, gq3, go2, go3 = joins
        out_a, col2, col3, block2, block3 = results
        place = Place(lines)
        t = place.t
        frames = FRAMES // 2
        (slots, held, ex_send, ex_recv, ex_local), *parts = take(
            rest, 5, PlaneReduce.n_scratch, PlaneReduce.n_scratch, LineReduce.n_scratch, LineReduce.n_scratch)
        q2 = PlaneReduce(place, gq2, col2, parts[0])
        q3 = PlaneReduce(place, gq3, col3, parts[1])
        o2 = LineReduce(place, go2, block2.at[0], parts[2])
        o3 = LineReduce(place, go3, block3.at[0], parts[3])
        out_load = pltpu.make_async_copy(out_b.at[pl.ds(frames * t, frames)], held, ex_local.at[steps])
        out_here = pltpu.make_async_copy(held, out_a.at[:, pl.ds(groups * t, groups)], ex_local.at[steps])
        out_there = remote(
            out_b.at[pl.ds(frames * (1 - t), frames)], out_a.at[:, pl.ds(groups * t, groups)],
            (ex_send, ex_recv), steps, place.core,
        )

        @pl.when(i == 0)
        def _():
            place.greet()

        at_step(0, (q2, 0), (o2, 0), (q3, 0), (o3, 0))

        @pl.when(i == 2)
        def _():
            out_load.start()
            out_there.start()

        @pl.when(i == 3)
        def _():
            out_load.wait()
            out_here.start()

        at_step(1, (q2, 1))
        at_step(2, (o2, 1), (q3, 1), (o3, 1))
        at_step(4, (q2, 2), (o2, 2), (o3, 2))
        at_step(5, (q3, 2))
        at_step(6, (q2, 3), *[(job, k) for k in range(3, lines) for job in (o2, o3)])

    live = lambda b: STEP_GROUPS * i + b < groups
    x = group_rows(x_ref[...], live)
    up = group_rows(up_ref[...], live)
    gx = attn_back_common(
        x, up.astype(BF), up, w_ref, wo_ref, vec_ref, 4, 11,
        lambda g: mix_ref[g],
        lambda g, j, rs: tuple(
            qkv_ref[g, rs, cols * t + 128 * j : cols * t + 128 * (j + 1)] for t in range(3)
        ),
        lambda pair, b: (
            p_ref[pair, 2 * GROUP * b : 2 * GROUP * (b + 1)],
            r_ref[2 * GROUP * b : 2 * GROUP * (b + 1), pair : pair + 1],
        ),
        gw_ref, go_ref, gv_ref, cols, x.shape[0] // GROUP,
    )

    @pl.when(i == steps - 1)
    def _():
        gbw_ref[...] = gw_ref[...].astype(BF)
        gbo_ref[...] = go_ref[...].astype(BF)

    if not linked:
        for b in range(STEP_GROUPS):
            gx_ref[:, b] = gx[GROUP * b : GROUP * (b + 1)].reshape(FRAMES, 8, gx.shape[1])
        return

    tail = groups % STEP_GROUPS or STEP_GROUPS

    def target(s, count):
        return gx_ref.at[:, pl.ds(groups * t + STEP_GROUPS * s, count)]

    def here(s, count):
        part = slots.at[s % 2, pl.ds(frames * t, frames), pl.ds(0, count)]
        return pltpu.make_async_copy(part, target(s, count), ex_local.at[s])

    def there(s, count):
        part = slots.at[s % 2, pl.ds(frames * (1 - t), frames), pl.ds(0, count)]
        return remote(part, target(s, count), (ex_send, ex_recv), s, place.core)

    def sent(s, count):
        here(s, count).wait()
        left(there(s, count))

    @pl.when(i >= 2)
    def _():
        sent(i - 2, STEP_GROUPS)

    for b in range(STEP_GROUPS):
        slots[i % 2, :, b] = gx[GROUP * b : GROUP * (b + 1)].reshape(FRAMES, 8, gx.shape[1])

    @pl.when(i < steps - 1)
    def _():
        here(i, STEP_GROUPS).start()
        there(i, STEP_GROUPS).start()

    @pl.when(i == steps - 1)
    def _():
        here(i, tail).start()
        there(i, tail).start()
        o2.stage(lines)
        o3.stage(lines)
        q3.stage(3)
        out_here.wait()
        out_there.wait()
        sent(i - 1, STEP_GROUPS)
        sent(i, tail)

        def body(s, _):
            arrived(there(s, STEP_GROUPS))
            return _

        lax.fori_loop(0, steps - 1, body, 0)
        arrived(there(i, tail))


def temporal_bwd(x, up, qkv, mix, p, r, w, wo, vec, links=None):
    groups, D = x.shape[1], x.shape[3]
    steps, stream, kept_specs, _ = temporal_specs(groups, D)
    in_specs = [stream, stream] + kept_specs + [whole_spec(v.shape) for v in (w, wo, vec)]
    out_specs = [stream, whole_spec(w.shape), whole_spec(wo.shape), whole_spec((8, D))]
    out_shape = [struct(x.shape, F32), struct(w.shape, BF), struct(wo.shape, BF), struct((8, D), F32)]
    args = [x, up, qkv, mix, p, r, w, wo, vec]
    scratch, lines, collective_id = [pltpu.VMEM(w.shape, F32), pltpu.VMEM(wo.shape, F32)], None, None
    if links is not None:
        out_b, gq2, gq3, go2, go3, lines, collective_id = links
        args += [out_b, gq2, gq3, go2, go3]
        q_block, o_block = gq2.shape[4:], go2.shape[4:]
        in_specs += [any_spec()] * 5
        out_specs[0] = any_spec()
        a_shape = (FRAMES // 2, 2 * groups, 8, D)
        out_shape[0] = struct(a_shape, F32)
        more = [struct((lines,) + q_block, BF)] * 2 + [struct((1, 2, 2) + o_block, BF)] * 2
        out_specs += [any_spec()] + [whole_spec(s.shape) for s in more]
        out_shape += [struct(a_shape, F32)] + more
        scratch += [pltpu.VMEM((2, FRAMES, STEP_GROUPS, 8, D), F32), pltpu.VMEM((FRAMES // 2, groups, 8, D), F32)]
        scratch += [dma_sems(steps + 1)] * 3
        scratch += PlaneReduce.scratch(lines, q_block, BF) * 2 + LineReduce.scratch(lines, o_block, BF) * 2
    return pl.pallas_call(
        functools.partial(temporal_bwd_kernel, lines, groups),
        grid=(steps,),
        in_specs=in_specs,
        out_specs=out_specs,
        out_shape=out_shape,
        scratch_shapes=scratch,
        name="temporal_bwd",
        compiler_params=kernel_params(collective_id),
    )(*args)


LAST_CUT = 640


def last_kernel(lines, *refs):
    (gq0, go0, tiles, sum_q1, sum_o1), mlp_parts, (grad_qkv, grad_out), mlp_grads, (grad_bias, grad_gain, grad_hidden), (
        sum_q0, sum_tile, col_a, col_b, col_tile, block0), *parts = take(
        refs, 5, 4, 2, 2, 3, 6, 9, 9, 9, 9, 4, 4, 4, 4)
    for n, grad in enumerate(mlp_grads):
        first, second = mlp_parts[2 * n : 2 * n + 2]
        grad[:, : first.shape[1]] = first[...]
        grad[:, first.shape[1] :] = second[0]
    sum_o0 = grad_out.at[pl.ds(0, 1)]
    grad_out[1] = sum_o1[0]
    place = Place(lines)
    place.greet()
    width = sum_q0.shape[1]
    qa = PlaneReduce(place, gq0, col_a, parts[0], pl.ds(0, LAST_CUT))
    qb = PlaneReduce(place, gq0, col_b, parts[1], pl.ds(LAST_CUT, width - LAST_CUT))
    small = PlaneReduce(place, tiles, col_tile, parts[2])
    o0 = LineReduce(place, go0, block0.at[0], parts[3])
    qa_line = LineSum(place, col_a, sum_q0.at[:, 0:LAST_CUT], parts[4])
    qb_line = LineSum(place, col_b, sum_q0.at[:, LAST_CUT:width], parts[5])
    small_line = LineSum(place, col_tile, sum_tile, parts[6])
    o0_plane = PlaneSum(place, block0, sum_o0, parts[7])
    n = lines
    o0.stage(0)
    qa.stage(0)
    qb.stage(0)
    small.stage(0)
    o0.stage(1)
    qa.stage(1)
    qb.stage(1)
    small.stage(1)
    o0.stage(2)
    qa.stage(2)
    small.stage(2)
    qb.stage(2)
    qa.stage(3)
    qa_line.stage(0)
    small.stage(3)
    small_line.stage(0)
    o0.stage(3)
    qb.stage(3)
    qb_line.stage(0)
    qa_line.stage(1)
    small_line.stage(1)
    for k in range(4, n + 1):
        o0.stage(k)
    o0_plane.stage(0)
    qb_line.stage(1)
    for k in range(2, n):
        qa_line.stage(k)
        small_line.stage(k)
        if k == 2:
            o0_plane.stage(1)
        qb_line.stage(k)
    o0_plane.stage(2)
    part = grad_qkv.shape[3]
    for n, total in enumerate((sum_q0, sum_q1)):
        for k in range(3):
            grad_qkv[n, k] = total[:, part * k : part * (k + 1)]
    grad_bias[...] = sum_tile[0:10, : grad_bias.shape[1]]
    grad_gain[...] = sum_tile[10:13, : grad_gain.shape[1]]
    grad_hidden[...] = sum_tile[16:17, : grad_hidden.shape[1]]


def last_call(gq0, go0, tiles, sum_q1, sum_o1, mlp_parts, share, lines, collective_id):
    q_block, o_block, tile = gq0.shape[4:], go0.shape[4:], tiles.shape[4:]
    rows, width = q_block
    cut_a, cut_b = (rows, LAST_CUT), (rows, width - LAST_CUT)
    whole_row = (rows, width + o_block[1])
    vmem = pl.BlockSpec(memory_space=pltpu.VMEM)
    return pl.pallas_call(
        functools.partial(last_kernel, lines),
        in_specs=[any_spec()] * 3 + [vmem] * 6,
        out_specs=[vmem] * 7,
        out_shape=[
            struct((2, 3, rows, width // 3), F32), struct((2,) + o_block, F32), struct(whole_row, F32),
            struct(whole_row, F32), struct((10, share), F32), struct((3, share), F32), struct((1, 4 * share), F32),
        ],
        scratch_shapes=[
            pltpu.VMEM(q_block, F32),
            pltpu.VMEM(tile, F32),
            pltpu.VMEM((lines,) + cut_a, BF),
            pltpu.VMEM((lines,) + cut_b, BF),
            pltpu.VMEM((lines,) + tile, F32),
            pltpu.VMEM((1, 2, 2) + o_block, BF),
        ]
        + PlaneReduce.scratch(lines, cut_a, BF)
        + PlaneReduce.scratch(lines, cut_b, BF)
        + PlaneReduce.scratch(lines, tile, F32)
        + LineReduce.scratch(lines, o_block, BF)
        + LineSum.scratch(lines, cut_a, BF)
        + LineSum.scratch(lines, cut_b, BF)
        + LineSum.scratch(lines, tile, F32)
        + PlaneSum.scratch(1, o_block, BF),
        name="last_reduce",
        compiler_params=kernel_params(collective_id),
    )(gq0, go0, tiles, sum_q1, sum_o1, *mlp_parts)


MLP_ROWS = 416
MLP_CHUNK = 1536
INV_SQRT2 = 0.7071067811865476
INV_SQRT2PI = 0.3989422804014327


def mlp_kernel(x_ref, cot_ref, wia, wib, woa, wob, vec_ref, hid_ref, out_ref, up_ref,
               gia, gib, goa, gob, gv_ref, gh_ref, wi_ref, wo_ref, ai_ref, ao_ref, dn_ref, sems):
    i = pl.program_id(0)
    last = pl.num_programs(0) - 1
    chunks = wi_ref.shape[0]
    per = chunks // 2
    wide, width = wia.shape[2], per * MLP_CHUNK

    def copies(table, out):
        found = []
        for vmem, first, second in table:
            for g in range(2):
                for c in range(per):
                    start, stop = MLP_CHUNK * c, MLP_CHUNK * (c + 1)
                    for array, low, high in ((first, 0, wide), (second, wide, width)):
                        lo, hi = max(start, low), min(stop, high)
                        if lo < hi:
                            here = vmem.at[g * per + c, :, pl.ds(lo - start, hi - lo)]
                            there = array.at[g, :, pl.ds(lo - low, hi - lo)]
                            sem = sems.at[int(out), len(found)]
                            found.append(pltpu.make_async_copy(*((here, there) if out else (there, here)), sem))
        return found

    @pl.when(i == 0)
    def _():
        loads = copies(((wi_ref, wia, wib), (wo_ref, woa, wob)), False)
        for copy in loads:
            copy.start()
        for ref in (ai_ref, ao_ref, gv_ref, gh_ref):
            ref[...] = jnp.zeros_like(ref)
        for copy in loads:
            copy.wait()

    x = x_ref[...]
    xhat, rstd = norm_parts(x)
    gain = vec_ref[12:13, :]
    normed = (xhat * gain + vec_ref[8:9, :]).astype(BF)
    up = cot_ref[...]
    ub = up.astype(BF)
    gv_ref[3:4, :] += jnp.sum(up, axis=0, keepdims=True)
    out_ref[...] = x + vec_ref[9:10, :]
    dn_ref[...] = jnp.zeros_like(dn_ref)

    def chunk(k, _):
        pre = dot(normed, wi_ref[k], NN) + hid_ref[k]
        cdf = 0.5 + 0.5 * lax.erf(pre * INV_SQRT2)
        act = (pre * cdf).astype(BF)
        out_ref[...] += dot(act, wo_ref[k], NT)
        ao_ref[k] += dot(ub, act, TN)
        dact = dot(ub, wo_ref[k], NN).astype(BF).astype(F32)
        slope = cdf + pre * (jnp.exp(pre * pre * -0.5) * INV_SQRT2PI)
        dpre = (dact * slope).astype(BF)
        gh_ref[k] += jnp.sum(dpre.astype(F32), axis=0, keepdims=True)
        ai_ref[k] += dot(normed, dpre, TN)
        dn_ref[...] += dot(dpre, wi_ref[k], NT)
        return _

    lax.fori_loop(0, chunks, chunk, 0)
    dn = dn_ref[...]
    gv_ref[0:1, :] += jnp.sum(dn, axis=0, keepdims=True)
    gv_ref[4:5, :] += jnp.sum(dn * xhat, axis=0, keepdims=True)
    up_ref[...] = up + norm_back(dn, xhat, rstd, gain)

    @pl.when(i == last)
    def _():
        def place(k, _):
            wi_ref[k] = ai_ref[k].astype(BF)
            wo_ref[k] = ao_ref[k].astype(BF)
            return _

        lax.fori_loop(0, chunks, place, 0)
        stores = copies(((wi_ref, gia, gib), (wo_ref, goa, gob)), True)
        for copy in stores:
            copy.start()
        for copy in stores:
            copy.wait()


def mlp_both(x, cot, wia, wib, woa, wob, vec, hidden):
    rows, D = x.shape
    width = hidden.shape[1]
    chunks = 2 * width // MLP_CHUNK
    row_spec = pl.BlockSpec((MLP_ROWS, D), lambda i: (i, 0))
    mats = [wia, wib, woa, wob]
    both = (chunks, D, MLP_CHUNK)
    units = (chunks, 1, MLP_CHUNK)
    outs = pl.pallas_call(
        mlp_kernel,
        grid=(rows // MLP_ROWS,),
        in_specs=[row_spec, row_spec] + [any_spec()] * 4 + [whole_spec(vec.shape), whole_spec(units)],
        out_specs=[row_spec, row_spec] + [any_spec()] * 4 + [whole_spec((8, D)), whole_spec(units)],
        out_shape=[struct((rows, D), F32)] * 2
        + [struct(m.shape, BF) for m in mats]
        + [struct((8, D), F32), struct(units, F32)],
        scratch_shapes=[pltpu.VMEM(both, BF)] * 2
        + [pltpu.VMEM(both, F32)] * 2
        + [pltpu.VMEM((MLP_ROWS, D), F32), pltpu.SemaphoreType.DMA((2, 6 * chunks))],
        name="mlp_both",
        compiler_params=kernel_params(None),
    )(x, cot, *mats, vec, hidden.reshape(units))
    return (*outs[:-1], outs[-1].reshape(hidden.shape))


def swap_to_patches(rows):
    return lax.all_to_all(rows, "tensor", split_axis=1, concat_axis=0, tiled=True)


def swap_to_frames(rows):
    return lax.all_to_all(rows, "tensor", split_axis=0, concat_axis=1, tiled=True)


def pad_frames(rows):
    D = rows.shape[1]
    return jnp.pad(rows.reshape(-1, PATCHES, D), ((0, 0), (0, PAD - PATCHES), (0, 0)))


def shards(tokens, cotangent, attn_qkv, attn_out, mlp_in, mlp_out, norm_gains, biases, hidden_bias):
    D = tokens.shape[1]
    depth = mlp_in.shape[1]
    cols = attn_qkv.shape[4]
    units = mlp_in.shape[2]
    frames = tokens.shape[0] // PATCHES
    everyone = ("dp", "tensor")
    chips = D // depth
    devices = 2 * chips
    share = D // devices
    wide = 3 * cols
    down = mlp_out[0].T

    def spread(gv_s, gv_t, gv_m, g_hidden):
        vec_grad = jnp.concatenate(
            [gv_s[0:4], gv_t[0:4], gv_m[0:1], gv_m[3:4], gv_s[4:5], gv_t[4:5], gv_m[4:5]]
        )
        return vec_grad.reshape(13, devices, share).transpose(1, 0, 2), g_hidden.reshape(devices, -1)

    flat = lambda w: w.reshape(2, D, w.shape[-1])
    rows_of = lambda v: v.reshape(-1, D)
    if depth % 16 == 0 and chips % 4 == 0:
        lines = chips // 4
        cut = lambda g: g.reshape(full_shape(lines, depth, g.shape[2]))
        x, cot, tiles, *w0, col_q1, block_o1 = first_call(
            tokens, cotangent, norm_gains[0], biases[0], hidden_bias,
            attn_qkv[0].transpose(0, 2, 1, 3), attn_out[0].transpose(0, 2, 1), lines, 1,
        )
        tiles = tiles.reshape((2, chips) + TILE)
        vec = tiles[:, :, :13, :share].transpose(2, 1, 0, 3).reshape(13, D)
        hidden = tiles[:, :, 16, : 2 * units // devices].transpose(1, 0, 2).reshape(2, units)
        w0 = [flat(w) for w in w0]
        x1, *kept_s, q1, o1, col_q2, col_q3, block_o2, block_o3 = spatial_fwd(
            x, *w0, vec, (col_q1, block_o1, mlp_in[0], down, lines, 2)
        )
        w1 = [flat(q1), flat(o1)]
        x2, *kept_t, q2, q3, o2, o3 = temporal_fwd(
            x1, *w1, vec, (col_q2, col_q3, block_o2, block_o3, lines, 3)
        )
        out_b, up2, gq2, go2, gq3, go3, gv_m, g_hidden = mlp_both(
            rows_of(x2), rows_of(cot), flat(q2), flat(o2), flat(q3), flat(o3), vec, hidden
        )
        up1, gq1, go1, gv_t, out_a, col2, col3, block2, block3 = temporal_bwd(
            x1, up2.reshape(x1.shape), *kept_t, *w1, vec,
            (out_b.reshape(x1.shape), cut(gq2), cut(gq3), cut(go2), cut(go3), lines, 4),
        )
        up0, gq0, go0, gv_s, output, gq1, go1, gq2, gq3, go2, go3 = spatial_bwd(
            x, up1, *kept_s, *w0, vec, (out_a, cut(gq1), cut(go1), col2, col3, block2, block3, lines, 5)
        )
        vec_grad, hidden_grad = spread(gv_s, gv_t, gv_m, g_hidden)
        place = lambda v, rows: jnp.pad(v, ((0, 0), (0, rows - v.shape[1]), (0, TILE[1] - v.shape[2])))
        tiles = jnp.concatenate([place(vec_grad, 16), place(hidden_grad[:, None], 8)], axis=1)
        tiles = tiles.reshape((chips, 2) + TILE).swapaxes(0, 1).reshape(full_shape(lines, *TILE))
        grad_qkv, grad_out, grad_in, grad_down, grad_biases, grad_gains, grad_hidden = last_call(
            cut(gq0), cut(go0), tiles, gq1, go1, (gq2, go2, gq3, go3), share, lines, 6
        )
        grad_qkv = grad_qkv.transpose(0, 2, 1, 3)
        grad_out = grad_out.transpose(0, 2, 1)
        grad_down = grad_down.T
    else:
        owns = []
        for s in range(2):
            owns += [attn_qkv[0, s].reshape(depth, wide), attn_out[0, s].T]
        owns += [mlp_in[0, :, :wide], mlp_in[0, :, wide:], down[:, :wide], down[:, wide:]]
        small = jnp.concatenate(
            [biases[0].reshape(-1), norm_gains[0].reshape(-1), hidden_bias[0].reshape(-1)]
        )
        small = lax.all_gather(small.reshape(1, -1), everyone, axis=0, tiled=True)
        vec = small[:, : 13 * share].reshape(devices, 13, share).transpose(1, 0, 2).reshape(13, D)
        hidden = small[:, 13 * share :].reshape(2, units)
        weights = [flat(lax.all_gather(w, ("tensor", "dp"), axis=0, tiled=True).reshape(2, D, -1)) for w in owns]
        x = pad_frames(tokens)
        fold = lambda v: v.reshape(frames, PAD // 8, 8, D)
        x1, *kept_s = spatial_fwd(x, *weights[0:2], vec)
        x1 = swap_to_patches(x1)
        x2, *kept_t = temporal_fwd(x1, *weights[2:4], vec)
        cot = swap_to_patches(fold(pad_frames(cotangent).astype(F32)))
        out_b, up2, *mlp_grads, gv_m, g_hidden = mlp_both(
            rows_of(x2), rows_of(cot), *weights[4:], vec, hidden
        )
        output = swap_to_frames(out_b.reshape(x1.shape)).reshape(frames, PAD, D)[:, :PATCHES].astype(BF)
        output = rows_of(output)
        up1, *grads1, gv_t = temporal_bwd(x1, up2.reshape(x1.shape), *kept_t, *weights[2:4], vec)
        up0, *grads0, gv_s = spatial_bwd(x, swap_to_frames(up1), *kept_s, *weights[0:2], vec)
        gq0, go0, gq1, go1, gq2, go2, gq3, go3 = [
            lax.psum_scatter(
                g.reshape(2 * D, g.shape[2]), ("tensor", "dp"), scatter_dimension=0, tiled=True
            ).astype(F32)
            for g in grads0 + grads1 + mlp_grads
        ]
        vec_grad, hidden_grad = spread(gv_s, gv_t, gv_m, g_hidden)
        small_grad = jnp.concatenate([vec_grad.reshape(devices, 13 * share), hidden_grad], axis=1)
        small_grad = lax.psum_scatter(small_grad, everyone, scatter_dimension=0, tiled=True)[0]
        grad_qkv = jnp.stack([gq0.reshape(depth, 3, cols), gq1.reshape(depth, 3, cols)])
        grad_out = jnp.stack([go0.T, go1.T])
        grad_in = jnp.concatenate([gq2, go2], axis=1)
        grad_down = jnp.concatenate([gq3, go3], axis=1).T
        grad_biases = small_grad[: 10 * share].reshape(10, share)
        grad_gains = small_grad[10 * share : 13 * share].reshape(3, share)
        grad_hidden = small_grad[13 * share :].reshape(1, -1)
    return (
        output,
        up0,
        grad_qkv[None],
        grad_out[None],
        grad_in[None],
        grad_down[None],
        grad_gains[None],
        grad_biases[None],
        grad_hidden,
    )


def solution(mesh):
    placed = (
        P(("dp", "tensor"), None),
        P(("dp", "tensor"), None),
        P(None, None, "dp", None, "tensor"),
        P(None, None, "tensor", "dp"),
        P(None, "dp", "tensor"),
        P(None, "tensor", "dp"),
        P(None, None, ("dp", "tensor")),
        P(None, None, ("dp", "tensor")),
        P(None, ("dp", "tensor")),
    )
    return jax.shard_map(
        shards, mesh=mesh, in_specs=placed, out_specs=placed, check_vma=False
    )
```

```python
import functools
import jax
import jax.numpy as jnp
from jax import lax
from jax.experimental import pallas as pl
from jax.experimental.pallas import tpu as pltpu
from jax.sharding import PartitionSpec as P

HEAD = 64
FRAMES = 16
PATCHES = 196
PAD = 208
EPSILON = 1e-06
BF = jnp.bfloat16
F32 = jnp.float32
NN = (((1,), (0,)), ((), ()))
NT = (((1,), (1,)), ((), ()))
TN = (((0,), (0,)), ((), ()))
VMEM_BYTES = 60 * 1024 * 1024


def dot(a, b, dims):
    return lax.dot_general(a, b, dims, preferred_element_type=F32)


def norm_parts(x):
    mean = jnp.mean(x, axis=-1, keepdims=True)
    centred = x - mean
    var = jnp.mean(centred * centred, axis=-1, keepdims=True)
    rstd = lax.rsqrt(var + EPSILON)
    return centred * rstd, rstd


def norm_back(grad_normed, xhat, rstd, gain):
    scaled = grad_normed * gain
    first = jnp.mean(scaled, axis=-1, keepdims=True)
    second = jnp.mean(scaled * xhat, axis=-1, keepdims=True)
    return rstd * (scaled - first - xhat * second)


def split_halves(pair):
    lane = lax.broadcasted_iota(jnp.int32, pair.shape, 1)
    zero = jnp.zeros_like(pair)
    return jnp.where(lane < HEAD, pair, zero), jnp.where(lane < HEAD, zero, pair)


def project(normed, w_ref, vec_ref, row_base, cols):
    parts = []
    for g in range(2):
        qkv = dot(normed, w_ref[g], NN)
        bq = vec_ref[row_base + 1 : row_base + 2, g * cols : (g + 1) * cols]
        bv = vec_ref[row_base + 2 : row_base + 3, g * cols : (g + 1) * cols]
        q = (qkv[:, :cols] + bq).astype(BF) * BF(0.125)
        k = qkv[:, cols : 2 * cols].astype(BF)
        v = (qkv[:, 2 * cols :] + bv).astype(BF)
        parts.append((q, k, v))
    return parts


def stack_halves(pair):
    return jnp.concatenate(split_halves(pair), axis=0)


def merge_halves(both):
    rows = both.shape[0] // 2
    lane = lax.broadcasted_iota(jnp.int32, (rows, both.shape[1]), 1)
    return jnp.where(lane < HEAD, both[:rows], both[rows:])


def heads_forward(pairs, mask):
    scores = [dot(stack_halves(q), k, NT) for q, k, _ in pairs]
    exps, recips = [], []
    for s in scores:
        s = jnp.where(mask, s, -1e30)
        e = jnp.exp(s - jnp.max(s, axis=-1, keepdims=True))
        recips.append(1.0 / jnp.sum(e, axis=-1, keepdims=True))
        exps.append(e.astype(BF))
    outs = [merge_halves(dot(e, v, NN) * r) for e, r, (_, _, v) in zip(exps, recips, pairs)]
    return outs, exps, recips


def heads_backward(pairs):
    dors, deltas = [], []
    for q, k, v, o, do, e, r in pairs:
        both = stack_halves(do.astype(F32)) * r
        deltas.append(jnp.sum(both * jnp.concatenate([o, o], axis=0).astype(F32), axis=-1, keepdims=True))
        dors.append(both.astype(BF))
    dps = [dot(dor, p[2], NT) for dor, p in zip(dors, pairs)]
    dss = [(p[5].astype(F32) * (dp - delta)).astype(BF) for dp, delta, p in zip(dps, deltas, pairs)]
    dq = [(merge_halves(dot(ds, p[1], NN)) * 0.125).astype(BF) for ds, p in zip(dss, pairs)]
    dk = [dot(ds, stack_halves(p[0]), TN).astype(BF) for ds, p in zip(dss, pairs)]
    dv = [dot(p[5], dor, TN).astype(BF) for dor, p in zip(dors, pairs)]
    return dq, dk, dv


def spatial_mask():
    return lax.broadcasted_iota(jnp.int32, (2 * PAD, PAD), 1) < PATCHES


def attn_back_common(x, ub, up, w_ref, wo_ref, vec_ref, row_base, gain_row, mix_of, qkv_of, exps_of, gw_ref, go_ref, gv_ref, cols, blocks):
    xhat, rstd = norm_parts(x)
    gain = vec_ref[gain_row : gain_row + 1, :]
    normed = (xhat * gain + vec_ref[row_base : row_base + 1, :]).astype(BF)
    dn = None
    gv_ref[3:4, :] += jnp.sum(up, axis=0, keepdims=True)
    rows = x.shape[0]
    step = rows // blocks
    for g in range(2):
        dmix = dot(ub, wo_ref[g], NN).astype(BF)
        mix = mix_of(g)
        go_ref[g] += dot(ub, mix, TN)
        parts = [[], [], []]
        for b in range(blocks):
            rs = slice(step * b, step * (b + 1))
            pairs = []
            for j in range(cols // 128):
                sl = slice(128 * j, 128 * (j + 1))
                q, k, v = qkv_of(g, j, rs)
                e, r = exps_of(g * (cols // 128) + j, b)
                pairs.append((q, k, v, mix[rs, sl], dmix[rs, sl], e, r))
            for part, got in zip(parts, heads_backward(pairs)):
                part.append(jnp.concatenate(got, axis=1))
        dq, dk, dv = [jnp.concatenate(part, axis=0) for part in parts]
        span = slice(g * cols, (g + 1) * cols)
        gv_ref[1:2, span] += jnp.sum(dq.astype(F32), axis=0, keepdims=True)
        gv_ref[2:3, span] += jnp.sum(dv.astype(F32), axis=0, keepdims=True)
        dqkv = jnp.concatenate([dq, dk, dv], axis=1)
        gw_ref[g] += dot(normed, dqkv, TN)
        term = dot(dqkv, w_ref[g], NT)
        dn = term if dn is None else dn + term
    gv_ref[0:1, :] += jnp.sum(dn, axis=0, keepdims=True)
    gv_ref[4:5, :] += jnp.sum(dn * xhat, axis=0, keepdims=True)
    return up + norm_back(dn, xhat, rstd, gain)


MESH = pl.DeviceIdType.MESH


class Place:
    def __init__(self, lines):
        self.lines = lines
        self.dp = lax.axis_index("dp")
        self.t = lax.axis_index("tensor")
        self.z = self.dp // 4
        self.y = (self.dp // 2) % 2
        self.x = self.dp % 2
        self.a = self.y * (1 - self.t) + self.x * self.t
        self.b = self.x * (1 - self.t) + self.y * self.t
        toward_y = self.dp + 2 - 4 * self.y
        toward_x = self.dp + 1 - 2 * self.x
        self.first = (toward_y * (1 - self.t) + toward_x * self.t, self.t)
        self.second = (toward_x * (1 - self.t) + toward_y * self.t, self.t)
        self.core = (self.dp, 1 - self.t)
        self.up = (self.dp + 4, self.t)
        self.down = (self.dp - 4, self.t)

    def yx(self, a, b, t):
        return a * (1 - t) + b * t, b * (1 - t) + a * t

    def greet(self):
        bar = pltpu.get_barrier_semaphore()
        for who in (self.core, self.first, self.second):
            pl.semaphore_signal(bar, inc=1, device_id=who, device_id_type=MESH)

        @pl.when(self.z > 0)
        def _():
            pl.semaphore_signal(bar, inc=1, device_id=self.down, device_id_type=MESH)

        @pl.when(self.z < self.lines - 1)
        def _():
            pl.semaphore_signal(bar, inc=1, device_id=self.up, device_id_type=MESH)

        inner = (self.z > 0).astype(jnp.int32) + (self.z < self.lines - 1).astype(jnp.int32)
        pl.semaphore_wait(bar, 3 + inner)


def remote(src, dst, sems, i, who):
    return pltpu.make_async_remote_copy(
        src_ref=src, dst_ref=dst, send_sem=sems[0].at[i], recv_sem=sems[1].at[i],
        device_id=who, device_id_type=MESH,
    )


def dma_sems(n):
    return pltpu.SemaphoreType.DMA((n,))


def begin(c):
    c.start()


def arrived(c):
    c.wait_recv()


def left(c):
    c.wait_send()


def whole(c):
    c.wait()


class LineGather:
    @staticmethod
    def scratch(lines):
        n = 2 * (lines - 1) + 1
        return [dma_sems(n), dma_sems(n), dma_sems(1)]

    n_scratch = 3

    def __init__(self, place, own, col, scratch, to_core=None, kept=False):
        self.p, self.own, self.col, self.to_core, self.kept = place, own, col, to_core, kept
        self.sems, self.local = scratch[:2], scratch[2]
        self.hops = place.lines - 1
        self.stages = self.hops + (1 if to_core is None else 2)

    def keep(self):
        return pltpu.make_async_copy(self.own, self.col.at[self.p.z], self.local.at[0])

    def _up(self, k):
        block = self.col.at[self.p.z - k]
        return remote(self.own if k == 0 else block, block, self.sems, k, self.p.up)

    def _down(self, k):
        block = self.col.at[self.p.z + k]
        return remote(self.own if k == 0 else block, block, self.sems, self.hops + k, self.p.down)

    def _sent(self, k, act):
        p = self.p

        @pl.when((p.z < self.hops) & (p.z >= k))
        def _():
            act(self._up(k))

        @pl.when((p.z > 0) & (p.z + k <= self.hops))
        def _():
            act(self._down(k))

    def _take(self, k):
        p = self.p

        @pl.when(p.z >= k + 1)
        def _():
            arrived(self._up(k))

        @pl.when(p.z + k + 1 <= self.hops)
        def _():
            arrived(self._down(k))

    def _core(self):
        return remote(self.to_core, self.to_core, self.sems, 2 * self.hops, self.p.core)

    def stage(self, k):
        if k == 0:
            if not self.kept:
                self.keep().start()
            self._sent(0, begin)
        elif k <= self.hops:
            self._take(k - 1)
            if k < self.hops:
                self._sent(k, begin)
                return
            if not self.kept:
                self.keep().wait()
            if self.to_core is not None:
                self._core().start()
            for i in range(self.hops):
                self._sent(i, left)
        else:
            self._core().wait()


class PlaneGather:
    @staticmethod
    def scratch():
        return [dma_sems(5), dma_sems(5), dma_sems(1)]

    n_scratch = 3
    stages = 4

    def __init__(self, place, block, spot, scratch, cores=True, kept=False):
        self.p, self.block, self.spot, self.cores, self.kept = place, block, spot, cores, kept
        self.sems, self.local = scratch[:2], scratch[2]

    def _keep(self):
        return pltpu.make_async_copy(self.block, self.spot(self.p.y, self.p.x), self.local.at[0])

    def _own(self, i, who):
        return remote(self.block, self.spot(self.p.y, self.p.x), self.sems, i, who)

    def _plane(self, i, who, b, act):
        p = self.p
        every = slice(None)

        @pl.when(p.t == 0)
        def _():
            part = self.spot(every, b)
            act(remote(part, part, self.sems, i, who))

        @pl.when(p.t == 1)
        def _():
            part = self.spot(b, every)
            act(remote(part, part, self.sems, i, who))

    def _pass_on(self):
        p = self.p
        part = self.spot(*p.yx(1 - p.a, p.b, p.t))
        return remote(part, part, self.sems, 3, p.core)

    def stage(self, k):
        p = self.p
        if k == 0:
            if not self.kept:
                self._keep().start()
            self._own(0, p.first).start()
            if self.cores:
                self._own(2, p.core).start()
        elif k == 1:
            if not self.kept:
                self._keep().wait()
            arrived(self._own(0, p.first))
            self._plane(1, p.second, p.b, begin)
            if self.cores:
                self._pass_on().start()
        elif k == 2:
            self._plane(1, p.second, p.b, arrived)
            if self.cores:
                self._plane(4, p.core, 1 - p.b, begin)
        else:
            if self.cores:
                self._own(2, p.core).wait()
                self._pass_on().wait()
                self._plane(4, p.core, 1 - p.b, whole)
            left(self._own(0, p.first))
            self._plane(1, p.second, p.b, left)


class When:
    def __init__(self, valid, make):
        self.valid, self.make = valid, make

    def stage(self, k):
        @pl.when(self.valid)
        def _():
            self.make().stage(k)


def add_blocks(u, v, dtype):
    if u.dtype == v.dtype == dtype:
        return u + v
    return (u.astype(F32) + v.astype(F32)).astype(dtype)


class CoreSum:
    @staticmethod
    def scratch(n, block, dtype):
        return [
            pltpu.VMEM((n, 2, 2) + block, dtype),
            pltpu.VMEM((n, 2, 2) + block, dtype),
            dma_sems(4),
            dma_sems(4),
            dma_sems(4),
        ]

    n_scratch = 5

    def __init__(self, place, g_ref, scratch, span=None):
        self.p, self.g, self.span = place, g_ref, span
        self.own, self.land, self.sems, self.local = scratch[0], scratch[1], scratch[2:4], scratch[4]

    def _part(self, t, y, x):
        if self.span is None:
            return self.g.at[t, :, y, x]
        return self.g.at[t, :, y, x, :, self.span]

    def _copies(self):
        p, copies = self.p, []
        for a in range(2):
            for b in range(2):
                y, x = p.yx(a, b, 1 - p.t)
                copies.append(
                    remote(self._part(1 - p.t, y, x), self.land.at[:, a, b], self.sems, 2 * a + b, p.core)
                )
                y, x = p.yx(a, b, p.t)
                copies.append(
                    pltpu.make_async_copy(self._part(p.t, y, x), self.own.at[:, a, b], self.local.at[2 * a + b])
                )
        return copies

    def start(self):
        for c in self._copies():
            c.start()

    def wait(self):
        for c in self._copies():
            c.wait()

    def add(self, a):
        def body(i, _):
            self.own[i, a] = add_blocks(self.own[i, a], self.land[i, a], self.own.dtype)
            return _

        lax.fori_loop(0, self.own.shape[0], body, 0)


class PlaneSum:
    @staticmethod
    def scratch(n, block, dtype):
        return [pltpu.VMEM((n, 2) + block, dtype), pltpu.VMEM((n,) + block, dtype), dma_sems(2), dma_sems(2)]

    n_scratch = 4
    stages = 3

    def __init__(self, place, own, col, scratch):
        self.p, self.own, self.col = place, own, col
        self.land1, self.land2, self.sems = scratch[0], scratch[1], scratch[2:4]
        self.n = self.land2.shape[0]

    def _first(self):
        return remote(self.own.at[:, 1 - self.p.a], self.land1, self.sems, 0, self.p.first)

    def _second(self):
        return remote(self.land1.at[:, 1 - self.p.b], self.land2, self.sems, 1, self.p.second)

    def stage(self, k):
        p = self.p
        if k == 0:
            self._first().start()
        elif k == 1:
            self._first().wait()

            def away(i, _):
                self.land1[i, 1 - p.b] = add_blocks(
                    self.own[i, p.a, 1 - p.b], self.land1[i, 1 - p.b], self.land1.dtype
                )
                return _

            lax.fori_loop(0, self.n, away, 0)
            self._second().start()
        else:
            self._second().wait()

            def body(i, _):
                total = self.own[i, p.a, p.b].astype(F32) + self.land1[i, p.b].astype(F32)
                self.col[i] = (total + self.land2[i].astype(F32)).astype(self.col.dtype)
                return _

            lax.fori_loop(0, self.n, body, 0)


class LineSum:
    @staticmethod
    def scratch(lines, block, dtype):
        return [
            pltpu.VMEM((lines,) + block, dtype),
            pltpu.VMEM((lines,) + block, dtype),
            dma_sems(2 * (lines - 1)),
            dma_sems(2 * (lines - 1)),
        ]

    n_scratch = 4

    def __init__(self, place, col, out, scratch):
        self.p, self.col, self.out = place, col, out
        self.from_down, self.from_up = scratch[:2]
        self.sems = scratch[2:4]
        self.stages = place.lines

    def _up(self, d):
        block = self.from_down.at[d]
        return remote(block, block, self.sems, d - 1, self.p.up)

    def _down(self, d):
        block = self.from_up.at[d]
        return remote(block, block, self.sems, self.p.lines - 1 + d, self.p.down)

    def stage(self, step):
        n = self.p.lines
        for z in range(n):
            up = [d for d in range(z + 1, n) if z + (n - 1 - d) == step]
            down = [d for d in range(z) if (n - 1 - z) + d == step]
            if step < n - 1 and not up and not down:
                continue
            pl.when(self.p.z == z)(functools.partial(self._at, z, up, down, step == n - 1))

    def _at(self, z, up, down, last):
        n, dtype = self.p.lines, self.from_down.dtype
        for d in up:
            if z > 0:
                arrived(self._up(d))
                self.from_down[d] = add_blocks(self.from_down[d], self.col[d], dtype)
            else:
                self.from_down[d] = self.col[d]
            self._up(d).start()
        for d in down:
            if z < n - 1:
                arrived(self._down(d))
                self.from_up[d] = add_blocks(self.from_up[d], self.col[d], dtype)
            else:
                self.from_up[d] = self.col[d]
            self._down(d).start()
        if not last:
            return
        total = self.col[z].astype(F32)
        if z > 0:
            arrived(self._up(z))
            total = total + self.from_down[z].astype(F32)
        if z < n - 1:
            arrived(self._down(z))
            total = total + self.from_up[z].astype(F32)
        self.out[...] = total.astype(self.out.dtype)
        for d in range(z + 1, n):
            left(self._up(d))
        for d in range(z):
            left(self._down(d))


class PlaneReduce:
    @staticmethod
    def scratch(n, block, dtype):
        return CoreSum.scratch(n, block, dtype) + PlaneSum.scratch(n, block, dtype)

    n_scratch = 9

    def __init__(self, place, g_ref, col, scratch, span=None):
        self.p = place
        self.cores = CoreSum(place, g_ref, scratch[:5], span)
        self.plane = PlaneSum(place, self.cores.own, col, scratch[5:])

    def stage(self, k):
        if k == 0:
            self.cores.start()
        elif k == 1:
            self.cores.wait()
            self.cores.add(1 - self.p.a)
            self.plane.stage(0)
            self.cores.add(self.p.a)
        else:
            self.plane.stage(k - 1)


class LineReduce:
    @staticmethod
    def scratch(n, block, dtype):
        return CoreSum.scratch(n, block, dtype) + LineSum.scratch(n, (2, 2) + block, dtype)

    n_scratch = 9

    def __init__(self, place, g_ref, out, scratch):
        self.cores = CoreSum(place, g_ref, scratch[:5])
        self.line = LineSum(place, self.cores.own, out, scratch[5:])

    def stage(self, k):
        if k == 0:
            self.cores.start()
            return
        if k == 1:
            self.cores.wait()
            self.cores.add(0)
            self.cores.add(1)
        self.line.stage(k - 1)


def at_step(step, *stages):
    @pl.when(pl.program_id(0) == step)
    def _():
        for job, k in stages:
            job.stage(k)


def take(refs, *counts):
    out, i = [], 0
    for c in counts:
        out.append(refs[i : i + c])
        i += c
    return out


GROUP = 8 * FRAMES
STEP_GROUPS = 2


def temporal_mask():
    a = lax.broadcasted_iota(jnp.int32, (2 * GROUP, GROUP), 0)
    b = lax.broadcasted_iota(jnp.int32, (2 * GROUP, GROUP), 1)
    return (a % 8) == (b % 8)


def any_spec():
    return pl.BlockSpec(memory_space=pl.ANY)


def whole_spec(shape):
    return pl.BlockSpec(tuple(shape), lambda i: (0,) * len(shape))


def struct(shape, dtype):
    return jax.ShapeDtypeStruct(tuple(shape), dtype)


def full_shape(lines, rows, width):
    return (2, lines, 2, 2, rows, width)


def kernel_params(collective_id):
    if collective_id is None:
        return pltpu.CompilerParams(vmem_limit_bytes=VMEM_BYTES)
    return pltpu.CompilerParams(
        vmem_limit_bytes=VMEM_BYTES, collective_id=collective_id, has_side_effects=True
    )


TILE = (24, 128)


def padded_frame(rows, f, frames):
    half = frames // 2
    start = half * PATCHES * (f // half)
    inside = PATCHES * (f % half)
    low = inside // 16 * 16
    high = -(-(inside + PATCHES) // 16) * 16
    block = rows[start + low : start + high].astype(F32)[inside - low : inside - low + PATCHES]
    return jnp.concatenate([block, jnp.zeros((PAD - PATCHES, rows.shape[1]), F32)], axis=0)


def first_kernel(lines, *refs):
    (tok, cot, gains, biases, hidden, qkv, outs), (x_out, cot_b, full_tile, full_q, full_o, *results), (
        tile, q0, q1, col_q1, block_o1, col_tile, block_o0, tok_v, cot_v, frames_v, ex_send, ex_recv, ex_local, loads), scratch = take(
        refs, 7, 7, 14, len(refs))
    place = Place(lines)
    t, z, y, x = place.t, place.z, place.y, place.x
    hops = lines - 1
    load_cot = pltpu.make_async_copy(cot, cot_v, loads.at[0])
    load_tok = pltpu.make_async_copy(tok, tok_v, loads.at[1])
    part = qkv.shape[3]
    load_qkv = [
        pltpu.make_async_copy(qkv.at[s, k], own.at[:, pl.ds(part * k, part)], loads.at[2 + 3 * s + k])
        for s, own in enumerate((q0, q1))
        for k in range(3)
    ]
    for copy in load_qkv:
        copy.start()
    load_cot.start()
    load_tok.start()
    tile[...] = jnp.zeros_like(tile)
    tile[0:10, 0 : biases.shape[1]] = biases[...]
    tile[10:13, 0 : gains.shape[1]] = gains[...]
    tile[16:17, 0 : hidden.shape[1]] = hidden[...]
    o0, o1 = outs.at[0], outs.at[1]
    place.greet()
    for copy in load_qkv:
        copy.wait()
    pool = list(scratch)

    def sems():
        three = pool[:3]
        del pool[:3]
        return three

    tile_line = LineGather(place, tile, col_tile, sems())
    q0_line = LineGather(place, q0, full_q.at[t, :, y, x], sems(), kept=True)
    o0_line = LineGather(place, block_o0, full_o.at[t], sems(), to_core=full_o.at[t])
    q1_line = LineGather(place, q1, col_q1, sems())
    tile_plane = PlaneGather(place, col_tile, lambda v, u: full_tile.at[t, :, v, u], sems())
    o0_plane = PlaneGather(place, o0, lambda v, u: block_o0.at[v, u], sems(), cores=False)
    o1_plane = PlaneGather(place, o1, lambda v, u: block_o1.at[v, u], sems(), cores=False)
    own_slab = PlaneGather(place, q0, lambda v, u: full_q.at[t, z, v, u], sems())
    slabs = {}
    for k in range(1, lines):
        for sign in (-1, 1):
            far, own_sems = z + sign * k, sems()
            slabs[k, sign] = When(
                (far >= 0) & (far <= hops),
                functools.partial(
                    PlaneGather, place, full_q.at[t, far, y, x],
                    lambda v, u, far=far: full_q.at[t, far, v, u], own_sems, kept=True,
                ),
            )

    def pair(k, stage):
        slabs[k, -1].stage(stage)
        slabs[k, 1].stage(stage)

    q0_line.stage(0)
    own_slab.stage(0)
    o0_plane.stage(0)
    tile_line.stage(0)
    D = tok.shape[1]
    frames = x_out.shape[0]
    pieces = [("cot", f) for f in range(frames)] + [("tok", f) for f in range(frames)]

    def work(count=1):
        for kind, f in [pieces.pop(0) for _ in range(min(count, len(pieces)))]:
            if f == 0:
                (load_cot if kind == "cot" else load_tok).wait()
            if kind == "cot":
                frames_v[f] = padded_frame(cot_v, f, frames).reshape(PAD // 8, 8, D)
            else:
                x_out[f] = padded_frame(tok_v, f, frames).astype(BF)

    work(5)
    own_slab.stage(1)
    q0_line.stage(1)
    pair(1, 0)
    o0_plane.stage(1)
    tile_line.stage(1)
    q1_line.stage(0)
    o1_plane.stage(0)
    groups = PAD // 16
    mine = pltpu.make_async_copy(
        frames_v.at[:, pl.ds(groups * t, groups)], cot_b.at[pl.ds(frames * t, frames)], ex_local.at[0]
    )
    theirs = remote(
        frames_v.at[:, pl.ds(groups * (1 - t), groups)], cot_b.at[pl.ds(frames * t, frames)],
        (ex_send, ex_recv), 0, place.core,
    )
    work(frames - 5)
    mine.start()
    theirs.start()
    o0_plane.stage(2)
    o0_plane.stage(3)
    o0_line.stage(0)
    pair(1, 1)
    own_slab.stage(2)
    work(2)
    for k in range(2, lines):
        q0_line.stage(k)
        pair(k, 0)
        tile_line.stage(k)
        q1_line.stage(k - 1)
        work()
        pair(k, 1)
        pair(k - 1, 2)
        work()
        o0_line.stage(k - 1)
    tile_plane.stage(0)
    o1_plane.stage(1)
    work()
    tile_plane.stage(1)
    o1_plane.stage(2)
    pair(hops, 2)
    work(frames)
    o0_line.stage(hops)
    tile_plane.stage(2)
    q1_line.stage(hops)
    o1_plane.stage(3)
    tile_plane.stage(3)
    o0_line.stage(hops + 1)
    own_slab.stage(3)
    for k in range(1, lines):
        pair(k, 3)
    for result, part in zip(results, (col_q1, block_o1)):
        result[...] = part[...]
    mine.wait()
    theirs.wait()


def first_call(tokens, cot, gains, biases, hidden, qkv, outs, lines, collective_id):
    rows, D = tokens.shape
    frames = rows // PATCHES
    groups = PAD // 16
    vmem = pl.BlockSpec(memory_space=pltpu.VMEM)
    depth, part = qkv.shape[2:]
    tile = struct(TILE, F32)
    q0 = q1 = struct((depth, 3 * part), BF)
    o0 = o1 = struct(outs.shape[1:], BF)
    col = lambda own: struct((lines,) + own.shape, own.dtype)
    block = lambda own: struct((2, 2) + own.shape, own.dtype)
    full = lambda own: struct(full_shape(lines, *own.shape), own.dtype)
    vmem_like = lambda s: pltpu.VMEM(s.shape, s.dtype)
    return pl.pallas_call(
        functools.partial(first_kernel, lines),
        in_specs=[any_spec()] * 2 + [vmem] * 3 + [any_spec(), vmem],
        out_specs=[vmem] + [any_spec()] * 4 + [vmem] * 2,
        out_shape=[
            struct((frames, PAD, D), BF),
            struct((2 * frames, groups, 8, D), F32),
            full(tile),
            full(q0),
            full(o0),
            col(q1),
            block(o1),
        ],
        scratch_shapes=[
            vmem_like(tile),
            vmem_like(q0),
            vmem_like(q1),
            vmem_like(col(q1)),
            vmem_like(block(o1)),
            vmem_like(col(tile)),
            vmem_like(block(o0)),
            pltpu.VMEM((rows, D), BF),
            pltpu.VMEM((rows, D), BF),
            pltpu.VMEM((frames, PAD // 8, 8, D), F32),
            dma_sems(1),
            dma_sems(1),
            dma_sems(1),
            dma_sems(8),
        ]
        + LineGather.scratch(lines) * 4
        + PlaneGather.scratch() * (4 + 2 * (lines - 1)),
        name="first_gather",
        compiler_params=kernel_params(collective_id),
    )(tokens, cot, gains, biases, hidden, qkv, outs)


def spatial_forward(x, w_ref, wo_ref, vec_ref, qkv_ref, mix_ref, p_ref, r_ref):
    cols = wo_ref.shape[2]
    xhat, _ = norm_parts(x)
    normed = (xhat * vec_ref[10:11, :] + vec_ref[0:1, :]).astype(BF)
    mask = spatial_mask()
    branch = vec_ref[3:4, :]
    for g, (q, k, v) in enumerate(project(normed, w_ref, vec_ref, 0, cols)):
        qkv_ref[0, g, :, 0:cols] = q
        qkv_ref[0, g, :, cols : 2 * cols] = k
        qkv_ref[0, g, :, 2 * cols : 3 * cols] = v
        pairs = []
        for j in range(cols // 128):
            sl = slice(128 * j, 128 * (j + 1))
            pairs.append((q[:, sl], k[:, sl], v[:, sl]))
        mixes, exps, recips = heads_forward(pairs, mask)
        for j in range(cols // 128):
            pair = g * (cols // 128) + j
            p_ref[0, pair] = exps[j]
            r_ref[0, :, pair : pair + 1] = recips[j]
        mix = jnp.concatenate(mixes, axis=1).astype(BF)
        mix_ref[0, g] = mix
        branch = branch + dot(mix, wo_ref[g], NT)
    return x + branch


def spatial_fwd_kernel(lines, *refs):
    if lines is None:
        x_ref, w_ref, wo_ref, vec_ref, s_ref, qkv_ref, mix_ref, p_ref, r_ref = refs
        s = spatial_forward(x_ref[0].astype(F32), w_ref, wo_ref, vec_ref, qkv_ref, mix_ref, p_ref, r_ref)
        s_ref[0] = s.reshape(s_ref.shape[1:])
        return
    (x_ref, w_ref, wo_ref, vec_ref), (col_q1, block_o1, own2, own3), (s_b, qkv_ref, mix_ref, p_ref, r_ref), (
        full_q1, full_o1), results, landed, (slots, ex_send, ex_recv, ex_local), *parts = take(
        refs, 4, 4, 5, 2, 4, 4, 4, 3, 3, 3, 3, 3, 3)
    col_q2, col_q3, block_o2, block_o3 = landed
    place = Place(lines)
    t = place.t
    i = pl.program_id(0)
    frames = pl.num_programs(0)
    groups = PAD // 16
    hops = lines - 1
    wide = col_q2.shape[2]
    q2, q3 = [own.at[:, pl.ds(0, wide)] for own in (own2, own3)]
    o2, o3 = [own.at[:, pl.ds(wide, own.shape[1] - wide)] for own in (own2, own3)]
    q1 = PlaneGather(place, col_q1, lambda v, u: full_q1.at[t, :, v, u], parts[0])
    o1 = LineGather(place, block_o1, full_o1.at[t], parts[1], to_core=full_o1.at[t])
    l2 = LineGather(place, q2, col_q2, parts[2])
    l3 = LineGather(place, q3, col_q3, parts[3])
    p2 = PlaneGather(place, o2, lambda v, u: block_o2.at[v, u], parts[4], cores=False)
    p3 = PlaneGather(place, o3, lambda v, u: block_o3.at[v, u], parts[5], cores=False)

    @pl.when(i == 0)
    def _():
        place.greet()

    at_step(0, (q1, 0), (o1, 0), (l2, 0), (l3, 0), (p2, 0), (p3, 0))
    at_step(2, (p2, 1), (p3, 1))
    at_step(3, (q1, 1), (o1, 1), (l2, 1), (l3, 1))
    at_step(5, (p2, 2), (p2, 3), (p3, 2), (p3, 3))
    at_step(6, *[(job, k) for k in range(2, hops) for job in (o1, l2, l3)])
    at_step(7, (q1, 2))

    def here(f):
        return pltpu.make_async_copy(
            slots.at[f % 2, pl.ds(groups * t, groups)], s_b.at[frames * t + f], ex_local.at[f]
        )

    def there(f):
        return remote(
            slots.at[f % 2, pl.ds(groups * (1 - t), groups)], s_b.at[frames * t + f], (ex_send, ex_recv), f, place.core
        )

    def sent(f):
        here(f).wait()
        left(there(f))

    s = spatial_forward(x_ref[0].astype(F32), w_ref, wo_ref, vec_ref, qkv_ref, mix_ref, p_ref, r_ref)

    @pl.when(i >= 2)
    def _():
        sent(i - 2)

    slots[i % 2] = s.reshape(slots.shape[1:])
    here(i).start()
    there(i).start()

    @pl.when(i == frames - 1)
    def _():
        o1.stage(hops)
        l2.stage(hops)
        l3.stage(hops)
        q1.stage(3)
        o1.stage(hops + 1)
        for result, part in zip(results, landed):
            result[...] = part[...]
        sent(i - 1)
        sent(i)

        def body(f, _):
            arrived(there(f))
            return _

        lax.fori_loop(0, frames, body, 0)


def spatial_fwd(x, w, wo, vec, links=None):
    frames, _, D = x.shape
    cols = D // 2
    pairs = D // 128
    groups = PAD // 16
    in_specs = [
        pl.BlockSpec((1, PAD, D), lambda i: (i, 0, 0)),
        whole_spec(w.shape),
        whole_spec(wo.shape),
        whole_spec(vec.shape),
    ]
    out_specs = [
        pl.BlockSpec((1, PAD // 8, 8, D), lambda i: (i, 0, 0, 0)),
        pl.BlockSpec((1, 2, PAD, 3 * cols), lambda i: (i, 0, 0, 0)),
        pl.BlockSpec((1, 2, PAD, cols), lambda i: (i, 0, 0, 0)),
        pl.BlockSpec((1, pairs, 2 * PAD, PAD), lambda i: (i, 0, 0, 0)),
        pl.BlockSpec((1, 2 * PAD, 128), lambda i: (i, 0, 0)),
    ]
    out_shape = [
        struct((frames, PAD // 8, 8, D), F32),
        struct((frames, 2, PAD, 3 * cols), BF),
        struct((frames, 2, PAD, cols), BF),
        struct((frames, pairs, 2 * PAD, PAD), BF),
        struct((frames, 2 * PAD, 128), F32),
    ]
    args, scratch, lines, collective_id = [x, w, wo, vec], [], None, None
    if links is not None:
        col_q1, block_o1, own2, own3, lines, collective_id = links
        args += [col_q1, block_o1, own2, own3]
        in_specs += [whole_spec(v.shape) for v in args[4:]]
        out_specs[0] = any_spec()
        out_shape[0] = struct((2 * frames, groups, 8, D), F32)
        col, block = col_q1.shape, block_o1.shape
        out_specs += [any_spec()] * 2 + [whole_spec(col)] * 2 + [whole_spec(block)] * 2
        out_shape += [struct(full_shape(*col), BF), struct((2, lines) + block, BF)]
        out_shape += [struct(col, BF)] * 2 + [struct(block, BF)] * 2
        scratch = [pltpu.VMEM(col, BF)] * 2 + [pltpu.VMEM(block, BF)] * 2
        scratch += [pltpu.VMEM((2, PAD // 8, 8, D), F32)] + [dma_sems(frames)] * 3
        scratch += PlaneGather.scratch() + LineGather.scratch(lines) * 3 + PlaneGather.scratch() * 2
    return pl.pallas_call(
        functools.partial(spatial_fwd_kernel, lines),
        grid=(frames,),
        in_specs=in_specs,
        out_specs=out_specs,
        out_shape=out_shape,
        scratch_shapes=scratch,
        name="spatial_fwd",
        compiler_params=kernel_params(collective_id),
    )(*args)


SHARED = 4


def place_frame(i, ref, rows):
    for f in range(SHARED):
        @pl.when(i % SHARED == f)
        def _():
            ref[PATCHES * f : PATCHES * (f + 1)] = rows


def spatial_bwd_kernel(lines, *refs):
    linked = lines is not None
    ins, joins, outs, results, (gw_ref, go_ref), rest = take(
        refs, 9, 7 if linked else 0, 4, 7 if linked else 0, 2, len(refs))
    x_ref, up_ref, qkv_ref, mix_ref, p_ref, r_ref, w_ref, wo_ref, vec_ref = ins
    gx_ref, gbw_ref, gbo_ref, gv_ref = outs
    cols = wo_ref.shape[2]
    i = pl.program_id(0)
    last = pl.num_programs(0) - 1

    @pl.when(i == 0)
    def _():
        gw_ref[...] = jnp.zeros_like(gw_ref)
        go_ref[...] = jnp.zeros_like(go_ref)
        gv_ref[...] = jnp.zeros_like(gv_ref)

    if linked:
        out_a, gw1, go1, col2, col3, block2, block3 = joins
        out_ref, sum_q1, sum_o1, sum_q2, sum_q3, sum_o2, sum_o3 = results
        (col1, block1), rest = rest[:2], rest[2:]
        place = Place(lines)
        parts = take(rest, PlaneReduce.n_scratch, LineReduce.n_scratch, 4, 4, 4, 4, 4, 4)
        q1 = PlaneReduce(place, gw1, col1, parts[0])
        o1 = LineReduce(place, go1, block1.at[0], parts[1])
        l2 = LineSum(place, col2, sum_q2, parts[2])
        l3 = LineSum(place, col3, sum_q3, parts[3])
        p2 = PlaneSum(place, block2, sum_o2, parts[4])
        p3 = PlaneSum(place, block3, sum_o3, parts[5])

        @pl.when(i == 0)
        def _():
            place.greet()

        l1 = LineSum(place, col1, sum_q1, parts[6])
        p1 = PlaneSum(place, block1, sum_o1, parts[7])
        at_step(0, (q1, 0), (o1, 0), (l2, 0), (l3, 0), (p2, 0), (p3, 0))
        at_step(1, (q1, 1), (o1, 1), (l2, 1), (l3, 1))
        at_step(2, (p2, 1), (p3, 1), (o1, 2), *[(job, k) for k in range(2, lines - 1) for job in (l2, l3)])
        at_step(3, (q1, 2), (p2, 2), (p3, 2), (l2, lines - 1), (l3, lines - 1), *[(o1, k) for k in range(3, lines)])
        at_step(4, (q1, 3), (l1, 0), (o1, lines), (p1, 0))
        at_step(5, (l1, 1), (p1, 1))
        at_step(6, (p1, 2), *[(l1, k) for k in range(2, lines - 1)])
        at_step(7, (l1, lines - 1))
        place_frame(i, rest[-1], out_a[0].reshape(PAD, out_a.shape[3])[:PATCHES])

        @pl.when(i % SHARED == SHARED - 1)
        def _():
            out_ref[...] = rest[-1][...].astype(BF)

    up = up_ref[0].reshape(PAD, up_ref.shape[3])
    gx = attn_back_common(
        x_ref[0].astype(F32), up.astype(BF), up, w_ref, wo_ref, vec_ref, 0, 10,
        lambda g: mix_ref[0, g],
        lambda g, j, rs: tuple(
            qkv_ref[0, g, :, cols * t + 128 * j : cols * t + 128 * (j + 1)] for t in range(3)
        ),
        lambda pair, b: (p_ref[0, pair], r_ref[0, :, pair : pair + 1]),
        gw_ref, go_ref, gv_ref, cols, 1,
    )
    place_frame(i, gx_ref, gx[:PATCHES])

    @pl.when(i == last)
    def _():
        gbw_ref[...] = gw_ref[...].astype(BF)
        gbo_ref[...] = go_ref[...].astype(BF)


def spatial_bwd(x, up, qkv, mix, p, r, w, wo, vec, links=None):
    frames, _, D = x.shape
    cols = D // 2
    pairs = D // 128
    frame_spec = pl.BlockSpec((1, PAD // 8, 8, D), lambda i: (i, 0, 0, 0))
    in_specs = [
        pl.BlockSpec((1, PAD, D), lambda i: (i, 0, 0)),
        frame_spec,
        pl.BlockSpec((1, 2, PAD, 3 * cols), lambda i: (i, 0, 0, 0)),
        pl.BlockSpec((1, 2, PAD, cols), lambda i: (i, 0, 0, 0)),
        pl.BlockSpec((1, pairs, 2 * PAD, PAD), lambda i: (i, 0, 0, 0)),
        pl.BlockSpec((1, 2 * PAD, 128), lambda i: (i, 0, 0)),
        whole_spec(w.shape),
        whole_spec(wo.shape),
        whole_spec(vec.shape),
    ]
    live_spec = pl.BlockSpec((SHARED * PATCHES, D), lambda i: (i // SHARED, 0))
    out_specs = [live_spec, whole_spec(w.shape), whole_spec(wo.shape), whole_spec((8, D))]
    out_shape = [
        struct((frames * PATCHES, D), F32), struct(w.shape, BF), struct(wo.shape, BF), struct((8, D), F32)
    ]
    args = [x, up, qkv, mix, p, r, w, wo, vec]
    scratch, lines, collective_id = [pltpu.VMEM(w.shape, F32), pltpu.VMEM(wo.shape, F32)], None, None
    if links is not None:
        out_a, gw1, go1, col2, col3, block2, block3, lines, collective_id = links
        args += [out_a, gw1, go1, col2, col3, block2, block3]
        q_block, o_block = gw1.shape[4:], go1.shape[4:]
        in_specs += [frame_spec] + [any_spec()] * 2 + [whole_spec(v.shape) for v in args[-4:]]
        more = [
            struct(q_block, F32), struct((1,) + o_block, F32), struct(q_block, F32), struct(q_block, F32),
            struct((1,) + o_block, F32), struct((1,) + o_block, F32),
        ]
        out_specs += [live_spec] + [whole_spec(s.shape) for s in more]
        out_shape += [struct((frames * PATCHES, D), BF)] + more
        scratch += [pltpu.VMEM(col2.shape, BF), pltpu.VMEM(block2.shape, BF)]
        scratch += PlaneReduce.scratch(lines, q_block, BF) + LineReduce.scratch(lines, o_block, BF)
        scratch += LineSum.scratch(lines, q_block, BF) * 2 + PlaneSum.scratch(1, o_block, BF) * 2
        scratch += LineSum.scratch(lines, q_block, BF) + PlaneSum.scratch(1, o_block, BF)
        scratch += [pltpu.VMEM((SHARED * PATCHES, D), F32)]
    return pl.pallas_call(
        functools.partial(spatial_bwd_kernel, lines),
        grid=(frames,),
        in_specs=in_specs,
        out_specs=out_specs,
        out_shape=out_shape,
        scratch_shapes=scratch,
        name="spatial_bwd",
        compiler_params=kernel_params(collective_id),
    )(*args)


def group_rows(block, live):
    parts = []
    for b in range(block.shape[1]):
        rows = block[:, b].reshape(GROUP, block.shape[3])
        parts.append(rows if b == 0 else jnp.where(live(b), rows, 0.0))
    return jnp.concatenate(parts, axis=0)


def temporal_forward(x, w_ref, wo_ref, vec_ref, qkv_ref, mix_ref, p_ref, r_ref):
    cols = wo_ref.shape[2]
    n = x.shape[0]
    xhat, _ = norm_parts(x)
    normed = (xhat * vec_ref[11:12, :] + vec_ref[4:5, :]).astype(BF)
    mask = temporal_mask()
    branch = vec_ref[7:8, :]
    for g, (q, k, v) in enumerate(project(normed, w_ref, vec_ref, 4, cols)):
        qkv_ref[g, :, 0:cols] = q
        qkv_ref[g, :, cols : 2 * cols] = k
        qkv_ref[g, :, 2 * cols : 3 * cols] = v
        pairs = []
        for b in range(n // GROUP):
            rs = slice(GROUP * b, GROUP * (b + 1))
            for j in range(cols // 128):
                sl = slice(128 * j, 128 * (j + 1))
                pairs.append((q[rs, sl], k[rs, sl], v[rs, sl]))
        mixes, exps, recips = heads_forward(pairs, mask)
        blocks = []
        for b in range(n // GROUP):
            for j in range(cols // 128):
                pair, i = g * (cols // 128) + j, b * (cols // 128) + j
                p_ref[pair, 2 * GROUP * b : 2 * GROUP * (b + 1)] = exps[i]
                r_ref[2 * GROUP * b : 2 * GROUP * (b + 1), pair : pair + 1] = recips[i]
            blocks.append(jnp.concatenate(mixes[b * (cols // 128) : (b + 1) * (cols // 128)], axis=1))
        mix = jnp.concatenate(blocks, axis=0).astype(BF)
        mix_ref[g] = mix
        branch = branch + dot(mix, wo_ref[g], NT)
    return x + branch


def temporal_fwd_kernel(lines, groups, *refs):
    linked = lines is not None
    (x_ref, w_ref, wo_ref, vec_ref), joins, (s_ref, qkv_ref, mix_ref, p_ref, r_ref), results, *parts = take(
        refs, 4, 4 if linked else 0, 5, 4 if linked else 0, 3, 3, 3, 3)
    i = pl.program_id(0)
    if linked:
        col_q2, col_q3, block_o2, block_o3 = joins
        full_q2, full_q3, full_o2, full_o3 = results
        place = Place(lines)
        t, hops = place.t, lines - 1
        q2 = PlaneGather(place, col_q2, lambda v, u: full_q2.at[t, :, v, u], parts[0])
        q3 = PlaneGather(place, col_q3, lambda v, u: full_q3.at[t, :, v, u], parts[1])
        o2 = LineGather(place, block_o2, full_o2.at[t], parts[2], to_core=full_o2.at[t])
        o3 = LineGather(place, block_o3, full_o3.at[t], parts[3], to_core=full_o3.at[t])

        @pl.when(i == 0)
        def _():
            place.greet()

        at_step(0, (q2, 0), (o2, 0), (o3, 0))
        at_step(2, (q2, 1), (q3, 0))
        at_step(3, (o2, 1), (o3, 1))
        at_step(5, (q3, 1), *[(job, k) for k in range(2, hops) for job in (o2, o3)])
    x = group_rows(x_ref[...], lambda b: STEP_GROUPS * i + b < groups)
    s = temporal_forward(x, w_ref, wo_ref, vec_ref, qkv_ref, mix_ref, p_ref, r_ref)
    for b in range(STEP_GROUPS):
        s_ref[:, b] = s[GROUP * b : GROUP * (b + 1)].reshape(FRAMES, 8, s.shape[1])
    if linked:
        at_step(
            6, (q2, 2), (o2, hops), (o3, hops), (q2, 3), (o2, hops + 1), (o3, hops + 1), (q3, 2), (q3, 3)
        )


def temporal_specs(groups, D):
    cols = D // 2
    n = STEP_GROUPS * GROUP
    steps = -(-groups // STEP_GROUPS)
    pairs = D // 128
    stream = pl.BlockSpec((FRAMES, STEP_GROUPS, 8, D), lambda i: (0, i, 0, 0))
    specs = [
        pl.BlockSpec((2, n, 3 * cols), lambda i: (0, i, 0)),
        pl.BlockSpec((2, n, cols), lambda i: (0, i, 0)),
        pl.BlockSpec((pairs, 2 * n, GROUP), lambda i: (0, i, 0)),
        pl.BlockSpec((2 * n, 128), lambda i: (i, 0)),
    ]
    shapes = [
        struct((2, steps * n, 3 * cols), BF),
        struct((2, steps * n, cols), BF),
        struct((pairs, 2 * steps * n, GROUP), BF),
        struct((2 * steps * n, 128), F32),
    ]
    return steps, stream, specs, shapes


def temporal_fwd(x, w, wo, vec, links=None):
    groups, D = x.shape[1], x.shape[3]
    steps, stream, kept_specs, kept_shapes = temporal_specs(groups, D)
    in_specs = [stream, whole_spec(w.shape), whole_spec(wo.shape), whole_spec(vec.shape)]
    out_specs = [stream] + kept_specs
    out_shape = [struct(x.shape, F32)] + kept_shapes
    args, scratch, lines, collective_id = [x, w, wo, vec], [], None, None
    if links is not None:
        col_q2, col_q3, block_o2, block_o3, lines, collective_id = links
        args += [col_q2, col_q3, block_o2, block_o3]
        in_specs += [whole_spec(v.shape) for v in args[4:]]
        out_specs += [any_spec()] * 4
        out_shape += [struct(full_shape(*col_q2.shape), BF)] * 2 + [struct((2, lines) + block_o2.shape, BF)] * 2
        scratch = PlaneGather.scratch() * 2 + LineGather.scratch(lines) * 2
    return pl.pallas_call(
        functools.partial(temporal_fwd_kernel, lines, groups),
        grid=(steps,),
        in_specs=in_specs,
        out_specs=out_specs,
        out_shape=out_shape,
        scratch_shapes=scratch,
        name="temporal_fwd",
        compiler_params=kernel_params(collective_id),
    )(*args)


def temporal_bwd_kernel(lines, groups, *refs):
    linked = lines is not None
    ins, joins, outs, results, (gw_ref, go_ref), rest = take(
        refs, 9, 5 if linked else 0, 4, 5 if linked else 0, 2, len(refs))
    x_ref, up_ref, qkv_ref, mix_ref, p_ref, r_ref, w_ref, wo_ref, vec_ref = ins
    gx_ref, gbw_ref, gbo_ref, gv_ref = outs
    cols = wo_ref.shape[2]
    i = pl.program_id(0)
    steps = pl.num_programs(0)

    @pl.when(i == 0)
    def _():
        gw_ref[...] = jnp.zeros_like(gw_ref)
        go_ref[...] = jnp.zeros_like(go_ref)
        gv_ref[...] = jnp.zeros_like(gv_ref)

    if linked:
        out_b, gq2, gq3, go2, go3 = joins
        out_a, col2, col3, block2, block3 = results
        place = Place(lines)
        t = place.t
        frames = FRAMES // 2
        (slots, held, ex_send, ex_recv, ex_local), *parts = take(
            rest, 5, PlaneReduce.n_scratch, PlaneReduce.n_scratch, LineReduce.n_scratch, LineReduce.n_scratch)
        q2 = PlaneReduce(place, gq2, col2, parts[0])
        q3 = PlaneReduce(place, gq3, col3, parts[1])
        o2 = LineReduce(place, go2, block2.at[0], parts[2])
        o3 = LineReduce(place, go3, block3.at[0], parts[3])
        out_load = pltpu.make_async_copy(out_b.at[pl.ds(frames * t, frames)], held, ex_local.at[steps])
        out_here = pltpu.make_async_copy(held, out_a.at[:, pl.ds(groups * t, groups)], ex_local.at[steps])
        out_there = remote(
            out_b.at[pl.ds(frames * (1 - t), frames)], out_a.at[:, pl.ds(groups * t, groups)],
            (ex_send, ex_recv), steps, place.core,
        )

        @pl.when(i == 0)
        def _():
            place.greet()

        at_step(0, (q2, 0), (o2, 0), (q3, 0), (o3, 0))

        @pl.when(i == 2)
        def _():
            out_load.start()
            out_there.start()

        @pl.when(i == 3)
        def _():
            out_load.wait()
            out_here.start()

        at_step(1, (q2, 1))
        at_step(2, (o2, 1), (q3, 1), (o3, 1))
        at_step(4, (q2, 2), (o2, 2), (o3, 2))
        at_step(5, (q3, 2))
        at_step(6, (q2, 3), *[(job, k) for k in range(3, lines) for job in (o2, o3)])

    live = lambda b: STEP_GROUPS * i + b < groups
    x = group_rows(x_ref[...], live)
    up = group_rows(up_ref[...], live)
    gx = attn_back_common(
        x, up.astype(BF), up, w_ref, wo_ref, vec_ref, 4, 11,
        lambda g: mix_ref[g],
        lambda g, j, rs: tuple(
            qkv_ref[g, rs, cols * t + 128 * j : cols * t + 128 * (j + 1)] for t in range(3)
        ),
        lambda pair, b: (
            p_ref[pair, 2 * GROUP * b : 2 * GROUP * (b + 1)],
            r_ref[2 * GROUP * b : 2 * GROUP * (b + 1), pair : pair + 1],
        ),
        gw_ref, go_ref, gv_ref, cols, x.shape[0] // GROUP,
    )

    @pl.when(i == steps - 1)
    def _():
        gbw_ref[...] = gw_ref[...].astype(BF)
        gbo_ref[...] = go_ref[...].astype(BF)

    if not linked:
        for b in range(STEP_GROUPS):
            gx_ref[:, b] = gx[GROUP * b : GROUP * (b + 1)].reshape(FRAMES, 8, gx.shape[1])
        return

    tail = groups % STEP_GROUPS or STEP_GROUPS

    def target(s, count):
        return gx_ref.at[:, pl.ds(groups * t + STEP_GROUPS * s, count)]

    def here(s, count):
        part = slots.at[s % 2, pl.ds(frames * t, frames), pl.ds(0, count)]
        return pltpu.make_async_copy(part, target(s, count), ex_local.at[s])

    def there(s, count):
        part = slots.at[s % 2, pl.ds(frames * (1 - t), frames), pl.ds(0, count)]
        return remote(part, target(s, count), (ex_send, ex_recv), s, place.core)

    def sent(s, count):
        here(s, count).wait()
        left(there(s, count))

    @pl.when(i >= 2)
    def _():
        sent(i - 2, STEP_GROUPS)

    for b in range(STEP_GROUPS):
        slots[i % 2, :, b] = gx[GROUP * b : GROUP * (b + 1)].reshape(FRAMES, 8, gx.shape[1])

    @pl.when(i < steps - 1)
    def _():
        here(i, STEP_GROUPS).start()
        there(i, STEP_GROUPS).start()

    @pl.when(i == steps - 1)
    def _():
        here(i, tail).start()
        there(i, tail).start()
        o2.stage(lines)
        o3.stage(lines)
        q3.stage(3)
        out_here.wait()
        out_there.wait()
        sent(i - 1, STEP_GROUPS)
        sent(i, tail)

        def body(s, _):
            arrived(there(s, STEP_GROUPS))
            return _

        lax.fori_loop(0, steps - 1, body, 0)
        arrived(there(i, tail))


def temporal_bwd(x, up, qkv, mix, p, r, w, wo, vec, links=None):
    groups, D = x.shape[1], x.shape[3]
    steps, stream, kept_specs, _ = temporal_specs(groups, D)
    in_specs = [stream, stream] + kept_specs + [whole_spec(v.shape) for v in (w, wo, vec)]
    out_specs = [stream, whole_spec(w.shape), whole_spec(wo.shape), whole_spec((8, D))]
    out_shape = [struct(x.shape, F32), struct(w.shape, BF), struct(wo.shape, BF), struct((8, D), F32)]
    args = [x, up, qkv, mix, p, r, w, wo, vec]
    scratch, lines, collective_id = [pltpu.VMEM(w.shape, F32), pltpu.VMEM(wo.shape, F32)], None, None
    if links is not None:
        out_b, gq2, gq3, go2, go3, lines, collective_id = links
        args += [out_b, gq2, gq3, go2, go3]
        q_block, o_block = gq2.shape[4:], go2.shape[4:]
        in_specs += [any_spec()] * 5
        out_specs[0] = any_spec()
        a_shape = (FRAMES // 2, 2 * groups, 8, D)
        out_shape[0] = struct(a_shape, F32)
        more = [struct((lines,) + q_block, BF)] * 2 + [struct((1, 2, 2) + o_block, BF)] * 2
        out_specs += [any_spec()] + [whole_spec(s.shape) for s in more]
        out_shape += [struct(a_shape, F32)] + more
        scratch += [pltpu.VMEM((2, FRAMES, STEP_GROUPS, 8, D), F32), pltpu.VMEM((FRAMES // 2, groups, 8, D), F32)]
        scratch += [dma_sems(steps + 1)] * 3
        scratch += PlaneReduce.scratch(lines, q_block, BF) * 2 + LineReduce.scratch(lines, o_block, BF) * 2
    return pl.pallas_call(
        functools.partial(temporal_bwd_kernel, lines, groups),
        grid=(steps,),
        in_specs=in_specs,
        out_specs=out_specs,
        out_shape=out_shape,
        scratch_shapes=scratch,
        name="temporal_bwd",
        compiler_params=kernel_params(collective_id),
    )(*args)


LAST_CUT = 768


def last_kernel(lines, *refs):
    (gq0, go0, tiles, sum_q1, sum_o1), mlp_parts, (grad_qkv, grad_out), mlp_grads, (grad_bias, grad_gain, grad_hidden), (
        sum_q0, sum_tile, col_a, col_b, col_tile, block0), *parts = take(
        refs, 5, 4, 2, 2, 3, 6, 9, 9, 9, 9, 4, 4, 4, 4)
    for n, grad in enumerate(mlp_grads):
        first, second = mlp_parts[2 * n : 2 * n + 2]
        grad[:, : first.shape[1]] = first[...]
        grad[:, first.shape[1] :] = second[0]
    sum_o0 = grad_out.at[pl.ds(0, 1)]
    grad_out[1] = sum_o1[0]
    place = Place(lines)
    place.greet()
    width = sum_q0.shape[1]
    qa = PlaneReduce(place, gq0, col_a, parts[0], pl.ds(0, LAST_CUT))
    qb = PlaneReduce(place, gq0, col_b, parts[1], pl.ds(LAST_CUT, width - LAST_CUT))
    small = PlaneReduce(place, tiles, col_tile, parts[2])
    o0 = LineReduce(place, go0, block0.at[0], parts[3])
    qa_line = LineSum(place, col_a, sum_q0.at[:, 0:LAST_CUT], parts[4])
    qb_line = LineSum(place, col_b, sum_q0.at[:, LAST_CUT:width], parts[5])
    small_line = LineSum(place, col_tile, sum_tile, parts[6])
    o0_plane = PlaneSum(place, block0, sum_o0, parts[7])
    n = lines
    o0.stage(0)
    qa.stage(0)
    qb.stage(0)
    small.stage(0)
    o0.stage(1)
    qa.stage(1)
    qb.stage(1)
    small.stage(1)
    o0.stage(2)
    qa.stage(2)
    small.stage(2)
    qb.stage(2)
    qa.stage(3)
    qa_line.stage(0)
    small.stage(3)
    small_line.stage(0)
    o0.stage(3)
    qb.stage(3)
    qb_line.stage(0)
    qa_line.stage(1)
    small_line.stage(1)
    for k in range(4, n + 1):
        o0.stage(k)
    o0_plane.stage(0)
    qb_line.stage(1)
    for k in range(2, n):
        qa_line.stage(k)
        small_line.stage(k)
        if k == 2:
            o0_plane.stage(1)
        qb_line.stage(k)
    o0_plane.stage(2)
    part = grad_qkv.shape[3]
    for n, total in enumerate((sum_q0, sum_q1)):
        for k in range(3):
            grad_qkv[n, k] = total[:, part * k : part * (k + 1)]
    grad_bias[...] = sum_tile[0:10, : grad_bias.shape[1]]
    grad_gain[...] = sum_tile[10:13, : grad_gain.shape[1]]
    grad_hidden[...] = sum_tile[16:17, : grad_hidden.shape[1]]


def last_call(gq0, go0, tiles, sum_q1, sum_o1, mlp_parts, share, lines, collective_id):
    q_block, o_block, tile = gq0.shape[4:], go0.shape[4:], tiles.shape[4:]
    rows, width = q_block
    cut_a, cut_b = (rows, LAST_CUT), (rows, width - LAST_CUT)
    whole_row = (rows, width + o_block[1])
    vmem = pl.BlockSpec(memory_space=pltpu.VMEM)
    return pl.pallas_call(
        functools.partial(last_kernel, lines),
        in_specs=[any_spec()] * 3 + [vmem] * 6,
        out_specs=[vmem] * 7,
        out_shape=[
            struct((2, 3, rows, width // 3), F32), struct((2,) + o_block, F32), struct(whole_row, F32),
            struct(whole_row, F32), struct((10, share), F32), struct((3, share), F32), struct((1, 4 * share), F32),
        ],
        scratch_shapes=[
            pltpu.VMEM(q_block, F32),
            pltpu.VMEM(tile, F32),
            pltpu.VMEM((lines,) + cut_a, BF),
            pltpu.VMEM((lines,) + cut_b, BF),
            pltpu.VMEM((lines,) + tile, F32),
            pltpu.VMEM((1, 2, 2) + o_block, BF),
        ]
        + PlaneReduce.scratch(lines, cut_a, BF)
        + PlaneReduce.scratch(lines, cut_b, BF)
        + PlaneReduce.scratch(lines, tile, F32)
        + LineReduce.scratch(lines, o_block, BF)
        + LineSum.scratch(lines, cut_a, BF)
        + LineSum.scratch(lines, cut_b, BF)
        + LineSum.scratch(lines, tile, F32)
        + PlaneSum.scratch(1, o_block, BF),
        name="last_reduce",
        compiler_params=kernel_params(collective_id),
    )(gq0, go0, tiles, sum_q1, sum_o1, *mlp_parts)


MLP_ROWS = 416
MLP_CHUNK = 1536
INV_SQRT2 = 0.7071067811865476
INV_SQRT2PI = 0.3989422804014327


def mlp_kernel(x_ref, cot_ref, wia, wib, woa, wob, vec_ref, hid_ref, out_ref, up_ref,
               gia, gib, goa, gob, gv_ref, gh_ref, wi_ref, wo_ref, ai_ref, ao_ref, dn_ref, sems):
    i = pl.program_id(0)
    last = pl.num_programs(0) - 1
    chunks = wi_ref.shape[0]
    per = chunks // 2
    wide, width = wia.shape[2], per * MLP_CHUNK

    def copies(table, out):
        found = []
        for vmem, first, second in table:
            for g in range(2):
                for c in range(per):
                    start, stop = MLP_CHUNK * c, MLP_CHUNK * (c + 1)
                    for array, low, high in ((first, 0, wide), (second, wide, width)):
                        lo, hi = max(start, low), min(stop, high)
                        if lo < hi:
                            here = vmem.at[g * per + c, :, pl.ds(lo - start, hi - lo)]
                            there = array.at[g, :, pl.ds(lo - low, hi - lo)]
                            sem = sems.at[int(out), len(found)]
                            found.append(pltpu.make_async_copy(*((here, there) if out else (there, here)), sem))
        return found

    @pl.when(i == 0)
    def _():
        loads = copies(((wi_ref, wia, wib), (wo_ref, woa, wob)), False)
        for copy in loads:
            copy.start()
        for ref in (ai_ref, ao_ref, gv_ref, gh_ref):
            ref[...] = jnp.zeros_like(ref)
        for copy in loads:
            copy.wait()

    x = x_ref[...]
    xhat, rstd = norm_parts(x)
    gain = vec_ref[12:13, :]
    normed = (xhat * gain + vec_ref[8:9, :]).astype(BF)
    up = cot_ref[...]
    ub = up.astype(BF)
    gv_ref[3:4, :] += jnp.sum(up, axis=0, keepdims=True)
    out_ref[...] = x + vec_ref[9:10, :]
    dn_ref[...] = jnp.zeros_like(dn_ref)

    def chunk(k, _):
        pre = dot(normed, wi_ref[k], NN) + hid_ref[k]
        cdf = 0.5 + 0.5 * lax.erf(pre * INV_SQRT2)
        act = (pre * cdf).astype(BF)
        out_ref[...] += dot(act, wo_ref[k], NT)
        ao_ref[k] += dot(ub, act, TN)
        dact = dot(ub, wo_ref[k], NN).astype(BF).astype(F32)
        slope = cdf + pre * (jnp.exp(pre * pre * -0.5) * INV_SQRT2PI)
        dpre = (dact * slope).astype(BF)
        gh_ref[k] += jnp.sum(dpre.astype(F32), axis=0, keepdims=True)
        ai_ref[k] += dot(normed, dpre, TN)
        dn_ref[...] += dot(dpre, wi_ref[k], NT)
        return _

    lax.fori_loop(0, chunks, chunk, 0)
    dn = dn_ref[...]
    gv_ref[0:1, :] += jnp.sum(dn, axis=0, keepdims=True)
    gv_ref[4:5, :] += jnp.sum(dn * xhat, axis=0, keepdims=True)
    up_ref[...] = up + norm_back(dn, xhat, rstd, gain)

    @pl.when(i == last)
    def _():
        def place(k, _):
            wi_ref[k] = ai_ref[k].astype(BF)
            wo_ref[k] = ao_ref[k].astype(BF)
            return _

        lax.fori_loop(0, chunks, place, 0)
        stores = copies(((wi_ref, gia, gib), (wo_ref, goa, gob)), True)
        for copy in stores:
            copy.start()
        for copy in stores:
            copy.wait()


def mlp_both(x, cot, wia, wib, woa, wob, vec, hidden):
    rows, D = x.shape
    width = hidden.shape[1]
    chunks = 2 * width // MLP_CHUNK
    row_spec = pl.BlockSpec((MLP_ROWS, D), lambda i: (i, 0))
    mats = [wia, wib, woa, wob]
    both = (chunks, D, MLP_CHUNK)
    units = (chunks, 1, MLP_CHUNK)
    outs = pl.pallas_call(
        mlp_kernel,
        grid=(rows // MLP_ROWS,),
        in_specs=[row_spec, row_spec] + [any_spec()] * 4 + [whole_spec(vec.shape), whole_spec(units)],
        out_specs=[row_spec, row_spec] + [any_spec()] * 4 + [whole_spec((8, D)), whole_spec(units)],
        out_shape=[struct((rows, D), F32)] * 2
        + [struct(m.shape, BF) for m in mats]
        + [struct((8, D), F32), struct(units, F32)],
        scratch_shapes=[pltpu.VMEM(both, BF)] * 2
        + [pltpu.VMEM(both, F32)] * 2
        + [pltpu.VMEM((MLP_ROWS, D), F32), pltpu.SemaphoreType.DMA((2, 6 * chunks))],
        name="mlp_both",
        compiler_params=kernel_params(None),
    )(x, cot, *mats, vec, hidden.reshape(units))
    return (*outs[:-1], outs[-1].reshape(hidden.shape))


def swap_to_patches(rows):
    return lax.all_to_all(rows, "tensor", split_axis=1, concat_axis=0, tiled=True)


def swap_to_frames(rows):
    return lax.all_to_all(rows, "tensor", split_axis=0, concat_axis=1, tiled=True)


def pad_frames(rows):
    D = rows.shape[1]
    return jnp.pad(rows.reshape(-1, PATCHES, D), ((0, 0), (0, PAD - PATCHES), (0, 0)))


def shards(tokens, cotangent, attn_qkv, attn_out, mlp_in, mlp_out, norm_gains, biases, hidden_bias):
    D = tokens.shape[1]
    depth = mlp_in.shape[1]
    cols = attn_qkv.shape[4]
    units = mlp_in.shape[2]
    frames = tokens.shape[0] // PATCHES
    everyone = ("dp", "tensor")
    chips = D // depth
    devices = 2 * chips
    share = D // devices
    wide = 3 * cols
    down = mlp_out[0].T

    def spread(gv_s, gv_t, gv_m, g_hidden):
        vec_grad = jnp.concatenate(
            [gv_s[0:4], gv_t[0:4], gv_m[0:1], gv_m[3:4], gv_s[4:5], gv_t[4:5], gv_m[4:5]]
        )
        return vec_grad.reshape(13, devices, share).transpose(1, 0, 2), g_hidden.reshape(devices, -1)

    flat = lambda w: w.reshape(2, D, w.shape[-1])
    rows_of = lambda v: v.reshape(-1, D)
    if depth % 16 == 0 and chips % 4 == 0:
        lines = chips // 4
        cut = lambda g: g.reshape(full_shape(lines, depth, g.shape[2]))
        x, cot, tiles, *w0, col_q1, block_o1 = first_call(
            tokens, cotangent, norm_gains[0], biases[0], hidden_bias,
            attn_qkv[0].transpose(0, 2, 1, 3), attn_out[0].transpose(0, 2, 1), lines, 1,
        )
        tiles = tiles.reshape((2, chips) + TILE)
        vec = tiles[:, :, :13, :share].transpose(2, 1, 0, 3).reshape(13, D)
        hidden = tiles[:, :, 16, : 2 * units // devices].transpose(1, 0, 2).reshape(2, units)
        w0 = [flat(w) for w in w0]
        x1, *kept_s, q1, o1, col_q2, col_q3, block_o2, block_o3 = spatial_fwd(
            x, *w0, vec, (col_q1, block_o1, mlp_in[0], down, lines, 2)
        )
        w1 = [flat(q1), flat(o1)]
        x2, *kept_t, q2, q3, o2, o3 = temporal_fwd(
            x1, *w1, vec, (col_q2, col_q3, block_o2, block_o3, lines, 3)
        )
        out_b, up2, gq2, go2, gq3, go3, gv_m, g_hidden = mlp_both(
            rows_of(x2), rows_of(cot), flat(q2), flat(o2), flat(q3), flat(o3), vec, hidden
        )
        up1, gq1, go1, gv_t, out_a, col2, col3, block2, block3 = temporal_bwd(
            x1, up2.reshape(x1.shape), *kept_t, *w1, vec,
            (out_b.reshape(x1.shape), cut(gq2), cut(gq3), cut(go2), cut(go3), lines, 4),
        )
        up0, gq0, go0, gv_s, output, gq1, go1, gq2, gq3, go2, go3 = spatial_bwd(
            x, up1, *kept_s, *w0, vec, (out_a, cut(gq1), cut(go1), col2, col3, block2, block3, lines, 5)
        )
        vec_grad, hidden_grad = spread(gv_s, gv_t, gv_m, g_hidden)
        place = lambda v, rows: jnp.pad(v, ((0, 0), (0, rows - v.shape[1]), (0, TILE[1] - v.shape[2])))
        tiles = jnp.concatenate([place(vec_grad, 16), place(hidden_grad[:, None], 8)], axis=1)
        tiles = tiles.reshape((chips, 2) + TILE).swapaxes(0, 1).reshape(full_shape(lines, *TILE))
        grad_qkv, grad_out, grad_in, grad_down, grad_biases, grad_gains, grad_hidden = last_call(
            cut(gq0), cut(go0), tiles, gq1, go1, (gq2, go2, gq3, go3), share, lines, 6
        )
        grad_qkv = grad_qkv.transpose(0, 2, 1, 3)
        grad_out = grad_out.transpose(0, 2, 1)
        grad_down = grad_down.T
    else:
        owns = []
        for s in range(2):
            owns += [attn_qkv[0, s].reshape(depth, wide), attn_out[0, s].T]
        owns += [mlp_in[0, :, :wide], mlp_in[0, :, wide:], down[:, :wide], down[:, wide:]]
        small = jnp.concatenate(
            [biases[0].reshape(-1), norm_gains[0].reshape(-1), hidden_bias[0].reshape(-1)]
        )
        small = lax.all_gather(small.reshape(1, -1), everyone, axis=0, tiled=True)
        vec = small[:, : 13 * share].reshape(devices, 13, share).transpose(1, 0, 2).reshape(13, D)
        hidden = small[:, 13 * share :].reshape(2, units)
        weights = [flat(lax.all_gather(w, ("tensor", "dp"), axis=0, tiled=True).reshape(2, D, -1)) for w in owns]
        x = pad_frames(tokens)
        fold = lambda v: v.reshape(frames, PAD // 8, 8, D)
        x1, *kept_s = spatial_fwd(x, *weights[0:2], vec)
        x1 = swap_to_patches(x1)
        x2, *kept_t = temporal_fwd(x1, *weights[2:4], vec)
        cot = swap_to_patches(fold(pad_frames(cotangent).astype(F32)))
        out_b, up2, *mlp_grads, gv_m, g_hidden = mlp_both(
            rows_of(x2), rows_of(cot), *weights[4:], vec, hidden
        )
        output = swap_to_frames(out_b.reshape(x1.shape)).reshape(frames, PAD, D)[:, :PATCHES].astype(BF)
        output = rows_of(output)
        up1, *grads1, gv_t = temporal_bwd(x1, up2.reshape(x1.shape), *kept_t, *weights[2:4], vec)
        up0, *grads0, gv_s = spatial_bwd(x, swap_to_frames(up1), *kept_s, *weights[0:2], vec)
        gq0, go0, gq1, go1, gq2, go2, gq3, go3 = [
            lax.psum_scatter(
                g.reshape(2 * D, g.shape[2]), ("tensor", "dp"), scatter_dimension=0, tiled=True
            ).astype(F32)
            for g in grads0 + grads1 + mlp_grads
        ]
        vec_grad, hidden_grad = spread(gv_s, gv_t, gv_m, g_hidden)
        small_grad = jnp.concatenate([vec_grad.reshape(devices, 13 * share), hidden_grad], axis=1)
        small_grad = lax.psum_scatter(small_grad, everyone, scatter_dimension=0, tiled=True)[0]
        grad_qkv = jnp.stack([gq0.reshape(depth, 3, cols), gq1.reshape(depth, 3, cols)])
        grad_out = jnp.stack([go0.T, go1.T])
        grad_in = jnp.concatenate([gq2, go2], axis=1)
        grad_down = jnp.concatenate([gq3, go3], axis=1).T
        grad_biases = small_grad[: 10 * share].reshape(10, share)
        grad_gains = small_grad[10 * share : 13 * share].reshape(3, share)
        grad_hidden = small_grad[13 * share :].reshape(1, -1)
    return (
        output,
        up0,
        grad_qkv[None],
        grad_out[None],
        grad_in[None],
        grad_down[None],
        grad_gains[None],
        grad_biases[None],
        grad_hidden,
    )


def solution(mesh):
    placed = (
        P(("dp", "tensor"), None),
        P(("dp", "tensor"), None),
        P(None, None, "dp", None, "tensor"),
        P(None, None, "tensor", "dp"),
        P(None, "dp", "tensor"),
        P(None, "tensor", "dp"),
        P(None, None, ("dp", "tensor")),
        P(None, None, ("dp", "tensor")),
        P(None, ("dp", "tensor")),
    )
    return jax.shard_map(
        shards, mesh=mesh, in_specs=placed, out_specs=placed, check_vma=False
    )
```

```python
import functools
import jax
import jax.numpy as jnp
from jax import lax
from jax.experimental import pallas as pl
from jax.experimental.pallas import tpu as pltpu
from jax.sharding import PartitionSpec as P

HEAD = 64
FRAMES = 16
PATCHES = 196
PAD = 208
EPSILON = 1e-06
BF = jnp.bfloat16
F32 = jnp.float32
NN = (((1,), (0,)), ((), ()))
NT = (((1,), (1,)), ((), ()))
TN = (((0,), (0,)), ((), ()))
VMEM_BYTES = 60 * 1024 * 1024


def dot(a, b, dims):
    return lax.dot_general(a, b, dims, preferred_element_type=F32)


def norm_parts(x):
    mean = jnp.mean(x, axis=-1, keepdims=True)
    centred = x - mean
    var = jnp.mean(centred * centred, axis=-1, keepdims=True)
    rstd = lax.rsqrt(var + EPSILON)
    return centred * rstd, rstd


def norm_back(grad_normed, xhat, rstd, gain):
    scaled = grad_normed * gain
    first = jnp.mean(scaled, axis=-1, keepdims=True)
    second = jnp.mean(scaled * xhat, axis=-1, keepdims=True)
    return rstd * (scaled - first - xhat * second)


def split_halves(pair):
    lane = lax.broadcasted_iota(jnp.int32, pair.shape, 1)
    zero = jnp.zeros_like(pair)
    return jnp.where(lane < HEAD, pair, zero), jnp.where(lane < HEAD, zero, pair)


def project(normed, w_ref, vec_ref, row_base, cols):
    parts = []
    for g in range(2):
        qkv = dot(normed, w_ref[g], NN)
        bq = vec_ref[row_base + 1 : row_base + 2, g * cols : (g + 1) * cols]
        bv = vec_ref[row_base + 2 : row_base + 3, g * cols : (g + 1) * cols]
        q = (qkv[:, :cols] + bq).astype(BF) * BF(0.125)
        k = qkv[:, cols : 2 * cols].astype(BF)
        v = (qkv[:, 2 * cols :] + bv).astype(BF)
        parts.append((q, k, v))
    return parts


def stack_halves(pair):
    return jnp.concatenate(split_halves(pair), axis=0)


def merge_halves(both):
    rows = both.shape[0] // 2
    lane = lax.broadcasted_iota(jnp.int32, (rows, both.shape[1]), 1)
    return jnp.where(lane < HEAD, both[:rows], both[rows:])


def heads_forward(pairs, mask):
    scores = [dot(stack_halves(q), k, NT) for q, k, _ in pairs]
    exps, recips = [], []
    for s in scores:
        s = jnp.where(mask, s, -1e30)
        e = jnp.exp(s - jnp.max(s, axis=-1, keepdims=True))
        recips.append(1.0 / jnp.sum(e, axis=-1, keepdims=True))
        exps.append(e.astype(BF))
    outs = [merge_halves(dot(e, v, NN) * r) for e, r, (_, _, v) in zip(exps, recips, pairs)]
    return outs, exps, recips


def heads_backward(pairs):
    dors, deltas = [], []
    for q, k, v, o, do, e, r in pairs:
        both = stack_halves(do.astype(F32)) * r
        deltas.append(jnp.sum(both * jnp.concatenate([o, o], axis=0).astype(F32), axis=-1, keepdims=True))
        dors.append(both.astype(BF))
    dps = [dot(dor, p[2], NT) for dor, p in zip(dors, pairs)]
    dss = [(p[5].astype(F32) * (dp - delta)).astype(BF) for dp, delta, p in zip(dps, deltas, pairs)]
    dq = [(merge_halves(dot(ds, p[1], NN)) * 0.125).astype(BF) for ds, p in zip(dss, pairs)]
    dk = [dot(ds, stack_halves(p[0]), TN).astype(BF) for ds, p in zip(dss, pairs)]
    dv = [dot(p[5], dor, TN).astype(BF) for dor, p in zip(dors, pairs)]
    return dq, dk, dv


def spatial_mask():
    return lax.broadcasted_iota(jnp.int32, (2 * PAD, PAD), 1) < PATCHES


def attn_back_common(x, ub, up, w_ref, wo_ref, vec_ref, row_base, gain_row, mix_of, qkv_of, exps_of, gw_ref, go_ref, gv_ref, cols, blocks):
    xhat, rstd = norm_parts(x)
    gain = vec_ref[gain_row : gain_row + 1, :]
    normed = (xhat * gain + vec_ref[row_base : row_base + 1, :]).astype(BF)
    dn = None
    gv_ref[3:4, :] += jnp.sum(up, axis=0, keepdims=True)
    rows = x.shape[0]
    step = rows // blocks
    for g in range(2):
        dmix = dot(ub, wo_ref[g], NN).astype(BF)
        mix = mix_of(g)
        go_ref[g] += dot(ub, mix, TN)
        parts = [[], [], []]
        for b in range(blocks):
            rs = slice(step * b, step * (b + 1))
            pairs = []
            for j in range(cols // 128):
                sl = slice(128 * j, 128 * (j + 1))
                q, k, v = qkv_of(g, j, rs)
                e, r = exps_of(g * (cols // 128) + j, b)
                pairs.append((q, k, v, mix[rs, sl], dmix[rs, sl], e, r))
            for part, got in zip(parts, heads_backward(pairs)):
                part.append(jnp.concatenate(got, axis=1))
        dq, dk, dv = [jnp.concatenate(part, axis=0) for part in parts]
        span = slice(g * cols, (g + 1) * cols)
        gv_ref[1:2, span] += jnp.sum(dq.astype(F32), axis=0, keepdims=True)
        gv_ref[2:3, span] += jnp.sum(dv.astype(F32), axis=0, keepdims=True)
        dqkv = jnp.concatenate([dq, dk, dv], axis=1)
        gw_ref[g] += dot(normed, dqkv, TN)
        term = dot(dqkv, w_ref[g], NT)
        dn = term if dn is None else dn + term
    gv_ref[0:1, :] += jnp.sum(dn, axis=0, keepdims=True)
    gv_ref[4:5, :] += jnp.sum(dn * xhat, axis=0, keepdims=True)
    return up + norm_back(dn, xhat, rstd, gain)


MESH = pl.DeviceIdType.MESH


class Place:
    def __init__(self, lines):
        self.lines = lines
        self.dp = lax.axis_index("dp")
        self.t = lax.axis_index("tensor")
        self.z = self.dp // 4
        self.y = (self.dp // 2) % 2
        self.x = self.dp % 2
        self.a = self.y * (1 - self.t) + self.x * self.t
        self.b = self.x * (1 - self.t) + self.y * self.t
        toward_y = self.dp + 2 - 4 * self.y
        toward_x = self.dp + 1 - 2 * self.x
        self.first = (toward_y * (1 - self.t) + toward_x * self.t, self.t)
        self.second = (toward_x * (1 - self.t) + toward_y * self.t, self.t)
        self.core = (self.dp, 1 - self.t)
        self.up = (self.dp + 4, self.t)
        self.down = (self.dp - 4, self.t)

    def yx(self, a, b, t):
        return a * (1 - t) + b * t, b * (1 - t) + a * t

    def greet(self):
        bar = pltpu.get_barrier_semaphore()
        for who in (self.core, self.first, self.second):
            pl.semaphore_signal(bar, inc=1, device_id=who, device_id_type=MESH)

        @pl.when(self.z > 0)
        def _():
            pl.semaphore_signal(bar, inc=1, device_id=self.down, device_id_type=MESH)

        @pl.when(self.z < self.lines - 1)
        def _():
            pl.semaphore_signal(bar, inc=1, device_id=self.up, device_id_type=MESH)

        inner = (self.z > 0).astype(jnp.int32) + (self.z < self.lines - 1).astype(jnp.int32)
        pl.semaphore_wait(bar, 3 + inner)


def remote(src, dst, sems, i, who):
    return pltpu.make_async_remote_copy(
        src_ref=src, dst_ref=dst, send_sem=sems[0].at[i], recv_sem=sems[1].at[i],
        device_id=who, device_id_type=MESH,
    )


def dma_sems(n):
    return pltpu.SemaphoreType.DMA((n,))


def begin(c):
    c.start()


def arrived(c):
    c.wait_recv()


def left(c):
    c.wait_send()


def whole(c):
    c.wait()


class LineGather:
    @staticmethod
    def scratch(lines):
        n = 2 * (lines - 1) + 1
        return [dma_sems(n), dma_sems(n), dma_sems(1)]

    n_scratch = 3

    def __init__(self, place, own, col, scratch, to_core=None, kept=False):
        self.p, self.own, self.col, self.to_core, self.kept = place, own, col, to_core, kept
        self.sems, self.local = scratch[:2], scratch[2]
        self.hops = place.lines - 1
        self.stages = self.hops + (1 if to_core is None else 2)

    def keep(self):
        return pltpu.make_async_copy(self.own, self.col.at[self.p.z], self.local.at[0])

    def _up(self, k):
        block = self.col.at[self.p.z - k]
        return remote(self.own if k == 0 else block, block, self.sems, k, self.p.up)

    def _down(self, k):
        block = self.col.at[self.p.z + k]
        return remote(self.own if k == 0 else block, block, self.sems, self.hops + k, self.p.down)

    def _sent(self, k, act):
        p = self.p

        @pl.when((p.z < self.hops) & (p.z >= k))
        def _():
            act(self._up(k))

        @pl.when((p.z > 0) & (p.z + k <= self.hops))
        def _():
            act(self._down(k))

    def _take(self, k):
        p = self.p

        @pl.when(p.z >= k + 1)
        def _():
            arrived(self._up(k))

        @pl.when(p.z + k + 1 <= self.hops)
        def _():
            arrived(self._down(k))

    def _core(self):
        return remote(self.to_core, self.to_core, self.sems, 2 * self.hops, self.p.core)

    def stage(self, k):
        if k == 0:
            if not self.kept:
                self.keep().start()
            self._sent(0, begin)
        elif k <= self.hops:
            self._take(k - 1)
            if k < self.hops:
                self._sent(k, begin)
                return
            if not self.kept:
                self.keep().wait()
            if self.to_core is not None:
                self._core().start()
            for i in range(self.hops):
                self._sent(i, left)
        else:
            self._core().wait()


class PlaneGather:
    @staticmethod
    def scratch():
        return [dma_sems(5), dma_sems(5), dma_sems(1)]

    n_scratch = 3
    stages = 4

    def __init__(self, place, block, spot, scratch, cores=True, kept=False):
        self.p, self.block, self.spot, self.cores, self.kept = place, block, spot, cores, kept
        self.sems, self.local = scratch[:2], scratch[2]

    def _keep(self):
        return pltpu.make_async_copy(self.block, self.spot(self.p.y, self.p.x), self.local.at[0])

    def _own(self, i, who):
        return remote(self.block, self.spot(self.p.y, self.p.x), self.sems, i, who)

    def _plane(self, i, who, b, act):
        p = self.p
        every = slice(None)

        @pl.when(p.t == 0)
        def _():
            part = self.spot(every, b)
            act(remote(part, part, self.sems, i, who))

        @pl.when(p.t == 1)
        def _():
            part = self.spot(b, every)
            act(remote(part, part, self.sems, i, who))

    def _pass_on(self):
        p = self.p
        part = self.spot(*p.yx(1 - p.a, p.b, p.t))
        return remote(part, part, self.sems, 3, p.core)

    def stage(self, k):
        p = self.p
        if k == 0:
            if not self.kept:
                self._keep().start()
            self._own(0, p.first).start()
            if self.cores:
                self._own(2, p.core).start()
        elif k == 1:
            if not self.kept:
                self._keep().wait()
            arrived(self._own(0, p.first))
            self._plane(1, p.second, p.b, begin)
            if self.cores:
                self._pass_on().start()
        elif k == 2:
            self._plane(1, p.second, p.b, arrived)
            if self.cores:
                self._plane(4, p.core, 1 - p.b, begin)
        else:
            if self.cores:
                self._own(2, p.core).wait()
                self._pass_on().wait()
                self._plane(4, p.core, 1 - p.b, whole)
            left(self._own(0, p.first))
            self._plane(1, p.second, p.b, left)


class When:
    def __init__(self, valid, make):
        self.valid, self.make = valid, make

    def stage(self, k):
        @pl.when(self.valid)
        def _():
            self.make().stage(k)


def add_blocks(u, v, dtype):
    if u.dtype == v.dtype == dtype:
        return u + v
    return (u.astype(F32) + v.astype(F32)).astype(dtype)


class CoreSum:
    @staticmethod
    def scratch(n, block, dtype):
        return [
            pltpu.VMEM((n, 2, 2) + block, dtype),
            pltpu.VMEM((n, 2, 2) + block, dtype),
            dma_sems(4),
            dma_sems(4),
            dma_sems(4),
        ]

    n_scratch = 5

    def __init__(self, place, g_ref, scratch, span=None):
        self.p, self.g, self.span = place, g_ref, span
        self.own, self.land, self.sems, self.local = scratch[0], scratch[1], scratch[2:4], scratch[4]

    def _part(self, t, y, x):
        if self.span is None:
            return self.g.at[t, :, y, x]
        return self.g.at[t, :, y, x, :, self.span]

    def _copies(self):
        p, copies = self.p, []
        for a in range(2):
            for b in range(2):
                y, x = p.yx(a, b, 1 - p.t)
                copies.append(
                    remote(self._part(1 - p.t, y, x), self.land.at[:, a, b], self.sems, 2 * a + b, p.core)
                )
                y, x = p.yx(a, b, p.t)
                copies.append(
                    pltpu.make_async_copy(self._part(p.t, y, x), self.own.at[:, a, b], self.local.at[2 * a + b])
                )
        return copies

    def start(self):
        for c in self._copies():
            c.start()

    def wait(self):
        for c in self._copies():
            c.wait()

    def add(self, a):
        def body(i, _):
            self.own[i, a] = add_blocks(self.own[i, a], self.land[i, a], self.own.dtype)
            return _

        lax.fori_loop(0, self.own.shape[0], body, 0)


class PlaneSum:
    @staticmethod
    def scratch(n, block, dtype):
        return [pltpu.VMEM((n, 2) + block, dtype), pltpu.VMEM((n,) + block, dtype), dma_sems(2), dma_sems(2)]

    n_scratch = 4
    stages = 3

    def __init__(self, place, own, col, scratch):
        self.p, self.own, self.col = place, own, col
        self.land1, self.land2, self.sems = scratch[0], scratch[1], scratch[2:4]
        self.n = self.land2.shape[0]

    def _first(self):
        return remote(self.own.at[:, 1 - self.p.a], self.land1, self.sems, 0, self.p.first)

    def _second(self):
        return remote(self.land1.at[:, 1 - self.p.b], self.land2, self.sems, 1, self.p.second)

    def stage(self, k):
        p = self.p
        if k == 0:
            self._first().start()
        elif k == 1:
            self._first().wait()

            def away(i, _):
                self.land1[i, 1 - p.b] = add_blocks(
                    self.own[i, p.a, 1 - p.b], self.land1[i, 1 - p.b], self.land1.dtype
                )
                return _

            lax.fori_loop(0, self.n, away, 0)
            self._second().start()
        else:
            self._second().wait()

            def body(i, _):
                total = self.own[i, p.a, p.b].astype(F32) + self.land1[i, p.b].astype(F32)
                self.col[i] = (total + self.land2[i].astype(F32)).astype(self.col.dtype)
                return _

            lax.fori_loop(0, self.n, body, 0)


class LineSum:
    @staticmethod
    def scratch(lines, block, dtype):
        return [
            pltpu.VMEM((lines,) + block, dtype),
            pltpu.VMEM((lines,) + block, dtype),
            dma_sems(2 * (lines - 1)),
            dma_sems(2 * (lines - 1)),
        ]

    n_scratch = 4

    def __init__(self, place, col, out, scratch):
        self.p, self.col, self.out = place, col, out
        self.from_down, self.from_up = scratch[:2]
        self.sems = scratch[2:4]
        self.stages = place.lines

    def _up(self, d):
        block = self.from_down.at[d]
        return remote(block, block, self.sems, d - 1, self.p.up)

    def _down(self, d):
        block = self.from_up.at[d]
        return remote(block, block, self.sems, self.p.lines - 1 + d, self.p.down)

    def stage(self, step):
        n = self.p.lines
        for z in range(n):
            up = [d for d in range(z + 1, n) if z + (n - 1 - d) == step]
            down = [d for d in range(z) if (n - 1 - z) + d == step]
            if step < n - 1 and not up and not down:
                continue
            pl.when(self.p.z == z)(functools.partial(self._at, z, up, down, step == n - 1))

    def _at(self, z, up, down, last):
        n, dtype = self.p.lines, self.from_down.dtype
        for d in up:
            if z > 0:
                arrived(self._up(d))
                self.from_down[d] = add_blocks(self.from_down[d], self.col[d], dtype)
            else:
                self.from_down[d] = self.col[d]
            self._up(d).start()
        for d in down:
            if z < n - 1:
                arrived(self._down(d))
                self.from_up[d] = add_blocks(self.from_up[d], self.col[d], dtype)
            else:
                self.from_up[d] = self.col[d]
            self._down(d).start()
        if not last:
            return
        total = self.col[z].astype(F32)
        if z > 0:
            arrived(self._up(z))
            total = total + self.from_down[z].astype(F32)
        if z < n - 1:
            arrived(self._down(z))
            total = total + self.from_up[z].astype(F32)
        self.out[...] = total.astype(self.out.dtype)
        for d in range(z + 1, n):
            left(self._up(d))
        for d in range(z):
            left(self._down(d))


class PlaneReduce:
    @staticmethod
    def scratch(n, block, dtype):
        return CoreSum.scratch(n, block, dtype) + PlaneSum.scratch(n, block, dtype)

    n_scratch = 9

    def __init__(self, place, g_ref, col, scratch, span=None):
        self.p = place
        self.cores = CoreSum(place, g_ref, scratch[:5], span)
        self.plane = PlaneSum(place, self.cores.own, col, scratch[5:])

    def stage(self, k):
        if k == 0:
            self.cores.start()
        elif k == 1:
            self.cores.wait()
            self.cores.add(1 - self.p.a)
            self.plane.stage(0)
            self.cores.add(self.p.a)
        else:
            self.plane.stage(k - 1)


class LineReduce:
    @staticmethod
    def scratch(n, block, dtype):
        return CoreSum.scratch(n, block, dtype) + LineSum.scratch(n, (2, 2) + block, dtype)

    n_scratch = 9

    def __init__(self, place, g_ref, out, scratch):
        self.cores = CoreSum(place, g_ref, scratch[:5])
        self.line = LineSum(place, self.cores.own, out, scratch[5:])

    def stage(self, k):
        if k == 0:
            self.cores.start()
            return
        if k == 1:
            self.cores.wait()
            self.cores.add(0)
            self.cores.add(1)
        self.line.stage(k - 1)


def at_step(step, *stages):
    @pl.when(pl.program_id(0) == step)
    def _():
        for job, k in stages:
            job.stage(k)


def take(refs, *counts):
    out, i = [], 0
    for c in counts:
        out.append(refs[i : i + c])
        i += c
    return out


GROUP = 8 * FRAMES
STEP_GROUPS = 2


def temporal_mask():
    a = lax.broadcasted_iota(jnp.int32, (2 * GROUP, GROUP), 0)
    b = lax.broadcasted_iota(jnp.int32, (2 * GROUP, GROUP), 1)
    return (a % 8) == (b % 8)


def any_spec():
    return pl.BlockSpec(memory_space=pl.ANY)


def whole_spec(shape):
    return pl.BlockSpec(tuple(shape), lambda i: (0,) * len(shape))


def struct(shape, dtype):
    return jax.ShapeDtypeStruct(tuple(shape), dtype)


def full_shape(lines, rows, width):
    return (2, lines, 2, 2, rows, width)


def kernel_params(collective_id):
    if collective_id is None:
        return pltpu.CompilerParams(vmem_limit_bytes=VMEM_BYTES)
    return pltpu.CompilerParams(
        vmem_limit_bytes=VMEM_BYTES, collective_id=collective_id, has_side_effects=True
    )


TILE = (24, 128)


def padded_frame(rows, f, frames):
    half = frames // 2
    start = half * PATCHES * (f // half)
    inside = PATCHES * (f % half)
    low = inside // 16 * 16
    high = -(-(inside + PATCHES) // 16) * 16
    block = rows[start + low : start + high].astype(F32)[inside - low : inside - low + PATCHES]
    return jnp.concatenate([block, jnp.zeros((PAD - PATCHES, rows.shape[1]), F32)], axis=0)


def first_kernel(lines, *refs):
    (tok, cot, gains, biases, hidden, qkv, outs), (x_out, cot_b, full_tile, full_q, full_o, *results), (
        tile, q0, q1, col_q1, block_o1, col_tile, block_o0, tok_v, cot_v, frames_v, ex_send, ex_recv, ex_local, loads), scratch = take(
        refs, 7, 7, 14, len(refs))
    place = Place(lines)
    t, z, y, x = place.t, place.z, place.y, place.x
    hops = lines - 1
    load_cot = pltpu.make_async_copy(cot, cot_v, loads.at[0])
    load_tok = pltpu.make_async_copy(tok, tok_v, loads.at[1])
    part = qkv.shape[3]
    load_qkv = [
        pltpu.make_async_copy(qkv.at[s, k], own.at[:, pl.ds(part * k, part)], loads.at[2 + 3 * s + k])
        for s, own in enumerate((q0, q1))
        for k in range(3)
    ]
    for copy in load_qkv:
        copy.start()
    load_cot.start()
    load_tok.start()
    tile[...] = jnp.zeros_like(tile)
    tile[0:10, 0 : biases.shape[1]] = biases[...]
    tile[10:13, 0 : gains.shape[1]] = gains[...]
    tile[16:17, 0 : hidden.shape[1]] = hidden[...]
    o0, o1 = outs.at[0], outs.at[1]
    place.greet()
    for copy in load_qkv:
        copy.wait()
    pool = list(scratch)

    def sems():
        three = pool[:3]
        del pool[:3]
        return three

    tile_line = LineGather(place, tile, col_tile, sems())
    q0_line = LineGather(place, q0, full_q.at[t, :, y, x], sems(), kept=True)
    o0_line = LineGather(place, block_o0, full_o.at[t], sems(), to_core=full_o.at[t])
    q1_line = LineGather(place, q1, col_q1, sems())
    tile_plane = PlaneGather(place, col_tile, lambda v, u: full_tile.at[t, :, v, u], sems())
    o0_plane = PlaneGather(place, o0, lambda v, u: block_o0.at[v, u], sems(), cores=False)
    o1_plane = PlaneGather(place, o1, lambda v, u: block_o1.at[v, u], sems(), cores=False)
    own_slab = PlaneGather(place, q0, lambda v, u: full_q.at[t, z, v, u], sems())
    slabs = {}
    for k in range(1, lines):
        for sign in (-1, 1):
            far, own_sems = z + sign * k, sems()
            slabs[k, sign] = When(
                (far >= 0) & (far <= hops),
                functools.partial(
                    PlaneGather, place, full_q.at[t, far, y, x],
                    lambda v, u, far=far: full_q.at[t, far, v, u], own_sems, kept=True,
                ),
            )

    def pair(k, stage):
        slabs[k, -1].stage(stage)
        slabs[k, 1].stage(stage)

    q0_line.stage(0)
    own_slab.stage(0)
    o0_plane.stage(0)
    tile_line.stage(0)
    D = tok.shape[1]
    frames = x_out.shape[0]
    pieces = [("cot", f) for f in range(frames)] + [("tok", f) for f in range(frames)]

    def work(count=1):
        for kind, f in [pieces.pop(0) for _ in range(min(count, len(pieces)))]:
            if f == 0:
                (load_cot if kind == "cot" else load_tok).wait()
            if kind == "cot":
                frames_v[f] = padded_frame(cot_v, f, frames).reshape(PAD // 8, 8, D)
            else:
                x_out[f] = padded_frame(tok_v, f, frames).astype(BF)

    work(5)
    own_slab.stage(1)
    q0_line.stage(1)
    pair(1, 0)
    o0_plane.stage(1)
    tile_line.stage(1)
    q1_line.stage(0)
    o1_plane.stage(0)
    groups = PAD // 16
    mine = pltpu.make_async_copy(
        frames_v.at[:, pl.ds(groups * t, groups)], cot_b.at[pl.ds(frames * t, frames)], ex_local.at[0]
    )
    theirs = remote(
        frames_v.at[:, pl.ds(groups * (1 - t), groups)], cot_b.at[pl.ds(frames * t, frames)],
        (ex_send, ex_recv), 0, place.core,
    )
    work(frames - 5)
    mine.start()
    theirs.start()
    o0_plane.stage(2)
    o0_plane.stage(3)
    o0_line.stage(0)
    pair(1, 1)
    own_slab.stage(2)
    work(2)
    for k in range(2, lines):
        q0_line.stage(k)
        pair(k, 0)
        tile_line.stage(k)
        q1_line.stage(k - 1)
        work()
        pair(k, 1)
        pair(k - 1, 2)
        work()
        o0_line.stage(k - 1)
    tile_plane.stage(0)
    o1_plane.stage(1)
    work()
    tile_plane.stage(1)
    o1_plane.stage(2)
    pair(hops, 2)
    work(frames)
    o0_line.stage(hops)
    tile_plane.stage(2)
    q1_line.stage(hops)
    o1_plane.stage(3)
    tile_plane.stage(3)
    o0_line.stage(hops + 1)
    own_slab.stage(3)
    for k in range(1, lines):
        pair(k, 3)
    for result, part in zip(results, (col_q1, block_o1)):
        result[...] = part[...]
    mine.wait()
    theirs.wait()


def first_call(tokens, cot, gains, biases, hidden, qkv, outs, lines, collective_id):
    rows, D = tokens.shape
    frames = rows // PATCHES
    groups = PAD // 16
    vmem = pl.BlockSpec(memory_space=pltpu.VMEM)
    depth, part = qkv.shape[2:]
    tile = struct(TILE, F32)
    q0 = q1 = struct((depth, 3 * part), BF)
    o0 = o1 = struct(outs.shape[1:], BF)
    col = lambda own: struct((lines,) + own.shape, own.dtype)
    block = lambda own: struct((2, 2) + own.shape, own.dtype)
    full = lambda own: struct(full_shape(lines, *own.shape), own.dtype)
    vmem_like = lambda s: pltpu.VMEM(s.shape, s.dtype)
    return pl.pallas_call(
        functools.partial(first_kernel, lines),
        in_specs=[any_spec()] * 2 + [vmem] * 3 + [any_spec(), vmem],
        out_specs=[vmem] + [any_spec()] * 4 + [vmem] * 2,
        out_shape=[
            struct((frames, PAD, D), BF),
            struct((2 * frames, groups, 8, D), F32),
            full(tile),
            full(q0),
            full(o0),
            col(q1),
            block(o1),
        ],
        scratch_shapes=[
            vmem_like(tile),
            vmem_like(q0),
            vmem_like(q1),
            vmem_like(col(q1)),
            vmem_like(block(o1)),
            vmem_like(col(tile)),
            vmem_like(block(o0)),
            pltpu.VMEM((rows, D), BF),
            pltpu.VMEM((rows, D), BF),
            pltpu.VMEM((frames, PAD // 8, 8, D), F32),
            dma_sems(1),
            dma_sems(1),
            dma_sems(1),
            dma_sems(8),
        ]
        + LineGather.scratch(lines) * 4
        + PlaneGather.scratch() * (4 + 2 * (lines - 1)),
        name="first_gather",
        compiler_params=kernel_params(collective_id),
    )(tokens, cot, gains, biases, hidden, qkv, outs)


def spatial_forward(x, w_ref, wo_ref, vec_ref, qkv_ref, mix_ref, p_ref, r_ref):
    cols = wo_ref.shape[2]
    xhat, _ = norm_parts(x)
    normed = (xhat * vec_ref[10:11, :] + vec_ref[0:1, :]).astype(BF)
    mask = spatial_mask()
    branch = vec_ref[3:4, :]
    for g, (q, k, v) in enumerate(project(normed, w_ref, vec_ref, 0, cols)):
        qkv_ref[0, g, :, 0:cols] = q
        qkv_ref[0, g, :, cols : 2 * cols] = k
        qkv_ref[0, g, :, 2 * cols : 3 * cols] = v
        pairs = []
        for j in range(cols // 128):
            sl = slice(128 * j, 128 * (j + 1))
            pairs.append((q[:, sl], k[:, sl], v[:, sl]))
        mixes, exps, recips = heads_forward(pairs, mask)
        for j in range(cols // 128):
            pair = g * (cols // 128) + j
            p_ref[0, pair] = exps[j]
            r_ref[0, :, pair : pair + 1] = recips[j]
        mix = jnp.concatenate(mixes, axis=1).astype(BF)
        mix_ref[0, g] = mix
        branch = branch + dot(mix, wo_ref[g], NT)
    return x + branch


def spatial_fwd_kernel(lines, *refs):
    if lines is None:
        x_ref, w_ref, wo_ref, vec_ref, s_ref, qkv_ref, mix_ref, p_ref, r_ref = refs
        s = spatial_forward(x_ref[0].astype(F32), w_ref, wo_ref, vec_ref, qkv_ref, mix_ref, p_ref, r_ref)
        s_ref[0] = s.reshape(s_ref.shape[1:])
        return
    (x_ref, w_ref, wo_ref, vec_ref), (col_q1, block_o1, own2, own3), (s_b, qkv_ref, mix_ref, p_ref, r_ref), (
        full_q1, full_o1), results, landed, (slots, ex_send, ex_recv, ex_local), *parts = take(
        refs, 4, 4, 5, 2, 4, 4, 4, 3, 3, 3, 3, 3, 3)
    col_q2, col_q3, block_o2, block_o3 = landed
    place = Place(lines)
    t = place.t
    i = pl.program_id(0)
    frames = pl.num_programs(0)
    groups = PAD // 16
    hops = lines - 1
    wide = col_q2.shape[2]
    q2, q3 = [own.at[:, pl.ds(0, wide)] for own in (own2, own3)]
    o2, o3 = [own.at[:, pl.ds(wide, own.shape[1] - wide)] for own in (own2, own3)]
    q1 = PlaneGather(place, col_q1, lambda v, u: full_q1.at[t, :, v, u], parts[0])
    o1 = LineGather(place, block_o1, full_o1.at[t], parts[1], to_core=full_o1.at[t])
    l2 = LineGather(place, q2, col_q2, parts[2])
    l3 = LineGather(place, q3, col_q3, parts[3])
    p2 = PlaneGather(place, o2, lambda v, u: block_o2.at[v, u], parts[4], cores=False)
    p3 = PlaneGather(place, o3, lambda v, u: block_o3.at[v, u], parts[5], cores=False)

    @pl.when(i == 0)
    def _():
        place.greet()

    at_step(0, (q1, 0), (o1, 0), (l2, 0), (l3, 0), (p2, 0), (p3, 0))
    at_step(2, (p2, 1), (p3, 1))
    at_step(3, (q1, 1), (o1, 1))
    at_step(4, (l2, 1), (l3, 1))
    at_step(5, *[(o1, k) for k in range(2, hops)], (p2, 2), (p2, 3), (p3, 2), (p3, 3))
    at_step(6, *[(job, k) for k in range(2, hops) for job in (l2, l3)])
    at_step(7, (o1, hops), (q1, 2))

    def here(f):
        return pltpu.make_async_copy(
            slots.at[f % 2, pl.ds(groups * t, groups)], s_b.at[frames * t + f], ex_local.at[f]
        )

    def there(f):
        return remote(
            slots.at[f % 2, pl.ds(groups * (1 - t), groups)], s_b.at[frames * t + f], (ex_send, ex_recv), f, place.core
        )

    def sent(f):
        here(f).wait()
        left(there(f))

    s = spatial_forward(x_ref[0].astype(F32), w_ref, wo_ref, vec_ref, qkv_ref, mix_ref, p_ref, r_ref)

    @pl.when(i >= 2)
    def _():
        sent(i - 2)

    slots[i % 2] = s.reshape(slots.shape[1:])
    here(i).start()
    there(i).start()

    @pl.when(i == frames - 1)
    def _():
        l2.stage(hops)
        l3.stage(hops)
        q1.stage(3)
        o1.stage(hops + 1)
        for result, part in zip(results, landed):
            result[...] = part[...]
        sent(i - 1)
        sent(i)

        def body(f, _):
            arrived(there(f))
            return _

        lax.fori_loop(0, frames, body, 0)


def spatial_fwd(x, w, wo, vec, links=None):
    frames, _, D = x.shape
    cols = D // 2
    pairs = D // 128
    groups = PAD // 16
    in_specs = [
        pl.BlockSpec((1, PAD, D), lambda i: (i, 0, 0)),
        whole_spec(w.shape),
        whole_spec(wo.shape),
        whole_spec(vec.shape),
    ]
    out_specs = [
        pl.BlockSpec((1, PAD // 8, 8, D), lambda i: (i, 0, 0, 0)),
        pl.BlockSpec((1, 2, PAD, 3 * cols), lambda i: (i, 0, 0, 0)),
        pl.BlockSpec((1, 2, PAD, cols), lambda i: (i, 0, 0, 0)),
        pl.BlockSpec((1, pairs, 2 * PAD, PAD), lambda i: (i, 0, 0, 0)),
        pl.BlockSpec((1, 2 * PAD, 128), lambda i: (i, 0, 0)),
    ]
    out_shape = [
        struct((frames, PAD // 8, 8, D), F32),
        struct((frames, 2, PAD, 3 * cols), BF),
        struct((frames, 2, PAD, cols), BF),
        struct((frames, pairs, 2 * PAD, PAD), BF),
        struct((frames, 2 * PAD, 128), F32),
    ]
    args, scratch, lines, collective_id = [x, w, wo, vec], [], None, None
    if links is not None:
        col_q1, block_o1, own2, own3, lines, collective_id = links
        args += [col_q1, block_o1, own2, own3]
        in_specs += [whole_spec(v.shape) for v in args[4:]]
        out_specs[0] = any_spec()
        out_shape[0] = struct((2 * frames, groups, 8, D), F32)
        col, block = col_q1.shape, block_o1.shape
        out_specs += [any_spec()] * 2 + [whole_spec(col)] * 2 + [whole_spec(block)] * 2
        out_shape += [struct(full_shape(*col), BF), struct((2, lines) + block, BF)]
        out_shape += [struct(col, BF)] * 2 + [struct(block, BF)] * 2
        scratch = [pltpu.VMEM(col, BF)] * 2 + [pltpu.VMEM(block, BF)] * 2
        scratch += [pltpu.VMEM((2, PAD // 8, 8, D), F32)] + [dma_sems(frames)] * 3
        scratch += PlaneGather.scratch() + LineGather.scratch(lines) * 3 + PlaneGather.scratch() * 2
    return pl.pallas_call(
        functools.partial(spatial_fwd_kernel, lines),
        grid=(frames,),
        in_specs=in_specs,
        out_specs=out_specs,
        out_shape=out_shape,
        scratch_shapes=scratch,
        name="spatial_fwd",
        compiler_params=kernel_params(collective_id),
    )(*args)


SHARED = 4


def place_frame(i, ref, rows):
    for f in range(SHARED):
        @pl.when(i % SHARED == f)
        def _():
            ref[PATCHES * f : PATCHES * (f + 1)] = rows


def spatial_bwd_kernel(lines, *refs):
    linked = lines is not None
    ins, joins, outs, results, (gw_ref, go_ref), rest = take(
        refs, 9, 7 if linked else 0, 4, 7 if linked else 0, 2, len(refs))
    x_ref, up_ref, qkv_ref, mix_ref, p_ref, r_ref, w_ref, wo_ref, vec_ref = ins
    gx_ref, gbw_ref, gbo_ref, gv_ref = outs
    cols = wo_ref.shape[2]
    i = pl.program_id(0)
    last = pl.num_programs(0) - 1

    @pl.when(i == 0)
    def _():
        gw_ref[...] = jnp.zeros_like(gw_ref)
        go_ref[...] = jnp.zeros_like(go_ref)
        gv_ref[...] = jnp.zeros_like(gv_ref)

    if linked:
        out_a, gw1, go1, col2, col3, block2, block3 = joins
        out_ref, sum_q1, sum_o1, sum_q2, sum_q3, sum_o2, sum_o3 = results
        (col1, block1), rest = rest[:2], rest[2:]
        place = Place(lines)
        parts = take(rest, PlaneReduce.n_scratch, LineReduce.n_scratch, 4, 4, 4, 4, 4, 4)
        q1 = PlaneReduce(place, gw1, col1, parts[0])
        o1 = LineReduce(place, go1, block1.at[0], parts[1])
        l2 = LineSum(place, col2, sum_q2, parts[2])
        l3 = LineSum(place, col3, sum_q3, parts[3])
        p2 = PlaneSum(place, block2, sum_o2, parts[4])
        p3 = PlaneSum(place, block3, sum_o3, parts[5])

        @pl.when(i == 0)
        def _():
            place.greet()

        l1 = LineSum(place, col1, sum_q1, parts[6])
        p1 = PlaneSum(place, block1, sum_o1, parts[7])
        at_step(0, (q1, 0), (o1, 0), (l2, 0), (l3, 0), (p2, 0), (p3, 0))
        at_step(1, (q1, 1), (o1, 1), (l2, 1), (l3, 1))
        at_step(2, (p2, 1), (p3, 1), (o1, 2), *[(job, k) for k in range(2, lines - 1) for job in (l2, l3)])
        at_step(3, (q1, 2), (p2, 2), (p3, 2), (l2, lines - 1), (l3, lines - 1), *[(o1, k) for k in range(3, lines)])
        at_step(4, (q1, 3), (l1, 0), (o1, lines), (p1, 0))
        at_step(5, (l1, 1), (p1, 1))
        at_step(6, (p1, 2), *[(l1, k) for k in range(2, lines - 1)])
        at_step(7, (l1, lines - 1))
        place_frame(i, rest[-1], out_a[0].reshape(PAD, out_a.shape[3])[:PATCHES])

        @pl.when(i % SHARED == SHARED - 1)
        def _():
            out_ref[...] = rest[-1][...].astype(BF)

    up = up_ref[0].reshape(PAD, up_ref.shape[3])
    gx = attn_back_common(
        x_ref[0].astype(F32), up.astype(BF), up, w_ref, wo_ref, vec_ref, 0, 10,
        lambda g: mix_ref[0, g],
        lambda g, j, rs: tuple(
            qkv_ref[0, g, :, cols * t + 128 * j : cols * t + 128 * (j + 1)] for t in range(3)
        ),
        lambda pair, b: (p_ref[0, pair], r_ref[0, :, pair : pair + 1]),
        gw_ref, go_ref, gv_ref, cols, 1,
    )
    place_frame(i, gx_ref, gx[:PATCHES])

    @pl.when(i == last)
    def _():
        gbw_ref[...] = gw_ref[...].astype(BF)
        gbo_ref[...] = go_ref[...].astype(BF)


def spatial_bwd(x, up, qkv, mix, p, r, w, wo, vec, links=None):
    frames, _, D = x.shape
    cols = D // 2
    pairs = D // 128
    frame_spec = pl.BlockSpec((1, PAD // 8, 8, D), lambda i: (i, 0, 0, 0))
    in_specs = [
        pl.BlockSpec((1, PAD, D), lambda i: (i, 0, 0)),
        frame_spec,
        pl.BlockSpec((1, 2, PAD, 3 * cols), lambda i: (i, 0, 0, 0)),
        pl.BlockSpec((1, 2, PAD, cols), lambda i: (i, 0, 0, 0)),
        pl.BlockSpec((1, pairs, 2 * PAD, PAD), lambda i: (i, 0, 0, 0)),
        pl.BlockSpec((1, 2 * PAD, 128), lambda i: (i, 0, 0)),
        whole_spec(w.shape),
        whole_spec(wo.shape),
        whole_spec(vec.shape),
    ]
    live_spec = pl.BlockSpec((SHARED * PATCHES, D), lambda i: (i // SHARED, 0))
    out_specs = [live_spec, whole_spec(w.shape), whole_spec(wo.shape), whole_spec((8, D))]
    out_shape = [
        struct((frames * PATCHES, D), F32), struct(w.shape, BF), struct(wo.shape, BF), struct((8, D), F32)
    ]
    args = [x, up, qkv, mix, p, r, w, wo, vec]
    scratch, lines, collective_id = [pltpu.VMEM(w.shape, F32), pltpu.VMEM(wo.shape, F32)], None, None
    if links is not None:
        out_a, gw1, go1, col2, col3, block2, block3, lines, collective_id = links
        args += [out_a, gw1, go1, col2, col3, block2, block3]
        q_block, o_block = gw1.shape[4:], go1.shape[4:]
        in_specs += [frame_spec] + [any_spec()] * 2 + [whole_spec(v.shape) for v in args[-4:]]
        more = [
            struct(q_block, F32), struct((1,) + o_block, F32), struct(q_block, F32), struct(q_block, F32),
            struct((1,) + o_block, F32), struct((1,) + o_block, F32),
        ]
        out_specs += [live_spec] + [whole_spec(s.shape) for s in more]
        out_shape += [struct((frames * PATCHES, D), BF)] + more
        scratch += [pltpu.VMEM(col2.shape, BF), pltpu.VMEM(block2.shape, BF)]
        scratch += PlaneReduce.scratch(lines, q_block, BF) + LineReduce.scratch(lines, o_block, BF)
        scratch += LineSum.scratch(lines, q_block, BF) * 2 + PlaneSum.scratch(1, o_block, BF) * 2
        scratch += LineSum.scratch(lines, q_block, BF) + PlaneSum.scratch(1, o_block, BF)
        scratch += [pltpu.VMEM((SHARED * PATCHES, D), F32)]
    return pl.pallas_call(
        functools.partial(spatial_bwd_kernel, lines),
        grid=(frames,),
        in_specs=in_specs,
        out_specs=out_specs,
        out_shape=out_shape,
        scratch_shapes=scratch,
        name="spatial_bwd",
        compiler_params=kernel_params(collective_id),
    )(*args)


def group_rows(block, live):
    parts = []
    for b in range(block.shape[1]):
        rows = block[:, b].reshape(GROUP, block.shape[3])
        parts.append(rows if b == 0 else jnp.where(live(b), rows, 0.0))
    return jnp.concatenate(parts, axis=0)


def temporal_forward(x, w_ref, wo_ref, vec_ref, qkv_ref, mix_ref, p_ref, r_ref):
    cols = wo_ref.shape[2]
    n = x.shape[0]
    xhat, _ = norm_parts(x)
    normed = (xhat * vec_ref[11:12, :] + vec_ref[4:5, :]).astype(BF)
    mask = temporal_mask()
    branch = vec_ref[7:8, :]
    for g, (q, k, v) in enumerate(project(normed, w_ref, vec_ref, 4, cols)):
        qkv_ref[g, :, 0:cols] = q
        qkv_ref[g, :, cols : 2 * cols] = k
        qkv_ref[g, :, 2 * cols : 3 * cols] = v
        pairs = []
        for b in range(n // GROUP):
            rs = slice(GROUP * b, GROUP * (b + 1))
            for j in range(cols // 128):
                sl = slice(128 * j, 128 * (j + 1))
                pairs.append((q[rs, sl], k[rs, sl], v[rs, sl]))
        mixes, exps, recips = heads_forward(pairs, mask)
        blocks = []
        for b in range(n // GROUP):
            for j in range(cols // 128):
                pair, i = g * (cols // 128) + j, b * (cols // 128) + j
                p_ref[pair, 2 * GROUP * b : 2 * GROUP * (b + 1)] = exps[i]
                r_ref[2 * GROUP * b : 2 * GROUP * (b + 1), pair : pair + 1] = recips[i]
            blocks.append(jnp.concatenate(mixes[b * (cols // 128) : (b + 1) * (cols // 128)], axis=1))
        mix = jnp.concatenate(blocks, axis=0).astype(BF)
        mix_ref[g] = mix
        branch = branch + dot(mix, wo_ref[g], NT)
    return x + branch


def temporal_fwd_kernel(lines, groups, *refs):
    linked = lines is not None
    (x_ref, w_ref, wo_ref, vec_ref), joins, (s_ref, qkv_ref, mix_ref, p_ref, r_ref), results, *parts = take(
        refs, 4, 4 if linked else 0, 5, 4 if linked else 0, 3, 3, 3, 3)
    i = pl.program_id(0)
    if linked:
        col_q2, col_q3, block_o2, block_o3 = joins
        full_q2, full_q3, full_o2, full_o3 = results
        place = Place(lines)
        t, hops = place.t, lines - 1
        q2 = PlaneGather(place, col_q2, lambda v, u: full_q2.at[t, :, v, u], parts[0])
        q3 = PlaneGather(place, col_q3, lambda v, u: full_q3.at[t, :, v, u], parts[1])
        o2 = LineGather(place, block_o2, full_o2.at[t], parts[2], to_core=full_o2.at[t])
        o3 = LineGather(place, block_o3, full_o3.at[t], parts[3], to_core=full_o3.at[t])

        @pl.when(i == 0)
        def _():
            place.greet()

        at_step(0, (q2, 0), (o2, 0), (o3, 0))
        at_step(2, (q2, 1), (q3, 0))
        at_step(3, (o2, 1), (o3, 1))
        at_step(5, (q3, 1), *[(job, k) for k in range(2, hops) for job in (o2, o3)])
    x = group_rows(x_ref[...], lambda b: STEP_GROUPS * i + b < groups)
    s = temporal_forward(x, w_ref, wo_ref, vec_ref, qkv_ref, mix_ref, p_ref, r_ref)
    for b in range(STEP_GROUPS):
        s_ref[:, b] = s[GROUP * b : GROUP * (b + 1)].reshape(FRAMES, 8, s.shape[1])
    if linked:
        at_step(
            6, (q2, 2), (o2, hops), (o3, hops), (q2, 3), (o2, hops + 1), (o3, hops + 1), (q3, 2), (q3, 3)
        )


def temporal_specs(groups, D):
    cols = D // 2
    n = STEP_GROUPS * GROUP
    steps = -(-groups // STEP_GROUPS)
    pairs = D // 128
    stream = pl.BlockSpec((FRAMES, STEP_GROUPS, 8, D), lambda i: (0, i, 0, 0))
    specs = [
        pl.BlockSpec((2, n, 3 * cols), lambda i: (0, i, 0)),
        pl.BlockSpec((2, n, cols), lambda i: (0, i, 0)),
        pl.BlockSpec((pairs, 2 * n, GROUP), lambda i: (0, i, 0)),
        pl.BlockSpec((2 * n, 128), lambda i: (i, 0)),
    ]
    shapes = [
        struct((2, steps * n, 3 * cols), BF),
        struct((2, steps * n, cols), BF),
        struct((pairs, 2 * steps * n, GROUP), BF),
        struct((2 * steps * n, 128), F32),
    ]
    return steps, stream, specs, shapes


def temporal_fwd(x, w, wo, vec, links=None):
    groups, D = x.shape[1], x.shape[3]
    steps, stream, kept_specs, kept_shapes = temporal_specs(groups, D)
    in_specs = [stream, whole_spec(w.shape), whole_spec(wo.shape), whole_spec(vec.shape)]
    out_specs = [stream] + kept_specs
    out_shape = [struct(x.shape, F32)] + kept_shapes
    args, scratch, lines, collective_id = [x, w, wo, vec], [], None, None
    if links is not None:
        col_q2, col_q3, block_o2, block_o3, lines, collective_id = links
        args += [col_q2, col_q3, block_o2, block_o3]
        in_specs += [whole_spec(v.shape) for v in args[4:]]
        out_specs += [any_spec()] * 4
        out_shape += [struct(full_shape(*col_q2.shape), BF)] * 2 + [struct((2, lines) + block_o2.shape, BF)] * 2
        scratch = PlaneGather.scratch() * 2 + LineGather.scratch(lines) * 2
    return pl.pallas_call(
        functools.partial(temporal_fwd_kernel, lines, groups),
        grid=(steps,),
        in_specs=in_specs,
        out_specs=out_specs,
        out_shape=out_shape,
        scratch_shapes=scratch,
        name="temporal_fwd",
        compiler_params=kernel_params(collective_id),
    )(*args)


def temporal_bwd_kernel(lines, groups, *refs):
    linked = lines is not None
    ins, joins, outs, results, (gw_ref, go_ref), rest = take(
        refs, 9, 5 if linked else 0, 4, 5 if linked else 0, 2, len(refs))
    x_ref, up_ref, qkv_ref, mix_ref, p_ref, r_ref, w_ref, wo_ref, vec_ref = ins
    gx_ref, gbw_ref, gbo_ref, gv_ref = outs
    cols = wo_ref.shape[2]
    i = pl.program_id(0)
    steps = pl.num_programs(0)

    @pl.when(i == 0)
    def _():
        gw_ref[...] = jnp.zeros_like(gw_ref)
        go_ref[...] = jnp.zeros_like(go_ref)
        gv_ref[...] = jnp.zeros_like(gv_ref)

    if linked:
        out_b, gq2, gq3, go2, go3 = joins
        out_a, col2, col3, block2, block3 = results
        place = Place(lines)
        t = place.t
        frames = FRAMES // 2
        (slots, held, ex_send, ex_recv, ex_local), *parts = take(
            rest, 5, PlaneReduce.n_scratch, PlaneReduce.n_scratch, LineReduce.n_scratch, LineReduce.n_scratch)
        q2 = PlaneReduce(place, gq2, col2, parts[0])
        q3 = PlaneReduce(place, gq3, col3, parts[1])
        o2 = LineReduce(place, go2, block2.at[0], parts[2])
        o3 = LineReduce(place, go3, block3.at[0], parts[3])
        out_load = pltpu.make_async_copy(out_b.at[pl.ds(frames * t, frames)], held, ex_local.at[steps])
        out_here = pltpu.make_async_copy(held, out_a.at[:, pl.ds(groups * t, groups)], ex_local.at[steps])
        out_there = remote(
            out_b.at[pl.ds(frames * (1 - t), frames)], out_a.at[:, pl.ds(groups * t, groups)],
            (ex_send, ex_recv), steps, place.core,
        )

        @pl.when(i == 0)
        def _():
            place.greet()

        at_step(0, (q2, 0), (o2, 0), (q3, 0), (o3, 0))

        @pl.when(i == 2)
        def _():
            out_load.start()
            out_there.start()

        @pl.when(i == 3)
        def _():
            out_load.wait()
            out_here.start()

        at_step(1, (q2, 1))
        at_step(2, (o2, 1), (q3, 1), (o3, 1))
        at_step(4, (q2, 2), (o2, 2), (o3, 2))
        at_step(5, (q3, 2))
        at_step(6, (q2, 3), *[(job, k) for k in range(3, lines) for job in (o2, o3)])

    live = lambda b: STEP_GROUPS * i + b < groups
    x = group_rows(x_ref[...], live)
    up = group_rows(up_ref[...], live)
    gx = attn_back_common(
        x, up.astype(BF), up, w_ref, wo_ref, vec_ref, 4, 11,
        lambda g: mix_ref[g],
        lambda g, j, rs: tuple(
            qkv_ref[g, rs, cols * t + 128 * j : cols * t + 128 * (j + 1)] for t in range(3)
        ),
        lambda pair, b: (
            p_ref[pair, 2 * GROUP * b : 2 * GROUP * (b + 1)],
            r_ref[2 * GROUP * b : 2 * GROUP * (b + 1), pair : pair + 1],
        ),
        gw_ref, go_ref, gv_ref, cols, x.shape[0] // GROUP,
    )

    @pl.when(i == steps - 1)
    def _():
        gbw_ref[...] = gw_ref[...].astype(BF)
        gbo_ref[...] = go_ref[...].astype(BF)

    if not linked:
        for b in range(STEP_GROUPS):
            gx_ref[:, b] = gx[GROUP * b : GROUP * (b + 1)].reshape(FRAMES, 8, gx.shape[1])
        return

    tail = groups % STEP_GROUPS or STEP_GROUPS

    def target(s, count):
        return gx_ref.at[:, pl.ds(groups * t + STEP_GROUPS * s, count)]

    def here(s, count):
        part = slots.at[s % 2, pl.ds(frames * t, frames), pl.ds(0, count)]
        return pltpu.make_async_copy(part, target(s, count), ex_local.at[s])

    def there(s, count):
        part = slots.at[s % 2, pl.ds(frames * (1 - t), frames), pl.ds(0, count)]
        return remote(part, target(s, count), (ex_send, ex_recv), s, place.core)

    def sent(s, count):
        here(s, count).wait()
        left(there(s, count))

    @pl.when(i >= 2)
    def _():
        sent(i - 2, STEP_GROUPS)

    for b in range(STEP_GROUPS):
        slots[i % 2, :, b] = gx[GROUP * b : GROUP * (b + 1)].reshape(FRAMES, 8, gx.shape[1])

    @pl.when(i < steps - 1)
    def _():
        here(i, STEP_GROUPS).start()
        there(i, STEP_GROUPS).start()

    @pl.when(i == steps - 1)
    def _():
        here(i, tail).start()
        there(i, tail).start()
        o2.stage(lines)
        o3.stage(lines)
        q3.stage(3)
        out_here.wait()
        out_there.wait()
        sent(i - 1, STEP_GROUPS)
        sent(i, tail)

        def body(s, _):
            arrived(there(s, STEP_GROUPS))
            return _

        lax.fori_loop(0, steps - 1, body, 0)
        arrived(there(i, tail))


def temporal_bwd(x, up, qkv, mix, p, r, w, wo, vec, links=None):
    groups, D = x.shape[1], x.shape[3]
    steps, stream, kept_specs, _ = temporal_specs(groups, D)
    in_specs = [stream, stream] + kept_specs + [whole_spec(v.shape) for v in (w, wo, vec)]
    out_specs = [stream, whole_spec(w.shape), whole_spec(wo.shape), whole_spec((8, D))]
    out_shape = [struct(x.shape, F32), struct(w.shape, BF), struct(wo.shape, BF), struct((8, D), F32)]
    args = [x, up, qkv, mix, p, r, w, wo, vec]
    scratch, lines, collective_id = [pltpu.VMEM(w.shape, F32), pltpu.VMEM(wo.shape, F32)], None, None
    if links is not None:
        out_b, gq2, gq3, go2, go3, lines, collective_id = links
        args += [out_b, gq2, gq3, go2, go3]
        q_block, o_block = gq2.shape[4:], go2.shape[4:]
        in_specs += [any_spec()] * 5
        out_specs[0] = any_spec()
        a_shape = (FRAMES // 2, 2 * groups, 8, D)
        out_shape[0] = struct(a_shape, F32)
        more = [struct((lines,) + q_block, BF)] * 2 + [struct((1, 2, 2) + o_block, BF)] * 2
        out_specs += [any_spec()] + [whole_spec(s.shape) for s in more]
        out_shape += [struct(a_shape, F32)] + more
        scratch += [pltpu.VMEM((2, FRAMES, STEP_GROUPS, 8, D), F32), pltpu.VMEM((FRAMES // 2, groups, 8, D), F32)]
        scratch += [dma_sems(steps + 1)] * 3
        scratch += PlaneReduce.scratch(lines, q_block, BF) * 2 + LineReduce.scratch(lines, o_block, BF) * 2
    return pl.pallas_call(
        functools.partial(temporal_bwd_kernel, lines, groups),
        grid=(steps,),
        in_specs=in_specs,
        out_specs=out_specs,
        out_shape=out_shape,
        scratch_shapes=scratch,
        name="temporal_bwd",
        compiler_params=kernel_params(collective_id),
    )(*args)


LAST_CUT = 768


def last_kernel(lines, *refs):
    (gq0, go0, tiles, sum_q1, sum_o1), mlp_parts, (grad_qkv, grad_out), mlp_grads, (grad_bias, grad_gain, grad_hidden), (
        sum_q0, sum_tile, col_a, col_b, col_tile, block0), *parts = take(
        refs, 5, 4, 2, 2, 3, 6, 9, 9, 9, 9, 4, 4, 4, 4)
    for n, grad in enumerate(mlp_grads):
        first, second = mlp_parts[2 * n : 2 * n + 2]
        grad[:, : first.shape[1]] = first[...]
        grad[:, first.shape[1] :] = second[0]
    sum_o0 = grad_out.at[pl.ds(0, 1)]
    grad_out[1] = sum_o1[0]
    place = Place(lines)
    place.greet()
    width = sum_q0.shape[1]
    qa = PlaneReduce(place, gq0, col_a, parts[0], pl.ds(0, LAST_CUT))
    qb = PlaneReduce(place, gq0, col_b, parts[1], pl.ds(LAST_CUT, width - LAST_CUT))
    small = PlaneReduce(place, tiles, col_tile, parts[2])
    o0 = LineReduce(place, go0, block0.at[0], parts[3])
    qa_line = LineSum(place, col_a, sum_q0.at[:, 0:LAST_CUT], parts[4])
    qb_line = LineSum(place, col_b, sum_q0.at[:, LAST_CUT:width], parts[5])
    small_line = LineSum(place, col_tile, sum_tile, parts[6])
    o0_plane = PlaneSum(place, block0, sum_o0, parts[7])
    n = lines
    o0.stage(0)
    qa.stage(0)
    qb.stage(0)
    small.stage(0)
    o0.stage(1)
    qa.stage(1)
    qb.stage(1)
    small.stage(1)
    o0.stage(2)
    qa.stage(2)
    small.stage(2)
    qb.stage(2)
    qa.stage(3)
    qa_line.stage(0)
    small.stage(3)
    small_line.stage(0)
    o0.stage(3)
    qb.stage(3)
    qb_line.stage(0)
    qa_line.stage(1)
    small_line.stage(1)
    for k in range(4, n + 1):
        o0.stage(k)
    o0_plane.stage(0)
    qb_line.stage(1)
    for k in range(2, n):
        qa_line.stage(k)
        small_line.stage(k)
        if k == 2:
            o0_plane.stage(1)
        qb_line.stage(k)
    o0_plane.stage(2)
    part = grad_qkv.shape[3]
    for n, total in enumerate((sum_q0, sum_q1)):
        for k in range(3):
            grad_qkv[n, k] = total[:, part * k : part * (k + 1)]
    grad_bias[...] = sum_tile[0:10, : grad_bias.shape[1]]
    grad_gain[...] = sum_tile[10:13, : grad_gain.shape[1]]
    grad_hidden[...] = sum_tile[16:17, : grad_hidden.shape[1]]


def last_call(gq0, go0, tiles, sum_q1, sum_o1, mlp_parts, share, lines, collective_id):
    q_block, o_block, tile = gq0.shape[4:], go0.shape[4:], tiles.shape[4:]
    rows, width = q_block
    cut_a, cut_b = (rows, LAST_CUT), (rows, width - LAST_CUT)
    whole_row = (rows, width + o_block[1])
    vmem = pl.BlockSpec(memory_space=pltpu.VMEM)
    return pl.pallas_call(
        functools.partial(last_kernel, lines),
        in_specs=[any_spec()] * 3 + [vmem] * 6,
        out_specs=[vmem] * 7,
        out_shape=[
            struct((2, 3, rows, width // 3), F32), struct((2,) + o_block, F32), struct(whole_row, F32),
            struct(whole_row, F32), struct((10, share), F32), struct((3, share), F32), struct((1, 4 * share), F32),
        ],
        scratch_shapes=[
            pltpu.VMEM(q_block, F32),
            pltpu.VMEM(tile, F32),
            pltpu.VMEM((lines,) + cut_a, BF),
            pltpu.VMEM((lines,) + cut_b, BF),
            pltpu.VMEM((lines,) + tile, F32),
            pltpu.VMEM((1, 2, 2) + o_block, BF),
        ]
        + PlaneReduce.scratch(lines, cut_a, BF)
        + PlaneReduce.scratch(lines, cut_b, BF)
        + PlaneReduce.scratch(lines, tile, F32)
        + LineReduce.scratch(lines, o_block, BF)
        + LineSum.scratch(lines, cut_a, BF)
        + LineSum.scratch(lines, cut_b, BF)
        + LineSum.scratch(lines, tile, F32)
        + PlaneSum.scratch(1, o_block, BF),
        name="last_reduce",
        compiler_params=kernel_params(collective_id),
    )(gq0, go0, tiles, sum_q1, sum_o1, *mlp_parts)


MLP_ROWS = 416
MLP_CHUNK = 1536
INV_SQRT2 = 0.7071067811865476
INV_SQRT2PI = 0.3989422804014327


def mlp_kernel(x_ref, cot_ref, wia, wib, woa, wob, vec_ref, hid_ref, out_ref, up_ref,
               gia, gib, goa, gob, gv_ref, gh_ref, wi_ref, wo_ref, ai_ref, ao_ref, dn_ref, sems):
    i = pl.program_id(0)
    last = pl.num_programs(0) - 1
    chunks = wi_ref.shape[0]
    per = chunks // 2
    wide, width = wia.shape[2], per * MLP_CHUNK

    def copies(table, out):
        found = []
        for vmem, first, second in table:
            for g in range(2):
                for c in range(per):
                    start, stop = MLP_CHUNK * c, MLP_CHUNK * (c + 1)
                    for array, low, high in ((first, 0, wide), (second, wide, width)):
                        lo, hi = max(start, low), min(stop, high)
                        if lo < hi:
                            here = vmem.at[g * per + c, :, pl.ds(lo - start, hi - lo)]
                            there = array.at[g, :, pl.ds(lo - low, hi - lo)]
                            sem = sems.at[int(out), len(found)]
                            found.append(pltpu.make_async_copy(*((here, there) if out else (there, here)), sem))
        return found

    @pl.when(i == 0)
    def _():
        loads = copies(((wi_ref, wia, wib), (wo_ref, woa, wob)), False)
        for copy in loads:
            copy.start()
        for ref in (ai_ref, ao_ref, gv_ref, gh_ref):
            ref[...] = jnp.zeros_like(ref)
        for copy in loads:
            copy.wait()

    x = x_ref[...]
    xhat, rstd = norm_parts(x)
    gain = vec_ref[12:13, :]
    normed = (xhat * gain + vec_ref[8:9, :]).astype(BF)
    up = cot_ref[...]
    ub = up.astype(BF)
    gv_ref[3:4, :] += jnp.sum(up, axis=0, keepdims=True)
    out_ref[...] = x + vec_ref[9:10, :]
    dn_ref[...] = jnp.zeros_like(dn_ref)

    def chunk(k, _):
        pre = dot(normed, wi_ref[k], NN) + hid_ref[k]
        cdf = 0.5 + 0.5 * lax.erf(pre * INV_SQRT2)
        act = (pre * cdf).astype(BF)
        out_ref[...] += dot(act, wo_ref[k], NT)
        ao_ref[k] += dot(ub, act, TN)
        dact = dot(ub, wo_ref[k], NN).astype(BF).astype(F32)
        slope = cdf + pre * (jnp.exp(pre * pre * -0.5) * INV_SQRT2PI)
        dpre = (dact * slope).astype(BF)
        gh_ref[k] += jnp.sum(dpre.astype(F32), axis=0, keepdims=True)
        ai_ref[k] += dot(normed, dpre, TN)
        dn_ref[...] += dot(dpre, wi_ref[k], NT)
        return _

    lax.fori_loop(0, chunks, chunk, 0)
    dn = dn_ref[...]
    gv_ref[0:1, :] += jnp.sum(dn, axis=0, keepdims=True)
    gv_ref[4:5, :] += jnp.sum(dn * xhat, axis=0, keepdims=True)
    up_ref[...] = up + norm_back(dn, xhat, rstd, gain)

    @pl.when(i == last)
    def _():
        def place(k, _):
            wi_ref[k] = ai_ref[k].astype(BF)
            wo_ref[k] = ao_ref[k].astype(BF)
            return _

        lax.fori_loop(0, chunks, place, 0)
        stores = copies(((wi_ref, gia, gib), (wo_ref, goa, gob)), True)
        for copy in stores:
            copy.start()
        for copy in stores:
            copy.wait()


def mlp_both(x, cot, wia, wib, woa, wob, vec, hidden):
    rows, D = x.shape
    width = hidden.shape[1]
    chunks = 2 * width // MLP_CHUNK
    row_spec = pl.BlockSpec((MLP_ROWS, D), lambda i: (i, 0))
    mats = [wia, wib, woa, wob]
    both = (chunks, D, MLP_CHUNK)
    units = (chunks, 1, MLP_CHUNK)
    outs = pl.pallas_call(
        mlp_kernel,
        grid=(rows // MLP_ROWS,),
        in_specs=[row_spec, row_spec] + [any_spec()] * 4 + [whole_spec(vec.shape), whole_spec(units)],
        out_specs=[row_spec, row_spec] + [any_spec()] * 4 + [whole_spec((8, D)), whole_spec(units)],
        out_shape=[struct((rows, D), F32)] * 2
        + [struct(m.shape, BF) for m in mats]
        + [struct((8, D), F32), struct(units, F32)],
        scratch_shapes=[pltpu.VMEM(both, BF)] * 2
        + [pltpu.VMEM(both, F32)] * 2
        + [pltpu.VMEM((MLP_ROWS, D), F32), pltpu.SemaphoreType.DMA((2, 6 * chunks))],
        name="mlp_both",
        compiler_params=kernel_params(None),
    )(x, cot, *mats, vec, hidden.reshape(units))
    return (*outs[:-1], outs[-1].reshape(hidden.shape))


def swap_to_patches(rows):
    return lax.all_to_all(rows, "tensor", split_axis=1, concat_axis=0, tiled=True)


def swap_to_frames(rows):
    return lax.all_to_all(rows, "tensor", split_axis=0, concat_axis=1, tiled=True)


def pad_frames(rows):
    D = rows.shape[1]
    return jnp.pad(rows.reshape(-1, PATCHES, D), ((0, 0), (0, PAD - PATCHES), (0, 0)))


def shards(tokens, cotangent, attn_qkv, attn_out, mlp_in, mlp_out, norm_gains, biases, hidden_bias):
    D = tokens.shape[1]
    depth = mlp_in.shape[1]
    cols = attn_qkv.shape[4]
    units = mlp_in.shape[2]
    frames = tokens.shape[0] // PATCHES
    everyone = ("dp", "tensor")
    chips = D // depth
    devices = 2 * chips
    share = D // devices
    wide = 3 * cols
    down = mlp_out[0].T

    def spread(gv_s, gv_t, gv_m, g_hidden):
        vec_grad = jnp.concatenate(
            [gv_s[0:4], gv_t[0:4], gv_m[0:1], gv_m[3:4], gv_s[4:5], gv_t[4:5], gv_m[4:5]]
        )
        return vec_grad.reshape(13, devices, share).transpose(1, 0, 2), g_hidden.reshape(devices, -1)

    flat = lambda w: w.reshape(2, D, w.shape[-1])
    rows_of = lambda v: v.reshape(-1, D)
    if depth % 16 == 0 and chips % 4 == 0:
        lines = chips // 4
        cut = lambda g: g.reshape(full_shape(lines, depth, g.shape[2]))
        x, cot, tiles, *w0, col_q1, block_o1 = first_call(
            tokens, cotangent, norm_gains[0], biases[0], hidden_bias,
            attn_qkv[0].transpose(0, 2, 1, 3), attn_out[0].transpose(0, 2, 1), lines, 1,
        )
        tiles = tiles.reshape((2, chips) + TILE)
        vec = tiles[:, :, :13, :share].transpose(2, 1, 0, 3).reshape(13, D)
        hidden = tiles[:, :, 16, : 2 * units // devices].transpose(1, 0, 2).reshape(2, units)
        w0 = [flat(w) for w in w0]
        x1, *kept_s, q1, o1, col_q2, col_q3, block_o2, block_o3 = spatial_fwd(
            x, *w0, vec, (col_q1, block_o1, mlp_in[0], down, lines, 2)
        )
        w1 = [flat(q1), flat(o1)]
        x2, *kept_t, q2, q3, o2, o3 = temporal_fwd(
            x1, *w1, vec, (col_q2, col_q3, block_o2, block_o3, lines, 3)
        )
        out_b, up2, gq2, go2, gq3, go3, gv_m, g_hidden = mlp_both(
            rows_of(x2), rows_of(cot), flat(q2), flat(o2), flat(q3), flat(o3), vec, hidden
        )
        up1, gq1, go1, gv_t, out_a, col2, col3, block2, block3 = temporal_bwd(
            x1, up2.reshape(x1.shape), *kept_t, *w1, vec,
            (out_b.reshape(x1.shape), cut(gq2), cut(gq3), cut(go2), cut(go3), lines, 4),
        )
        up0, gq0, go0, gv_s, output, gq1, go1, gq2, gq3, go2, go3 = spatial_bwd(
            x, up1, *kept_s, *w0, vec, (out_a, cut(gq1), cut(go1), col2, col3, block2, block3, lines, 5)
        )
        vec_grad, hidden_grad = spread(gv_s, gv_t, gv_m, g_hidden)
        place = lambda v, rows: jnp.pad(v, ((0, 0), (0, rows - v.shape[1]), (0, TILE[1] - v.shape[2])))
        tiles = jnp.concatenate([place(vec_grad, 16), place(hidden_grad[:, None], 8)], axis=1)
        tiles = tiles.reshape((chips, 2) + TILE).swapaxes(0, 1).reshape(full_shape(lines, *TILE))
        grad_qkv, grad_out, grad_in, grad_down, grad_biases, grad_gains, grad_hidden = last_call(
            cut(gq0), cut(go0), tiles, gq1, go1, (gq2, go2, gq3, go3), share, lines, 6
        )
        grad_qkv = grad_qkv.transpose(0, 2, 1, 3)
        grad_out = grad_out.transpose(0, 2, 1)
        grad_down = grad_down.T
    else:
        owns = []
        for s in range(2):
            owns += [attn_qkv[0, s].reshape(depth, wide), attn_out[0, s].T]
        owns += [mlp_in[0, :, :wide], mlp_in[0, :, wide:], down[:, :wide], down[:, wide:]]
        small = jnp.concatenate(
            [biases[0].reshape(-1), norm_gains[0].reshape(-1), hidden_bias[0].reshape(-1)]
        )
        small = lax.all_gather(small.reshape(1, -1), everyone, axis=0, tiled=True)
        vec = small[:, : 13 * share].reshape(devices, 13, share).transpose(1, 0, 2).reshape(13, D)
        hidden = small[:, 13 * share :].reshape(2, units)
        weights = [flat(lax.all_gather(w, ("tensor", "dp"), axis=0, tiled=True).reshape(2, D, -1)) for w in owns]
        x = pad_frames(tokens)
        fold = lambda v: v.reshape(frames, PAD // 8, 8, D)
        x1, *kept_s = spatial_fwd(x, *weights[0:2], vec)
        x1 = swap_to_patches(x1)
        x2, *kept_t = temporal_fwd(x1, *weights[2:4], vec)
        cot = swap_to_patches(fold(pad_frames(cotangent).astype(F32)))
        out_b, up2, *mlp_grads, gv_m, g_hidden = mlp_both(
            rows_of(x2), rows_of(cot), *weights[4:], vec, hidden
        )
        output = swap_to_frames(out_b.reshape(x1.shape)).reshape(frames, PAD, D)[:, :PATCHES].astype(BF)
        output = rows_of(output)
        up1, *grads1, gv_t = temporal_bwd(x1, up2.reshape(x1.shape), *kept_t, *weights[2:4], vec)
        up0, *grads0, gv_s = spatial_bwd(x, swap_to_frames(up1), *kept_s, *weights[0:2], vec)
        gq0, go0, gq1, go1, gq2, go2, gq3, go3 = [
            lax.psum_scatter(
                g.reshape(2 * D, g.shape[2]), ("tensor", "dp"), scatter_dimension=0, tiled=True
            ).astype(F32)
            for g in grads0 + grads1 + mlp_grads
        ]
        vec_grad, hidden_grad = spread(gv_s, gv_t, gv_m, g_hidden)
        small_grad = jnp.concatenate([vec_grad.reshape(devices, 13 * share), hidden_grad], axis=1)
        small_grad = lax.psum_scatter(small_grad, everyone, scatter_dimension=0, tiled=True)[0]
        grad_qkv = jnp.stack([gq0.reshape(depth, 3, cols), gq1.reshape(depth, 3, cols)])
        grad_out = jnp.stack([go0.T, go1.T])
        grad_in = jnp.concatenate([gq2, go2], axis=1)
        grad_down = jnp.concatenate([gq3, go3], axis=1).T
        grad_biases = small_grad[: 10 * share].reshape(10, share)
        grad_gains = small_grad[10 * share : 13 * share].reshape(3, share)
        grad_hidden = small_grad[13 * share :].reshape(1, -1)
    return (
        output,
        up0,
        grad_qkv[None],
        grad_out[None],
        grad_in[None],
        grad_down[None],
        grad_gains[None],
        grad_biases[None],
        grad_hidden,
    )


def solution(mesh):
    placed = (
        P(("dp", "tensor"), None),
        P(("dp", "tensor"), None),
        P(None, None, "dp", None, "tensor"),
        P(None, None, "tensor", "dp"),
        P(None, "dp", "tensor"),
        P(None, "tensor", "dp"),
        P(None, None, ("dp", "tensor")),
        P(None, None, ("dp", "tensor")),
        P(None, ("dp", "tensor")),
    )
    return jax.shard_map(
        shards, mesh=mesh, in_specs=placed, out_specs=placed, check_vma=False
    )
```
